32 devices in a mesh: batch: 4 (over y, core), ctx: 8 (over z, x).
Axes of the slice: x: 2, y: 2, z: 4, core: 2. Of those that a mesh axis runs over, the one named last changes fastest.
Arguments:
- tokens: bfloat16 [4, 1024, 1024], P('batch', 'ctx'), may hold values from -6 to 6
- cotangent: bfloat16 [4, 1024, 1024], P('batch', 'ctx'), may hold values from -6 to 6
- ln1_gain: bfloat16 [1024], P('batch'), may hold values from 0.099609375 to 1.8984375
- ln1_bias: bfloat16 [1024], P('batch'), may hold values from -3 to 3
- qkv_weight: bfloat16 [1024, 3072], P('batch'), may hold values from -0.1875 to 0.1875
- qv_bias: bfloat16 [2048], P('batch'), may hold values from -3 to 3
- proj_weight: bfloat16 [1024, 1024], P('batch'), may hold values from -0.5 to 0.5
- proj_bias: bfloat16 [1024], P('batch'), may hold values from -3 to 3
- ln2_gain: bfloat16 [1024], P('batch'), may hold values from 0.099609375 to 1.8984375
- ln2_bias: bfloat16 [1024], P('batch'), may hold values from -3 to 3
- fc_weight: bfloat16 [1024, 4096], P('batch'), may hold values from -0.1875 to 0.1875
- fc_bias: bfloat16 [4096], P('batch'), may hold values from -3 to 3
- out_weight: bfloat16 [4096, 1024], P('batch'), may hold values from -0.125 to 0.125
- out_bias: bfloat16 [1024], P('batch'), may hold values from -3 to 3
Outputs:
- layer_out: bfloat16 [4, 1024, 1024], P('batch', 'ctx')
- grad_tokens: bfloat16 [4, 1024, 1024], P('batch', 'ctx')
- grad_ln1_gain: float32 [1024], P('batch')
- grad_ln1_bias: float32 [1024], P('batch')
- grad_qkv_weight: float32 [1024, 3072], P('batch')
- grad_qv_bias: float32 [2048], P('batch')
- grad_proj_weight: float32 [1024, 1024], P('batch')
- grad_proj_bias: float32 [1024], P('batch')
- grad_ln2_gain: float32 [1024], P('batch')
- grad_ln2_bias: float32 [1024], P('batch')
- grad_fc_weight: float32 [1024, 4096], P('batch')
- grad_fc_bias: float32 [4096], P('batch')
- grad_out_weight: float32 [4096, 1024], P('batch')
- grad_out_bias: float32 [1024], P('batch')
The draws below stay inside these ranges and needn't reach their ends.
All inputs are finite; a program needn't handle non-finite values.
Results may differ from the reference program's by a relative error of at most 0.019.
Values may be sent and summed in bfloat16 or wider, within the bound.
A program may use at most 320 MiB of HBM per device.

```python
import math
from functools import partial
import jax
import jax.numpy as jnp
from jax import lax

D = 1024
HEADS = 16
HEAD_DIM = 64
FF = 4096
SEQS = 4
LENGTH = 1024


def level_of(rng, extent, pieces, least, top_value):
    gain, own = 1.0, jax.random.fold_in(rng, 6)
    for dim, parts in pieces:
        draws = jnp.exp(jax.random.uniform(jax.random.fold_in(own, dim), (parts,), jnp.float32, least / len(pieces), top_value / len(pieces)))
        gain = gain * jnp.repeat(draws, extent[dim] // parts).reshape([-1 if axis == dim else 1 for axis in range(len(extent))])
    return gain


def normal_values(own_key, extent, width, bound, pieces=(), dtype=jnp.bfloat16):
    drawn = jax.random.normal(own_key, extent, jnp.float32) * width
    if len(pieces) > 0:
        drawn = level_of(own_key, extent, pieces, -0.22, 0.18) * drawn
    return jnp.clip(drawn, min=-bound, max=bound).astype(dtype)


def setup_inputs(seed: int = 0) -> dict:
    keys = jax.random.split(jax.random.key(seed), 15)
    tokens = normal_values(keys[0], (SEQS, LENGTH, D), 1.0, 6.0, ((0, 4), (1, 8)))
    cotangent = normal_values(keys[1], (SEQS, LENGTH, D), 1.0, 6.0, ((0, 4), (1, 8)))
    ln1_gain = jnp.clip(1.0 + 0.18 * jax.random.normal(keys[2], (D,), jnp.float32), 0.099609375, 1.8984375).astype(jnp.bfloat16)
    ln1_bias = normal_values(keys[3], (D,), 0.3, 3.0, ((0, 4),))
    qkv_weight = normal_values(keys[4], (D, 3 * D), D ** -0.5, 0.1875, ((0, 4),))
    qv_bias = normal_values(keys[5], (2 * D,), 0.5, 3.0, ((0, 4),))
    proj_weight = normal_values(keys[6], (D, D), (D // 8) ** -0.5, 0.5, ((0, 4),))
    proj_bias = normal_values(keys[7], (D,), 0.3, 3.0, ((0, 4),))
    ln2_gain = jnp.clip(1.0 + 0.18 * jax.random.normal(keys[8], (D,), jnp.float32), 0.099609375, 1.8984375).astype(jnp.bfloat16)
    ln2_bias = normal_values(keys[9], (D,), 0.3, 3.0, ((0, 4),))
    fc_weight = normal_values(keys[10], (D, FF), D ** -0.5, 0.1875, ((0, 4),))
    fc_bias = normal_values(keys[11], (FF,), 0.5, 3.0, ((0, 4),))
    out_weight = normal_values(keys[12], (FF, D), (FF // 2) ** -0.5, 0.125, ((0, 4),))
    out_bias = normal_values(keys[13], (D,), 0.3, 3.0, ((0, 4),))
    return {"tokens": tokens, "cotangent": cotangent, "ln1_gain": ln1_gain, "ln1_bias": ln1_bias, "qkv_weight": qkv_weight, "qv_bias": qv_bias, "proj_weight": proj_weight, "proj_bias": proj_bias, "ln2_gain": ln2_gain, "ln2_bias": ln2_bias, "fc_weight": fc_weight, "fc_bias": fc_bias, "out_weight": out_weight, "out_bias": out_bias}


precise = lax.Precision.HIGHEST
epsilon = 1e-05
masked_value = -1e+30

@jax.custom_vjp
def low(v):
    return lax.optimization_barrier(v.astype(jnp.bfloat16)).astype(jnp.float32)

@jax.custom_vjp
def low_back(v):
    return v

def low_keep(v):
    return (low(v), None)

def low_pass(kept, grad):
    return (grad,)

def back_keep(v):
    return (v, None)

def back_low(kept, grad):
    return (low(grad),)
low.defvjp(low_keep, low_pass)
low_back.defvjp(back_keep, back_low)

def layer_norm(inputs, gain_vec, bias_vec):
    centre = inputs - lax.optimization_barrier(jnp.mean(inputs, -1, keepdims=True))
    spread = lax.optimization_barrier(jnp.mean(centre * centre, -1, keepdims=True))
    return centre * lax.rsqrt(spread + epsilon) * gain_vec + bias_vec

def matmul(left, right):
    return jnp.dot(left, right, precision=precise, preferred_element_type=jnp.float32)

def attend_block(query_block, key_all, value_all, block_start):
    block_rows = query_block.shape[0]
    scores = jnp.einsum('qhd,khd->hqk', query_block, key_all, precision=precise) * 0.125
    scores = low_back(scores)
    query_pos = block_start + jnp.arange(block_rows)
    key_pos = jnp.arange(key_all.shape[0])
    allowed = key_pos[None, :] <= query_pos[:, None]
    scores = jnp.where(allowed[None], scores, masked_value)
    probs = jax.nn.softmax(scores, axis=-1)
    return jnp.einsum('hqk,khd->qhd', low(probs), value_all, precision=precise)

def one_sequence(weights, seq_in):
    gain_one, bias_one, weight_qkv, bias_qv, weight_proj, bias_proj, gain_two, bias_two, weight_fc, bias_fc, weight_out, bias_out = weights
    norm_one = low(layer_norm(seq_in, gain_one, bias_one))
    bias_full = jnp.concatenate([bias_qv[:D], jnp.zeros((D,), jnp.float32), bias_qv[D:]])
    mixed_proj = low(low_back(matmul(norm_one, weight_qkv) + bias_full))
    query_heads = mixed_proj[:, :D].reshape(LENGTH, HEADS, HEAD_DIM)
    key_heads = mixed_proj[:, D:2 * D].reshape(LENGTH, HEADS, HEAD_DIM)
    value_heads = mixed_proj[:, 2 * D:].reshape(LENGTH, HEADS, HEAD_DIM)
    block_rows = math.gcd(LENGTH, 512)
    block_count = LENGTH // block_rows
    starts = jnp.arange(block_count) * block_rows
    query_blocks = query_heads.reshape(block_count, block_rows, HEADS, HEAD_DIM)

    def one_block(block_item):
        return attend_block(block_item[0], key_heads, value_heads, block_item[1])
    attended = lax.map(jax.checkpoint(one_block), (query_blocks, starts))
    attended_low = low(low_back(attended.reshape(LENGTH, D)))
    middle = seq_in + low_back(matmul(attended_low, weight_proj) + bias_proj)
    norm_two = low(layer_norm(middle, gain_two, bias_two))
    pre_act = low_back(matmul(norm_two, weight_fc) + bias_fc)
    hidden = low(jax.nn.gelu(pre_act, approximate=True))
    return middle + low_back(matmul(hidden, weight_out) + bias_out)

def reference(tokens, cotangent, ln1_gain, ln1_bias, qkv_weight, qv_bias, proj_weight, proj_bias, ln2_gain, ln2_bias, fc_weight, fc_bias, out_weight, out_bias):
    weights = tuple((item.astype(jnp.float32) for item in (ln1_gain, ln1_bias, qkv_weight, qv_bias, proj_weight, proj_bias, ln2_gain, ln2_bias, fc_weight, fc_bias, out_weight, out_bias)))

    def forward(inputs, params):
        return lax.map(jax.checkpoint(partial(one_sequence, params)), inputs)
    output, pull = jax.vjp(forward, tokens.astype(jnp.float32), weights)
    grad_in, grads = pull(cotangent.astype(jnp.float32))
    return (output.astype(jnp.bfloat16), grad_in.astype(jnp.bfloat16), grads[0], grads[1], grads[2], grads[3], grads[4], grads[5], grads[6], grads[7], grads[8], grads[9], grads[10], grads[11])
```

```python
from functools import partial
from types import SimpleNamespace

import jax
import jax.numpy as jnp
from jax import lax
from jax.experimental import pallas as pl
from jax.experimental.pallas import tpu as pltpu
from jax.sharding import PartitionSpec as P

HEADS = 16
HEAD_DIM = 64


epsilon = 1e-05
masked_value = -1e30


def shifted(block, axis, distance):
    devices = range(lax.axis_size(axis))
    route = [(i - distance, i) for i in devices if i - distance in devices]
    return lax.ppermute(block, axis, route)


def from_behind(block, axis, distance):
    devices = range(lax.axis_size(axis))
    route = [((i - distance) % len(devices), i) for i in devices]
    return lax.ppermute(block, axis, route)


def layer_norm(inputs, gain_vec, bias_vec):
    centre = inputs - jnp.mean(inputs, -1, keepdims=True)
    spread = jnp.mean(centre * centre, -1, keepdims=True)
    return centre * lax.rsqrt(spread + epsilon) * gain_vec + bias_vec


def keep_same(running):
    return running


def per_device(
    tokens,
    cotangent,
    ln1_gain,
    ln1_bias,
    qkv_weight,
    qv_bias,
    proj_weight,
    proj_bias,
    ln2_gain,
    ln2_bias,
    fc_weight,
    fc_bias,
    out_weight,
    out_bias,
):
    (
        gain_one,
        bias_one,
        weight_qkv,
        bias_qv,
        weight_proj,
        bias_proj,
        gain_two,
        bias_two,
        weight_fc,
        bias_fc,
        weight_out,
        bias_out,
    ) = (
        lax.all_gather(ln1_gain, "batch", axis=0, tiled=True),
        lax.all_gather(ln1_bias, "batch", axis=0, tiled=True),
        lax.all_gather(qkv_weight, "batch", axis=0, tiled=True),
        lax.all_gather(qv_bias, "batch", axis=0, tiled=True),
        lax.all_gather(proj_weight, "batch", axis=0, tiled=True),
        lax.all_gather(proj_bias, "batch", axis=0, tiled=True),
        lax.all_gather(ln2_gain, "batch", axis=0, tiled=True),
        lax.all_gather(ln2_bias, "batch", axis=0, tiled=True),
        lax.all_gather(fc_weight, "batch", axis=0, tiled=True),
        lax.all_gather(fc_bias, "batch", axis=0, tiled=True),
        lax.all_gather(out_weight, "batch", axis=0, tiled=True),
        lax.all_gather(out_bias, "batch", axis=0, tiled=True),
    )
    seq_count, ctx_rows, model_width = tokens.shape
    row_count = seq_count * ctx_rows
    inputs = tokens.astype(jnp.float32).reshape(row_count, model_width)
    norm_one, norm_one_pull = jax.vjp(
        layer_norm, inputs, gain_one.astype(jnp.float32), bias_one.astype(jnp.float32)
    )
    normed_low = norm_one.astype(jnp.bfloat16)
    bias_float = bias_qv.astype(jnp.float32)
    bias_full = jnp.concatenate(
        [bias_float[:model_width], jnp.zeros((model_width,), jnp.float32), bias_float[model_width:]]
    )
    mixed_proj = (
        jnp.dot(normed_low, weight_qkv, preferred_element_type=jnp.float32) + bias_full
    ).astype(jnp.bfloat16)
    query_flat = mixed_proj[:, :model_width].reshape(seq_count, ctx_rows, model_width)
    key_flat = mixed_proj[:, model_width : 2 * model_width].reshape(
        seq_count, ctx_rows, model_width
    )
    value_flat = mixed_proj[:, 2 * model_width :].reshape(seq_count, ctx_rows, model_width)
    query_heads = query_flat.reshape(seq_count, ctx_rows, HEADS, HEAD_DIM)
    own_index = lax.axis_index("ctx")
    position = own_index * ctx_rows
    query_pos = position + jnp.arange(ctx_rows, dtype=jnp.int32)
    last_pos = position + ctx_rows - 1
    start_state = (
        jnp.full((seq_count, ctx_rows, HEADS), masked_value, jnp.float32),
        jnp.zeros((seq_count, ctx_rows, HEADS), jnp.float32),
        jnp.zeros((seq_count, ctx_rows, HEADS, HEAD_DIM), jnp.float32),
    )
    key_piece = lax.all_gather(key_flat, "ctx", axis=1, tiled=True)
    value_piece = lax.all_gather(value_flat, "ctx", axis=1, tiled=True)
    piece_rows = key_piece.shape[1]

    def compute(running):
        run_max, run_sum, accum = running
        key_split = key_piece.reshape(seq_count, piece_rows, HEADS, HEAD_DIM)
        value_split = value_piece.reshape(seq_count, piece_rows, HEADS, HEAD_DIM)
        scores = (
            jnp.einsum(
                "bqhd,bkhd->bqhk", query_heads, key_split, preferred_element_type=jnp.float32
            )
            * 0.125
        )
        key_pos = jnp.arange(piece_rows, dtype=jnp.int32)
        allowed = (key_pos[None, :] <= query_pos[:, None])[None, :, None, :]
        scores = jnp.where(allowed, scores, masked_value)
        new_max = jnp.maximum(run_max, jnp.max(scores, -1))
        weights_exp = jnp.where(allowed, jnp.exp(scores - new_max[..., None]), 0.0)
        new_sum = jnp.sum(weights_exp, -1)
        product = jnp.einsum(
            "bqhk,bkhd->bqhd",
            weights_exp.astype(jnp.bfloat16),
            value_split,
            preferred_element_type=jnp.float32,
        )
        return (new_max, new_sum, product)

    run_max, run_sum, accum = lax.cond(jnp.int32(0) <= last_pos, compute, keep_same, start_state)
    log_total = run_max + jnp.log(run_sum)
    attended = accum / run_sum[..., None]
    attended_low = attended.reshape(row_count, model_width).astype(jnp.bfloat16)
    middle = (
        inputs
        + jnp.dot(attended_low, weight_proj, preferred_element_type=jnp.float32)
        + bias_proj.astype(jnp.float32)
    )
    norm_two, norm_two_pull = jax.vjp(
        layer_norm, middle, gain_two.astype(jnp.float32), bias_two.astype(jnp.float32)
    )
    normed_two = norm_two.astype(jnp.bfloat16)
    pre_act = jnp.dot(normed_two, weight_fc, preferred_element_type=jnp.float32) + bias_fc.astype(
        jnp.float32
    )
    activated, gelu_pull = jax.vjp(partial(jax.nn.gelu, approximate=True), pre_act)
    hidden_low = activated.astype(jnp.bfloat16)
    output = (
        middle
        + jnp.dot(hidden_low, weight_out, preferred_element_type=jnp.float32)
        + bias_out.astype(jnp.float32)
    )
    layer_out = output.astype(jnp.bfloat16).reshape(tokens.shape)
    grad_out = cotangent.reshape(row_count, model_width)
    grad_out_float = grad_out.astype(jnp.float32)
    grad_w_out = jnp.einsum("rf,rd->fd", hidden_low, grad_out, preferred_element_type=jnp.float32)
    grad_b_out = jnp.sum(grad_out_float, 0)
    grad_hidden = jnp.einsum("rd,fd->rf", grad_out, weight_out, preferred_element_type=jnp.float32)
    (grad_pre,) = gelu_pull(grad_hidden)
    grad_pre_low = grad_pre.astype(jnp.bfloat16)
    grad_w_fc = jnp.einsum(
        "rd,rf->df", normed_two, grad_pre_low, preferred_element_type=jnp.float32
    )
    grad_b_fc = jnp.sum(grad_pre_low.astype(jnp.float32), 0)
    grad_norm_two = jnp.einsum(
        "rf,df->rd", grad_pre_low, weight_fc, preferred_element_type=jnp.float32
    )
    grad_mid_norm, grad_g_two, grad_b_two = norm_two_pull(grad_norm_two)
    grad_middle = grad_out_float + grad_mid_norm
    grad_branch = grad_middle.astype(jnp.bfloat16)
    grad_w_proj = jnp.einsum(
        "rd,re->de", attended_low, grad_branch, preferred_element_type=jnp.float32
    )
    grad_b_proj = jnp.sum(grad_branch.astype(jnp.float32), 0)
    grad_attended = jnp.einsum(
        "re,de->rd", grad_branch, weight_proj, preferred_element_type=jnp.float32
    ).astype(jnp.bfloat16)
    grad_att_flat = grad_attended.reshape(seq_count, ctx_rows, model_width)
    grad_att_heads = grad_att_flat.reshape(seq_count, ctx_rows, HEADS, HEAD_DIM)
    delta_mine = jnp.sum(grad_att_heads.astype(jnp.float32) * attended, -1)
    zero_heads = jnp.zeros((seq_count, ctx_rows, HEADS, HEAD_DIM), jnp.float32)
    cycle_count = lax.axis_size("ctx")

    def cycle_turn(turn, state):
        owner = (own_index - turn) % cycle_count
        first_row = owner * ctx_rows

        def visit(inner):
            key_piece, value_piece, grad_k, grad_v, grad_q = inner
            key_split = key_piece.reshape(seq_count, ctx_rows, HEADS, HEAD_DIM)
            value_split = value_piece.reshape(seq_count, ctx_rows, HEADS, HEAD_DIM)
            piece_pos = first_row + jnp.arange(ctx_rows, dtype=jnp.int32)
            scores = (
                jnp.einsum(
                    "bqhd,bkhd->bqhk", query_heads, key_split, preferred_element_type=jnp.float32
                )
                * 0.125
            )
            allowed = (piece_pos[None, :] <= query_pos[:, None])[None, :, None, :]
            probs = jnp.where(allowed, jnp.exp(scores - log_total[..., None]), 0.0)
            grad_probs = jnp.einsum(
                "bqhd,bkhd->bqhk", grad_att_heads, value_split, preferred_element_type=jnp.float32
            )
            grad_scores = (probs * (grad_probs - delta_mine[..., None])).astype(jnp.bfloat16)
            grad_q = (
                grad_q
                + jnp.einsum(
                    "bqhk,bkhd->bqhd", grad_scores, key_split, preferred_element_type=jnp.float32
                )
                * 0.125
            )
            grad_k = (
                grad_k
                + jnp.einsum(
                    "bqhk,bqhd->bkhd", grad_scores, query_heads, preferred_element_type=jnp.float32
                )
                * 0.125
            )
            grad_v = grad_v + jnp.einsum(
                "bqhk,bqhd->bkhd",
                probs.astype(jnp.bfloat16),
                grad_att_heads,
                preferred_element_type=jnp.float32,
            )
            return (key_piece, value_piece, grad_k, grad_v, grad_q)

        key_piece, value_piece, grad_k, grad_v, grad_q = lax.cond(
            owner <= own_index, visit, keep_same, state
        )
        key_piece, value_piece = shifted((key_piece, value_piece), "ctx", 1)
        grad_k, grad_v = (
            from_behind(grad_k.astype(jnp.bfloat16), "ctx", 1).astype(grad_k.dtype),
            from_behind(grad_v.astype(jnp.bfloat16), "ctx", 1).astype(grad_v.dtype),
        )
        return (key_piece, value_piece, grad_k, grad_v, grad_q)

    cycle_state = lax.fori_loop(
        0, cycle_count, cycle_turn, (key_flat, value_flat, zero_heads, zero_heads, zero_heads)
    )
    grad_k, grad_v, grad_q = (cycle_state[2], cycle_state[3], cycle_state[4])
    grad_mixed = jnp.concatenate(
        [
            grad_q.reshape(row_count, model_width),
            grad_k.reshape(row_count, model_width),
            grad_v.reshape(row_count, model_width),
        ],
        axis=1,
    ).astype(jnp.bfloat16)
    grad_w_qkv = jnp.einsum("rd,re->de", normed_low, grad_mixed, preferred_element_type=jnp.float32)
    grad_bias_all = jnp.sum(grad_mixed.astype(jnp.float32), 0)
    grad_b_qv = jnp.concatenate([grad_bias_all[:model_width], grad_bias_all[2 * model_width :]])
    grad_norm_one = jnp.einsum(
        "re,de->rd", grad_mixed, weight_qkv, preferred_element_type=jnp.float32
    )
    grad_in_norm, grad_g_one, grad_b_one = norm_one_pull(grad_norm_one)
    grad_tokens = (grad_middle + grad_in_norm).astype(jnp.bfloat16).reshape(tokens.shape)
    local_grads = (
        grad_g_one,
        grad_b_one,
        grad_w_qkv,
        grad_b_qv,
        grad_w_proj,
        grad_b_proj,
        grad_g_two,
        grad_b_two,
        grad_w_fc,
        grad_b_fc,
        grad_w_out,
        grad_b_out,
    )
    partial_grads = (
        lax.psum_scatter(
            local_grads[0].astype(jnp.bfloat16), "batch", scatter_dimension=0, tiled=True
        ).astype(jnp.float32),
        lax.psum_scatter(
            local_grads[1].astype(jnp.bfloat16), "batch", scatter_dimension=0, tiled=True
        ).astype(jnp.float32),
        lax.psum_scatter(
            local_grads[2].astype(jnp.bfloat16), "batch", scatter_dimension=0, tiled=True
        ).astype(jnp.float32),
        lax.psum_scatter(
            local_grads[3].astype(jnp.bfloat16), "batch", scatter_dimension=0, tiled=True
        ).astype(jnp.float32),
        lax.psum_scatter(
            local_grads[4].astype(jnp.bfloat16), "batch", scatter_dimension=0, tiled=True
        ).astype(jnp.float32),
        lax.psum_scatter(
            local_grads[5].astype(jnp.bfloat16), "batch", scatter_dimension=0, tiled=True
        ).astype(jnp.float32),
        lax.psum_scatter(
            local_grads[6].astype(jnp.bfloat16), "batch", scatter_dimension=0, tiled=True
        ).astype(jnp.float32),
        lax.psum_scatter(
            local_grads[7].astype(jnp.bfloat16), "batch", scatter_dimension=0, tiled=True
        ).astype(jnp.float32),
        lax.psum_scatter(
            local_grads[8].astype(jnp.bfloat16), "batch", scatter_dimension=0, tiled=True
        ).astype(jnp.float32),
        lax.psum_scatter(
            local_grads[9].astype(jnp.bfloat16), "batch", scatter_dimension=0, tiled=True
        ).astype(jnp.float32),
        lax.psum_scatter(
            local_grads[10].astype(jnp.bfloat16), "batch", scatter_dimension=0, tiled=True
        ).astype(jnp.float32),
        lax.psum_scatter(
            local_grads[11].astype(jnp.bfloat16), "batch", scatter_dimension=0, tiled=True
        ).astype(jnp.float32),
    )
    summed_grads = lax.psum(
        (
            partial_grads[0],
            partial_grads[1],
            partial_grads[2],
            partial_grads[3],
            partial_grads[4],
            partial_grads[5],
            partial_grads[6],
            partial_grads[7],
            partial_grads[8],
            partial_grads[9],
            partial_grads[10],
            partial_grads[11],
        ),
        "ctx",
    )
    return (
        layer_out,
        grad_tokens,
        summed_grads[0],
        summed_grads[1],
        summed_grads[2],
        summed_grads[3],
        summed_grads[4],
        summed_grads[5],
        summed_grads[6],
        summed_grads[7],
        summed_grads[8],
        summed_grads[9],
        summed_grads[10],
        summed_grads[11],
    )


BF, F32 = jnp.bfloat16, jnp.float32
NN = (((1,), (0,)), ((), ()))
NT = (((1,), (1,)), ((), ()))
TN = (((0,), (0,)), ((), ()))
MESH = pl.DeviceIdType.MESH
NB, NC, WIDTH, ROWS, FF, PAIR = 4, 8, 1024, 128, 4096, 128
SHARD = WIDTH // NB
LENGTH = ROWS * NC
SMALL_ROWS = 16


def mm(left, right, dims=NN):
    return lax.dot_general(left, right, dims, preferred_element_type=F32)


def run(when, action):
    if when is None:
        action()
    else:
        pl.when(when)(action)


def both(one, two):
    return two if one is None else (one if two is None else jnp.logical_and(one, two))


class Net:
    def __init__(self, b, c, send_sems, recv_sems):
        self.b, self.c, self.z, self.x = b, c, c // 2, c % 2
        self.side = c + 1 - 2 * self.x
        self.core = b % 2
        self.sib = b + 1 - 2 * self.core
        self.across = lax.rem(b + 2, NB)
        self.diag = lax.rem(self.sib + 2, NB)
        self.send_sems, self.recv_sems = send_sems, recv_sems
        self.sent, self.taken, self.pending = 0, 0, []

    def slots(self, count):
        base = self.taken
        self.taken += count
        assert self.taken <= self.recv_sems.shape[0]
        return base

    def send(self, src, dst, device, slot, when=None):
        assert self.sent < self.send_sems.shape[0]
        copy = pltpu.make_async_remote_copy(
            src_ref=src,
            dst_ref=dst,
            send_sem=self.send_sems.at[self.sent],
            recv_sem=self.recv_sems.at[slot],
            device_id=device,
            device_id_type=MESH,
        )
        self.sent += 1
        run(when, copy.start)
        self.pending.append((when, copy))

    def wait(self, slot, ref):
        pltpu.make_async_remote_copy(
            src_ref=ref,
            dst_ref=ref,
            send_sem=self.send_sems.at[0],
            recv_sem=self.recv_sems.at[slot],
            device_id=(self.sib, self.c),
            device_id_type=MESH,
        ).wait_recv()

    def drain(self):
        for when, copy in self.pending:
            run(when, copy.wait_send)


class GatherCtx:
    def __init__(self, net, views, count):
        self.net, self.views, self.count = net, views, count
        self.along, self.beside = net.slots(4 * count), net.slots(4 * count)

    def hand_on(self, zz, srcs, up, down):
        net, count = self.net, self.count
        dsts = self.views(2 * zz + net.x)
        for i in range(count):
            if up is not False:
                net.send(srcs[i], dsts[i], (net.b, net.c + 2), self.along + zz * count + i, up)
            if down is not False:
                net.send(srcs[i], dsts[i], (net.b, net.c - 2), self.along + zz * count + i, down)

    def beside_send(self, zz, srcs, when):
        net, count = self.net, self.count
        dsts = self.views(2 * zz + net.x)
        for i in range(count):
            net.send(srcs[i], dsts[i], (net.b, net.side), self.beside + zz * count + i, when)

    def start(self, srcs):
        net = self.net
        self.hand_on(net.z, srcs, net.z < 3, net.z > 0)
        self.beside_send(net.z, srcs, None)

    def stage(self, d):
        net, count = self.net, self.count
        for sign in (-1, 1):
            zz = net.z + sign * d
            here = zz >= 0 if sign < 0 else zz <= 3
            refs = self.views(2 * zz + net.x)

            def arrive(refs=refs, zz=zz):
                for i in range(count):
                    net.wait(self.along + zz * count + i, refs[i])

            pl.when(here)(arrive)
            if d < 3:
                if sign < 0:
                    self.hand_on(zz, refs, both(here, net.z < 3), False)
                else:
                    self.hand_on(zz, refs, False, both(here, net.z > 0))
            self.beside_send(zz, refs, here)

    def finish(self):
        net, count = self.net, self.count
        for zz in range(4):
            refs = self.views(2 * zz + 1 - net.x)
            for i in range(count):
                net.wait(self.beside + zz * count + i, refs[i])


def chunks(ref):
    if len(ref.shape) == 3:
        return ref.shape[0], lambda i: (i,)
    rows = min(32, ref.shape[0])
    return ref.shape[0] // rows, lambda i: (pl.ds(pl.multiple_of(i * rows, rows), rows),)


def add_into(target, terms, dtype=BF):
    count, at = chunks(target)

    def body(i, carry):
        total = terms[0][at(i)].astype(F32)
        for term in terms[1:]:
            total = total + term[at(i)].astype(F32)
        target[at(i)] = total.astype(dtype)
        return carry

    lax.fori_loop(0, count, body, 0)


class ReduceCtx:
    def __init__(self, net, mine, beside, up, down):
        self.net, self.mine, self.beside, self.up, self.down = net, mine, beside, up, down
        self.s_beside, self.s_up, self.s_down = net.slots(4), net.slots(4), net.slots(4)

    def start(self, order=(3, 0, 2, 1)):
        net = self.net
        for zz in order:
            net.send(self.mine(2 * zz + 1 - net.x), self.beside.at[zz], (net.b, net.side), self.s_beside + zz)

    def fold(self, zz):
        net = self.net
        net.wait(self.s_beside + zz, self.beside.at[zz])
        add_into(self.mine(2 * zz + net.x), [self.mine(2 * zz + net.x), self.beside.at[zz]])

    def stage(self, d):
        net = self.net
        for sign in (1, -1):
            zz = net.z + sign * d
            here = zz <= 3 if sign > 0 else zz >= 0
            inner = net.z >= 1 if sign > 0 else net.z <= 2
            box, slot = (self.up, self.s_up) if sign > 0 else (self.down, self.s_down)
            mine = self.mine(2 * zz + net.x)

            def work(zz=zz, inner=inner, box=box, slot=slot, mine=mine):
                self.fold(zz)

                @pl.when(inner)
                def _():
                    net.wait(slot + zz, box.at[zz])
                    add_into(mine, [mine, box.at[zz]])

            pl.when(here)(work)
            net.send(mine, box.at[zz], (net.b, net.c + 2 * sign), slot + zz, here)

    def finish(self, target):
        net, z = self.net, self.net.z
        net.wait(self.s_beside + z, self.beside.at[z])
        mine, beside = self.mine(net.c), self.beside.at[z]

        @pl.when(z >= 1)
        def _():
            net.wait(self.s_up + z, self.up.at[z])

        @pl.when(z <= 2)
        def _():
            net.wait(self.s_down + z, self.down.at[z])

        pl.when(z == 0)(lambda: add_into(target, [mine, beside, self.down.at[z]]))
        pl.when(z == 3)(lambda: add_into(target, [mine, beside, self.up.at[z]]))
        pl.when(jnp.logical_and(z > 0, z < 3))(
            lambda: add_into(target, [mine, beside, self.up.at[z], self.down.at[z]])
        )


class SwapCtx:
    def __init__(self, net, src, dst, count):
        self.net, self.src, self.dst, self.count = net, src, dst, count
        self.base = net.slots(NC * count)

    def start(self):
        net, count = self.net, self.count
        for step in range(1, NC):
            j = lax.rem(net.c + step, NC)
            srcs, dsts = self.src(j), self.dst(net.c)
            for i in range(count):
                net.send(srcs[i], dsts[i], (net.b, j), self.base + net.c * count + i)
        for one, two in zip(self.src(net.c), self.dst(net.c)):
            two[...] = one[...]

    def finish(self):
        net, count = self.net, self.count
        for step in range(1, NC):
            j = lax.rem(net.c - step + NC, NC)
            dsts = self.dst(j)
            for i in range(count):
                net.wait(self.base + j * count + i, dsts[i])


class GatherBatch:
    def __init__(self, net, views, count=1):
        self.net, self.views, self.count = net, views, count
        self.base = net.slots(NB * count)

    def start(self, srcs):
        net = self.net
        dsts = self.views(net.b)
        for i in range(self.count):
            slot = self.base + net.b * self.count + i
            net.send(srcs[i], dsts[i], (net.across, net.c), slot)
        for i in range(self.count):
            slot = self.base + net.b * self.count + i
            net.send(srcs[i], dsts[i], (net.sib, net.c), slot)

    def relay(self):
        net = self.net
        refs = self.views(net.across)
        for i in range(self.count):
            slot = self.base + net.across * self.count + i
            net.wait(slot, refs[i])
            net.send(refs[i], refs[i], (net.sib, net.c), slot)

    def finish(self):
        net = self.net
        for j in (net.sib, net.diag):
            refs = self.views(j)
            for i in range(self.count):
                net.wait(self.base + j * self.count + i, refs[i])


class ReduceBatch:
    def __init__(self, net, mine, boxes):
        self.net, self.mine, self.boxes = net, mine, boxes
        self.base = net.slots(3)

    def give(self):
        net = self.net
        net.send(self.mine(net.diag), self.boxes.at[0], (net.sib, net.c), self.base)

    def cross(self):
        net = self.net
        net.wait(self.base, self.boxes.at[0])
        block = self.mine(net.across)
        add_into(block, [block, self.boxes.at[0]])
        net.send(block, self.boxes.at[1], (net.across, net.c), self.base + 1)

    def keep(self):
        net = self.net
        net.send(self.mine(net.sib), self.boxes.at[2], (net.sib, net.c), self.base + 2)

    def finish(self):
        net = self.net
        net.wait(self.base + 2, self.boxes.at[2])
        net.wait(self.base + 1, self.boxes.at[1])
        return [self.mine(net.b), self.boxes.at[1], self.boxes.at[2]]


def row_of(parts, index):
    return jnp.concatenate([parts[j, index : index + 1, :] for j in range(NB)], axis=1)


def put_row(target, index, row):
    for j in range(NB):
        target[j, index : index + 1, :] = row[:, j * SHARD : (j + 1) * SHARD]


def rows_of(block, size):
    return lambda j: block.at[pl.ds(pl.multiple_of(j * size, size), size)]


def normalise(inputs):
    centre = inputs - jnp.mean(inputs, -1, keepdims=True)
    spread = jnp.mean(centre * centre, -1, keepdims=True)
    scale = lax.rsqrt(spread + epsilon)
    return centre * scale, scale


def head_lanes(h, rows):
    lane = lax.broadcasted_iota(jnp.int32, (rows, PAIR), 1)
    return (lane >= h * HEAD_DIM) & (lane < (h + 1) * HEAD_DIM)


QB = 256


def scores_of(keys, query, masked):
    scores = mm(keys, query, NT) * 0.125
    if masked:
        key_pos = lax.broadcasted_iota(jnp.int32, scores.shape, 0)
        query_pos = lax.broadcasted_iota(jnp.int32, scores.shape, 1)
        scores = jnp.where(key_pos <= query_pos, scores, masked_value)
    return scores


def attend(mix, value_t, att, lse, work, low_work):
    value_t[...] = mix[:, 2 * PAIR :].astype(F32).T.astype(BF)
    for qb in range(LENGTH // QB):
        here = slice(qb * QB, (qb + 1) * QB)
        outs = []
        for h in range(2):
            query = jnp.where(head_lanes(h, QB), mix[here, :PAIR], jnp.zeros((), BF))
            top = None
            for kb in range(qb + 1):
                keys = slice(kb * QB, (kb + 1) * QB)
                scores = scores_of(mix[keys, PAIR : 2 * PAIR], query, kb == qb)
                work[h, keys, :] = scores
                peak = jnp.max(scores, axis=0, keepdims=True)
                top = peak if top is None else jnp.maximum(top, peak)
            total = None
            for kb in range(qb + 1):
                keys = slice(kb * QB, (kb + 1) * QB)
                grown = jnp.exp(work[h, keys, :] - top)
                part = jnp.sum(grown, axis=0, keepdims=True)
                total = part if total is None else total + part
                low_work[h, keys, :] = grown.astype(BF)
            count = (qb + 1) * QB
            lanes = slice(h * HEAD_DIM, (h + 1) * HEAD_DIM)
            out = mm(value_t[lanes, :count], low_work[h, :count, :])
            outs.append(out / total)
            lse[h * 4 + qb : h * 4 + qb + 1, :] = top + jnp.log(total)
        att[here, :] = jnp.concatenate(outs, axis=0).T.astype(BF)


def attend_back(mix, key_t, dout, lse, gmix, grad_k, grad_v, work, more, low_work, low_more):
    key_t[...] = mix[:, PAIR : 2 * PAIR].astype(F32).T.astype(BF)
    grad_k[...] = jnp.zeros_like(grad_k)
    grad_v[...] = jnp.zeros_like(grad_v)
    for qb in range(LENGTH // QB):
        here = slice(qb * QB, (qb + 1) * QB)
        outs = []
        count = (qb + 1) * QB
        for h in range(2):
            lanes = head_lanes(h, QB)
            query = jnp.where(lanes, mix[here, :PAIR], jnp.zeros((), BF))
            grad = jnp.where(lanes, dout[here, :], jnp.zeros((), BF))
            level = lse[h * 4 + qb : h * 4 + qb + 1, :]
            delta = None
            for kb in range(qb + 1):
                keys = slice(kb * QB, (kb + 1) * QB)
                probs = jnp.exp(scores_of(mix[keys, PAIR : 2 * PAIR], query, kb == qb) - level)
                grad_probs = mm(mix[keys, 2 * PAIR :], grad, NT)
                part = jnp.sum(probs * grad_probs, axis=0, keepdims=True)
                delta = part if delta is None else delta + part
                work[h, keys, :] = probs
                more[h, keys, :] = grad_probs
                low_work[h, keys, :] = probs.astype(BF)
            for kb in range(qb + 1):
                keys = slice(kb * QB, (kb + 1) * QB)
                low_more[h, keys, :] = (work[h, keys, :] * (more[h, keys, :] - delta)).astype(BF)
            grad_v[:count, :] += mm(low_work[h, :count, :], grad)
            grad_k[:count, :] += mm(low_more[h, :count, :], query)
            rows = slice(h * HEAD_DIM, (h + 1) * HEAD_DIM)
            outs.append(mm(key_t[rows, :count], low_more[h, :count, :]) * 0.125)
        gmix[here, :PAIR] = jnp.concatenate(outs, axis=0).T.astype(BF)
    gmix[:, PAIR : 2 * PAIR] = (grad_k[...] * 0.125).astype(BF)
    gmix[:, 2 * PAIR :] = grad_v[...].astype(BF)


gelu_scale = 0.7978845608028654
gelu_cubic = 0.044715


def gelu_pair(x):
    square = x * x
    bent = jnp.tanh(gelu_scale * x * (1.0 + gelu_cubic * square))
    half = 0.5 * (1.0 + bent)
    slope = half + 0.5 * x * (1.0 - bent * bent) * (gelu_scale * (1.0 + 3.0 * gelu_cubic * square))
    return x * half, slope


SCRATCH = dict(
    parts=((NB, SMALL_ROWS, SHARD), F32),
    qv_rows=((16, PAIR), F32),
    wpair=((WIDTH, 3 * PAIR), BF),
    wfull=((WIDTH, 3 * WIDTH), BF),
    wproj_all=((WIDTH, WIDTH), BF),
    wfc_mine=((WIDTH, WIDTH), BF),
    wout_mine=((WIDTH, WIDTH), BF),
    g_all=((NB * ROWS, WIDTH), BF),
    hat_one=((ROWS, WIDTH), F32),
    scale_one=((ROWS, 1), F32),
    n_one=((LENGTH, WIDTH), BF),
    mix=((LENGTH, 3 * PAIR), BF),
    turned=((PAIR, LENGTH), BF),
    att=((LENGTH, PAIR), BF),
    lse=((8, QB), F32),
    work=((2, LENGTH, QB), F32),
    more=((2, LENGTH, QB), F32),
    low_work=((2, LENGTH, QB), BF),
    low_more=((2, LENGTH, QB), BF),
    att_own=((ROWS, WIDTH), BF),
    middle=((ROWS, WIDTH), F32),
    hat_two=((ROWS, WIDTH), F32),
    scale_two=((ROWS, 1), F32),
    n_two=((NB * ROWS, WIDTH), BF),
    hidden=((NB * ROWS, WIDTH), BF),
    grad_pre=((NB * ROWS, WIDTH), BF),
    p_norm=((NB * ROWS, WIDTH), BF),
    p_norm_box=((3, ROWS, WIDTH), BF),
    p_layer=((NB * ROWS, WIDTH), BF),
    p_layer_box=((3, ROWS, WIDTH), BF),
    p_out=((WIDTH, WIDTH), BF),
    out_beside=((4, ROWS, WIDTH), BF),
    out_up=((4, ROWS, WIDTH), BF),
    out_down=((4, ROWS, WIDTH), BF),
    out_block=((ROWS, WIDTH), BF),
    p_fc=((NB, NC, 32, WIDTH), BF),
    fc_beside=((4, NB, 32, WIDTH), BF),
    fc_up=((4, NB, 32, WIDTH), BF),
    fc_down=((4, NB, 32, WIDTH), BF),
    fc_sum=((NB, 32, WIDTH), BF),
    fc_block=((32, FF), BF),
    p_proj=((WIDTH, WIDTH), BF),
    p_proj_box=((3, SHARD, WIDTH), BF),
    proj_sum=((SHARD, WIDTH), BF),
    proj_beside=((4, 32, WIDTH), BF),
    proj_up=((4, 32, WIDTH), BF),
    proj_down=((4, 32, WIDTH), BF),
    proj_block=((32, WIDTH), BF),
    grad_middle=((ROWS, WIDTH), F32),
    branch=((ROWS, WIDTH), BF),
    g_att=((ROWS, WIDTH), BF),
    dout=((LENGTH, PAIR), BF),
    gmix=((LENGTH, 3 * PAIR), BF),
    grad_k=((LENGTH, PAIR), F32),
    grad_v=((LENGTH, PAIR), F32),
    gmix_own=((ROWS, 3 * WIDTH), BF),
    p_qkv=((WIDTH, 3 * PAIR), BF),
    p_qkv_box=((3, SHARD, 3 * PAIR), BF),
    qkv_block=((SHARD, 3 * PAIR), BF),
    gn_one=((ROWS, WIDTH), F32),
    gs=((NB, SMALL_ROWS, SHARD), F32),
    gqv=((16, PAIR), F32),
    gs_box=((NB, SMALL_ROWS, SHARD), F32),
    gs_sum=((SMALL_ROWS, SHARD), F32),
    gs_far=((NC, SMALL_ROWS, SHARD), F32),
)
SENDS, RECVS, LOCALS = 320, 400, 24


def layer_kernel(
    tokens, cotangent, small, wqkv, wproj, wfc, wout,
    layer_out, grad_tokens, grad_small, o_qkv, o_proj, o_fc, o_out,
    *scratch, stop=99,
):
    s = SimpleNamespace(**dict(zip(SCRATCH, scratch)))
    send_sems, recv_sems, local_sems = scratch[len(SCRATCH) :]
    b, c = lax.axis_index("batch"), lax.axis_index("ctx")
    net = Net(b, c, send_sems, recv_sems)
    locals_open = []

    def local(src, dst):
        copy = pltpu.make_async_copy(src, dst, local_sems.at[len(locals_open)])
        copy.start()
        locals_open.append(copy)
        return copy

    def own(ref, size):
        return rows_of(ref, size)(b)

    def cols(ref, start):
        return ref.at[:, pl.ds(pl.multiple_of(start, 128), PAIR)]

    get_pair = [
        local(cols(wqkv, t * WIDTH + c * PAIR), own(s.wpair, SHARD).at[:, t * PAIR : (t + 1) * PAIR])
        for t in range(3)
    ]
    get_proj = local(wproj, own(s.wproj_all, SHARD))
    get_fc = local(wfc.at[:, pl.ds(pl.multiple_of(b * WIDTH, WIDTH), WIDTH)], own(s.wfc_mine, SHARD))
    get_out = local(wout, s.wout_mine)
    get_full = local(wqkv, own(s.wfull, SHARD))
    get_g = local(cotangent, own(s.g_all, ROWS))

    barrier = pltpu.get_barrier_semaphore()
    others = [(lax.rem(b + i, NB), c) for i in range(1, NB)]
    others += [(b, lax.rem(c + i, NC)) for i in range(1, NC)]
    for device in others:
        pl.semaphore_signal(barrier, inc=1, device_id=device, device_id_type=MESH)
    pl.semaphore_wait(barrier, len(others))

    small_slots, pair_slots, fc_slots = net.slots(NB), net.slots(NB * 3), net.slots(NB)
    for i in range(1, NB):
        j = lax.rem(b + i, NB)
        net.send(small, s.parts.at[b], (j, c), small_slots + b)
    for i in range(1, NB):
        j = lax.rem(b + i, NB)
        for t in range(3):
            net.send(
                cols(wqkv, t * WIDTH + c * PAIR),
                own(s.wpair, SHARD).at[:, t * PAIR : (t + 1) * PAIR],
                (j, c),
                pair_slots + b * 3 + t,
            )

    scale, hat = s.scale_one, s.hat_one

    def norm_rows(i, carry):
        at = pl.ds(pl.multiple_of(i * 32, 32), 32)
        hat[at, :], scale[at, :] = normalise(tokens[at, :].astype(F32))
        return carry

    lax.fori_loop(0, ROWS // 32, norm_rows, 0)
    s.parts[pl.ds(b, 1)] = small[...][None]
    for i in range(1, NB):
        j = lax.rem(b + i, NB)
        net.wait(small_slots + j, s.parts.at[j])
    gain, bias = row_of(s.parts, 0), row_of(s.parts, 1)
    n_mine = rows_of(s.n_one, ROWS)(c)

    def gain_rows(i, carry):
        at = pl.ds(pl.multiple_of(i * 32, 32), 32)
        n_mine[at, :] = (hat[at, :] * gain + bias).astype(BF)
        return carry

    lax.fori_loop(0, ROWS // 32, gain_rows, 0)
    gather_one = GatherCtx(net, lambda j: [rows_of(s.n_one, ROWS)(j)], 1)
    gather_one.start([n_mine])
    gather_g = GatherBatch(net, lambda j: [rows_of(s.g_all, ROWS)(j)])
    gather_g.start([cotangent])
    gather_proj = GatherBatch(net, lambda j: [rows_of(s.wproj_all, SHARD)(j)])
    gather_proj.start([wproj])
    for p in range(NC):
        at = p * PAIR
        row, lane = 2 + (at % 512) // SHARD, at % SHARD
        s.qv_rows[p : p + 1, :] = s.parts[at // 512, row : row + 1, lane : lane + PAIR]
        s.qv_rows[8 + p : 9 + p, :] = s.parts[2 + at // 512, row : row + 1, lane : lane + PAIR]
    gather_one.stage(1)
    for i in range(1, NB):
        j = lax.rem(b + i, NB)
        net.send(
            wfc.at[:, pl.ds(pl.multiple_of(j * WIDTH, WIDTH), WIDTH)],
            own(s.wfc_mine, SHARD),
            (j, c),
            fc_slots + b,
        )
    gather_one.stage(2)
    gather_g.relay()
    gather_one.stage(3)
    gather_one.finish()
    for copy in get_pair:
        copy.wait()
    for i in range(1, NB):
        j = lax.rem(b + i, NB)
        for t in range(3):
            net.wait(pair_slots + j * 3 + t, rows_of(s.wpair, SHARD)(j).at[:, t * PAIR : (t + 1) * PAIR])
    mix_bias = jnp.concatenate(
        [s.qv_rows[pl.ds(c, 1), :], jnp.zeros((1, PAIR), F32), s.qv_rows[pl.ds(8 + c, 1), :]], axis=1
    )

    def mix_rows(i, carry):
        at = pl.ds(pl.multiple_of(i * QB, QB), QB)
        s.mix[at, :] = (mm(s.n_one[at, :], s.wpair[...]) + mix_bias).astype(BF)
        return carry

    lax.fori_loop(0, LENGTH // QB, mix_rows, 0)
    gather_proj.relay()

    attend(s.mix, s.turned, s.att, s.lse, s.work, s.low_work)
    swap_att = SwapCtx(
        net, lambda j: [rows_of(s.att, ROWS)(j)], lambda j: [cols(s.att_own, j * PAIR)], 1
    )
    swap_att.start()
    get_proj.wait()
    gather_proj.finish()
    swap_att.finish()
    proj_bias = row_of(s.parts, 4)

    def middle_cols(i, carry):
        at = pl.ds(pl.multiple_of(i * 256, 256), 256)
        s.middle[:, at] = mm(s.att_own[...], s.wproj_all[:, at]) + tokens[:, at].astype(F32)
        return carry

    lax.fori_loop(0, WIDTH // 256, middle_cols, 0)
    gain_two, bias_two = row_of(s.parts, 5), row_of(s.parts, 6)
    n_two_mine = own(s.n_two, ROWS)

    def norm_two_rows(i, carry):
        at = pl.ds(pl.multiple_of(i * 32, 32), 32)
        middle = s.middle[at, :] + proj_bias
        s.middle[at, :] = middle
        norm, width = normalise(middle)
        s.hat_two[at, :], s.scale_two[at, :] = norm, width
        n_two_mine[at, :] = (norm * gain_two + bias_two).astype(BF)
        return carry

    lax.fori_loop(0, ROWS // 32, norm_two_rows, 0)

    def halves(ref, j):
        block = rows_of(ref, ROWS)(j)
        return [block.at[0:64], block.at[64:128]]

    gather_two = GatherBatch(net, lambda j: halves(s.n_two, j), 2)
    gather_two.start(halves(s.n_two, b))
    gather_two.relay()
    for copy in (get_fc, get_out, get_g, get_full):
        copy.wait()
    gather_g.finish()
    for i in range(1, NB):
        j = lax.rem(b + i, NB)
        net.wait(fc_slots + j, rows_of(s.wfc_mine, SHARD)(j))
    gather_two.finish()

    s.gs[...] = jnp.zeros_like(s.gs)
    for n in range(4):
        at = slice(n * 256, (n + 1) * 256)
        pre = mm(s.n_two[...], s.wfc_mine[:, at]) + small[7 + n : 8 + n, :]
        value, slope = gelu_pair(pre)
        s.hidden[:, at] = value.astype(BF)
        grad = (mm(s.g_all[...], s.wout_mine[at, :], NT) * slope).astype(BF)
        s.grad_pre[:, at] = grad
        s.gs[pl.ds(b, 1), 7 + n : 8 + n, :] = jnp.sum(grad.astype(F32), 0, keepdims=True)[None]

    reduce_out = ReduceCtx(net, rows_of(s.p_out, ROWS), s.out_beside, s.out_up, s.out_down)

    def out_rows(i, carry):
        at = pl.ds(pl.multiple_of(i * 256, 256), 256)
        s.p_out[at, :] = mm(s.hidden[:, at], s.g_all[...], TN).astype(BF)
        return carry

    lax.fori_loop(0, 4, out_rows, 0)
    reduce_out.start()

    reduce_norm = ReduceBatch(net, rows_of(s.p_norm, ROWS), s.p_norm_box)

    def norm_block(j):
        at = pl.ds(pl.multiple_of(j * ROWS, ROWS), ROWS)
        s.p_norm[at, :] = mm(s.grad_pre[at, :], s.wfc_mine[...], NT).astype(BF)

    norm_block(net.diag)
    reduce_norm.give()
    norm_block(net.across)
    reduce_norm.cross()
    norm_block(net.sib)
    reduce_norm.keep()
    norm_block(b)
    reduce_fc = ReduceCtx(net, lambda j: s.p_fc.at[:, j], s.fc_beside, s.fc_up, s.fc_down)

    def fc_rows(i, carry):
        at = pl.ds(pl.multiple_of(i * 256, 256), 256)
        s.p_fc[pl.ds(i, 1)] = (
            mm(s.n_two[:, at], s.grad_pre[...], TN).astype(BF).reshape(1, NC, 32, WIDTH)
        )
        return carry

    lax.fori_loop(0, 4, fc_rows, 0)
    terms = reduce_norm.finish()
    g_mine = own(s.g_all, ROWS)
    grad_gain, grad_bias, sum_branch, sum_g = [jnp.zeros((1, WIDTH), F32)] * 4

    def back_rows(i, carry):
        at = pl.ds(pl.multiple_of(i * 32, 32), 32)
        grad_gain, grad_bias, sum_branch, sum_g = carry
        grad = terms[0][at, :].astype(F32) + terms[1][at, :].astype(F32) + terms[2][at, :].astype(F32)
        norm = s.hat_two[at, :]
        scaled = grad * gain_two
        inner = scaled - jnp.mean(scaled, -1, keepdims=True)
        inner = inner - norm * jnp.mean(scaled * norm, -1, keepdims=True)
        g = g_mine[at, :].astype(F32)
        total = g + s.scale_two[at, :] * inner
        s.grad_middle[at, :] = total
        low = total.astype(BF)
        s.branch[at, :] = low
        return (
            grad_gain + jnp.sum(grad * norm, 0, keepdims=True),
            grad_bias + jnp.sum(grad, 0, keepdims=True),
            sum_branch + jnp.sum(low.astype(F32), 0, keepdims=True),
            sum_g + jnp.sum(g, 0, keepdims=True),
        )

    sums = lax.fori_loop(0, ROWS // 32, back_rows, (grad_gain, grad_bias, sum_branch, sum_g))
    put_row(s.gs, 5, sums[0])
    put_row(s.gs, 6, sums[1])
    put_row(s.gs, 4, sums[2])
    put_row(s.gs, 11, sums[3])

    def att_cols(i, carry):
        at = pl.ds(pl.multiple_of(i * 256, 256), 256)
        s.g_att[:, at] = mm(s.branch[...], s.wproj_all[at, :], NT).astype(BF)
        return carry

    lax.fori_loop(0, 4, att_cols, 0)
    swap_grad = SwapCtx(
        net, lambda j: [cols(s.g_att, j * PAIR)], lambda j: [rows_of(s.dout, ROWS)(j)], 1
    )
    swap_grad.start()

    reduce_layer = ReduceBatch(net, rows_of(s.p_layer, ROWS), s.p_layer_box)

    def layer_block(j):
        at = pl.ds(pl.multiple_of(j * ROWS, ROWS), ROWS)
        s.p_layer[at, :] = mm(s.hidden[at, :], s.wout_mine[...]).astype(BF)

    layer_block(net.diag)
    reduce_layer.give()
    layer_block(net.across)
    reduce_layer.cross()
    layer_block(net.sib)
    reduce_layer.keep()
    layer_block(b)
    reduce_proj = ReduceBatch(net, rows_of(s.p_proj, SHARD), s.p_proj_box)

    def proj_rows(i, carry):
        at = pl.ds(pl.multiple_of(i * 256, 256), 256)
        s.p_proj[at, :] = mm(s.att_own[:, at], s.branch[...], TN).astype(BF)
        return carry

    lax.fori_loop(0, 4, proj_rows, 0)
    reduce_proj.give()
    reduce_proj.cross()
    reduce_proj.keep()
    gather_full = GatherBatch(net, lambda j: [rows_of(s.wfull, SHARD)(j)])
    gather_full.start([wqkv])
    swap_grad.finish()

    attend_back(
        s.mix, s.turned, s.dout, s.lse, s.gmix, s.grad_k, s.grad_v, s.work, s.more, s.low_work, s.low_more
    )
    swap_mix = SwapCtx(
        net,
        lambda j: [rows_of(s.gmix, ROWS)(j).at[:, t * PAIR : (t + 1) * PAIR] for t in range(3)],
        lambda j: [cols(s.gmix_own, t * WIDTH + j * PAIR) for t in range(3)],
        3,
    )
    swap_mix.start()
    reduce_qkv = ReduceBatch(net, rows_of(s.p_qkv, SHARD), s.p_qkv_box)

    def qkv_block(j):
        at = pl.ds(pl.multiple_of(j * SHARD, SHARD), SHARD)
        s.p_qkv[at, :] = mm(s.n_one[:, at], s.gmix[...], TN).astype(BF)

    qkv_block(net.diag)
    reduce_qkv.give()
    qkv_block(net.across)
    reduce_qkv.cross()
    qkv_block(net.sib)
    reduce_qkv.keep()
    qkv_block(b)
    s.gqv[...] = jnp.zeros_like(s.gqv)
    s.gqv[pl.ds(c, 1), :] = jnp.sum(s.gmix[:, :PAIR].astype(F32), 0, keepdims=True)
    s.gqv[pl.ds(8 + c, 1), :] = jnp.sum(s.gmix[:, 2 * PAIR :].astype(F32), 0, keepdims=True)
    for p in range(NC):
        at = p * PAIR
        row, lane = 2 + (at % 512) // SHARD, at % SHARD
        s.gs[at // 512, row : row + 1, lane : lane + PAIR] = s.gqv[p : p + 1, :]
        s.gs[2 + at // 512, row : row + 1, lane : lane + PAIR] = s.gqv[8 + p : 9 + p, :]

    reduce_out.stage(3)
    reduce_out.stage(2)
    reduce_out.stage(1)
    reduce_out.finish(s.out_block)
    gather_out = GatherCtx(net, lambda j: [rows_of(o_out, ROWS)(j)], 1)
    gather_out.start([s.out_block])
    keep_out = local(s.out_block, rows_of(o_out, ROWS)(c))
    reduce_fc.start()
    gather_full.relay()

    layer_bias = row_of(s.parts, 11)
    terms = reduce_layer.finish()

    def layer_rows(i, carry):
        at = pl.ds(pl.multiple_of(i * 32, 32), 32)
        total = terms[0][at, :].astype(F32) + terms[1][at, :].astype(F32) + terms[2][at, :].astype(F32)
        layer_out[at, :] = (s.middle[at, :] + total + layer_bias).astype(BF)
        return carry

    lax.fori_loop(0, ROWS // 32, layer_rows, 0)
    terms = reduce_qkv.finish()
    add_into(s.qkv_block, terms)
    gather_qkv = GatherCtx(
        net, lambda j: [cols(o_qkv, t * WIDTH + j * PAIR) for t in range(3)], 3
    )
    qkv_parts = [s.qkv_block.at[:, t * PAIR : (t + 1) * PAIR] for t in range(3)]
    gather_qkv.start(qkv_parts)
    keep_qkv = [local(one, cols(o_qkv, t * WIDTH + c * PAIR)) for t, one in enumerate(qkv_parts)]
    add_into(s.proj_sum, reduce_proj.finish())
    reduce_part = ReduceCtx(net, rows_of(s.proj_sum, 32), s.proj_beside, s.proj_up, s.proj_down)
    reduce_part.start()

    gather_full.finish()
    swap_mix.finish()

    def one_cols(i, carry):
        at = pl.ds(pl.multiple_of(i * 256, 256), 256)
        s.gn_one[:, at] = mm(s.gmix_own[...], s.wfull[at, :], NT)
        return carry

    lax.fori_loop(0, 4, one_cols, 0)

    def token_rows(i, carry):
        at = pl.ds(pl.multiple_of(i * 32, 32), 32)
        grad_gain, grad_bias = carry
        grad, norm = s.gn_one[at, :], s.hat_one[at, :]
        scaled = grad * gain
        inner = scaled - jnp.mean(scaled, -1, keepdims=True)
        inner = inner - norm * jnp.mean(scaled * norm, -1, keepdims=True)
        grad_tokens[at, :] = (s.grad_middle[at, :] + s.scale_one[at, :] * inner).astype(BF)
        return (
            grad_gain + jnp.sum(grad * norm, 0, keepdims=True),
            grad_bias + jnp.sum(grad, 0, keepdims=True),
        )

    sums = lax.fori_loop(0, ROWS // 32, token_rows, (jnp.zeros((1, WIDTH), F32),) * 2)
    put_row(s.gs, 0, sums[0])
    put_row(s.gs, 1, sums[1])
    gs_slots, far_slots = net.slots(NB), net.slots(NC)
    for i in range(1, NB):
        j = lax.rem(b + i, NB)
        net.send(s.gs.at[j], s.gs_box.at[b], (j, c), gs_slots + b)

    reduce_part.stage(3)
    gather_out.stage(1)
    reduce_part.stage(2)
    reduce_fc.stage(3)
    reduce_part.stage(1)
    gather_out.stage(2)
    reduce_part.finish(s.proj_block)
    gather_part = GatherCtx(net, lambda j: [rows_of(o_proj, 32)(j)], 1)
    gather_part.start([s.proj_block])
    keep_part = local(s.proj_block, rows_of(o_proj, 32)(c))
    reduce_fc.stage(2)
    gather_out.stage(3)
    reduce_fc.stage(1)
    gather_qkv.stage(1)
    reduce_fc.finish(s.fc_sum)
    swap_slots = net.slots(NB)
    for i in range(1, NB):
        j = lax.rem(b + i, NB)
        net.send(
            s.fc_sum.at[j],
            s.fc_block.at[:, pl.ds(pl.multiple_of(b * WIDTH, WIDTH), WIDTH)],
            (j, c),
            swap_slots + b,
        )
    at = pl.ds(pl.multiple_of(b * WIDTH, WIDTH), WIDTH)
    s.fc_block[:, at] = s.fc_sum[pl.ds(b, 1)][0]
    gather_qkv.stage(2)
    total = s.gs[pl.ds(b, 1)][0]
    for i in range(1, NB):
        j = lax.rem(b + i, NB)
        net.wait(gs_slots + j, s.gs_box.at[j])
        total = total + s.gs_box[pl.ds(j, 1)][0]
    s.gs_sum[...] = total
    for i in range(1, NC):
        j = lax.rem(c + i, NC)
        net.send(s.gs_sum, s.gs_far.at[c], (b, j), far_slots + c)
    for i in range(1, NB):
        j = lax.rem(b + i, NB)
        net.wait(swap_slots + j, s.fc_block.at[:, pl.ds(pl.multiple_of(j * WIDTH, WIDTH), WIDTH)])
    gather_fc = GatherCtx(net, lambda j: [rows_of(o_fc, 32)(j)], 1)
    gather_fc.start([s.fc_block])
    keep_fc = local(s.fc_block, rows_of(o_fc, 32)(c))
    gather_part.stage(1)
    gather_qkv.stage(3)
    gather_part.stage(2)
    gather_part.stage(3)
    for i in range(1, NC):
        j = lax.rem(c - i + NC, NC)
        net.wait(far_slots + j, s.gs_far.at[j])
        total = total + s.gs_far[pl.ds(j, 1)][0]
    grad_small[...] = total
    gather_fc.stage(1)
    gather_fc.stage(2)
    gather_fc.stage(3)
    for gather in (gather_out, gather_qkv, gather_part, gather_fc):
        gather.finish()
    for copy in [keep_out, keep_part, keep_fc] + keep_qkv:
        copy.wait()
    net.drain()


def per_device_fast(
    tokens, cotangent, ln1_gain, ln1_bias, qkv_weight, qv_bias, proj_weight, proj_bias,
    ln2_gain, ln2_bias, fc_weight, fc_bias, out_weight, out_bias,
):
    small = jnp.concatenate(
        [ln1_gain, ln1_bias, qv_bias, proj_bias, ln2_gain, ln2_bias, fc_bias, out_bias,
         jnp.zeros((4 * SHARD,), BF)]
    ).astype(F32).reshape(SMALL_ROWS, SHARD)
    vmem, anywhere = pl.BlockSpec(memory_space=pltpu.VMEM), pl.BlockSpec(memory_space=pl.ANY)
    shape = jax.ShapeDtypeStruct
    layer, grad_in, grad_small, w_qkv, w_proj, w_fc, w_out = pl.pallas_call(
        layer_kernel,
        out_shape=(
            shape((ROWS, WIDTH), BF),
            shape((ROWS, WIDTH), BF),
            shape((SMALL_ROWS, SHARD), F32),
            shape((SHARD, 3 * WIDTH), BF),
            shape((SHARD, WIDTH), BF),
            shape((SHARD, FF), BF),
            shape((FF // NB, WIDTH), BF),
        ),
        in_specs=[vmem, vmem, vmem, anywhere, anywhere, anywhere, anywhere],
        out_specs=(vmem, vmem, vmem, anywhere, anywhere, anywhere, anywhere),
        scratch_shapes=[pltpu.VMEM(*item) for item in SCRATCH.values()]
        + [
            pltpu.SemaphoreType.DMA((SENDS,)),
            pltpu.SemaphoreType.DMA((RECVS,)),
            pltpu.SemaphoreType.DMA((LOCALS,)),
        ],
        compiler_params=pltpu.CompilerParams(
            collective_id=0, has_side_effects=True, vmem_limit_bytes=VMEM_BYTES
        ),
    )(
        tokens.reshape(ROWS, WIDTH), cotangent.reshape(ROWS, WIDTH), small,
        qkv_weight, proj_weight, fc_weight, out_weight,
    )
    flat = grad_small.reshape(-1)
    sizes = [SHARD, SHARD, 2 * SHARD, SHARD, SHARD, SHARD, 4 * SHARD, SHARD]
    smalls, at = [], 0
    for size in sizes:
        smalls.append(lax.slice(flat, (at,), (at + size,)))
        at += size
    return (
        layer.reshape(tokens.shape),
        grad_in.reshape(tokens.shape),
        smalls[0],
        smalls[1],
        w_qkv.astype(F32),
        smalls[2],
        w_proj.astype(F32),
        smalls[3],
        smalls[4],
        smalls[5],
        w_fc.astype(F32),
        smalls[6],
        w_out.astype(F32),
        smalls[7],
    )


VMEM_BYTES = 62 * 1024 * 1024


def solution(mesh):
    placed = (
        P("batch", "ctx", None),
        P("batch", "ctx", None),
        P("batch"),
        P("batch"),
        P("batch", None),
        P("batch"),
        P("batch", None),
        P("batch"),
        P("batch"),
        P("batch"),
        P("batch", None),
        P("batch"),
        P("batch", None),
        P("batch"),
    )
    fits = dict(mesh.shape) == {"batch": NB, "ctx": NC}
    return jax.shard_map(
        per_device_fast if fits else per_device,
        mesh=mesh,
        in_specs=placed,
        out_specs=(
            P("batch", "ctx", None),
            P("batch", "ctx", None),
            P("batch"),
            P("batch"),
            P("batch", None),
            P("batch"),
            P("batch", None),
            P("batch"),
            P("batch"),
            P("batch"),
            P("batch", None),
            P("batch"),
            P("batch", None),
            P("batch"),
        ),
        check_vma=False,
    )
```

```python
from functools import partial
from types import SimpleNamespace

import jax
import jax.numpy as jnp
from jax import lax
from jax.experimental import pallas as pl
from jax.experimental.pallas import tpu as pltpu
from jax.sharding import PartitionSpec as P

HEADS = 16
HEAD_DIM = 64


epsilon = 1e-05
masked_value = -1e30


def shifted(block, axis, distance):
    devices = range(lax.axis_size(axis))
    route = [(i - distance, i) for i in devices if i - distance in devices]
    return lax.ppermute(block, axis, route)


def from_behind(block, axis, distance):
    devices = range(lax.axis_size(axis))
    route = [((i - distance) % len(devices), i) for i in devices]
    return lax.ppermute(block, axis, route)


def layer_norm(inputs, gain_vec, bias_vec):
    centre = inputs - jnp.mean(inputs, -1, keepdims=True)
    spread = jnp.mean(centre * centre, -1, keepdims=True)
    return centre * lax.rsqrt(spread + epsilon) * gain_vec + bias_vec


def keep_same(running):
    return running


def per_device(
    tokens,
    cotangent,
    ln1_gain,
    ln1_bias,
    qkv_weight,
    qv_bias,
    proj_weight,
    proj_bias,
    ln2_gain,
    ln2_bias,
    fc_weight,
    fc_bias,
    out_weight,
    out_bias,
):
    (
        gain_one,
        bias_one,
        weight_qkv,
        bias_qv,
        weight_proj,
        bias_proj,
        gain_two,
        bias_two,
        weight_fc,
        bias_fc,
        weight_out,
        bias_out,
    ) = (
        lax.all_gather(ln1_gain, "batch", axis=0, tiled=True),
        lax.all_gather(ln1_bias, "batch", axis=0, tiled=True),
        lax.all_gather(qkv_weight, "batch", axis=0, tiled=True),
        lax.all_gather(qv_bias, "batch", axis=0, tiled=True),
        lax.all_gather(proj_weight, "batch", axis=0, tiled=True),
        lax.all_gather(proj_bias, "batch", axis=0, tiled=True),
        lax.all_gather(ln2_gain, "batch", axis=0, tiled=True),
        lax.all_gather(ln2_bias, "batch", axis=0, tiled=True),
        lax.all_gather(fc_weight, "batch", axis=0, tiled=True),
        lax.all_gather(fc_bias, "batch", axis=0, tiled=True),
        lax.all_gather(out_weight, "batch", axis=0, tiled=True),
        lax.all_gather(out_bias, "batch", axis=0, tiled=True),
    )
    seq_count, ctx_rows, model_width = tokens.shape
    row_count = seq_count * ctx_rows
    inputs = tokens.astype(jnp.float32).reshape(row_count, model_width)
    norm_one, norm_one_pull = jax.vjp(
        layer_norm, inputs, gain_one.astype(jnp.float32), bias_one.astype(jnp.float32)
    )
    normed_low = norm_one.astype(jnp.bfloat16)
    bias_float = bias_qv.astype(jnp.float32)
    bias_full = jnp.concatenate(
        [bias_float[:model_width], jnp.zeros((model_width,), jnp.float32), bias_float[model_width:]]
    )
    mixed_proj = (
        jnp.dot(normed_low, weight_qkv, preferred_element_type=jnp.float32) + bias_full
    ).astype(jnp.bfloat16)
    query_flat = mixed_proj[:, :model_width].reshape(seq_count, ctx_rows, model_width)
    key_flat = mixed_proj[:, model_width : 2 * model_width].reshape(
        seq_count, ctx_rows, model_width
    )
    value_flat = mixed_proj[:, 2 * model_width :].reshape(seq_count, ctx_rows, model_width)
    query_heads = query_flat.reshape(seq_count, ctx_rows, HEADS, HEAD_DIM)
    own_index = lax.axis_index("ctx")
    position = own_index * ctx_rows
    query_pos = position + jnp.arange(ctx_rows, dtype=jnp.int32)
    last_pos = position + ctx_rows - 1
    start_state = (
        jnp.full((seq_count, ctx_rows, HEADS), masked_value, jnp.float32),
        jnp.zeros((seq_count, ctx_rows, HEADS), jnp.float32),
        jnp.zeros((seq_count, ctx_rows, HEADS, HEAD_DIM), jnp.float32),
    )
    key_piece = lax.all_gather(key_flat, "ctx", axis=1, tiled=True)
    value_piece = lax.all_gather(value_flat, "ctx", axis=1, tiled=True)
    piece_rows = key_piece.shape[1]

    def compute(running):
        run_max, run_sum, accum = running
        key_split = key_piece.reshape(seq_count, piece_rows, HEADS, HEAD_DIM)
        value_split = value_piece.reshape(seq_count, piece_rows, HEADS, HEAD_DIM)
        scores = (
            jnp.einsum(
                "bqhd,bkhd->bqhk", query_heads, key_split, preferred_element_type=jnp.float32
            )
            * 0.125
        )
        key_pos = jnp.arange(piece_rows, dtype=jnp.int32)
        allowed = (key_pos[None, :] <= query_pos[:, None])[None, :, None, :]
        scores = jnp.where(allowed, scores, masked_value)
        new_max = jnp.maximum(run_max, jnp.max(scores, -1))
        weights_exp = jnp.where(allowed, jnp.exp(scores - new_max[..., None]), 0.0)
        new_sum = jnp.sum(weights_exp, -1)
        product = jnp.einsum(
            "bqhk,bkhd->bqhd",
            weights_exp.astype(jnp.bfloat16),
            value_split,
            preferred_element_type=jnp.float32,
        )
        return (new_max, new_sum, product)

    run_max, run_sum, accum = lax.cond(jnp.int32(0) <= last_pos, compute, keep_same, start_state)
    log_total = run_max + jnp.log(run_sum)
    attended = accum / run_sum[..., None]
    attended_low = attended.reshape(row_count, model_width).astype(jnp.bfloat16)
    middle = (
        inputs
        + jnp.dot(attended_low, weight_proj, preferred_element_type=jnp.float32)
        + bias_proj.astype(jnp.float32)
    )
    norm_two, norm_two_pull = jax.vjp(
        layer_norm, middle, gain_two.astype(jnp.float32), bias_two.astype(jnp.float32)
    )
    normed_two = norm_two.astype(jnp.bfloat16)
    pre_act = jnp.dot(normed_two, weight_fc, preferred_element_type=jnp.float32) + bias_fc.astype(
        jnp.float32
    )
    activated, gelu_pull = jax.vjp(partial(jax.nn.gelu, approximate=True), pre_act)
    hidden_low = activated.astype(jnp.bfloat16)
    output = (
        middle
        + jnp.dot(hidden_low, weight_out, preferred_element_type=jnp.float32)
        + bias_out.astype(jnp.float32)
    )
    layer_out = output.astype(jnp.bfloat16).reshape(tokens.shape)
    grad_out = cotangent.reshape(row_count, model_width)
    grad_out_float = grad_out.astype(jnp.float32)
    grad_w_out = jnp.einsum("rf,rd->fd", hidden_low, grad_out, preferred_element_type=jnp.float32)
    grad_b_out = jnp.sum(grad_out_float, 0)
    grad_hidden = jnp.einsum("rd,fd->rf", grad_out, weight_out, preferred_element_type=jnp.float32)
    (grad_pre,) = gelu_pull(grad_hidden)
    grad_pre_low = grad_pre.astype(jnp.bfloat16)
    grad_w_fc = jnp.einsum(
        "rd,rf->df", normed_two, grad_pre_low, preferred_element_type=jnp.float32
    )
    grad_b_fc = jnp.sum(grad_pre_low.astype(jnp.float32), 0)
    grad_norm_two = jnp.einsum(
        "rf,df->rd", grad_pre_low, weight_fc, preferred_element_type=jnp.float32
    )
    grad_mid_norm, grad_g_two, grad_b_two = norm_two_pull(grad_norm_two)
    grad_middle = grad_out_float + grad_mid_norm
    grad_branch = grad_middle.astype(jnp.bfloat16)
    grad_w_proj = jnp.einsum(
        "rd,re->de", attended_low, grad_branch, preferred_element_type=jnp.float32
    )
    grad_b_proj = jnp.sum(grad_branch.astype(jnp.float32), 0)
    grad_attended = jnp.einsum(
        "re,de->rd", grad_branch, weight_proj, preferred_element_type=jnp.float32
    ).astype(jnp.bfloat16)
    grad_att_flat = grad_attended.reshape(seq_count, ctx_rows, model_width)
    grad_att_heads = grad_att_flat.reshape(seq_count, ctx_rows, HEADS, HEAD_DIM)
    delta_mine = jnp.sum(grad_att_heads.astype(jnp.float32) * attended, -1)
    zero_heads = jnp.zeros((seq_count, ctx_rows, HEADS, HEAD_DIM), jnp.float32)
    cycle_count = lax.axis_size("ctx")

    def cycle_turn(turn, state):
        owner = (own_index - turn) % cycle_count
        first_row = owner * ctx_rows

        def visit(inner):
            key_piece, value_piece, grad_k, grad_v, grad_q = inner
            key_split = key_piece.reshape(seq_count, ctx_rows, HEADS, HEAD_DIM)
            value_split = value_piece.reshape(seq_count, ctx_rows, HEADS, HEAD_DIM)
            piece_pos = first_row + jnp.arange(ctx_rows, dtype=jnp.int32)
            scores = (
                jnp.einsum(
                    "bqhd,bkhd->bqhk", query_heads, key_split, preferred_element_type=jnp.float32
                )
                * 0.125
            )
            allowed = (piece_pos[None, :] <= query_pos[:, None])[None, :, None, :]
            probs = jnp.where(allowed, jnp.exp(scores - log_total[..., None]), 0.0)
            grad_probs = jnp.einsum(
                "bqhd,bkhd->bqhk", grad_att_heads, value_split, preferred_element_type=jnp.float32
            )
            grad_scores = (probs * (grad_probs - delta_mine[..., None])).astype(jnp.bfloat16)
            grad_q = (
                grad_q
                + jnp.einsum(
                    "bqhk,bkhd->bqhd", grad_scores, key_split, preferred_element_type=jnp.float32
                )
                * 0.125
            )
            grad_k = (
                grad_k
                + jnp.einsum(
                    "bqhk,bqhd->bkhd", grad_scores, query_heads, preferred_element_type=jnp.float32
                )
                * 0.125
            )
            grad_v = grad_v + jnp.einsum(
                "bqhk,bqhd->bkhd",
                probs.astype(jnp.bfloat16),
                grad_att_heads,
                preferred_element_type=jnp.float32,
            )
            return (key_piece, value_piece, grad_k, grad_v, grad_q)

        key_piece, value_piece, grad_k, grad_v, grad_q = lax.cond(
            owner <= own_index, visit, keep_same, state
        )
        key_piece, value_piece = shifted((key_piece, value_piece), "ctx", 1)
        grad_k, grad_v = (
            from_behind(grad_k.astype(jnp.bfloat16), "ctx", 1).astype(grad_k.dtype),
            from_behind(grad_v.astype(jnp.bfloat16), "ctx", 1).astype(grad_v.dtype),
        )
        return (key_piece, value_piece, grad_k, grad_v, grad_q)

    cycle_state = lax.fori_loop(
        0, cycle_count, cycle_turn, (key_flat, value_flat, zero_heads, zero_heads, zero_heads)
    )
    grad_k, grad_v, grad_q = (cycle_state[2], cycle_state[3], cycle_state[4])
    grad_mixed = jnp.concatenate(
        [
            grad_q.reshape(row_count, model_width),
            grad_k.reshape(row_count, model_width),
            grad_v.reshape(row_count, model_width),
        ],
        axis=1,
    ).astype(jnp.bfloat16)
    grad_w_qkv = jnp.einsum("rd,re->de", normed_low, grad_mixed, preferred_element_type=jnp.float32)
    grad_bias_all = jnp.sum(grad_mixed.astype(jnp.float32), 0)
    grad_b_qv = jnp.concatenate([grad_bias_all[:model_width], grad_bias_all[2 * model_width :]])
    grad_norm_one = jnp.einsum(
        "re,de->rd", grad_mixed, weight_qkv, preferred_element_type=jnp.float32
    )
    grad_in_norm, grad_g_one, grad_b_one = norm_one_pull(grad_norm_one)
    grad_tokens = (grad_middle + grad_in_norm).astype(jnp.bfloat16).reshape(tokens.shape)
    local_grads = (
        grad_g_one,
        grad_b_one,
        grad_w_qkv,
        grad_b_qv,
        grad_w_proj,
        grad_b_proj,
        grad_g_two,
        grad_b_two,
        grad_w_fc,
        grad_b_fc,
        grad_w_out,
        grad_b_out,
    )
    partial_grads = (
        lax.psum_scatter(
            local_grads[0].astype(jnp.bfloat16), "batch", scatter_dimension=0, tiled=True
        ).astype(jnp.float32),
        lax.psum_scatter(
            local_grads[1].astype(jnp.bfloat16), "batch", scatter_dimension=0, tiled=True
        ).astype(jnp.float32),
        lax.psum_scatter(
            local_grads[2].astype(jnp.bfloat16), "batch", scatter_dimension=0, tiled=True
        ).astype(jnp.float32),
        lax.psum_scatter(
            local_grads[3].astype(jnp.bfloat16), "batch", scatter_dimension=0, tiled=True
        ).astype(jnp.float32),
        lax.psum_scatter(
            local_grads[4].astype(jnp.bfloat16), "batch", scatter_dimension=0, tiled=True
        ).astype(jnp.float32),
        lax.psum_scatter(
            local_grads[5].astype(jnp.bfloat16), "batch", scatter_dimension=0, tiled=True
        ).astype(jnp.float32),
        lax.psum_scatter(
            local_grads[6].astype(jnp.bfloat16), "batch", scatter_dimension=0, tiled=True
        ).astype(jnp.float32),
        lax.psum_scatter(
            local_grads[7].astype(jnp.bfloat16), "batch", scatter_dimension=0, tiled=True
        ).astype(jnp.float32),
        lax.psum_scatter(
            local_grads[8].astype(jnp.bfloat16), "batch", scatter_dimension=0, tiled=True
        ).astype(jnp.float32),
        lax.psum_scatter(
            local_grads[9].astype(jnp.bfloat16), "batch", scatter_dimension=0, tiled=True
        ).astype(jnp.float32),
        lax.psum_scatter(
            local_grads[10].astype(jnp.bfloat16), "batch", scatter_dimension=0, tiled=True
        ).astype(jnp.float32),
        lax.psum_scatter(
            local_grads[11].astype(jnp.bfloat16), "batch", scatter_dimension=0, tiled=True
        ).astype(jnp.float32),
    )
    summed_grads = lax.psum(
        (
            partial_grads[0],
            partial_grads[1],
            partial_grads[2],
            partial_grads[3],
            partial_grads[4],
            partial_grads[5],
            partial_grads[6],
            partial_grads[7],
            partial_grads[8],
            partial_grads[9],
            partial_grads[10],
            partial_grads[11],
        ),
        "ctx",
    )
    return (
        layer_out,
        grad_tokens,
        summed_grads[0],
        summed_grads[1],
        summed_grads[2],
        summed_grads[3],
        summed_grads[4],
        summed_grads[5],
        summed_grads[6],
        summed_grads[7],
        summed_grads[8],
        summed_grads[9],
        summed_grads[10],
        summed_grads[11],
    )


BF, F32 = jnp.bfloat16, jnp.float32
NN = (((1,), (0,)), ((), ()))
NT = (((1,), (1,)), ((), ()))
TN = (((0,), (0,)), ((), ()))
MESH = pl.DeviceIdType.MESH
NB, NC, WIDTH, ROWS, FF, PAIR = 4, 8, 1024, 128, 4096, 128
SHARD = WIDTH // NB
LENGTH = ROWS * NC
SMALL_ROWS = 16


def mm(left, right, dims=NN):
    return lax.dot_general(left, right, dims, preferred_element_type=F32)


def run(when, action):
    if when is None:
        action()
    else:
        pl.when(when)(action)


def both(one, two):
    return two if one is None else (one if two is None else jnp.logical_and(one, two))


class Marks:
    def __init__(self):
        self.scope = None

    def __call__(self, name):
        if self.scope is not None:
            self.scope.__exit__(None, None, None)
        self.scope = None if name is None else jax.named_scope(name)
        if self.scope is not None:
            self.scope.__enter__()


class Net:
    def __init__(self, b, c, send_sems, recv_sems):
        self.b, self.c, self.z, self.x = b, c, c // 2, c % 2
        self.side = c + 1 - 2 * self.x
        self.core = b % 2
        self.sib = b + 1 - 2 * self.core
        self.across = lax.rem(b + 2, NB)
        self.diag = lax.rem(self.sib + 2, NB)
        self.send_sems, self.recv_sems = send_sems, recv_sems
        self.taken, self.pending = 0, []

    def slots(self, count):
        base = self.taken
        self.taken += count
        assert self.taken <= self.recv_sems.shape[0]
        return base

    def send(self, src, dst, device, slot, when=None):
        index = len(self.pending)
        if index == self.send_sems.shape[0]:
            done, copy, index = self.pending.pop(0)
            run(done, copy.wait_send)
        copy = pltpu.make_async_remote_copy(
            src_ref=src,
            dst_ref=dst,
            send_sem=self.send_sems.at[index],
            recv_sem=self.recv_sems.at[slot],
            device_id=device,
            device_id_type=MESH,
        )
        run(when, copy.start)
        self.pending.append((when, copy, index))

    def wait(self, slot, ref):
        pltpu.make_async_remote_copy(
            src_ref=ref,
            dst_ref=ref,
            send_sem=self.send_sems.at[0],
            recv_sem=self.recv_sems.at[slot],
            device_id=(self.sib, self.c),
            device_id_type=MESH,
        ).wait_recv()

    def drain(self):
        for when, copy, _ in self.pending:
            run(when, copy.wait_send)


class GatherCtx:
    def __init__(self, net, views, count, turn=False):
        self.net, self.views, self.count, self.turn = net, views, count, turn
        self.along, self.beside = net.slots(4 * count), net.slots(4 * count)
        self.turned = net.slots(2) if turn else None

    def begin(self, i, src):
        net, count = self.net, self.count
        dst, at = self.views(net.c)[i], net.z * count + i
        net.send(src, dst, (net.b, net.side), self.beside + at)
        net.send(src, dst, (net.b, net.c + 2), self.along + at, net.z < 3)
        net.send(src, dst, (net.b, net.c - 2), self.along + at, net.z > 0)

    def start(self, srcs):
        for i, src in enumerate(srcs):
            self.begin(i, src)

    def stage(self, d):
        net, count = self.net, self.count
        for sign in (-1, 1):
            zz = net.z + sign * d
            here = zz >= 0 if sign < 0 else zz <= 3
            refs = self.views(2 * zz + net.x)
            onward = both(here, net.z < 3 if sign < 0 else net.z > 0)
            dsts = self.views(2 * zz + net.x)
            for i in range(count):
                slot = self.along + zz * count + i
                pl.when(here)(lambda slot=slot, ref=refs[i]: net.wait(slot, ref))
                if d < 3:
                    net.send(refs[i], dsts[i], (net.b, net.c - 2 * sign), slot, onward)
                goes = here
                if self.turn and i == count - 1:
                    goes = both(here, jnp.logical_and(zz > 0, zz < 3))
                net.send(refs[i], dsts[i], (net.b, net.side), self.beside + zz * count + i, goes)
        if self.turn:
            if d == 1:
                self.corner()
            self.pass_on(d)

    def piece(self, end):
        return self.views(2 * end + 1 - self.net.x)[self.count - 1]

    def corner(self):
        net, count = self.net, self.count
        for end, step in ((0, 2), (3, -2)):
            ref, slot = self.piece(end), self.beside + end * count + count - 1
            pl.when(net.z == end)(lambda slot=slot, ref=ref: net.wait(slot, ref))
            net.send(ref, ref, (net.b, net.c + step), self.turned + (end > 0), net.z == end)

    def pass_on(self, d):
        net = self.net
        for end, step in ((0, 2), (3, -2)):
            here = net.z == (end + d if end == 0 else end - d)
            ref, slot = self.piece(end), self.turned + (end > 0)
            pl.when(here)(lambda slot=slot, ref=ref: net.wait(slot, ref))
            if d < 3:
                net.send(ref, ref, (net.b, net.c + step), slot, here)

    def finish(self):
        net, count = self.net, self.count
        for zz in range(4):
            refs = self.views(2 * zz + 1 - net.x)
            for i in range(count):
                if not (self.turn and i == count - 1 and zz in (0, 3)):
                    net.wait(self.beside + zz * count + i, refs[i])


def chunks(ref):
    if len(ref.shape) == 3:
        return ref.shape[0], lambda i: (i,)
    rows = min(32, ref.shape[0])
    return ref.shape[0] // rows, lambda i: (pl.ds(pl.multiple_of(i * rows, rows), rows),)


def add_into(target, terms, dtype=BF):
    count, at = chunks(target)

    def body(i, carry):
        total = terms[0][at(i)].astype(F32)
        for term in terms[1:]:
            total = total + term[at(i)].astype(F32)
        target[at(i)] = total.astype(dtype)
        return carry

    lax.fori_loop(0, count, body, 0)


class ReduceLine:
    def __init__(self, net, mine, up, down):
        self.net, self.mine, self.up, self.down = net, mine, up, down
        self.s_up, self.s_down = net.slots(4), net.slots(4)

    def give(self, k, upward, when):
        net = self.net
        if upward:
            net.send(self.mine(k), self.up.at[k], (net.b, net.c + 2), self.s_up + k, when)
        else:
            net.send(self.mine(k), self.down.at[k], (net.b, net.c - 2), self.s_down + k, when)

    def take(self, k, upward, when):
        box, slot = (self.up, self.s_up) if upward else (self.down, self.s_down)
        mine = self.mine(k)

        @pl.when(when)
        def _():
            self.net.wait(slot + k, box.at[k])
            add_into(mine, [mine, box.at[k]])

        self.give(k, upward, when)

    def launch(self):
        for k in (1, 2, 3):
            self.give(4 - k, True, self.net.z == 0)
            self.give(k - 1, False, self.net.z == 3)

    def pass_one(self):
        for k in (0, 1):
            self.take(3 - k, True, self.net.z == 1)
            self.take(k, False, self.net.z == 2)

    def pass_two(self):
        self.take(0, False, self.net.z == 1)
        self.take(3, True, self.net.z == 2)

    def finish(self, target):
        net, z = self.net, self.net.z
        mine = self.mine(z)

        @pl.when(z >= 1)
        def _():
            net.wait(self.s_up + z, self.up.at[z])

        @pl.when(z <= 2)
        def _():
            net.wait(self.s_down + z, self.down.at[z])

        pl.when(z == 0)(lambda: add_into(target, [mine, self.down.at[z]]))
        pl.when(z == 3)(lambda: add_into(target, [mine, self.up.at[z]]))
        pl.when(jnp.logical_and(z > 0, z < 3))(
            lambda: add_into(target, [mine, self.up.at[z], self.down.at[z]])
        )


class ReduceCtx:
    def __init__(self, net, mine, beside, up, down):
        self.net, self.mine, self.beside = net, mine, beside
        self.slots = net.slots(4)
        self.line = ReduceLine(net, lambda k: mine(2 * k + net.x), up, down)

    def start(self):
        net = self.net
        for k in (3, 0, 2, 1):
            net.send(self.mine(2 * k + 1 - net.x), self.beside.at[k], (net.b, net.side), self.slots + k)

    def fold(self):
        for k in (3, 0, 2, 1):
            self.net.wait(self.slots + k, self.beside.at[k])
            mine = self.line.mine(k)
            add_into(mine, [mine, self.beside.at[k]])
        self.line.launch()


class SwapCtx:
    def __init__(self, net, src, dst, count):
        self.net, self.src, self.dst, self.count = net, src, dst, count
        self.base = net.slots(NC * count)

    def give(self, j):
        net, count = self.net, self.count
        srcs, dsts = self.src(j), self.dst(net.c)
        for i in range(count):
            net.send(srcs[i], dsts[i], (net.b, j), self.base + net.c * count + i, net.c != j)

        @pl.when(net.c == j)
        def _():
            for one, two in zip(srcs, dsts):
                two[...] = one[...]

    def start(self):
        for j in range(NC):
            self.give(j)

    def finish(self):
        net, count = self.net, self.count
        for step in range(1, NC):
            j = lax.rem(net.c - step + NC, NC)
            dsts = self.dst(j)
            for i in range(count):
                net.wait(self.base + j * count + i, dsts[i])


class GatherSide:
    def __init__(self, net, views):
        self.net, self.views = net, views
        self.far, self.near = net.slots(NB), net.slots(NB)

    def give(self, j, src):
        net = self.net
        net.send(src, self.views(j), (net.b, net.side), self.far + j)

    def relay(self, j):
        net, ref = self.net, self.views(j)
        net.wait(self.far + j, ref)
        net.send(ref, ref, (net.sib, net.c), self.near + j)

    def finish(self):
        net = self.net
        for j in (net.sib, net.diag):
            net.wait(self.near + j, self.views(j))


class GatherBatch:
    def __init__(self, net, views, count=1):
        self.net, self.views, self.count = net, views, count
        self.base = net.slots(NB * count)

    def start(self, srcs):
        net = self.net
        dsts = self.views(net.b)
        for i in range(self.count):
            slot = self.base + net.b * self.count + i
            net.send(srcs[i], dsts[i], (net.across, net.c), slot)
        for i in range(self.count):
            slot = self.base + net.b * self.count + i
            net.send(srcs[i], dsts[i], (net.sib, net.c), slot)

    def relay(self):
        net = self.net
        refs = self.views(net.across)
        for i in range(self.count):
            slot = self.base + net.across * self.count + i
            net.wait(slot, refs[i])
            net.send(refs[i], refs[i], (net.sib, net.c), slot)

    def finish(self):
        net = self.net
        for j in (net.sib, net.diag):
            refs = self.views(j)
            for i in range(self.count):
                net.wait(self.base + j * self.count + i, refs[i])


class ReduceBatch:
    def __init__(self, net, mine, boxes):
        self.net, self.mine, self.boxes = net, mine, boxes
        self.base = net.slots(3)

    def give(self):
        net = self.net
        net.send(self.mine(net.diag), self.boxes.at[0], (net.sib, net.c), self.base)

    def cross(self):
        net = self.net
        net.wait(self.base, self.boxes.at[0])
        block = self.mine(net.across)
        add_into(block, [block, self.boxes.at[0]])
        net.send(block, self.boxes.at[1], (net.across, net.c), self.base + 1)

    def keep(self):
        net = self.net
        net.send(self.mine(net.sib), self.boxes.at[2], (net.sib, net.c), self.base + 2)

    def finish(self):
        net = self.net
        net.wait(self.base + 2, self.boxes.at[2])
        net.wait(self.base + 1, self.boxes.at[1])
        return [self.mine(net.b), self.boxes.at[1], self.boxes.at[2]]


def row_of(parts, index):
    return jnp.concatenate([parts[j, index : index + 1, :] for j in range(NB)], axis=1)


def put_row(target, index, row):
    for j in range(NB):
        target[j, index : index + 1, :] = row[:, j * SHARD : (j + 1) * SHARD]


def rows_of(block, size):
    return lambda j: block.at[pl.ds(pl.multiple_of(j * size, size), size)]


def normalise(inputs):
    centre = inputs - jnp.mean(inputs, -1, keepdims=True)
    spread = jnp.mean(centre * centre, -1, keepdims=True)
    scale = lax.rsqrt(spread + epsilon)
    return centre * scale, scale


def head_lanes(h, rows):
    lane = lax.broadcasted_iota(jnp.int32, (rows, PAIR), 1)
    return (lane >= h * HEAD_DIM) & (lane < (h + 1) * HEAD_DIM)


QB = 256


def scores_of(keys, query, masked):
    scores = mm(keys, query, NT) * 0.125
    if masked:
        key_pos = lax.broadcasted_iota(jnp.int32, scores.shape, 0)
        query_pos = lax.broadcasted_iota(jnp.int32, scores.shape, 1)
        scores = jnp.where(key_pos <= query_pos, scores, masked_value)
    return scores


def attend(mix, value_t, att, lse, work, low_work, ready):
    value_t[...] = mix[:, 2 * PAIR :].astype(F32).T.astype(BF)
    for qb in reversed(range(LENGTH // QB)):
        here = slice(qb * QB, (qb + 1) * QB)
        outs = []
        for h in range(2):
            query = jnp.where(head_lanes(h, QB), mix[here, :PAIR], jnp.zeros((), BF))
            top = None
            for kb in range(qb + 1):
                keys = slice(kb * QB, (kb + 1) * QB)
                scores = scores_of(mix[keys, PAIR : 2 * PAIR], query, kb == qb)
                work[h, keys, :] = scores
                peak = jnp.max(scores, axis=0, keepdims=True)
                top = peak if top is None else jnp.maximum(top, peak)
            total = None
            for kb in range(qb + 1):
                keys = slice(kb * QB, (kb + 1) * QB)
                grown = jnp.exp(work[h, keys, :] - top)
                part = jnp.sum(grown, axis=0, keepdims=True)
                total = part if total is None else total + part
                low_work[h, keys, :] = grown.astype(BF)
            count = (qb + 1) * QB
            lanes = slice(h * HEAD_DIM, (h + 1) * HEAD_DIM)
            out = mm(value_t[lanes, :count], low_work[h, :count, :])
            outs.append(out / total)
            lse[h * 4 + qb : h * 4 + qb + 1, :] = top + jnp.log(total)
        att[here, :] = jnp.concatenate(outs, axis=0).T.astype(BF)
        ready(qb)


def attend_back(mix, key_t, dout, lse, gmix, grad_k, grad_v, work, more, low_work, low_more, ready):
    key_t[...] = mix[:, PAIR : 2 * PAIR].astype(F32).T.astype(BF)
    grad_k[...] = jnp.zeros_like(grad_k)
    grad_v[...] = jnp.zeros_like(grad_v)
    for qb in reversed(range(LENGTH // QB)):
        here = slice(qb * QB, (qb + 1) * QB)
        outs = []
        count = (qb + 1) * QB
        for h in range(2):
            lanes = head_lanes(h, QB)
            query = jnp.where(lanes, mix[here, :PAIR], jnp.zeros((), BF))
            grad = jnp.where(lanes, dout[here, :], jnp.zeros((), BF))
            level = lse[h * 4 + qb : h * 4 + qb + 1, :]
            delta = None
            for kb in range(qb + 1):
                keys = slice(kb * QB, (kb + 1) * QB)
                probs = jnp.exp(scores_of(mix[keys, PAIR : 2 * PAIR], query, kb == qb) - level)
                grad_probs = mm(mix[keys, 2 * PAIR :], grad, NT)
                part = jnp.sum(probs * grad_probs, axis=0, keepdims=True)
                delta = part if delta is None else delta + part
                work[h, keys, :] = probs
                more[h, keys, :] = grad_probs
                low_work[h, keys, :] = probs.astype(BF)
            for kb in range(qb + 1):
                keys = slice(kb * QB, (kb + 1) * QB)
                low_more[h, keys, :] = (work[h, keys, :] * (more[h, keys, :] - delta)).astype(BF)
            grad_v[:count, :] += mm(low_work[h, :count, :], grad)
            grad_k[:count, :] += mm(low_more[h, :count, :], query)
            rows = slice(h * HEAD_DIM, (h + 1) * HEAD_DIM)
            outs.append(mm(key_t[rows, :count], low_more[h, :count, :]) * 0.125)
        gmix[here, :PAIR] = jnp.concatenate(outs, axis=0).T.astype(BF)
        gmix[here, PAIR : 2 * PAIR] = (grad_k[here, :] * 0.125).astype(BF)
        gmix[here, 2 * PAIR :] = grad_v[here, :].astype(BF)
        ready(qb)


gelu_scale = 0.7978845608028654
gelu_cubic = 0.044715


def gelu_pair(x):
    square = x * x
    bent = jnp.tanh(gelu_scale * x * (1.0 + gelu_cubic * square))
    half = 0.5 * (1.0 + bent)
    slope = half + 0.5 * x * (1.0 - bent * bent) * (gelu_scale * (1.0 + 3.0 * gelu_cubic * square))
    return x * half, slope


SCRATCH = dict(
    small=((SMALL_ROWS, SHARD), F32),
    parts=((NB, SMALL_ROWS, SHARD), F32),
    qv_rows=((16, PAIR), F32),
    wpair=((WIDTH, 3 * PAIR), BF),
    wfull=((WIDTH, 3 * WIDTH), BF),
    wproj_all=((WIDTH, WIDTH), BF),
    wfc_mine=((WIDTH, WIDTH), BF),
    wout_mine=((WIDTH, WIDTH), BF),
    g_all=((NB * ROWS, WIDTH), BF),
    hat_one=((ROWS, WIDTH), F32),
    scale_one=((ROWS, 1), F32),
    n_one=((LENGTH, WIDTH), BF),
    mix=((LENGTH, 3 * PAIR), BF),
    turned=((PAIR, LENGTH), BF),
    att=((LENGTH, PAIR), BF),
    lse=((8, QB), F32),
    work=((2, LENGTH, QB), F32),
    more=((2, LENGTH, QB), F32),
    low_work=((2, LENGTH, QB), BF),
    low_more=((2, LENGTH, QB), BF),
    att_own=((ROWS, WIDTH), BF),
    middle=((ROWS, WIDTH), F32),
    hat_two=((ROWS, WIDTH), F32),
    scale_two=((ROWS, 1), F32),
    n_two=((NB * ROWS, WIDTH), BF),
    hidden=((NB * ROWS, WIDTH), BF),
    grad_pre=((NB * ROWS, WIDTH), BF),
    p_norm=((NB * ROWS, WIDTH), BF),
    p_norm_box=((3, ROWS, WIDTH), BF),
    p_layer=((NB * ROWS, WIDTH), BF),
    p_layer_box=((3, ROWS, WIDTH), BF),
    g_side=((NB * ROWS, WIDTH), BF),
    n_side=((NB * ROWS, WIDTH), BF),
    hidden_side=((NB * ROWS, WIDTH // 2), BF),
    pre_side=((NB * ROWS, WIDTH // 2), BF),
    p_out=((2, 256, WIDTH), BF),
    out_up=((2, 4, 64, WIDTH), BF),
    out_down=((2, 4, 64, WIDTH), BF),
    out_block=((ROWS, WIDTH), BF),
    p_fc=((2, NB, 4, 64, 256), BF),
    fc_up=((2, 4, NB, 64, 256), BF),
    fc_down=((2, 4, NB, 64, 256), BF),
    fc_sum=((2, NB, 64, 256), BF),
    fc_block=((64, FF // 2), BF),
    p_proj=((WIDTH, WIDTH), BF),
    p_proj_box=((3, SHARD, WIDTH), BF),
    proj_sum=((SHARD, WIDTH), BF),
    proj_beside=((4, 32, WIDTH), BF),
    proj_up=((4, 32, WIDTH), BF),
    proj_down=((4, 32, WIDTH), BF),
    proj_block=((32, WIDTH), BF),
    grad_middle=((ROWS, WIDTH), F32),
    branch=((ROWS, WIDTH), BF),
    g_att=((ROWS, WIDTH), BF),
    dout=((LENGTH, PAIR), BF),
    gmix=((LENGTH, 3 * PAIR), BF),
    grad_k=((LENGTH, PAIR), F32),
    grad_v=((LENGTH, PAIR), F32),
    gmix_own=((NC, ROWS, 3 * PAIR), BF),
    gmix_all=((ROWS, 3 * WIDTH), BF),
    p_qkv=((WIDTH, 3 * PAIR), BF),
    p_qkv_box=((3, SHARD, 3 * PAIR), BF),
    qkv_block=((SHARD, 3 * PAIR), BF),
    gn_one=((ROWS, WIDTH), F32),
    gs=((NB, SMALL_ROWS, SHARD), F32),
    gqv=((16, PAIR), F32),
    gs_box=((NB, SMALL_ROWS, SHARD), F32),
    gs_sum=((SMALL_ROWS, SHARD), F32),
    gs_far=((NC, SMALL_ROWS, SHARD), F32),
)
SENDS, RECVS, LOCALS = 96, 248, 16


def layer_kernel(*refs):
    tokens, cotangent = refs[:2]
    vectors = refs[2:10]
    wqkv, wproj, wfc, wout = refs[10:14]
    layer_out, grad_tokens, grad_small, o_qkv, o_proj, o_fc, o_out = refs[14:21]
    scratch = refs[21:]
    s = SimpleNamespace(**dict(zip(SCRATCH, scratch)))
    send_sems, recv_sems, local_sems = scratch[len(SCRATCH) :]
    b, c = lax.axis_index("batch"), lax.axis_index("ctx")
    net = Net(b, c, send_sems, recv_sems)
    mark = Marks()
    locals_open = []

    def local(src, dst):
        copy = pltpu.make_async_copy(src, dst, local_sems.at[len(locals_open)])
        copy.start()
        locals_open.append(copy)
        return copy

    def own(ref, size):
        return rows_of(ref, size)(b)

    def cols(ref, start, count=PAIR):
        return ref.at[:, pl.ds(pl.multiple_of(start, 128), count)]

    def halves(ref, size, j):
        block = rows_of(ref, size)(j)
        return [block.at[0 : size // 2], block.at[size // 2 : size]]

    mark("enter")
    get_pair = [
        local(cols(wqkv, t * WIDTH + c * PAIR), own(s.wpair, SHARD).at[:, t * PAIR : (t + 1) * PAIR])
        for t in range(3)
    ]
    get_proj = local(wproj, own(s.wproj_all, SHARD))
    get_fc = local(cols(wfc, b * WIDTH, WIDTH), own(s.wfc_mine, SHARD))
    get_out = local(wout, s.wout_mine)
    get_full = local(wqkv, own(s.wfull, SHARD))
    get_g = local(cotangent, own(s.g_all, ROWS))

    s.small[...] = jnp.zeros_like(s.small)
    row = 0
    for vector in vectors:
        for i in range(vector.shape[0] // SHARD):
            piece = vector[i * SHARD : (i + 1) * SHARD].astype(F32)
            s.small[row : row + 1, :] = piece.reshape(1, SHARD)
            row += 1

    mark("barrier")
    barrier = pltpu.get_barrier_semaphore()
    others = [(lax.rem(b + i, NB), c) for i in range(1, NB)]
    others += [(b, lax.rem(c + i, NC)) for i in range(1, NC)]
    for device in others:
        pl.semaphore_signal(barrier, inc=1, device_id=device, device_id_type=MESH)
    scale, hat = s.scale_one, s.hat_one

    def norm_rows(i, carry):
        at = pl.ds(pl.multiple_of(i * 32, 32), 32)
        hat[at, :], scale[at, :] = normalise(tokens[at, :].astype(F32))
        return carry

    lax.fori_loop(0, ROWS // 32, norm_rows, 0)
    pl.semaphore_wait(barrier, len(others))

    mark("send_params")
    batch_others = [lax.rem(b + i, NB) for i in range(1, NB)]
    small_slots, pair_slots = net.slots(NB), net.slots(NB * 3)
    for j in batch_others:
        net.send(s.small, s.parts.at[b], (j, c), small_slots + b)
    for j in batch_others:
        for t in range(3):
            net.send(
                cols(wqkv, t * WIDTH + c * PAIR),
                own(s.wpair, SHARD).at[:, t * PAIR : (t + 1) * PAIR],
                (j, c),
                pair_slots + b * 3 + t,
            )

    mark("norm_one")
    s.parts[pl.ds(b, 1)] = s.small[...][None]
    for j in batch_others:
        net.wait(small_slots + j, s.parts.at[j])
    gain, bias = row_of(s.parts, 0), row_of(s.parts, 1)
    n_mine = rows_of(s.n_one, ROWS)(c)

    def gain_rows(i, carry):
        at = pl.ds(pl.multiple_of(i * 32, 32), 32)
        n_mine[at, :] = (hat[at, :] * gain + bias).astype(BF)
        return carry

    lax.fori_loop(0, ROWS // 32, gain_rows, 0)

    mark("gather_one_start")
    gather_one = GatherCtx(net, lambda j: halves(s.n_one, ROWS, j), 2, True)
    gather_one.start(halves(s.n_one, ROWS, c))
    gather_proj = GatherBatch(net, lambda j: [rows_of(s.wproj_all, SHARD)(j)])
    gather_proj.start([wproj])
    for p in range(NC):
        at = p * PAIR
        row, lane = 2 + (at % 512) // SHARD, at % SHARD
        s.qv_rows[p : p + 1, :] = s.parts[at // 512, row : row + 1, lane : lane + PAIR]
        s.qv_rows[8 + p : 9 + p, :] = s.parts[2 + at // 512, row : row + 1, lane : lane + PAIR]
    mark("gather_one_1")
    gather_one.stage(1)

    fc_slots, fc_near_slots = net.slots(NB), net.slots(NB)
    half, pair_z = net.z % 2, net.c + 2 - 4 * (net.z % 2)
    half_rows = pl.ds(pl.multiple_of(half * (SHARD // 2), SHARD // 2), SHARD // 2)
    net.send(cols(wfc, net.sib * WIDTH, WIDTH), own(s.wfc_mine, SHARD), (net.sib, c), fc_slots + b)
    for j in (net.across, net.diag):
        net.send(
            wfc.at[half_rows, pl.ds(pl.multiple_of(j * WIDTH, WIDTH), WIDTH)],
            own(s.wfc_mine, SHARD).at[half_rows],
            (j, c),
            fc_slots + b,
        )
    mark("gather_one_2")
    gather_one.stage(2)
    gather_g = GatherBatch(net, lambda j: [rows_of(s.g_all, ROWS)(j)])
    gather_g.start([cotangent])
    mark("gather_one_3")
    gather_one.stage(3)
    side_slot = net.slots(1)
    g_mine = own(s.g_all, ROWS)
    gather_gs = GatherSide(net, rows_of(s.g_side, ROWS))
    gather_gs.give(b, cotangent)
    mark("gather_one_finish")
    gather_one.finish()
    mark("wait_pair")
    for copy in get_pair:
        copy.wait()
    for j in batch_others:
        for t in range(3):
            net.wait(pair_slots + j * 3 + t, rows_of(s.wpair, SHARD)(j).at[:, t * PAIR : (t + 1) * PAIR])
    mark("mix")
    mix_bias = jnp.concatenate(
        [s.qv_rows[pl.ds(c, 1), :], jnp.zeros((1, PAIR), F32), s.qv_rows[pl.ds(8 + c, 1), :]], axis=1
    )

    def mix_rows(i, carry):
        at = pl.ds(pl.multiple_of(i * QB, QB), QB)
        s.mix[at, :] = (mm(s.n_one[at, :], s.wpair[...]) + mix_bias).astype(BF)
        return carry

    lax.fori_loop(0, LENGTH // QB, mix_rows, 0)

    mark("attend")
    swap_att = SwapCtx(
        net, lambda j: [rows_of(s.att, ROWS)(j)], lambda j: [cols(s.att_own, j * PAIR)], 1
    )

    def att_ready(qb):
        swap_att.give(2 * qb)
        swap_att.give(2 * qb + 1)

    attend(s.mix, s.turned, s.att, s.lse, s.work, s.low_work, att_ready)
    mark("relays")
    gather_proj.relay()
    for j in (net.across, net.diag):
        block = rows_of(s.wfc_mine, SHARD)(j).at[half_rows]
        net.wait(fc_slots + j, block)
        net.send(block, block, (b, pair_z), fc_near_slots + j)
    get_proj.wait()
    gather_proj.finish()
    mark("swap_att_finish")
    swap_att.finish()

    mark("middle")
    proj_bias = row_of(s.parts, 4)

    def middle_cols(i, carry):
        at = pl.ds(pl.multiple_of(i * 256, 256), 256)
        s.middle[:, at] = mm(s.att_own[...], s.wproj_all[:, at]) + tokens[:, at].astype(F32)
        return carry

    lax.fori_loop(0, WIDTH // 256, middle_cols, 0)
    gain_two, bias_two = row_of(s.parts, 5), row_of(s.parts, 6)
    n_two_mine = own(s.n_two, ROWS)

    def norm_two_rows(i, carry):
        at = pl.ds(pl.multiple_of(i * 32, 32), 32)
        middle = s.middle[at, :] + proj_bias
        s.middle[at, :] = middle
        norm, width = normalise(middle)
        s.hat_two[at, :], s.scale_two[at, :] = norm, width
        n_two_mine[at, :] = (norm * gain_two + bias_two).astype(BF)
        return carry

    lax.fori_loop(0, ROWS // 32, norm_two_rows, 0)

    mark("gather_two")
    gather_two = GatherBatch(net, lambda j: halves(s.n_two, ROWS, j), 2)
    gather_two.start(halves(s.n_two, ROWS, b))
    n_beside = own(s.n_side, ROWS)
    gather_g.relay()
    gather_gs.give(net.across, rows_of(s.g_all, ROWS)(net.across))
    gather_gs.relay(b)
    net.send(n_two_mine, n_beside, (b, net.side), side_slot)
    s.gs[...] = jnp.zeros_like(s.gs)
    mark("gather_two_relay")
    gather_two.relay()
    mark("wait_feed")
    for copy in (get_fc, get_out, get_g, get_full):
        copy.wait()
    gather_g.finish()
    net.wait(fc_slots + net.sib, rows_of(s.wfc_mine, SHARD)(net.sib))
    other_rows = pl.ds(pl.multiple_of((1 - half) * (SHARD // 2), SHARD // 2), SHARD // 2)
    for j in (net.across, net.diag):
        net.wait(fc_near_slots + j, rows_of(s.wfc_mine, SHARD)(j).at[other_rows])
    mark("gather_two_finish")
    gather_two.finish()

    mark("feed")
    hidden_slots, pre_slots = net.slots(2), net.slots(2)

    def feed_cols(i, carry):
        n = lax.rem(2 * (1 - net.x) + i, 4)
        at = pl.ds(pl.multiple_of(n * 256, 256), 256)
        pre = mm(s.n_two[...], s.wfc_mine[:, at]) + s.small[pl.ds(7 + n, 1), :]
        value, slope = gelu_pair(pre)
        s.hidden[:, at] = value.astype(BF)
        grad = (mm(s.g_all[...], s.wout_mine[at, :], NT) * slope).astype(BF)
        s.grad_pre[:, at] = grad
        s.gs[pl.ds(b, 1), pl.ds(7 + n, 1), :] = jnp.sum(grad.astype(F32), 0, keepdims=True)[None]
        return carry

    for i in range(2):
        feed_cols(i, 0)
        source = cols(s.hidden, (2 * (1 - net.x) + i) * 256, 256)
        net.send(source, s.hidden_side.at[:, i * 256 : (i + 1) * 256], (b, net.side), hidden_slots + i)
    for i in range(2):
        source = cols(s.grad_pre, (2 * (1 - net.x) + i) * 256, 256)
        net.send(source, s.pre_side.at[:, i * 256 : (i + 1) * 256], (b, net.side), pre_slots + i)
    lax.fori_loop(2, 4, feed_cols, 0)

    mark("p_norm")
    reduce_norm = ReduceBatch(net, rows_of(s.p_norm, ROWS), s.p_norm_box)

    def norm_block(j):
        at = pl.ds(pl.multiple_of(j * ROWS, ROWS), ROWS)
        s.p_norm[at, :] = mm(s.grad_pre[at, :], s.wfc_mine[...], NT).astype(BF)

    norm_block(net.diag)
    reduce_norm.give()
    norm_block(net.across)
    reduce_norm.cross()
    norm_block(net.sib)
    reduce_norm.keep()
    norm_block(b)

    mark("sides")
    gather_ns = GatherBatch(net, lambda j: [rows_of(s.n_side, ROWS)(j)])
    net.wait(side_slot, n_beside)
    gather_ns.start([n_beside])
    gather_gs.relay(net.across)
    gather_gs.finish()

    def out_views(j):
        return [rows_of(o_out, 64)(8 * (j % 2) + 4 * i + j // 2) for i in range(2)]

    reduce_out = [
        ReduceLine(net, rows_of(s.p_out.at[i], 64), s.out_up.at[i], s.out_down.at[i]) for i in range(2)
    ]
    gather_out = GatherCtx(net, out_views, 2, True)

    def p_out(i):
        at = slice(i * 256, (i + 1) * 256)
        net.wait(hidden_slots + i, s.hidden_side.at[:, at])
        mine = cols(s.hidden, net.x * 512 + i * 256, 256)
        s.p_out[i] = (
            mm(mine[...], s.g_all[...], TN) + mm(s.hidden_side[:, at], s.g_side[...], TN)
        ).astype(BF)
        reduce_out[i].launch()

    keep = []

    def out_done(i):
        part = s.out_block.at[i * 64 : (i + 1) * 64]
        reduce_out[i].finish(part)
        gather_out.begin(i, part)
        keep.append(local(part, out_views(c)[i]))

    mark("p_out_0")
    p_out(0)
    mark("wait_norm")
    terms = reduce_norm.finish()

    mark("back_two")

    def back_rows(i, carry):
        at = pl.ds(pl.multiple_of(i * 32, 32), 32)
        grad_gain, grad_bias, sum_branch, sum_g = carry
        grad = terms[0][at, :].astype(F32) + terms[1][at, :].astype(F32) + terms[2][at, :].astype(F32)
        norm = s.hat_two[at, :]
        scaled = grad * gain_two
        inner = scaled - jnp.mean(scaled, -1, keepdims=True)
        inner = inner - norm * jnp.mean(scaled * norm, -1, keepdims=True)
        g = g_mine[at, :].astype(F32)
        total = g + s.scale_two[at, :] * inner
        s.grad_middle[at, :] = total
        low = total.astype(BF)
        s.branch[at, :] = low
        return (
            grad_gain + jnp.sum(grad * norm, 0, keepdims=True),
            grad_bias + jnp.sum(grad, 0, keepdims=True),
            sum_branch + jnp.sum(low.astype(F32), 0, keepdims=True),
            sum_g + jnp.sum(g, 0, keepdims=True),
        )

    sums = lax.fori_loop(0, ROWS // 32, back_rows, (jnp.zeros((1, WIDTH), F32),) * 4)
    put_row(s.gs, 5, sums[0])
    put_row(s.gs, 6, sums[1])
    put_row(s.gs, 4, sums[2])
    put_row(s.gs, 11, sums[3])

    def att_cols(i, carry):
        at = pl.ds(pl.multiple_of(i * 256, 256), 256)
        s.g_att[:, at] = mm(s.branch[...], s.wproj_all[at, :], NT).astype(BF)
        return carry

    lax.fori_loop(0, 4, att_cols, 0)
    mark("swap_grad")
    swap_grad = SwapCtx(
        net, lambda j: [cols(s.g_att, j * PAIR)], lambda j: [rows_of(s.dout, ROWS)(j)], 1
    )
    swap_grad.start()

    mark("p_out_1")
    p_out(1)
    mark("out_0_one")
    reduce_out[0].pass_one()
    mark("p_proj")
    reduce_proj = ReduceBatch(net, rows_of(s.p_proj, SHARD), s.p_proj_box)

    def proj_rows(i, carry):
        at = pl.ds(pl.multiple_of(i * 256, 256), 256)
        s.p_proj[at, :] = mm(s.att_own[:, at], s.branch[...], TN).astype(BF)
        return carry

    lax.fori_loop(0, 4, proj_rows, 0)
    reduce_proj.give()
    mark("ns_relay")
    gather_ns.relay()
    reduce_proj.cross()
    reduce_proj.keep()
    mark("out_0_two")
    reduce_out[0].pass_two()
    mark("out_1_one")
    reduce_out[1].pass_one()
    mark("p_layer")
    reduce_layer = ReduceBatch(net, rows_of(s.p_layer, ROWS), s.p_layer_box)

    def layer_block(j):
        at = pl.ds(pl.multiple_of(j * ROWS, ROWS), ROWS)
        s.p_layer[at, :] = mm(s.hidden[at, :], s.wout_mine[...]).astype(BF)

    layer_block(net.diag)
    reduce_layer.give()
    layer_block(net.across)
    reduce_layer.cross()
    layer_block(net.sib)
    reduce_layer.keep()
    layer_block(b)
    mark("out_0_done")
    out_done(0)
    mark("out_1_two")
    reduce_out[1].pass_two()
    mark("swap_grad_finish")
    swap_grad.finish()
    mark("ns_finish")
    gather_ns.finish()

    reduce_fc = [
        ReduceLine(net, lambda zz, i=i: s.p_fc.at[i, :, zz], s.fc_up.at[i], s.fc_down.at[i])
        for i in range(2)
    ]

    def p_fc(i):
        at = slice(i * 256, (i + 1) * 256)
        net.wait(pre_slots + i, s.pre_side.at[:, at])
        mine = cols(s.grad_pre, net.x * 512 + i * 256, 256)

        def fc_rows(k, carry):
            rows = pl.ds(pl.multiple_of(k * 256, 256), 256)
            total = mm(s.n_two[:, rows], mine[...], TN) + mm(s.n_side[:, rows], s.pre_side[:, at], TN)
            s.p_fc[i, pl.ds(k, 1)] = total.astype(BF).reshape(1, 4, 64, 256)
            return carry

        lax.fori_loop(0, 4, fc_rows, 0)
        reduce_fc[i].launch()

    mark("p_fc_0")
    p_fc(0)

    mark("attend_back")
    swap_mix = SwapCtx(
        net,
        lambda j: [rows_of(s.gmix, ROWS)(j)],
        lambda j: [s.gmix_own.at[j]],
        1,
    )
    attend_back(
        s.mix, s.turned, s.dout, s.lse, s.gmix, s.grad_k, s.grad_v,
        s.work, s.more, s.low_work, s.low_more, lambda qb: None,
    )
    mark("out_1_done")
    out_done(1)
    mark("fc_0_one")
    reduce_fc[0].pass_one()
    mark("p_qkv")
    reduce_qkv = ReduceBatch(net, rows_of(s.p_qkv, SHARD), s.p_qkv_box)

    def qkv_block(j):
        at = pl.ds(pl.multiple_of(j * SHARD, SHARD), SHARD)
        s.p_qkv[at, :] = mm(s.n_one[:, at], s.gmix[...], TN).astype(BF)

    qkv_block(net.diag)
    reduce_qkv.give()
    qkv_block(net.across)
    reduce_qkv.cross()
    gather_full = GatherBatch(net, lambda j: [rows_of(s.wfull, SHARD)(j)])
    gather_full.start([wqkv])
    qkv_block(net.sib)
    reduce_qkv.keep()
    qkv_block(b)
    mark("p_fc_1")
    p_fc(1)
    mark("fc_0_two")
    reduce_fc[0].pass_two()
    mark("proj_sum")
    add_into(s.proj_sum, reduce_proj.finish())
    reduce_part = ReduceCtx(net, rows_of(s.proj_sum, 32), s.proj_beside, s.proj_up, s.proj_down)
    reduce_part.start()
    mark("gather_out_1")
    gather_out.stage(1)
    mark("fc_1_one")
    reduce_fc[1].pass_one()
    swap_mix.give(0)
    swap_mix.give(1)
    mark("gqv")
    s.gqv[...] = jnp.zeros_like(s.gqv)
    s.gqv[pl.ds(c, 1), :] = jnp.sum(s.gmix[:, :PAIR].astype(F32), 0, keepdims=True)
    s.gqv[pl.ds(8 + c, 1), :] = jnp.sum(s.gmix[:, 2 * PAIR :].astype(F32), 0, keepdims=True)
    for p in range(NC):
        at = p * PAIR
        row, lane = 2 + (at % 512) // SHARD, at % SHARD
        s.gs[at // 512, row : row + 1, lane : lane + PAIR] = s.gqv[p : p + 1, :]
        s.gs[2 + at // 512, row : row + 1, lane : lane + PAIR] = s.gqv[8 + p : 9 + p, :]

    mark("wait_qkv")
    terms = reduce_qkv.finish()
    add_into(s.qkv_block, terms)
    gather_qkv = GatherCtx(net, lambda j: halves(o_qkv.at[j], SHARD, 0), 2, True)
    gather_qkv.start(halves(s.qkv_block, SHARD, 0))
    keep.append(local(s.qkv_block, o_qkv.at[c]))
    swap_slots = net.slots(2 * NB)

    def fc_done(i):
        reduce_fc[i].finish(s.fc_sum.at[i])
        for j in batch_others:
            net.send(
                s.fc_sum.at[i, j], cols(s.fc_block, b * 512 + i * 256, 256), (j, c), swap_slots + 2 * b + i
            )
        s.fc_block[:, pl.ds(pl.multiple_of(b * 512 + i * 256, 256), 256)] = s.fc_sum[i, pl.ds(b, 1)][0]

    mark("fc_0_done")
    fc_done(0)
    swap_mix.give(2)
    swap_mix.give(3)
    mark("part_fold")
    reduce_part.fold()
    mark("fc_1_two")
    reduce_fc[1].pass_two()
    mark("gather_out_2")
    gather_out.stage(2)
    swap_mix.give(4)
    swap_mix.give(5)
    mark("part_one")
    reduce_part.line.pass_one()
    mark("layer_out")
    layer_bias = row_of(s.parts, 11)
    layer_terms = reduce_layer.finish()

    def layer_rows(i, carry):
        at = pl.ds(pl.multiple_of(i * 32, 32), 32)
        total = [term[at, :].astype(F32) for term in layer_terms]
        layer_out[at, :] = (s.middle[at, :] + (total[0] + total[1] + total[2]) + layer_bias).astype(BF)
        return carry

    lax.fori_loop(0, ROWS // 32, layer_rows, 0)
    mark("fc_1_done")
    fc_done(1)
    swap_mix.give(6)
    swap_mix.give(7)
    mark("part_two")
    reduce_part.line.pass_two()
    mark("gather_qkv_1")
    gather_qkv.stage(1)
    mark("gather_out_3")
    gather_out.stage(3)
    mark("fc_swap")
    for j in batch_others:
        for i in range(2):
            net.wait(swap_slots + 2 * j + i, cols(s.fc_block, j * 512 + i * 256, 256))

    def fc_views(j):
        block = o_fc.at[j % 2, pl.ds(pl.multiple_of((j // 2) * 64, 64), 64)]
        return [block.at[0:32], block.at[32:64]]

    gather_fc = GatherCtx(net, fc_views, 2, True)
    gather_fc.start([s.fc_block.at[0:32], s.fc_block.at[32:64]])
    keep.append(local(s.fc_block, o_fc.at[net.x, pl.ds(pl.multiple_of(net.z * 64, 64), 64)]))
    mark("part_finish")
    reduce_part.line.finish(s.proj_block)
    gather_part = GatherCtx(net, lambda j: [rows_of(o_proj, 32)(j)], 1)
    gather_part.start([s.proj_block])
    keep.append(local(s.proj_block, rows_of(o_proj, 32)(c)))
    mark("gather_qkv_2")
    gather_qkv.stage(2)
    mark("gather_part_1")
    gather_part.stage(1)
    mark("gather_fc_1")
    gather_fc.stage(1)
    mark("full_relay")
    gather_full.relay()
    mark("gather_qkv_3")
    gather_qkv.stage(3)

    mark("wait_mix")
    gather_full.finish()
    swap_mix.finish()
    for j in range(NC):
        for t in range(3):
            to, at = t * WIDTH + j * PAIR, t * PAIR
            s.gmix_all[:, to : to + PAIR] = s.gmix_own[j, :, at : at + PAIR]
    mark("grad_tokens")

    def one_cols(i, carry):
        at = pl.ds(pl.multiple_of(i * 256, 256), 256)
        s.gn_one[:, at] = mm(s.gmix_all[...], s.wfull[at, :], NT)
        return carry

    lax.fori_loop(0, 4, one_cols, 0)

    def token_rows(i, carry):
        at = pl.ds(pl.multiple_of(i * 32, 32), 32)
        grad_gain, grad_bias = carry
        grad, norm = s.gn_one[at, :], s.hat_one[at, :]
        scaled = grad * gain
        inner = scaled - jnp.mean(scaled, -1, keepdims=True)
        inner = inner - norm * jnp.mean(scaled * norm, -1, keepdims=True)
        grad_tokens[at, :] = (s.grad_middle[at, :] + s.scale_one[at, :] * inner).astype(BF)
        return (
            grad_gain + jnp.sum(grad * norm, 0, keepdims=True),
            grad_bias + jnp.sum(grad, 0, keepdims=True),
        )

    sums = lax.fori_loop(0, ROWS // 32, token_rows, (jnp.zeros((1, WIDTH), F32),) * 2)
    put_row(s.gs, 0, sums[0])
    put_row(s.gs, 1, sums[1])
    gs_slots, far_slots = net.slots(NB), net.slots(NC)
    for j in batch_others:
        net.send(s.gs.at[j], s.gs_box.at[b], (j, c), gs_slots + b)

    mark("gs_sum")
    total = s.gs[pl.ds(b, 1)][0]
    for j in batch_others:
        net.wait(gs_slots + j, s.gs_box.at[j])
        total = total + s.gs_box[pl.ds(j, 1)][0]
    s.gs_sum[...] = total
    for i in range(1, NC):
        j = lax.rem(c + i, NC)
        net.send(s.gs_sum, s.gs_far.at[c], (b, j), far_slots + c)
    mark("gather_part_2")
    gather_part.stage(2)
    mark("gather_fc_2")
    gather_fc.stage(2)
    mark("gather_part_3")
    gather_part.stage(3)
    mark("gather_fc_3")
    gather_fc.stage(3)
    mark("far_sum")
    for i in range(1, NC):
        j = lax.rem(c - i + NC, NC)
        net.wait(far_slots + j, s.gs_far.at[j])
        total = total + s.gs_far[pl.ds(j, 1)][0]
    grad_small[...] = total
    mark("out_end")
    gather_out.finish()
    mark("qkv_end")
    gather_qkv.finish()
    mark("part_end")
    gather_part.finish()
    mark("fc_end")
    gather_fc.finish()
    mark("drain")
    for copy in keep:
        copy.wait()
    net.drain()
    mark(None)


VECTOR_ROWS = (1, 1, 2, 1, 1, 1, 4, 1)
STEPS = 8


def widen_kernel(layer, grad_in, small, w_qkv, w_proj, w_fc, w_out, *outs):
    o_layer, o_grad_in, o_qkv, o_proj, o_fc, o_out = outs[:6]
    o_layer[...] = layer[...]
    o_grad_in[...] = grad_in[...]
    for j in range(NC):
        for t in range(3):
            to, at = t * WIDTH + j * PAIR, t * PAIR
            o_qkv[:, to : to + PAIR] = w_qkv[j, :, at : at + PAIR].astype(F32)
    o_proj[...] = w_proj[...].astype(F32)
    o_out[...] = w_out[...].astype(F32)
    for j in range(NB):
        for x in range(2):
            to, at = j * WIDTH + x * 512, j * 512
            o_fc[:, to : to + 512] = w_fc[x, :, at : at + 512].astype(F32)

    @pl.when(pl.program_id(0) == 0)
    def _():
        row = 0
        for out in outs[6:]:
            for i in range(out.shape[0] // SHARD):
                out[i * SHARD : (i + 1) * SHARD] = small[row, :]
                row += 1


def per_device_fast(
    tokens, cotangent, ln1_gain, ln1_bias, qkv_weight, qv_bias, proj_weight, proj_bias,
    ln2_gain, ln2_bias, fc_weight, fc_bias, out_weight, out_bias,
):
    vmem, anywhere = pl.BlockSpec(memory_space=pltpu.VMEM), pl.BlockSpec(memory_space=pl.ANY)
    shape = jax.ShapeDtypeStruct
    layer, grad_in, grad_small, w_qkv, w_proj, w_fc, w_out = pl.pallas_call(
        layer_kernel,
        out_shape=(
            shape((ROWS, WIDTH), BF),
            shape((ROWS, WIDTH), BF),
            shape((SMALL_ROWS, SHARD), F32),
            shape((NC, SHARD, 3 * PAIR), BF),
            shape((SHARD, WIDTH), BF),
            shape((2, SHARD, FF // 2), BF),
            shape((FF // NB, WIDTH), BF),
        ),
        in_specs=[vmem] * 10 + [anywhere] * 4,
        out_specs=(vmem, vmem, vmem, anywhere, anywhere, anywhere, anywhere),
        scratch_shapes=[pltpu.VMEM(*item) for item in SCRATCH.values()]
        + [
            pltpu.SemaphoreType.DMA((SENDS,)),
            pltpu.SemaphoreType.DMA((RECVS,)),
            pltpu.SemaphoreType.DMA((LOCALS,)),
        ],
        compiler_params=pltpu.CompilerParams(
            collective_id=0, has_side_effects=True, vmem_limit_bytes=VMEM_BYTES
        ),
    )(
        tokens.reshape(ROWS, WIDTH), cotangent.reshape(ROWS, WIDTH),
        ln1_gain, ln1_bias, qv_bias, proj_bias, ln2_gain, ln2_bias, fc_bias, out_bias,
        qkv_weight, proj_weight, fc_weight, out_weight,
    )

    def rows(count, width):
        return pl.BlockSpec((count // STEPS, width), lambda i: (i, 0))

    half = pl.BlockSpec((2, SHARD // STEPS, FF // 2), lambda i: (0, i, 0))
    smalls = [pl.BlockSpec((n * SHARD,), lambda i: (0,)) for n in VECTOR_ROWS]
    layer, grad_in, w_qkv, w_proj, w_fc, w_out, *vectors = pl.pallas_call(
        widen_kernel,
        grid=(STEPS,),
        out_shape=(
            shape((ROWS, WIDTH), BF),
            shape((ROWS, WIDTH), BF),
            shape((SHARD, 3 * WIDTH), F32),
            shape((SHARD, WIDTH), F32),
            shape((SHARD, FF), F32),
            shape((FF // NB, WIDTH), F32),
            *[shape((n * SHARD,), F32) for n in VECTOR_ROWS],
        ),
        in_specs=[
            rows(ROWS, WIDTH),
            rows(ROWS, WIDTH),
            pl.BlockSpec((SMALL_ROWS, SHARD), lambda i: (0, 0)),
            pl.BlockSpec((NC, SHARD // STEPS, 3 * PAIR), lambda i: (0, i, 0)),
            rows(SHARD, WIDTH),
            half,
            rows(FF // NB, WIDTH),
        ],
        out_specs=(
            rows(ROWS, WIDTH),
            rows(ROWS, WIDTH),
            rows(SHARD, 3 * WIDTH),
            rows(SHARD, WIDTH),
            rows(SHARD, FF),
            rows(FF // NB, WIDTH),
            *smalls,
        ),
        compiler_params=pltpu.CompilerParams(vmem_limit_bytes=VMEM_BYTES),
    )(layer, grad_in, grad_small, w_qkv, w_proj, w_fc, w_out)
    return (
        layer.reshape(tokens.shape),
        grad_in.reshape(tokens.shape),
        vectors[0],
        vectors[1],
        w_qkv,
        vectors[2],
        w_proj,
        vectors[3],
        vectors[4],
        vectors[5],
        w_fc,
        vectors[6],
        w_out,
        vectors[7],
    )


VMEM_BYTES = 62 * 1024 * 1024


def solution(mesh):
    placed = (
        P("batch", "ctx", None),
        P("batch", "ctx", None),
        P("batch"),
        P("batch"),
        P("batch", None),
        P("batch"),
        P("batch", None),
        P("batch"),
        P("batch"),
        P("batch"),
        P("batch", None),
        P("batch"),
        P("batch", None),
        P("batch"),
    )
    fits = dict(mesh.shape) == {"batch": NB, "ctx": NC}
    return jax.shard_map(
        per_device_fast if fits else per_device,
        mesh=mesh,
        in_specs=placed,
        out_specs=(
            P("batch", "ctx", None),
            P("batch", "ctx", None),
            P("batch"),
            P("batch"),
            P("batch", None),
            P("batch"),
            P("batch", None),
            P("batch"),
            P("batch"),
            P("batch"),
            P("batch", None),
            P("batch"),
            P("batch", None),
            P("batch"),
        ),
        check_vma=False,
    )
```

```python
from functools import partial
from types import SimpleNamespace

import jax
import jax.numpy as jnp
from jax import lax
from jax.experimental import pallas as pl
from jax.experimental.pallas import tpu as pltpu
from jax.sharding import PartitionSpec as P

HEADS = 16
HEAD_DIM = 64


epsilon = 1e-05
masked_value = -1e30


def shifted(block, axis, distance):
    devices = range(lax.axis_size(axis))
    route = [(i - distance, i) for i in devices if i - distance in devices]
    return lax.ppermute(block, axis, route)


def from_behind(block, axis, distance):
    devices = range(lax.axis_size(axis))
    route = [((i - distance) % len(devices), i) for i in devices]
    return lax.ppermute(block, axis, route)


def layer_norm(inputs, gain_vec, bias_vec):
    centre = inputs - jnp.mean(inputs, -1, keepdims=True)
    spread = jnp.mean(centre * centre, -1, keepdims=True)
    return centre * lax.rsqrt(spread + epsilon) * gain_vec + bias_vec


def keep_same(running):
    return running


def per_device(
    tokens,
    cotangent,
    ln1_gain,
    ln1_bias,
    qkv_weight,
    qv_bias,
    proj_weight,
    proj_bias,
    ln2_gain,
    ln2_bias,
    fc_weight,
    fc_bias,
    out_weight,
    out_bias,
):
    (
        gain_one,
        bias_one,
        weight_qkv,
        bias_qv,
        weight_proj,
        bias_proj,
        gain_two,
        bias_two,
        weight_fc,
        bias_fc,
        weight_out,
        bias_out,
    ) = (
        lax.all_gather(ln1_gain, "batch", axis=0, tiled=True),
        lax.all_gather(ln1_bias, "batch", axis=0, tiled=True),
        lax.all_gather(qkv_weight, "batch", axis=0, tiled=True),
        lax.all_gather(qv_bias, "batch", axis=0, tiled=True),
        lax.all_gather(proj_weight, "batch", axis=0, tiled=True),
        lax.all_gather(proj_bias, "batch", axis=0, tiled=True),
        lax.all_gather(ln2_gain, "batch", axis=0, tiled=True),
        lax.all_gather(ln2_bias, "batch", axis=0, tiled=True),
        lax.all_gather(fc_weight, "batch", axis=0, tiled=True),
        lax.all_gather(fc_bias, "batch", axis=0, tiled=True),
        lax.all_gather(out_weight, "batch", axis=0, tiled=True),
        lax.all_gather(out_bias, "batch", axis=0, tiled=True),
    )
    seq_count, ctx_rows, model_width = tokens.shape
    row_count = seq_count * ctx_rows
    inputs = tokens.astype(jnp.float32).reshape(row_count, model_width)
    norm_one, norm_one_pull = jax.vjp(
        layer_norm, inputs, gain_one.astype(jnp.float32), bias_one.astype(jnp.float32)
    )
    normed_low = norm_one.astype(jnp.bfloat16)
    bias_float = bias_qv.astype(jnp.float32)
    bias_full = jnp.concatenate(
        [bias_float[:model_width], jnp.zeros((model_width,), jnp.float32), bias_float[model_width:]]
    )
    mixed_proj = (
        jnp.dot(normed_low, weight_qkv, preferred_element_type=jnp.float32) + bias_full
    ).astype(jnp.bfloat16)
    query_flat = mixed_proj[:, :model_width].reshape(seq_count, ctx_rows, model_width)
    key_flat = mixed_proj[:, model_width : 2 * model_width].reshape(
        seq_count, ctx_rows, model_width
    )
    value_flat = mixed_proj[:, 2 * model_width :].reshape(seq_count, ctx_rows, model_width)
    query_heads = query_flat.reshape(seq_count, ctx_rows, HEADS, HEAD_DIM)
    own_index = lax.axis_index("ctx")
    position = own_index * ctx_rows
    query_pos = position + jnp.arange(ctx_rows, dtype=jnp.int32)
    last_pos = position + ctx_rows - 1
    start_state = (
        jnp.full((seq_count, ctx_rows, HEADS), masked_value, jnp.float32),
        jnp.zeros((seq_count, ctx_rows, HEADS), jnp.float32),
        jnp.zeros((seq_count, ctx_rows, HEADS, HEAD_DIM), jnp.float32),
    )
    key_piece = lax.all_gather(key_flat, "ctx", axis=1, tiled=True)
    value_piece = lax.all_gather(value_flat, "ctx", axis=1, tiled=True)
    piece_rows = key_piece.shape[1]

    def compute(running):
        run_max, run_sum, accum = running
        key_split = key_piece.reshape(seq_count, piece_rows, HEADS, HEAD_DIM)
        value_split = value_piece.reshape(seq_count, piece_rows, HEADS, HEAD_DIM)
        scores = (
            jnp.einsum(
                "bqhd,bkhd->bqhk", query_heads, key_split, preferred_element_type=jnp.float32
            )
            * 0.125
        )
        key_pos = jnp.arange(piece_rows, dtype=jnp.int32)
        allowed = (key_pos[None, :] <= query_pos[:, None])[None, :, None, :]
        scores = jnp.where(allowed, scores, masked_value)
        new_max = jnp.maximum(run_max, jnp.max(scores, -1))
        weights_exp = jnp.where(allowed, jnp.exp(scores - new_max[..., None]), 0.0)
        new_sum = jnp.sum(weights_exp, -1)
        product = jnp.einsum(
            "bqhk,bkhd->bqhd",
            weights_exp.astype(jnp.bfloat16),
            value_split,
            preferred_element_type=jnp.float32,
        )
        return (new_max, new_sum, product)

    run_max, run_sum, accum = lax.cond(jnp.int32(0) <= last_pos, compute, keep_same, start_state)
    log_total = run_max + jnp.log(run_sum)
    attended = accum / run_sum[..., None]
    attended_low = attended.reshape(row_count, model_width).astype(jnp.bfloat16)
    middle = (
        inputs
        + jnp.dot(attended_low, weight_proj, preferred_element_type=jnp.float32)
        + bias_proj.astype(jnp.float32)
    )
    norm_two, norm_two_pull = jax.vjp(
        layer_norm, middle, gain_two.astype(jnp.float32), bias_two.astype(jnp.float32)
    )
    normed_two = norm_two.astype(jnp.bfloat16)
    pre_act = jnp.dot(normed_two, weight_fc, preferred_element_type=jnp.float32) + bias_fc.astype(
        jnp.float32
    )
    activated, gelu_pull = jax.vjp(partial(jax.nn.gelu, approximate=True), pre_act)
    hidden_low = activated.astype(jnp.bfloat16)
    output = (
        middle
        + jnp.dot(hidden_low, weight_out, preferred_element_type=jnp.float32)
        + bias_out.astype(jnp.float32)
    )
    layer_out = output.astype(jnp.bfloat16).reshape(tokens.shape)
    grad_out = cotangent.reshape(row_count, model_width)
    grad_out_float = grad_out.astype(jnp.float32)
    grad_w_out = jnp.einsum("rf,rd->fd", hidden_low, grad_out, preferred_element_type=jnp.float32)
    grad_b_out = jnp.sum(grad_out_float, 0)
    grad_hidden = jnp.einsum("rd,fd->rf", grad_out, weight_out, preferred_element_type=jnp.float32)
    (grad_pre,) = gelu_pull(grad_hidden)
    grad_pre_low = grad_pre.astype(jnp.bfloat16)
    grad_w_fc = jnp.einsum(
        "rd,rf->df", normed_two, grad_pre_low, preferred_element_type=jnp.float32
    )
    grad_b_fc = jnp.sum(grad_pre_low.astype(jnp.float32), 0)
    grad_norm_two = jnp.einsum(
        "rf,df->rd", grad_pre_low, weight_fc, preferred_element_type=jnp.float32
    )
    grad_mid_norm, grad_g_two, grad_b_two = norm_two_pull(grad_norm_two)
    grad_middle = grad_out_float + grad_mid_norm
    grad_branch = grad_middle.astype(jnp.bfloat16)
    grad_w_proj = jnp.einsum(
        "rd,re->de", attended_low, grad_branch, preferred_element_type=jnp.float32
    )
    grad_b_proj = jnp.sum(grad_branch.astype(jnp.float32), 0)
    grad_attended = jnp.einsum(
        "re,de->rd", grad_branch, weight_proj, preferred_element_type=jnp.float32
    ).astype(jnp.bfloat16)
    grad_att_flat = grad_attended.reshape(seq_count, ctx_rows, model_width)
    grad_att_heads = grad_att_flat.reshape(seq_count, ctx_rows, HEADS, HEAD_DIM)
    delta_mine = jnp.sum(grad_att_heads.astype(jnp.float32) * attended, -1)
    zero_heads = jnp.zeros((seq_count, ctx_rows, HEADS, HEAD_DIM), jnp.float32)
    cycle_count = lax.axis_size("ctx")

    def cycle_turn(turn, state):
        owner = (own_index - turn) % cycle_count
        first_row = owner * ctx_rows

        def visit(inner):
            key_piece, value_piece, grad_k, grad_v, grad_q = inner
            key_split = key_piece.reshape(seq_count, ctx_rows, HEADS, HEAD_DIM)
            value_split = value_piece.reshape(seq_count, ctx_rows, HEADS, HEAD_DIM)
            piece_pos = first_row + jnp.arange(ctx_rows, dtype=jnp.int32)
            scores = (
                jnp.einsum(
                    "bqhd,bkhd->bqhk", query_heads, key_split, preferred_element_type=jnp.float32
                )
                * 0.125
            )
            allowed = (piece_pos[None, :] <= query_pos[:, None])[None, :, None, :]
            probs = jnp.where(allowed, jnp.exp(scores - log_total[..., None]), 0.0)
            grad_probs = jnp.einsum(
                "bqhd,bkhd->bqhk", grad_att_heads, value_split, preferred_element_type=jnp.float32
            )
            grad_scores = (probs * (grad_probs - delta_mine[..., None])).astype(jnp.bfloat16)
            grad_q = (
                grad_q
                + jnp.einsum(
                    "bqhk,bkhd->bqhd", grad_scores, key_split, preferred_element_type=jnp.float32
                )
                * 0.125
            )
            grad_k = (
                grad_k
                + jnp.einsum(
                    "bqhk,bqhd->bkhd", grad_scores, query_heads, preferred_element_type=jnp.float32
                )
                * 0.125
            )
            grad_v = grad_v + jnp.einsum(
                "bqhk,bqhd->bkhd",
                probs.astype(jnp.bfloat16),
                grad_att_heads,
                preferred_element_type=jnp.float32,
            )
            return (key_piece, value_piece, grad_k, grad_v, grad_q)

        key_piece, value_piece, grad_k, grad_v, grad_q = lax.cond(
            owner <= own_index, visit, keep_same, state
        )
        key_piece, value_piece = shifted((key_piece, value_piece), "ctx", 1)
        grad_k, grad_v = (
            from_behind(grad_k.astype(jnp.bfloat16), "ctx", 1).astype(grad_k.dtype),
            from_behind(grad_v.astype(jnp.bfloat16), "ctx", 1).astype(grad_v.dtype),
        )
        return (key_piece, value_piece, grad_k, grad_v, grad_q)

    cycle_state = lax.fori_loop(
        0, cycle_count, cycle_turn, (key_flat, value_flat, zero_heads, zero_heads, zero_heads)
    )
    grad_k, grad_v, grad_q = (cycle_state[2], cycle_state[3], cycle_state[4])
    grad_mixed = jnp.concatenate(
        [
            grad_q.reshape(row_count, model_width),
            grad_k.reshape(row_count, model_width),
            grad_v.reshape(row_count, model_width),
        ],
        axis=1,
    ).astype(jnp.bfloat16)
    grad_w_qkv = jnp.einsum("rd,re->de", normed_low, grad_mixed, preferred_element_type=jnp.float32)
    grad_bias_all = jnp.sum(grad_mixed.astype(jnp.float32), 0)
    grad_b_qv = jnp.concatenate([grad_bias_all[:model_width], grad_bias_all[2 * model_width :]])
    grad_norm_one = jnp.einsum(
        "re,de->rd", grad_mixed, weight_qkv, preferred_element_type=jnp.float32
    )
    grad_in_norm, grad_g_one, grad_b_one = norm_one_pull(grad_norm_one)
    grad_tokens = (grad_middle + grad_in_norm).astype(jnp.bfloat16).reshape(tokens.shape)
    local_grads = (
        grad_g_one,
        grad_b_one,
        grad_w_qkv,
        grad_b_qv,
        grad_w_proj,
        grad_b_proj,
        grad_g_two,
        grad_b_two,
        grad_w_fc,
        grad_b_fc,
        grad_w_out,
        grad_b_out,
    )
    partial_grads = (
        lax.psum_scatter(
            local_grads[0].astype(jnp.bfloat16), "batch", scatter_dimension=0, tiled=True
        ).astype(jnp.float32),
        lax.psum_scatter(
            local_grads[1].astype(jnp.bfloat16), "batch", scatter_dimension=0, tiled=True
        ).astype(jnp.float32),
        lax.psum_scatter(
            local_grads[2].astype(jnp.bfloat16), "batch", scatter_dimension=0, tiled=True
        ).astype(jnp.float32),
        lax.psum_scatter(
            local_grads[3].astype(jnp.bfloat16), "batch", scatter_dimension=0, tiled=True
        ).astype(jnp.float32),
        lax.psum_scatter(
            local_grads[4].astype(jnp.bfloat16), "batch", scatter_dimension=0, tiled=True
        ).astype(jnp.float32),
        lax.psum_scatter(
            local_grads[5].astype(jnp.bfloat16), "batch", scatter_dimension=0, tiled=True
        ).astype(jnp.float32),
        lax.psum_scatter(
            local_grads[6].astype(jnp.bfloat16), "batch", scatter_dimension=0, tiled=True
        ).astype(jnp.float32),
        lax.psum_scatter(
            local_grads[7].astype(jnp.bfloat16), "batch", scatter_dimension=0, tiled=True
        ).astype(jnp.float32),
        lax.psum_scatter(
            local_grads[8].astype(jnp.bfloat16), "batch", scatter_dimension=0, tiled=True
        ).astype(jnp.float32),
        lax.psum_scatter(
            local_grads[9].astype(jnp.bfloat16), "batch", scatter_dimension=0, tiled=True
        ).astype(jnp.float32),
        lax.psum_scatter(
            local_grads[10].astype(jnp.bfloat16), "batch", scatter_dimension=0, tiled=True
        ).astype(jnp.float32),
        lax.psum_scatter(
            local_grads[11].astype(jnp.bfloat16), "batch", scatter_dimension=0, tiled=True
        ).astype(jnp.float32),
    )
    summed_grads = lax.psum(
        (
            partial_grads[0],
            partial_grads[1],
            partial_grads[2],
            partial_grads[3],
            partial_grads[4],
            partial_grads[5],
            partial_grads[6],
            partial_grads[7],
            partial_grads[8],
            partial_grads[9],
            partial_grads[10],
            partial_grads[11],
        ),
        "ctx",
    )
    return (
        layer_out,
        grad_tokens,
        summed_grads[0],
        summed_grads[1],
        summed_grads[2],
        summed_grads[3],
        summed_grads[4],
        summed_grads[5],
        summed_grads[6],
        summed_grads[7],
        summed_grads[8],
        summed_grads[9],
        summed_grads[10],
        summed_grads[11],
    )


BF, F32 = jnp.bfloat16, jnp.float32
NN = (((1,), (0,)), ((), ()))
NT = (((1,), (1,)), ((), ()))
TN = (((0,), (0,)), ((), ()))
MESH = pl.DeviceIdType.MESH
NB, NC, WIDTH, ROWS, FF, PAIR = 4, 8, 1024, 128, 4096, 128
SHARD = WIDTH // NB
LENGTH = ROWS * NC
SMALL_ROWS = 16


def mm(left, right, dims=NN):
    return lax.dot_general(left, right, dims, preferred_element_type=F32)


def run(when, action):
    if when is None:
        action()
    else:
        pl.when(when)(action)


def both(one, two):
    return two if one is None else (one if two is None else jnp.logical_and(one, two))


class Net:
    def __init__(self, b, c, send_sems, recv_sems):
        self.b, self.c, self.z, self.x = b, c, c // 2, c % 2
        self.side = c + 1 - 2 * self.x
        self.core = b % 2
        self.sib = b + 1 - 2 * self.core
        self.across = lax.rem(b + 2, NB)
        self.diag = lax.rem(self.sib + 2, NB)
        self.send_sems, self.recv_sems = send_sems, recv_sems
        self.taken, self.pending = 0, []

    def slots(self, count):
        base = self.taken
        self.taken += count
        assert self.taken <= self.recv_sems.shape[0]
        return base

    def send(self, src, dst, device, slot, when=None):
        index = len(self.pending)
        if index == self.send_sems.shape[0]:
            done, copy, index = self.pending.pop(0)
            run(done, copy.wait_send)
        copy = pltpu.make_async_remote_copy(
            src_ref=src,
            dst_ref=dst,
            send_sem=self.send_sems.at[index],
            recv_sem=self.recv_sems.at[slot],
            device_id=device,
            device_id_type=MESH,
        )
        run(when, copy.start)
        self.pending.append((when, copy, index))

    def wait(self, slot, ref):
        pltpu.make_async_remote_copy(
            src_ref=ref,
            dst_ref=ref,
            send_sem=self.send_sems.at[0],
            recv_sem=self.recv_sems.at[slot],
            device_id=(self.sib, self.c),
            device_id_type=MESH,
        ).wait_recv()

    def drain(self):
        for when, copy, _ in self.pending:
            run(when, copy.wait_send)


class GatherCtx:
    def __init__(self, net, views, count, turn=False):
        self.net, self.views, self.count, self.turn = net, views, count, turn
        self.along, self.beside = net.slots(4 * count), net.slots(4 * count)
        self.turned = net.slots(2) if turn else None

    def begin(self, i, src):
        net, count = self.net, self.count
        dst, at = self.views(net.c)[i], net.z * count + i
        net.send(src, dst, (net.b, net.side), self.beside + at)
        net.send(src, dst, (net.b, net.c + 2), self.along + at, net.z < 3)
        net.send(src, dst, (net.b, net.c - 2), self.along + at, net.z > 0)

    def start(self, srcs):
        for i, src in enumerate(srcs):
            self.begin(i, src)

    def stage(self, d):
        net, count = self.net, self.count
        for sign in (-1, 1):
            zz = net.z + sign * d
            here = zz >= 0 if sign < 0 else zz <= 3
            refs = self.views(2 * zz + net.x)
            onward = both(here, net.z < 3 if sign < 0 else net.z > 0)
            dsts = self.views(2 * zz + net.x)
            for i in range(count):
                slot = self.along + zz * count + i
                pl.when(here)(lambda slot=slot, ref=refs[i]: net.wait(slot, ref))
                if d < 3:
                    net.send(refs[i], dsts[i], (net.b, net.c - 2 * sign), slot, onward)
                goes = here
                if self.turn and i == count - 1:
                    goes = both(here, jnp.logical_and(zz > 0, zz < 3))
                net.send(refs[i], dsts[i], (net.b, net.side), self.beside + zz * count + i, goes)

    def piece(self, end):
        return self.views(2 * end + 1 - self.net.x)[self.count - 1]

    def corner(self):
        net, count = self.net, self.count
        for end, step in ((0, 2), (3, -2)):
            ref, slot = self.piece(end), self.beside + end * count + count - 1
            pl.when(net.z == end)(lambda slot=slot, ref=ref: net.wait(slot, ref))
            net.send(ref, ref, (net.b, net.c + step), self.turned + (end > 0), net.z == end)

    def pass_on(self, d):
        net = self.net
        for end, step in ((0, 2), (3, -2)):
            here = net.z == (end + d if end == 0 else end - d)
            ref, slot = self.piece(end), self.turned + (end > 0)
            pl.when(here)(lambda slot=slot, ref=ref: net.wait(slot, ref))
            if d < 3:
                net.send(ref, ref, (net.b, net.c + step), slot, here)

    def finish(self):
        net, count = self.net, self.count
        for zz in range(4):
            refs = self.views(2 * zz + 1 - net.x)
            for i in range(count):
                if not (self.turn and i == count - 1 and zz in (0, 3)):
                    net.wait(self.beside + zz * count + i, refs[i])


def chunks(ref):
    if len(ref.shape) == 3:
        return ref.shape[0], lambda i: (i,)
    rows = min(32, ref.shape[0])
    return ref.shape[0] // rows, lambda i: (pl.ds(pl.multiple_of(i * rows, rows), rows),)


def add_into(target, terms, dtype=BF):
    count, at = chunks(target)

    def body(i, carry):
        total = terms[0][at(i)].astype(F32)
        for term in terms[1:]:
            total = total + term[at(i)].astype(F32)
        target[at(i)] = total.astype(dtype)
        return carry

    lax.fori_loop(0, count, body, 0)


class ReduceLine:
    def __init__(self, net, mine, up, down):
        self.net, self.mine, self.up, self.down = net, mine, up, down
        self.s_up, self.s_down = net.slots(4), net.slots(4)

    def give(self, k, upward, when):
        net = self.net
        if upward:
            net.send(self.mine(k), self.up.at[k], (net.b, net.c + 2), self.s_up + k, when)
        else:
            net.send(self.mine(k), self.down.at[k], (net.b, net.c - 2), self.s_down + k, when)

    def take(self, k, upward, when):
        box, slot = (self.up, self.s_up) if upward else (self.down, self.s_down)
        mine = self.mine(k)

        @pl.when(when)
        def _():
            self.net.wait(slot + k, box.at[k])
            add_into(mine, [mine, box.at[k]])

        self.give(k, upward, when)

    def launch(self):
        for k in (1, 2, 3):
            self.give(4 - k, True, self.net.z == 0)
            self.give(k - 1, False, self.net.z == 3)

    def pass_one(self):
        for k in (0, 1):
            self.take(3 - k, True, self.net.z == 1)
            self.take(k, False, self.net.z == 2)

    def pass_two(self):
        self.take(0, False, self.net.z == 1)
        self.take(3, True, self.net.z == 2)

    def finish(self, target):
        net, z = self.net, self.net.z
        mine = self.mine(z)

        @pl.when(z >= 1)
        def _():
            net.wait(self.s_up + z, self.up.at[z])

        @pl.when(z <= 2)
        def _():
            net.wait(self.s_down + z, self.down.at[z])

        pl.when(z == 0)(lambda: add_into(target, [mine, self.down.at[z]]))
        pl.when(z == 3)(lambda: add_into(target, [mine, self.up.at[z]]))
        pl.when(jnp.logical_and(z > 0, z < 3))(
            lambda: add_into(target, [mine, self.up.at[z], self.down.at[z]])
        )


class ReduceCtx:
    def __init__(self, net, mine, beside, up, down):
        self.net, self.mine, self.beside = net, mine, beside
        self.slots = net.slots(4)
        self.line = ReduceLine(net, lambda k: mine(2 * k + net.x), up, down)

    def start(self):
        net = self.net
        for k in (3, 0, 2, 1):
            net.send(self.mine(2 * k + 1 - net.x), self.beside.at[k], (net.b, net.side), self.slots + k)

    def fold(self):
        for k in (3, 0, 2, 1):
            self.net.wait(self.slots + k, self.beside.at[k])
            mine = self.line.mine(k)
            add_into(mine, [mine, self.beside.at[k]])
        self.line.launch()


class SwapCtx:
    def __init__(self, net, src, dst, count):
        self.net, self.src, self.dst, self.count = net, src, dst, count
        self.base = net.slots(NC * count)

    def give(self, j):
        net, count = self.net, self.count
        srcs, dsts = self.src(j), self.dst(net.c)
        for i in range(count):
            net.send(srcs[i], dsts[i], (net.b, j), self.base + net.c * count + i, net.c != j)

        @pl.when(net.c == j)
        def _():
            for one, two in zip(srcs, dsts):
                two[...] = one[...]

    def start(self):
        for j in range(NC):
            self.give(j)

    def finish(self):
        net, count = self.net, self.count
        for step in range(1, NC):
            j = lax.rem(net.c - step + NC, NC)
            dsts = self.dst(j)
            for i in range(count):
                net.wait(self.base + j * count + i, dsts[i])


class GatherSide:
    def __init__(self, net, views):
        self.net, self.views = net, views
        self.far, self.near = net.slots(NB), net.slots(NB)

    def give(self, j, src):
        net = self.net
        net.send(src, self.views(j), (net.b, net.side), self.far + j)

    def relay(self, j):
        net, ref = self.net, self.views(j)
        net.wait(self.far + j, ref)
        net.send(ref, ref, (net.sib, net.c), self.near + j)

    def finish(self):
        net = self.net
        for j in (net.sib, net.diag):
            net.wait(self.near + j, self.views(j))


class GatherBatch:
    def __init__(self, net, views, count=1):
        self.net, self.views, self.count = net, views, count
        self.base = net.slots(NB * count)

    def start(self, srcs):
        net = self.net
        dsts = self.views(net.b)
        for i in range(self.count):
            slot = self.base + net.b * self.count + i
            net.send(srcs[i], dsts[i], (net.across, net.c), slot)
        for i in range(self.count):
            slot = self.base + net.b * self.count + i
            net.send(srcs[i], dsts[i], (net.sib, net.c), slot)

    def relay(self):
        net = self.net
        refs = self.views(net.across)
        for i in range(self.count):
            slot = self.base + net.across * self.count + i
            net.wait(slot, refs[i])
            net.send(refs[i], refs[i], (net.sib, net.c), slot)

    def take(self, j):
        refs = self.views(j)
        for i in range(self.count):
            self.net.wait(self.base + j * self.count + i, refs[i])

    def near(self):
        self.take(self.net.sib)

    def far(self):
        self.take(self.net.diag)

    def finish(self):
        self.near()
        self.far()


class ReduceBatch:
    def __init__(self, net, mine, boxes):
        self.net, self.mine, self.boxes = net, mine, boxes
        self.base = net.slots(3)

    def give(self):
        net = self.net
        net.send(self.mine(net.diag), self.boxes.at[0], (net.sib, net.c), self.base)

    def cross(self):
        net = self.net
        net.wait(self.base, self.boxes.at[0])
        block = self.mine(net.across)
        add_into(block, [block, self.boxes.at[0]])
        net.send(block, self.boxes.at[1], (net.across, net.c), self.base + 1)

    def keep(self):
        net = self.net
        net.send(self.mine(net.sib), self.boxes.at[2], (net.sib, net.c), self.base + 2)

    def finish(self):
        net = self.net
        net.wait(self.base + 2, self.boxes.at[2])
        net.wait(self.base + 1, self.boxes.at[1])
        return [self.mine(net.b), self.boxes.at[1], self.boxes.at[2]]


def row_of(parts, index):
    return jnp.concatenate([parts[j, index : index + 1, :] for j in range(NB)], axis=1)


def put_row(target, index, row):
    for j in range(NB):
        target[j, index : index + 1, :] = row[:, j * SHARD : (j + 1) * SHARD]


def rows_of(block, size):
    return lambda j: block.at[pl.ds(pl.multiple_of(j * size, size), size)]


def normalise(inputs):
    centre = inputs - jnp.mean(inputs, -1, keepdims=True)
    spread = jnp.mean(centre * centre, -1, keepdims=True)
    scale = lax.rsqrt(spread + epsilon)
    return centre * scale, scale


def head_lanes(h, rows):
    lane = lax.broadcasted_iota(jnp.int32, (rows, PAIR), 1)
    return (lane >= h * HEAD_DIM) & (lane < (h + 1) * HEAD_DIM)


QB = 256


def scores_of(keys, query, masked):
    scores = mm(keys, query, NT) * 0.125
    if masked:
        key_pos = lax.broadcasted_iota(jnp.int32, scores.shape, 0)
        query_pos = lax.broadcasted_iota(jnp.int32, scores.shape, 1)
        scores = jnp.where(key_pos <= query_pos, scores, masked_value)
    return scores


def attend(mix, value_t, att, lse, work, low_work, ready):
    value_t[...] = mix[:, 2 * PAIR :].astype(F32).T.astype(BF)
    for qb in reversed(range(LENGTH // QB)):
        here = slice(qb * QB, (qb + 1) * QB)
        outs = []
        for h in range(2):
            query = jnp.where(head_lanes(h, QB), mix[here, :PAIR], jnp.zeros((), BF))
            top = None
            for kb in range(qb + 1):
                keys = slice(kb * QB, (kb + 1) * QB)
                scores = scores_of(mix[keys, PAIR : 2 * PAIR], query, kb == qb)
                work[h, keys, :] = scores
                peak = jnp.max(scores, axis=0, keepdims=True)
                top = peak if top is None else jnp.maximum(top, peak)
            total = None
            for kb in range(qb + 1):
                keys = slice(kb * QB, (kb + 1) * QB)
                grown = jnp.exp(work[h, keys, :] - top)
                part = jnp.sum(grown, axis=0, keepdims=True)
                total = part if total is None else total + part
                low_work[h, keys, :] = grown.astype(BF)
            count = (qb + 1) * QB
            lanes = slice(h * HEAD_DIM, (h + 1) * HEAD_DIM)
            out = mm(value_t[lanes, :count], low_work[h, :count, :])
            outs.append(out / total)
            lse[h * 4 + qb : h * 4 + qb + 1, :] = top + jnp.log(total)
        att[here, :] = jnp.concatenate(outs, axis=0).T.astype(BF)
        ready(qb)


def attend_back(mix, key_t, dout, lse, gmix, grad_k, grad_v, work, more, low_work, low_more):
    key_t[...] = mix[:, PAIR : 2 * PAIR].astype(F32).T.astype(BF)
    grad_k[...] = jnp.zeros_like(grad_k)
    grad_v[...] = jnp.zeros_like(grad_v)
    for qb in reversed(range(LENGTH // QB)):
        here = slice(qb * QB, (qb + 1) * QB)
        outs = []
        count = (qb + 1) * QB
        for h in range(2):
            lanes = head_lanes(h, QB)
            query = jnp.where(lanes, mix[here, :PAIR], jnp.zeros((), BF))
            grad = jnp.where(lanes, dout[here, :], jnp.zeros((), BF))
            level = lse[h * 4 + qb : h * 4 + qb + 1, :]
            delta = None
            for kb in range(qb + 1):
                keys = slice(kb * QB, (kb + 1) * QB)
                probs = jnp.exp(scores_of(mix[keys, PAIR : 2 * PAIR], query, kb == qb) - level)
                grad_probs = mm(mix[keys, 2 * PAIR :], grad, NT)
                part = jnp.sum(probs * grad_probs, axis=0, keepdims=True)
                delta = part if delta is None else delta + part
                work[h, keys, :] = probs
                more[h, keys, :] = grad_probs
                low_work[h, keys, :] = probs.astype(BF)
            for kb in range(qb + 1):
                keys = slice(kb * QB, (kb + 1) * QB)
                low_more[h, keys, :] = (work[h, keys, :] * (more[h, keys, :] - delta)).astype(BF)
            grad_v[:count, :] += mm(low_work[h, :count, :], grad)
            grad_k[:count, :] += mm(low_more[h, :count, :], query)
            rows = slice(h * HEAD_DIM, (h + 1) * HEAD_DIM)
            outs.append(mm(key_t[rows, :count], low_more[h, :count, :]) * 0.125)
        gmix[here, :PAIR] = jnp.concatenate(outs, axis=0).T.astype(BF)
        gmix[here, PAIR : 2 * PAIR] = (grad_k[here, :] * 0.125).astype(BF)
        gmix[here, 2 * PAIR :] = grad_v[here, :].astype(BF)


gelu_scale = 0.7978845608028654
gelu_cubic = 0.044715


def gelu_pair(x):
    square = x * x
    bent = jnp.tanh(gelu_scale * x * (1.0 + gelu_cubic * square))
    half = 0.5 * (1.0 + bent)
    slope = half + 0.5 * x * (1.0 - bent * bent) * (gelu_scale * (1.0 + 3.0 * gelu_cubic * square))
    return x * half, slope


SCRATCH = dict(
    small=((SMALL_ROWS, SHARD), F32),
    parts=((NB, SMALL_ROWS, SHARD), F32),
    qv_rows=((16, PAIR), F32),
    wpair=((WIDTH, 3 * PAIR), BF),
    wfull=((WIDTH, 3 * WIDTH), BF),
    wproj_all=((WIDTH, WIDTH), BF),
    wfc_mine=((WIDTH, WIDTH), BF),
    wout_mine=((WIDTH, WIDTH), BF),
    g_all=((NB * ROWS, WIDTH), BF),
    hat_one=((ROWS, WIDTH), F32),
    scale_one=((ROWS, 1), F32),
    n_one=((LENGTH, WIDTH), BF),
    mix=((LENGTH, 3 * PAIR), BF),
    turned=((PAIR, LENGTH), BF),
    att=((LENGTH, PAIR), BF),
    lse=((8, QB), F32),
    work=((2, LENGTH, QB), F32),
    more=((2, LENGTH, QB), F32),
    low_work=((2, LENGTH, QB), BF),
    low_more=((2, LENGTH, QB), BF),
    att_own=((ROWS, WIDTH), BF),
    middle=((ROWS, WIDTH), F32),
    hat_two=((ROWS, WIDTH), F32),
    scale_two=((ROWS, 1), F32),
    n_two=((NB * ROWS, WIDTH), BF),
    hidden=((NB * ROWS, WIDTH), BF),
    grad_pre=((NB * ROWS, WIDTH), BF),
    p_norm=((NB * ROWS, WIDTH), BF),
    p_norm_box=((3, ROWS, WIDTH), BF),
    p_layer=((NB * ROWS, WIDTH), BF),
    p_layer_box=((3, ROWS, WIDTH), BF),
    g_side=((NB * ROWS, WIDTH), BF),
    n_side=((NB * ROWS, WIDTH), BF),
    hidden_side=((NB * ROWS, WIDTH // 2), BF),
    pre_side=((NB * ROWS, WIDTH // 2), BF),
    p_out=((2, 256, WIDTH), BF),
    out_up=((2, 4, 64, WIDTH), BF),
    out_down=((2, 4, 64, WIDTH), BF),
    out_block=((ROWS, WIDTH), BF),
    p_fc=((2, NB, 4, 64, 256), BF),
    fc_up=((2, 4, NB, 64, 256), BF),
    fc_down=((2, 4, NB, 64, 256), BF),
    fc_sum=((2, NB, 64, 256), BF),
    fc_block=((2, 64, WIDTH), BF),
    p_proj=((WIDTH, WIDTH), BF),
    p_proj_box=((3, SHARD, WIDTH), BF),
    proj_sum=((SHARD, WIDTH), BF),
    proj_beside=((4, 32, WIDTH), BF),
    proj_up=((4, 32, WIDTH), BF),
    proj_down=((4, 32, WIDTH), BF),
    proj_block=((32, WIDTH), BF),
    grad_middle=((ROWS, WIDTH), F32),
    branch=((ROWS, WIDTH), BF),
    g_att=((ROWS, WIDTH), BF),
    dout=((LENGTH, PAIR), BF),
    gmix=((LENGTH, 3 * PAIR), BF),
    grad_k=((LENGTH, PAIR), F32),
    grad_v=((LENGTH, PAIR), F32),
    gmix_own=((NC, ROWS, 3 * PAIR), BF),
    gmix_all=((ROWS, 3 * WIDTH), BF),
    p_qkv=((WIDTH, 3 * PAIR), BF),
    p_qkv_box=((3, SHARD, 3 * PAIR), BF),
    qkv_block=((SHARD, 3 * PAIR), BF),
    gn_one=((ROWS, WIDTH), F32),
    gs=((NB, SMALL_ROWS, SHARD), F32),
    gqv=((16, PAIR), F32),
    gs_box=((NB, SMALL_ROWS, SHARD), F32),
    gs_sum=((SMALL_ROWS, SHARD), F32),
    gs_far=((NC, SMALL_ROWS, SHARD), F32),
)
TURN_OUT, TURN_FC = (False, True), (False, True)
SENDS, RECVS, LOCALS = 64, 260, 16


def layer_kernel(*refs):
    tokens, cotangent = refs[:2]
    vectors = refs[2:10]
    wqkv, wproj, wfc, wout = refs[10:14]
    layer_out, grad_tokens, grad_small, o_qkv, o_proj, o_fc, o_out = refs[14:21]
    scratch = refs[21:]
    s = SimpleNamespace(**dict(zip(SCRATCH, scratch)))
    send_sems, recv_sems, local_sems = scratch[len(SCRATCH) :]
    b, c = lax.axis_index("batch"), lax.axis_index("ctx")
    net = Net(b, c, send_sems, recv_sems)
    v = SimpleNamespace(keep=[])
    locals_open = []

    def local(src, dst):
        copy = pltpu.make_async_copy(src, dst, local_sems.at[len(locals_open)])
        copy.start()
        locals_open.append(copy)
        return copy

    def own(ref, size):
        return rows_of(ref, size)(b)

    def cols(ref, start, count=PAIR):
        return ref.at[:, pl.ds(pl.multiple_of(start, 128), count)]

    def halves(ref, size, j):
        block = rows_of(ref, size)(j)
        return [block.at[0 : size // 2], block.at[size // 2 : size]]

    def loop(count, size, body):
        def step(i, carry):
            body(pl.ds(pl.multiple_of(i * size, size), size))
            return carry

        lax.fori_loop(0, count, step, 0)

    batch_others = [lax.rem(b + i, NB) for i in range(1, NB)]

    small_slots, fc_slots, fc_near_slots = net.slots(NB), net.slots(NB), net.slots(NB)
    hidden_slots, pre_slots, side_slot, swap_slots = net.slots(4), net.slots(4), net.slots(1), net.slots(2 * NB)
    proj_slots, proj_side_slot, proj_near_slots = net.slots(NB), net.slots(1), net.slots(2)
    gs_slots, far_slots = net.slots(NB), net.slots(NC)
    gather_pair = GatherBatch(net, lambda j: [rows_of(s.wpair, SHARD)(j)])
    gather_one = GatherCtx(net, lambda j: halves(s.n_one, ROWS, j), 2, True)
    gather_g = GatherBatch(net, lambda j: [rows_of(s.g_all, ROWS)(j)])
    gather_gs = GatherSide(net, rows_of(s.g_side, ROWS))
    gather_ns = GatherBatch(net, lambda j: [rows_of(s.n_side, ROWS)(j)])
    gather_two = GatherBatch(net, lambda j: halves(s.n_two, ROWS, j), 2)
    gather_full = [
        GatherBatch(net, lambda j, i=i: [rows_of(s.wfull, SHARD // 2)(2 * j + i)]) for i in range(2)
    ]
    swap_att = SwapCtx(
        net, lambda j: [rows_of(s.att, ROWS)(j)], lambda j: [cols(s.att_own, j * PAIR)], 1
    )
    swap_grad = SwapCtx(
        net, lambda j: [cols(s.g_att, j * PAIR)], lambda j: [rows_of(s.dout, ROWS)(j)], 1
    )
    swap_mix = SwapCtx(
        net, lambda j: [rows_of(s.gmix, ROWS)(j)], lambda j: [s.gmix_own.at[j]], 1
    )
    reduce_norm = ReduceBatch(net, rows_of(s.p_norm, ROWS), s.p_norm_box)
    reduce_layer = ReduceBatch(net, rows_of(s.p_layer, ROWS), s.p_layer_box)
    reduce_proj = ReduceBatch(net, rows_of(s.p_proj, SHARD), s.p_proj_box)
    reduce_qkv = ReduceBatch(net, rows_of(s.p_qkv, SHARD), s.p_qkv_box)
    reduce_part = ReduceCtx(net, rows_of(s.proj_sum, 32), s.proj_beside, s.proj_up, s.proj_down)
    reduce_out = [
        ReduceLine(net, rows_of(s.p_out.at[i], 64), s.out_up.at[i], s.out_down.at[i]) for i in range(2)
    ]
    reduce_fc = [
        ReduceLine(net, lambda k, i=i: s.p_fc.at[i, :, k], s.fc_up.at[i], s.fc_down.at[i])
        for i in range(2)
    ]

    def out_view(i, j):
        return rows_of(o_out, 64)(8 * (j % 2) + 4 * i + j // 2)

    def fc_view(i, j):
        return o_fc.at[j % 2, i, pl.ds(pl.multiple_of((j // 2) * 64, 64), 64)]

    gather_out = [GatherCtx(net, lambda j, i=i: [out_view(i, j)], 1, TURN_OUT[i]) for i in range(2)]
    gather_fc = [GatherCtx(net, lambda j, i=i: [fc_view(i, j)], 1, TURN_FC[i]) for i in range(2)]
    gather_qkv = GatherCtx(net, lambda j: halves(o_qkv.at[j], SHARD, 0), 2, True)
    gather_part = GatherCtx(net, lambda j: [rows_of(o_proj, 32)(j)], 1)

    scale, hat = s.scale_one, s.hat_one
    half, pair_z = net.z % 2, net.c + 2 - 4 * (net.z % 2)
    half_rows = pl.ds(pl.multiple_of(half * (SHARD // 2), SHARD // 2), SHARD // 2)
    other_rows = pl.ds(pl.multiple_of((1 - half) * (SHARD // 2), SHARD // 2), SHARD // 2)
    side_rows = pl.ds(pl.multiple_of(net.x * (SHARD // 2), SHARD // 2), SHARD // 2)
    other_side_rows = pl.ds(pl.multiple_of((1 - net.x) * (SHARD // 2), SHARD // 2), SHARD // 2)
    chip_rows = [
        pl.ds(pl.multiple_of(first * 256, 256), 256) for first in (b // 2, 1 - b // 2)
    ]
    n_mine = rows_of(s.n_one, ROWS)(c)
    n_two_mine = own(s.n_two, ROWS)
    g_mine = own(s.g_all, ROWS)
    n_beside = own(s.n_side, ROWS)

    def enter():
        v.get_pair = [
            local(cols(wqkv, t * WIDTH + c * PAIR), own(s.wpair, SHARD).at[:, t * PAIR : (t + 1) * PAIR])
            for t in range(3)
        ]
        v.get_proj = local(wproj, own(s.wproj_all, SHARD))
        v.get_rest = [
            local(cols(wfc, b * WIDTH, WIDTH), own(s.wfc_mine, SHARD)),
            local(wout, s.wout_mine),
            local(wqkv, own(s.wfull, SHARD)),
            local(cotangent, g_mine),
        ]
        barrier = pltpu.get_barrier_semaphore()
        others = [(j, c) for j in batch_others]
        others += [(b, lax.rem(c + i, NC)) for i in range(1, NC)]
        for device in others:
            pl.semaphore_signal(barrier, inc=1, device_id=device, device_id_type=MESH)
        s.small[...] = jnp.zeros_like(s.small)
        row = 0
        for vector in vectors:
            for i in range(vector.shape[0] // SHARD):
                piece = vector[i * SHARD : (i + 1) * SHARD].astype(F32)
                s.small[row : row + 1, :] = piece.reshape(1, SHARD)
                row += 1

        def norm_rows(at):
            hat[at, :], scale[at, :] = normalise(tokens[at, :].astype(F32))

        loop(ROWS // 32, 32, norm_rows)
        for copy in v.get_pair:
            copy.wait()
        s.parts[pl.ds(b, 1)] = s.small[...][None]
        pl.semaphore_wait(barrier, len(others))

    def send_small():
        for j in batch_others:
            net.send(s.small, s.parts.at[b], (j, c), small_slots + b)

    def pair_start():
        gather_pair.start([own(s.wpair, SHARD)])

    def g_start():
        gather_g.start([cotangent])

    def norm_one():
        for j in batch_others:
            net.wait(small_slots + j, s.parts.at[j])
        gain, bias = row_of(s.parts, 0), row_of(s.parts, 1)

        def gain_rows(at):
            n_mine[at, :] = (hat[at, :] * gain + bias).astype(BF)

        loop(ROWS // 32, 32, gain_rows)
        gather_one.start(halves(s.n_one, ROWS, c))

    def proj_start():
        mine = own(s.wproj_all, SHARD)
        net.send(wproj.at[side_rows], mine.at[side_rows], (net.across, c), proj_slots + b)
        net.send(wproj, mine, (net.sib, c), proj_slots + b)

    def proj_relay():
        block = rows_of(s.wproj_all, SHARD)(net.across).at[side_rows]
        net.wait(proj_slots + net.across, block)
        net.send(block, block, (b, net.side), proj_side_slot)
        net.send(block, block, (net.sib, c), proj_near_slots)

    def proj_side():
        block = rows_of(s.wproj_all, SHARD)(net.across).at[other_side_rows]
        net.wait(proj_side_slot, block)
        net.send(block, block, (net.sib, c), proj_near_slots + 1)

    def fc_start():
        net.send(cols(wfc, net.sib * WIDTH, WIDTH), own(s.wfc_mine, SHARD), (net.sib, c), fc_slots + b)
        for j in (net.across, net.diag):
            net.send(
                wfc.at[half_rows, pl.ds(pl.multiple_of(j * WIDTH, WIDTH), WIDTH)],
                own(s.wfc_mine, SHARD).at[half_rows],
                (j, c),
                fc_slots + b,
            )

    def fc_relay():
        for j in (net.across, net.diag):
            block = rows_of(s.wfc_mine, SHARD)(j).at[half_rows]
            net.wait(fc_slots + j, block)
            net.send(block, block, (b, pair_z), fc_near_slots + j)

    def qv_rows():
        for p in range(NC):
            at = p * PAIR
            row, lane = 2 + (at % 512) // SHARD, at % SHARD
            s.qv_rows[p : p + 1, :] = s.parts[at // 512, row : row + 1, lane : lane + PAIR]
            s.qv_rows[8 + p : 9 + p, :] = s.parts[2 + at // 512, row : row + 1, lane : lane + PAIR]

    def g_relay():
        gather_g.relay()

    def gs_give_own():
        gather_gs.give(b, cotangent)

    def gs_give_across():
        gather_gs.give(net.across, rows_of(s.g_all, ROWS)(net.across))

    def gs_relay_own():
        gather_gs.relay(b)

    def gs_relay_across():
        gather_gs.relay(net.across)

    def mix():
        mix_bias = jnp.concatenate(
            [s.qv_rows[pl.ds(c, 1), :], jnp.zeros((1, PAIR), F32), s.qv_rows[pl.ds(8 + c, 1), :]], axis=1
        )

        def mix_rows(at):
            s.mix[at, :] = (mm(s.n_one[at, :], s.wpair[...]) + mix_bias).astype(BF)

        loop(LENGTH // QB, QB, mix_rows)

    def att():
        def ready(qb):
            swap_att.give(2 * qb)
            swap_att.give(2 * qb + 1)

        attend(s.mix, s.turned, s.att, s.lse, s.work, s.low_work, ready)

    def proj_finish():
        v.get_proj.wait()
        net.wait(proj_slots + net.sib, rows_of(s.wproj_all, SHARD)(net.sib))
        block = rows_of(s.wproj_all, SHARD)(net.diag)
        net.wait(proj_near_slots, block.at[side_rows])
        net.wait(proj_near_slots + 1, block.at[other_side_rows])

    def middle():
        def middle_cols(at):
            s.middle[:, at] = mm(s.att_own[...], s.wproj_all[:, at]) + tokens[:, at].astype(F32)

        loop(WIDTH // 256, 256, middle_cols)
        proj_bias, gain_two, bias_two = row_of(s.parts, 4), row_of(s.parts, 5), row_of(s.parts, 6)

        def norm_two_rows(at):
            middle = s.middle[at, :] + proj_bias
            s.middle[at, :] = middle
            norm, width = normalise(middle)
            s.hat_two[at, :], s.scale_two[at, :] = norm, width
            n_two_mine[at, :] = (norm * gain_two + bias_two).astype(BF)

        loop(ROWS // 32, 32, norm_two_rows)
        gather_two.start(halves(s.n_two, ROWS, b))

    def ns_give():
        net.send(n_two_mine, n_beside, (b, net.side), side_slot)

    def ns_start():
        net.wait(side_slot, n_beside)
        gather_ns.start([n_beside])

    def feed_wait():
        for copy in v.get_rest:
            copy.wait()
        gather_g.finish()
        net.wait(fc_slots + net.sib, rows_of(s.wfc_mine, SHARD)(net.sib))
        for j in (net.across, net.diag):
            net.wait(fc_near_slots + j, rows_of(s.wfc_mine, SHARD)(j).at[other_rows])
        s.gs[...] = jnp.zeros_like(s.gs)

    def feed_cols(r, i):
        n = lax.rem(2 * (1 - net.x) + i, 4)
        rows, at = chip_rows[r], pl.ds(pl.multiple_of(n * 256, 256), 256)
        pre = mm(s.n_two[rows, :], s.wfc_mine[:, at]) + s.small[pl.ds(7 + n, 1), :]
        value, slope = gelu_pair(pre)
        s.hidden[rows, at] = value.astype(BF)
        grad = (mm(s.g_all[rows, :], s.wout_mine[at, :], NT) * slope).astype(BF)
        s.grad_pre[rows, at] = grad
        s.gs[pl.ds(b, 1), pl.ds(7 + n, 1), :] += jnp.sum(grad.astype(F32), 0, keepdims=True)[None]

    def tile(ref, r, i):
        return ref.at[chip_rows[r], pl.ds(pl.multiple_of((2 * (1 - net.x) + i) * 256, 256), 256)]

    def side_tile(ref, r, i):
        return ref.at[chip_rows[r], i * 256 : (i + 1) * 256]

    def feed_i(r, i):
        feed_cols(r, i)
        net.send(tile(s.hidden, r, i), side_tile(s.hidden_side, r, i), (b, net.side), hidden_slots + 2 * r + i)

    def pre_give(r, i):
        net.send(tile(s.grad_pre, r, i), side_tile(s.pre_side, r, i), (b, net.side), pre_slots + 2 * r + i)

    def feed_rest(r):
        def step(i, carry):
            feed_cols(r, i)
            return carry

        lax.fori_loop(2, 4, step, 0)

    def norm_block(j):
        at = pl.ds(pl.multiple_of(j * ROWS, ROWS), ROWS)
        s.p_norm[at, :] = mm(s.grad_pre[at, :], s.wfc_mine[...], NT).astype(BF)

    def norm_diag():
        norm_block(net.diag)
        reduce_norm.give()

    def norm_across():
        norm_block(net.across)

    def norm_sib():
        norm_block(net.sib)
        reduce_norm.keep()

    def norm_own():
        norm_block(b)

    def back_two():
        gain_two = row_of(s.parts, 5)
        terms = reduce_norm.finish()

        def back_rows(i, carry):
            at = pl.ds(pl.multiple_of(i * 32, 32), 32)
            grad_gain, grad_bias, sum_branch, sum_g = carry
            grad = terms[0][at, :].astype(F32) + terms[1][at, :].astype(F32) + terms[2][at, :].astype(F32)
            norm = s.hat_two[at, :]
            scaled = grad * gain_two
            inner = scaled - jnp.mean(scaled, -1, keepdims=True)
            inner = inner - norm * jnp.mean(scaled * norm, -1, keepdims=True)
            g = g_mine[at, :].astype(F32)
            total = g + s.scale_two[at, :] * inner
            s.grad_middle[at, :] = total
            low = total.astype(BF)
            s.branch[at, :] = low
            return (
                grad_gain + jnp.sum(grad * norm, 0, keepdims=True),
                grad_bias + jnp.sum(grad, 0, keepdims=True),
                sum_branch + jnp.sum(low.astype(F32), 0, keepdims=True),
                sum_g + jnp.sum(g, 0, keepdims=True),
            )

        sums = lax.fori_loop(0, ROWS // 32, back_rows, (jnp.zeros((1, WIDTH), F32),) * 4)
        put_row(s.gs, 5, sums[0])
        put_row(s.gs, 6, sums[1])
        put_row(s.gs, 4, sums[2])
        put_row(s.gs, 11, sums[3])

        def att_cols(at):
            s.g_att[:, at] = mm(s.branch[...], s.wproj_all[at, :], NT).astype(BF)

        loop(4, 256, att_cols)
        swap_grad.start()

    def p_out(i):
        at = slice(i * 256, (i + 1) * 256)
        for r in range(2):
            net.wait(hidden_slots + 2 * r + i, side_tile(s.hidden_side, r, i))
        mine = cols(s.hidden, net.x * 512 + i * 256, 256)
        s.p_out[i] = (
            mm(mine[...], s.g_all[...], TN) + mm(s.hidden_side[:, at], s.g_side[...], TN)
        ).astype(BF)
        reduce_out[i].launch()

    def out_done(i):
        part = s.out_block.at[i * 64 : (i + 1) * 64]
        reduce_out[i].finish(part)
        gather_out[i].begin(0, part)
        v.keep.append(local(part, out_view(i, c)))

    def p_fc(i):
        at = slice(i * 256, (i + 1) * 256)
        for r in range(2):
            net.wait(pre_slots + 2 * r + i, side_tile(s.pre_side, r, i))
        mine = cols(s.grad_pre, net.x * 512 + i * 256, 256)

        def fc_rows(k, carry):
            rows = pl.ds(pl.multiple_of(k * 256, 256), 256)
            total = mm(s.n_two[:, rows], mine[...], TN) + mm(s.n_side[:, rows], s.pre_side[:, at], TN)
            s.p_fc[i, pl.ds(k, 1)] = total.astype(BF).reshape(1, 4, 64, 256)
            return carry

        lax.fori_loop(0, 4, fc_rows, 0)
        reduce_fc[i].launch()

    def fc_done(i):
        reduce_fc[i].finish(s.fc_sum.at[i])
        mine = pl.ds(pl.multiple_of(b * 256, 256), 256)
        for j in batch_others:
            net.send(s.fc_sum.at[i, j], s.fc_block.at[i, :, mine], (j, c), swap_slots + 2 * b + i)
        s.fc_block[i, :, mine] = s.fc_sum[i, pl.ds(b, 1)][0]

    def fc_swap(i):
        for j in batch_others:
            at = pl.ds(pl.multiple_of(j * 256, 256), 256)
            net.wait(swap_slots + 2 * j + i, s.fc_block.at[i, :, at])
        gather_fc[i].begin(0, s.fc_block.at[i])
        v.keep.append(local(s.fc_block.at[i], fc_view(i, c)))

    def p_proj():
        def proj_rows(at):
            s.p_proj[at, :] = mm(s.att_own[:, at], s.branch[...], TN).astype(BF)

        loop(4, 256, proj_rows)
        reduce_proj.give()
        reduce_proj.keep()

    def proj_done():
        add_into(s.proj_sum, reduce_proj.finish())
        reduce_part.start()

    def part_done():
        reduce_part.line.finish(s.proj_block)
        gather_part.begin(0, s.proj_block)
        v.keep.append(local(s.proj_block, rows_of(o_proj, 32)(c)))

    def p_layer():
        def layer_block(j):
            at = pl.ds(pl.multiple_of(j * ROWS, ROWS), ROWS)
            s.p_layer[at, :] = mm(s.hidden[at, :], s.wout_mine[...]).astype(BF)

        layer_block(net.diag)
        reduce_layer.give()
        layer_block(net.sib)
        reduce_layer.keep()
        layer_block(net.across)
        layer_block(b)

    def layer_end():
        layer_bias = row_of(s.parts, 11)
        terms = reduce_layer.finish()

        def layer_rows(at):
            total = terms[0][at, :].astype(F32) + terms[1][at, :].astype(F32) + terms[2][at, :].astype(F32)
            layer_out[at, :] = (s.middle[at, :] + total + layer_bias).astype(BF)

        loop(ROWS // 32, 32, layer_rows)

    def att_back():
        attend_back(
            s.mix, s.turned, s.dout, s.lse, s.gmix, s.grad_k, s.grad_v,
            s.work, s.more, s.low_work, s.low_more,
        )

    def mix_give(k):
        swap_mix.give(2 * k)
        swap_mix.give(2 * k + 1)

    def p_qkv():
        def qkv_block(j):
            at = pl.ds(pl.multiple_of(j * SHARD, SHARD), SHARD)
            s.p_qkv[at, :] = mm(s.n_one[:, at], s.gmix[...], TN).astype(BF)

        qkv_block(net.diag)
        reduce_qkv.give()
        qkv_block(net.across)
        qkv_block(net.sib)
        reduce_qkv.keep()
        qkv_block(b)

    def qkv_done():
        terms = reduce_qkv.finish()
        add_into(s.qkv_block, terms)
        gather_qkv.start(halves(s.qkv_block, SHARD, 0))
        v.keep.append(local(s.qkv_block, o_qkv.at[c]))

    def gqv():
        s.gqv[...] = jnp.zeros_like(s.gqv)
        s.gqv[pl.ds(c, 1), :] = jnp.sum(s.gmix[:, :PAIR].astype(F32), 0, keepdims=True)
        s.gqv[pl.ds(8 + c, 1), :] = jnp.sum(s.gmix[:, 2 * PAIR :].astype(F32), 0, keepdims=True)
        for p in range(NC):
            at = p * PAIR
            row, lane = 2 + (at % 512) // SHARD, at % SHARD
            s.gs[at // 512, row : row + 1, lane : lane + PAIR] = s.gqv[p : p + 1, :]
            s.gs[2 + at // 512, row : row + 1, lane : lane + PAIR] = s.gqv[8 + p : 9 + p, :]

    def full_start(i):
        gather_full[i].start([rows_of(wqkv, SHARD // 2)(i)])

    def grad_in():
        for gather in gather_full:
            gather.finish()
        swap_mix.finish()
        for j in range(NC):
            for t in range(3):
                to, at = t * WIDTH + j * PAIR, t * PAIR
                s.gmix_all[:, to : to + PAIR] = s.gmix_own[j, :, at : at + PAIR]
        gain = row_of(s.parts, 0)

        def one_cols(at):
            s.gn_one[:, at] = mm(s.gmix_all[...], s.wfull[at, :], NT)

        loop(4, 256, one_cols)

        def token_rows(i, carry):
            at = pl.ds(pl.multiple_of(i * 32, 32), 32)
            grad_gain, grad_bias = carry
            grad, norm = s.gn_one[at, :], s.hat_one[at, :]
            scaled = grad * gain
            inner = scaled - jnp.mean(scaled, -1, keepdims=True)
            inner = inner - norm * jnp.mean(scaled * norm, -1, keepdims=True)
            grad_tokens[at, :] = (s.grad_middle[at, :] + s.scale_one[at, :] * inner).astype(BF)
            return (
                grad_gain + jnp.sum(grad * norm, 0, keepdims=True),
                grad_bias + jnp.sum(grad, 0, keepdims=True),
            )

        sums = lax.fori_loop(0, ROWS // 32, token_rows, (jnp.zeros((1, WIDTH), F32),) * 2)
        put_row(s.gs, 0, sums[0])
        put_row(s.gs, 1, sums[1])
        for j in batch_others:
            net.send(s.gs.at[j], s.gs_box.at[b], (j, c), gs_slots + b)

    def gs_sum():
        total = s.gs[pl.ds(b, 1)][0]
        for j in batch_others:
            net.wait(gs_slots + j, s.gs_box.at[j])
            total = total + s.gs_box[pl.ds(j, 1)][0]
        s.gs_sum[...] = total
        for i in range(1, NC):
            j = lax.rem(c + i, NC)
            net.send(s.gs_sum, s.gs_far.at[c], (b, j), far_slots + c)

    def far_sum():
        total = s.gs_sum[...]
        for i in range(1, NC):
            j = lax.rem(c - i + NC, NC)
            net.wait(far_slots + j, s.gs_far.at[j])
            total = total + s.gs_far[pl.ds(j, 1)][0]
        grad_small[...] = total

    enter()
    send_small()
    norm_one()
    g_start()
    pair_start()
    gather_one.stage(1)
    gather_one.corner()
    proj_start()
    gather_one.pass_on(1)
    gather_one.stage(2)
    gather_pair.relay()
    qv_rows()
    gather_one.stage(3)
    proj_relay()
    gather_pair.finish()
    fc_start()
    g_relay()
    gs_give_own()
    gather_one.pass_on(2)
    gather_one.pass_on(3)
    gather_one.finish()
    mix()
    att()
    fc_relay()
    gs_give_across()
    proj_side()
    proj_finish()
    swap_att.finish()
    middle()
    ns_give()
    gs_relay_across()
    gs_relay_own()
    gather_gs.finish()
    gather_two.near()
    feed_wait()
    feed_i(0,0)
    gather_two.relay()
    gather_two.far()
    feed_i(1,0)
    feed_i(1,1)
    feed_i(0,1)
    feed_rest(1)
    feed_rest(0)
    norm_sib()
    ns_start()
    norm_across()
    p_out(0)
    norm_diag()
    reduce_norm.cross()
    pre_give(1,0)
    reduce_out[0].pass_one()
    p_out(1)
    pre_give(0,0)
    full_start(1)
    pre_give(1,1)
    norm_own()
    back_two()
    reduce_out[0].pass_two()
    reduce_out[1].pass_one()
    pre_give(0,1)
    gather_ns.relay()
    gather_ns.finish()
    out_done(0)
    p_proj()
    reduce_proj.cross()
    reduce_out[1].pass_two()
    p_fc(0)
    out_done(1)
    p_fc(1)
    swap_grad.finish()
    gather_out[1].corner()
    gather_out[0].stage(1)
    att_back()
    mix_give(0)
    mix_give(3)
    gqv()
    p_qkv()
    reduce_qkv.cross()
    reduce_fc[0].pass_one()
    proj_done()
    gather_out[1].stage(1)
    gather_out[0].stage(2)
    full_start(0)
    reduce_fc[1].pass_one()
    reduce_fc[0].pass_two()
    fc_done(0)
    qkv_done()
    gather_out[1].pass_on(1)
    gather_full[1].relay()
    gather_out[0].stage(3)
    gather_out[1].stage(2)
    reduce_fc[1].pass_two()
    reduce_part.fold()
    reduce_part.line.pass_one()
    fc_swap(0)
    mix_give(1)
    gather_qkv.stage(1)
    mix_give(2)
    gather_full[0].relay()
    reduce_part.line.pass_two()
    gather_fc[0].stage(1)
    gather_out[1].pass_on(2)
    fc_done(1)
    p_layer()
    fc_swap(1)
    reduce_layer.cross()
    gather_out[1].pass_on(3)
    gather_qkv.stage(2)
    part_done()
    gather_fc[0].stage(2)
    gather_fc[1].corner()
    gather_fc[1].pass_on(1)
    gather_fc[1].stage(1)
    gather_qkv.stage(3)
    gather_part.stage(1)
    gather_qkv.corner()
    gather_qkv.pass_on(1)
    gather_fc[0].stage(3)
    gather_out[1].stage(3)
    gather_fc[1].pass_on(2)
    grad_in()
    gather_fc[1].stage(2)
    gather_fc[1].pass_on(3)
    gather_part.stage(2)
    gs_sum()
    gather_part.stage(3)
    gather_qkv.pass_on(2)
    gather_fc[1].stage(3)
    layer_end()
    gather_qkv.pass_on(3)
    far_sum()
    for gather in gather_out + gather_fc + [gather_qkv, gather_part]:
        gather.finish()
    for copy in v.keep:
        copy.wait()
    net.drain()


VECTOR_ROWS = (1, 1, 2, 1, 1, 1, 4, 1)
STEPS = 2


def widen_kernel(layer, grad_in, small, w_qkv, w_proj, w_fc, w_out, *outs):
    o_layer, o_grad_in, o_qkv, o_proj, o_fc, o_out = outs[:6]
    o_layer[...] = layer[...]
    o_grad_in[...] = grad_in[...]
    for j in range(NC):
        for t in range(3):
            to, at = t * WIDTH + j * PAIR, t * PAIR
            o_qkv[:, to : to + PAIR] = w_qkv[j, :, at : at + PAIR].astype(F32)
    o_proj[...] = w_proj[...].astype(F32)
    o_out[...] = w_out[...].astype(F32)
    for j in range(NB):
        for x in range(2):
            for i in range(2):
                to, at = j * WIDTH + x * 512 + i * 256, j * 256
                o_fc[:, to : to + 256] = w_fc[x, i, :, at : at + 256].astype(F32)

    @pl.when(pl.program_id(0) == 0)
    def _():
        row = 0
        for out in outs[6:]:
            for i in range(out.shape[0] // SHARD):
                out[i * SHARD : (i + 1) * SHARD] = small[row, :]
                row += 1


def per_device_fast(
    tokens, cotangent, ln1_gain, ln1_bias, qkv_weight, qv_bias, proj_weight, proj_bias,
    ln2_gain, ln2_bias, fc_weight, fc_bias, out_weight, out_bias,
):
    vmem, anywhere = pl.BlockSpec(memory_space=pltpu.VMEM), pl.BlockSpec(memory_space=pl.ANY)
    shape = jax.ShapeDtypeStruct
    layer, grad_in, grad_small, w_qkv, w_proj, w_fc, w_out = pl.pallas_call(
        layer_kernel,
        out_shape=(
            shape((ROWS, WIDTH), BF),
            shape((ROWS, WIDTH), BF),
            shape((SMALL_ROWS, SHARD), F32),
            shape((NC, SHARD, 3 * PAIR), BF),
            shape((SHARD, WIDTH), BF),
            shape((2, 2, SHARD, WIDTH), BF),
            shape((FF // NB, WIDTH), BF),
        ),
        in_specs=[vmem] * 10 + [anywhere] * 4,
        out_specs=(vmem, vmem, vmem, anywhere, anywhere, anywhere, anywhere),
        scratch_shapes=[pltpu.VMEM(*item) for item in SCRATCH.values()]
        + [
            pltpu.SemaphoreType.DMA((SENDS,)),
            pltpu.SemaphoreType.DMA((RECVS,)),
            pltpu.SemaphoreType.DMA((LOCALS,)),
        ],
        compiler_params=pltpu.CompilerParams(
            collective_id=0, has_side_effects=True, vmem_limit_bytes=VMEM_BYTES
        ),
    )(
        tokens.reshape(ROWS, WIDTH), cotangent.reshape(ROWS, WIDTH),
        ln1_gain, ln1_bias, qv_bias, proj_bias, ln2_gain, ln2_bias, fc_bias, out_bias,
        qkv_weight, proj_weight, fc_weight, out_weight,
    )

    def rows(count, width):
        return pl.BlockSpec((count // STEPS, width), lambda i: (i, 0))

    half = pl.BlockSpec((2, 2, SHARD // STEPS, WIDTH), lambda i: (0, 0, i, 0))
    smalls = [pl.BlockSpec((n * SHARD,), lambda i: (0,)) for n in VECTOR_ROWS]
    layer, grad_in, w_qkv, w_proj, w_fc, w_out, *vectors = pl.pallas_call(
        widen_kernel,
        grid=(STEPS,),
        out_shape=(
            shape((ROWS, WIDTH), BF),
            shape((ROWS, WIDTH), BF),
            shape((SHARD, 3 * WIDTH), F32),
            shape((SHARD, WIDTH), F32),
            shape((SHARD, FF), F32),
            shape((FF // NB, WIDTH), F32),
            *[shape((n * SHARD,), F32) for n in VECTOR_ROWS],
        ),
        in_specs=[
            rows(ROWS, WIDTH),
            rows(ROWS, WIDTH),
            pl.BlockSpec((SMALL_ROWS, SHARD), lambda i: (0, 0)),
            pl.BlockSpec((NC, SHARD // STEPS, 3 * PAIR), lambda i: (0, i, 0)),
            rows(SHARD, WIDTH),
            half,
            rows(FF // NB, WIDTH),
        ],
        out_specs=(
            rows(ROWS, WIDTH),
            rows(ROWS, WIDTH),
            rows(SHARD, 3 * WIDTH),
            rows(SHARD, WIDTH),
            rows(SHARD, FF),
            rows(FF // NB, WIDTH),
            *smalls,
        ),
        compiler_params=pltpu.CompilerParams(vmem_limit_bytes=VMEM_BYTES),
    )(layer, grad_in, grad_small, w_qkv, w_proj, w_fc, w_out)
    return (
        layer.reshape(tokens.shape),
        grad_in.reshape(tokens.shape),
        vectors[0],
        vectors[1],
        w_qkv,
        vectors[2],
        w_proj,
        vectors[3],
        vectors[4],
        vectors[5],
        w_fc,
        vectors[6],
        w_out,
        vectors[7],
    )


VMEM_BYTES = 62 * 1024 * 1024


def solution(mesh):
    placed = (
        P("batch", "ctx", None),
        P("batch", "ctx", None),
        P("batch"),
        P("batch"),
        P("batch", None),
        P("batch"),
        P("batch", None),
        P("batch"),
        P("batch"),
        P("batch"),
        P("batch", None),
        P("batch"),
        P("batch", None),
        P("batch"),
    )
    fits = dict(mesh.shape) == {"batch": NB, "ctx": NC}
    return jax.shard_map(
        per_device_fast if fits else per_device,
        mesh=mesh,
        in_specs=placed,
        out_specs=(
            P("batch", "ctx", None),
            P("batch", "ctx", None),
            P("batch"),
            P("batch"),
            P("batch", None),
            P("batch"),
            P("batch", None),
            P("batch"),
            P("batch"),
            P("batch"),
            P("batch", None),
            P("batch"),
            P("batch", None),
            P("batch"),
        ),
        check_vma=False,
    )
```

```python
from functools import partial
from types import SimpleNamespace

import jax
import jax.numpy as jnp
from jax import lax
from jax.experimental import pallas as pl
from jax.experimental.pallas import tpu as pltpu
from jax.sharding import PartitionSpec as P

HEADS = 16
HEAD_DIM = 64


epsilon = 1e-05
masked_value = -1e30


def shifted(block, axis, distance):
    devices = range(lax.axis_size(axis))
    route = [(i - distance, i) for i in devices if i - distance in devices]
    return lax.ppermute(block, axis, route)


def from_behind(block, axis, distance):
    devices = range(lax.axis_size(axis))
    route = [((i - distance) % len(devices), i) for i in devices]
    return lax.ppermute(block, axis, route)


def layer_norm(inputs, gain_vec, bias_vec):
    centre = inputs - jnp.mean(inputs, -1, keepdims=True)
    spread = jnp.mean(centre * centre, -1, keepdims=True)
    return centre * lax.rsqrt(spread + epsilon) * gain_vec + bias_vec


def keep_same(running):
    return running


def per_device(
    tokens,
    cotangent,
    ln1_gain,
    ln1_bias,
    qkv_weight,
    qv_bias,
    proj_weight,
    proj_bias,
    ln2_gain,
    ln2_bias,
    fc_weight,
    fc_bias,
    out_weight,
    out_bias,
):
    (
        gain_one,
        bias_one,
        weight_qkv,
        bias_qv,
        weight_proj,
        bias_proj,
        gain_two,
        bias_two,
        weight_fc,
        bias_fc,
        weight_out,
        bias_out,
    ) = (
        lax.all_gather(ln1_gain, "batch", axis=0, tiled=True),
        lax.all_gather(ln1_bias, "batch", axis=0, tiled=True),
        lax.all_gather(qkv_weight, "batch", axis=0, tiled=True),
        lax.all_gather(qv_bias, "batch", axis=0, tiled=True),
        lax.all_gather(proj_weight, "batch", axis=0, tiled=True),
        lax.all_gather(proj_bias, "batch", axis=0, tiled=True),
        lax.all_gather(ln2_gain, "batch", axis=0, tiled=True),
        lax.all_gather(ln2_bias, "batch", axis=0, tiled=True),
        lax.all_gather(fc_weight, "batch", axis=0, tiled=True),
        lax.all_gather(fc_bias, "batch", axis=0, tiled=True),
        lax.all_gather(out_weight, "batch", axis=0, tiled=True),
        lax.all_gather(out_bias, "batch", axis=0, tiled=True),
    )
    seq_count, ctx_rows, model_width = tokens.shape
    row_count = seq_count * ctx_rows
    inputs = tokens.astype(jnp.float32).reshape(row_count, model_width)
    norm_one, norm_one_pull = jax.vjp(
        layer_norm, inputs, gain_one.astype(jnp.float32), bias_one.astype(jnp.float32)
    )
    normed_low = norm_one.astype(jnp.bfloat16)
    bias_float = bias_qv.astype(jnp.float32)
    bias_full = jnp.concatenate(
        [bias_float[:model_width], jnp.zeros((model_width,), jnp.float32), bias_float[model_width:]]
    )
    mixed_proj = (
        jnp.dot(normed_low, weight_qkv, preferred_element_type=jnp.float32) + bias_full
    ).astype(jnp.bfloat16)
    query_flat = mixed_proj[:, :model_width].reshape(seq_count, ctx_rows, model_width)
    key_flat = mixed_proj[:, model_width : 2 * model_width].reshape(
        seq_count, ctx_rows, model_width
    )
    value_flat = mixed_proj[:, 2 * model_width :].reshape(seq_count, ctx_rows, model_width)
    query_heads = query_flat.reshape(seq_count, ctx_rows, HEADS, HEAD_DIM)
    own_index = lax.axis_index("ctx")
    position = own_index * ctx_rows
    query_pos = position + jnp.arange(ctx_rows, dtype=jnp.int32)
    last_pos = position + ctx_rows - 1
    start_state = (
        jnp.full((seq_count, ctx_rows, HEADS), masked_value, jnp.float32),
        jnp.zeros((seq_count, ctx_rows, HEADS), jnp.float32),
        jnp.zeros((seq_count, ctx_rows, HEADS, HEAD_DIM), jnp.float32),
    )
    key_piece = lax.all_gather(key_flat, "ctx", axis=1, tiled=True)
    value_piece = lax.all_gather(value_flat, "ctx", axis=1, tiled=True)
    piece_rows = key_piece.shape[1]

    def compute(running):
        run_max, run_sum, accum = running
        key_split = key_piece.reshape(seq_count, piece_rows, HEADS, HEAD_DIM)
        value_split = value_piece.reshape(seq_count, piece_rows, HEADS, HEAD_DIM)
        scores = (
            jnp.einsum(
                "bqhd,bkhd->bqhk", query_heads, key_split, preferred_element_type=jnp.float32
            )
            * 0.125
        )
        key_pos = jnp.arange(piece_rows, dtype=jnp.int32)
        allowed = (key_pos[None, :] <= query_pos[:, None])[None, :, None, :]
        scores = jnp.where(allowed, scores, masked_value)
        new_max = jnp.maximum(run_max, jnp.max(scores, -1))
        weights_exp = jnp.where(allowed, jnp.exp(scores - new_max[..., None]), 0.0)
        new_sum = jnp.sum(weights_exp, -1)
        product = jnp.einsum(
            "bqhk,bkhd->bqhd",
            weights_exp.astype(jnp.bfloat16),
            value_split,
            preferred_element_type=jnp.float32,
        )
        return (new_max, new_sum, product)

    run_max, run_sum, accum = lax.cond(jnp.int32(0) <= last_pos, compute, keep_same, start_state)
    log_total = run_max + jnp.log(run_sum)
    attended = accum / run_sum[..., None]
    attended_low = attended.reshape(row_count, model_width).astype(jnp.bfloat16)
    middle = (
        inputs
        + jnp.dot(attended_low, weight_proj, preferred_element_type=jnp.float32)
        + bias_proj.astype(jnp.float32)
    )
    norm_two, norm_two_pull = jax.vjp(
        layer_norm, middle, gain_two.astype(jnp.float32), bias_two.astype(jnp.float32)
    )
    normed_two = norm_two.astype(jnp.bfloat16)
    pre_act = jnp.dot(normed_two, weight_fc, preferred_element_type=jnp.float32) + bias_fc.astype(
        jnp.float32
    )
    activated, gelu_pull = jax.vjp(partial(jax.nn.gelu, approximate=True), pre_act)
    hidden_low = activated.astype(jnp.bfloat16)
    output = (
        middle
        + jnp.dot(hidden_low, weight_out, preferred_element_type=jnp.float32)
        + bias_out.astype(jnp.float32)
    )
    layer_out = output.astype(jnp.bfloat16).reshape(tokens.shape)
    grad_out = cotangent.reshape(row_count, model_width)
    grad_out_float = grad_out.astype(jnp.float32)
    grad_w_out = jnp.einsum("rf,rd->fd", hidden_low, grad_out, preferred_element_type=jnp.float32)
    grad_b_out = jnp.sum(grad_out_float, 0)
    grad_hidden = jnp.einsum("rd,fd->rf", grad_out, weight_out, preferred_element_type=jnp.float32)
    (grad_pre,) = gelu_pull(grad_hidden)
    grad_pre_low = grad_pre.astype(jnp.bfloat16)
    grad_w_fc = jnp.einsum(
        "rd,rf->df", normed_two, grad_pre_low, preferred_element_type=jnp.float32
    )
    grad_b_fc = jnp.sum(grad_pre_low.astype(jnp.float32), 0)
    grad_norm_two = jnp.einsum(
        "rf,df->rd", grad_pre_low, weight_fc, preferred_element_type=jnp.float32
    )
    grad_mid_norm, grad_g_two, grad_b_two = norm_two_pull(grad_norm_two)
    grad_middle = grad_out_float + grad_mid_norm
    grad_branch = grad_middle.astype(jnp.bfloat16)
    grad_w_proj = jnp.einsum(
        "rd,re->de", attended_low, grad_branch, preferred_element_type=jnp.float32
    )
    grad_b_proj = jnp.sum(grad_branch.astype(jnp.float32), 0)
    grad_attended = jnp.einsum(
        "re,de->rd", grad_branch, weight_proj, preferred_element_type=jnp.float32
    ).astype(jnp.bfloat16)
    grad_att_flat = grad_attended.reshape(seq_count, ctx_rows, model_width)
    grad_att_heads = grad_att_flat.reshape(seq_count, ctx_rows, HEADS, HEAD_DIM)
    delta_mine = jnp.sum(grad_att_heads.astype(jnp.float32) * attended, -1)
    zero_heads = jnp.zeros((seq_count, ctx_rows, HEADS, HEAD_DIM), jnp.float32)
    cycle_count = lax.axis_size("ctx")

    def cycle_turn(turn, state):
        owner = (own_index - turn) % cycle_count
        first_row = owner * ctx_rows

        def visit(inner):
            key_piece, value_piece, grad_k, grad_v, grad_q = inner
            key_split = key_piece.reshape(seq_count, ctx_rows, HEADS, HEAD_DIM)
            value_split = value_piece.reshape(seq_count, ctx_rows, HEADS, HEAD_DIM)
            piece_pos = first_row + jnp.arange(ctx_rows, dtype=jnp.int32)
            scores = (
                jnp.einsum(
                    "bqhd,bkhd->bqhk", query_heads, key_split, preferred_element_type=jnp.float32
                )
                * 0.125
            )
            allowed = (piece_pos[None, :] <= query_pos[:, None])[None, :, None, :]
            probs = jnp.where(allowed, jnp.exp(scores - log_total[..., None]), 0.0)
            grad_probs = jnp.einsum(
                "bqhd,bkhd->bqhk", grad_att_heads, value_split, preferred_element_type=jnp.float32
            )
            grad_scores = (probs * (grad_probs - delta_mine[..., None])).astype(jnp.bfloat16)
            grad_q = (
                grad_q
                + jnp.einsum(
                    "bqhk,bkhd->bqhd", grad_scores, key_split, preferred_element_type=jnp.float32
                )
                * 0.125
            )
            grad_k = (
                grad_k
                + jnp.einsum(
                    "bqhk,bqhd->bkhd", grad_scores, query_heads, preferred_element_type=jnp.float32
                )
                * 0.125
            )
            grad_v = grad_v + jnp.einsum(
                "bqhk,bqhd->bkhd",
                probs.astype(jnp.bfloat16),
                grad_att_heads,
                preferred_element_type=jnp.float32,
            )
            return (key_piece, value_piece, grad_k, grad_v, grad_q)

        key_piece, value_piece, grad_k, grad_v, grad_q = lax.cond(
            owner <= own_index, visit, keep_same, state
        )
        key_piece, value_piece = shifted((key_piece, value_piece), "ctx", 1)
        grad_k, grad_v = (
            from_behind(grad_k.astype(jnp.bfloat16), "ctx", 1).astype(grad_k.dtype),
            from_behind(grad_v.astype(jnp.bfloat16), "ctx", 1).astype(grad_v.dtype),
        )
        return (key_piece, value_piece, grad_k, grad_v, grad_q)

    cycle_state = lax.fori_loop(
        0, cycle_count, cycle_turn, (key_flat, value_flat, zero_heads, zero_heads, zero_heads)
    )
    grad_k, grad_v, grad_q = (cycle_state[2], cycle_state[3], cycle_state[4])
    grad_mixed = jnp.concatenate(
        [
            grad_q.reshape(row_count, model_width),
            grad_k.reshape(row_count, model_width),
            grad_v.reshape(row_count, model_width),
        ],
        axis=1,
    ).astype(jnp.bfloat16)
    grad_w_qkv = jnp.einsum("rd,re->de", normed_low, grad_mixed, preferred_element_type=jnp.float32)
    grad_bias_all = jnp.sum(grad_mixed.astype(jnp.float32), 0)
    grad_b_qv = jnp.concatenate([grad_bias_all[:model_width], grad_bias_all[2 * model_width :]])
    grad_norm_one = jnp.einsum(
        "re,de->rd", grad_mixed, weight_qkv, preferred_element_type=jnp.float32
    )
    grad_in_norm, grad_g_one, grad_b_one = norm_one_pull(grad_norm_one)
    grad_tokens = (grad_middle + grad_in_norm).astype(jnp.bfloat16).reshape(tokens.shape)
    local_grads = (
        grad_g_one,
        grad_b_one,
        grad_w_qkv,
        grad_b_qv,
        grad_w_proj,
        grad_b_proj,
        grad_g_two,
        grad_b_two,
        grad_w_fc,
        grad_b_fc,
        grad_w_out,
        grad_b_out,
    )
    partial_grads = (
        lax.psum_scatter(
            local_grads[0].astype(jnp.bfloat16), "batch", scatter_dimension=0, tiled=True
        ).astype(jnp.float32),
        lax.psum_scatter(
            local_grads[1].astype(jnp.bfloat16), "batch", scatter_dimension=0, tiled=True
        ).astype(jnp.float32),
        lax.psum_scatter(
            local_grads[2].astype(jnp.bfloat16), "batch", scatter_dimension=0, tiled=True
        ).astype(jnp.float32),
        lax.psum_scatter(
            local_grads[3].astype(jnp.bfloat16), "batch", scatter_dimension=0, tiled=True
        ).astype(jnp.float32),
        lax.psum_scatter(
            local_grads[4].astype(jnp.bfloat16), "batch", scatter_dimension=0, tiled=True
        ).astype(jnp.float32),
        lax.psum_scatter(
            local_grads[5].astype(jnp.bfloat16), "batch", scatter_dimension=0, tiled=True
        ).astype(jnp.float32),
        lax.psum_scatter(
            local_grads[6].astype(jnp.bfloat16), "batch", scatter_dimension=0, tiled=True
        ).astype(jnp.float32),
        lax.psum_scatter(
            local_grads[7].astype(jnp.bfloat16), "batch", scatter_dimension=0, tiled=True
        ).astype(jnp.float32),
        lax.psum_scatter(
            local_grads[8].astype(jnp.bfloat16), "batch", scatter_dimension=0, tiled=True
        ).astype(jnp.float32),
        lax.psum_scatter(
            local_grads[9].astype(jnp.bfloat16), "batch", scatter_dimension=0, tiled=True
        ).astype(jnp.float32),
        lax.psum_scatter(
            local_grads[10].astype(jnp.bfloat16), "batch", scatter_dimension=0, tiled=True
        ).astype(jnp.float32),
        lax.psum_scatter(
            local_grads[11].astype(jnp.bfloat16), "batch", scatter_dimension=0, tiled=True
        ).astype(jnp.float32),
    )
    summed_grads = lax.psum(
        (
            partial_grads[0],
            partial_grads[1],
            partial_grads[2],
            partial_grads[3],
            partial_grads[4],
            partial_grads[5],
            partial_grads[6],
            partial_grads[7],
            partial_grads[8],
            partial_grads[9],
            partial_grads[10],
            partial_grads[11],
        ),
        "ctx",
    )
    return (
        layer_out,
        grad_tokens,
        summed_grads[0],
        summed_grads[1],
        summed_grads[2],
        summed_grads[3],
        summed_grads[4],
        summed_grads[5],
        summed_grads[6],
        summed_grads[7],
        summed_grads[8],
        summed_grads[9],
        summed_grads[10],
        summed_grads[11],
    )


BF, F32 = jnp.bfloat16, jnp.float32
NN = (((1,), (0,)), ((), ()))
NT = (((1,), (1,)), ((), ()))
TN = (((0,), (0,)), ((), ()))
MESH = pl.DeviceIdType.MESH
NB, NC, WIDTH, ROWS, FF, PAIR = 4, 8, 1024, 128, 4096, 128
SHARD = WIDTH // NB
LENGTH = ROWS * NC
SMALL_ROWS = 16


def mm(left, right, dims=NN):
    return lax.dot_general(left, right, dims, preferred_element_type=F32)


def run(when, action):
    if when is None:
        action()
    else:
        pl.when(when)(action)


def both(one, two):
    return two if one is None else (one if two is None else jnp.logical_and(one, two))


class Net:
    def __init__(self, b, c, send_sems, recv_sems):
        self.b, self.c, self.z, self.x = b, c, c // 2, c % 2
        self.side = c + 1 - 2 * self.x
        self.core = b % 2
        self.sib = b + 1 - 2 * self.core
        self.across = lax.rem(b + 2, NB)
        self.diag = lax.rem(self.sib + 2, NB)
        self.send_sems, self.recv_sems = send_sems, recv_sems
        self.taken, self.pending = 0, []

    def slots(self, count):
        base = self.taken
        self.taken += count
        assert self.taken <= self.recv_sems.shape[0]
        return base

    def send(self, src, dst, device, slot, when=None):
        index = len(self.pending)
        if index == self.send_sems.shape[0]:
            done, copy, index = self.pending.pop(0)
            run(done, copy.wait_send)
        copy = pltpu.make_async_remote_copy(
            src_ref=src,
            dst_ref=dst,
            send_sem=self.send_sems.at[index],
            recv_sem=self.recv_sems.at[slot],
            device_id=device,
            device_id_type=MESH,
        )
        run(when, copy.start)
        self.pending.append((when, copy, index))

    def wait(self, slot, ref):
        pltpu.make_async_remote_copy(
            src_ref=ref,
            dst_ref=ref,
            send_sem=self.send_sems.at[0],
            recv_sem=self.recv_sems.at[slot],
            device_id=(self.sib, self.c),
            device_id_type=MESH,
        ).wait_recv()

    def drain(self):
        for when, copy, _ in self.pending:
            run(when, copy.wait_send)


class GatherCtx:
    def __init__(self, net, views, count, turn=False):
        self.net, self.views, self.count, self.turn = net, views, count, turn
        self.along, self.beside = net.slots(4 * count), net.slots(4 * count)
        self.turned = net.slots(2) if turn else None

    def begin(self, i, src):
        net, count = self.net, self.count
        dst, at = self.views(net.c)[i], net.z * count + i
        net.send(src, dst, (net.b, net.side), self.beside + at)
        net.send(src, dst, (net.b, net.c + 2), self.along + at, net.z < 3)
        net.send(src, dst, (net.b, net.c - 2), self.along + at, net.z > 0)

    def start(self, srcs):
        for i, src in enumerate(srcs):
            self.begin(i, src)

    def stage(self, d, sign):
        net, count = self.net, self.count
        zz = net.z + sign * d
        here = zz >= 0 if sign < 0 else zz <= 3
        refs = self.views(2 * zz + net.x)
        onward = both(here, net.z < 3 if sign < 0 else net.z > 0)
        for i in range(count):
            slot = self.along + zz * count + i
            pl.when(here)(lambda slot=slot, ref=refs[i]: net.wait(slot, ref))
            if d < 3:
                net.send(refs[i], refs[i], (net.b, net.c - 2 * sign), slot, onward)
            goes = here
            if self.turn and i == count - 1:
                goes = both(here, jnp.logical_and(zz > 0, zz < 3))
            net.send(refs[i], refs[i], (net.b, net.side), self.beside + zz * count + i, goes)

    def piece(self, end):
        return self.views(2 * end + 1 - self.net.x)[self.count - 1]

    def corner(self):
        net, count = self.net, self.count
        for end, step in ((0, 2), (3, -2)):
            ref, slot = self.piece(end), self.beside + end * count + count - 1
            pl.when(net.z == end)(lambda slot=slot, ref=ref: net.wait(slot, ref))
            net.send(ref, ref, (net.b, net.c + step), self.turned + (end > 0), net.z == end)

    def pass_on(self, d):
        net = self.net
        for end, step in ((0, 2), (3, -2)):
            here = net.z == (end + d if end == 0 else end - d)
            ref, slot = self.piece(end), self.turned + (end > 0)
            pl.when(here)(lambda slot=slot, ref=ref: net.wait(slot, ref))
            if d < 3:
                net.send(ref, ref, (net.b, net.c + step), slot, here)

    def finish(self):
        net, count = self.net, self.count
        for zz in range(4):
            refs = self.views(2 * zz + 1 - net.x)
            for i in range(count):
                if not (self.turn and i == count - 1 and zz in (0, 3)):
                    net.wait(self.beside + zz * count + i, refs[i])


def chunks(ref):
    if len(ref.shape) == 3:
        return ref.shape[0], lambda i: (i,)
    rows = min(32, ref.shape[0])
    return ref.shape[0] // rows, lambda i: (pl.ds(pl.multiple_of(i * rows, rows), rows),)


def add_into(target, terms, dtype=BF):
    count, at = chunks(target)

    def body(i, carry):
        total = terms[0][at(i)].astype(F32)
        for term in terms[1:]:
            total = total + term[at(i)].astype(F32)
        target[at(i)] = total.astype(dtype)
        return carry

    lax.fori_loop(0, count, body, 0)


class ReduceLine:
    def __init__(self, net, mine, up, down):
        self.net, self.mine, self.up, self.down = net, mine, up, down
        self.s_up, self.s_down = net.slots(4), net.slots(4)

    def give(self, k, upward, when):
        net = self.net
        if upward:
            net.send(self.mine(k), self.up.at[k], (net.b, net.c + 2), self.s_up + k, when)
        else:
            net.send(self.mine(k), self.down.at[k], (net.b, net.c - 2), self.s_down + k, when)

    def take(self, k, upward, when):
        box, slot = (self.up, self.s_up) if upward else (self.down, self.s_down)
        mine = self.mine(k)

        @pl.when(when)
        def _():
            self.net.wait(slot + k, box.at[k])
            add_into(mine, [mine, box.at[k]])

        self.give(k, upward, when)

    def launch(self, k):
        self.give(3 - k, True, self.net.z == 0)
        self.give(k, False, self.net.z == 3)

    def pass_one(self, k):
        self.take(3 - k, True, self.net.z == 1)
        self.take(k, False, self.net.z == 2)

    def pass_two(self):
        self.take(0, False, self.net.z == 1)
        self.take(3, True, self.net.z == 2)

    def finish(self, target):
        net, z = self.net, self.net.z
        mine = self.mine(z)

        @pl.when(z >= 1)
        def _():
            net.wait(self.s_up + z, self.up.at[z])

        @pl.when(z <= 2)
        def _():
            net.wait(self.s_down + z, self.down.at[z])

        pl.when(z == 0)(lambda: add_into(target, [mine, self.down.at[z]]))
        pl.when(z == 3)(lambda: add_into(target, [mine, self.up.at[z]]))
        pl.when(jnp.logical_and(z > 0, z < 3))(
            lambda: add_into(target, [mine, self.up.at[z], self.down.at[z]])
        )


class ReduceCtx:
    def __init__(self, net, mine, beside, up, down):
        self.net, self.mine, self.beside = net, mine, beside
        self.slots = net.slots(4)
        self.line = ReduceLine(net, lambda k: mine(2 * k + net.x), up, down)

    def start(self):
        net = self.net
        for k in (3, 0, 2, 1):
            net.send(self.mine(2 * k + 1 - net.x), self.beside.at[k], (net.b, net.side), self.slots + k)

    def fold(self):
        for k in (3, 0, 2, 1):
            self.net.wait(self.slots + k, self.beside.at[k])
            mine = self.line.mine(k)
            add_into(mine, [mine, self.beside.at[k]])


class SwapCtx:
    def __init__(self, net, src, dst, count):
        self.net, self.src, self.dst, self.count = net, src, dst, count
        self.base = net.slots(NC * count)

    def give(self, j):
        net, count = self.net, self.count
        srcs, dsts = self.src(j), self.dst(net.c)
        for i in range(count):
            net.send(srcs[i], dsts[i], (net.b, j), self.base + net.c * count + i, net.c != j)

        @pl.when(net.c == j)
        def _():
            for one, two in zip(srcs, dsts):
                two[...] = one[...]

    def start(self):
        for j in range(NC):
            self.give(j)

    def finish(self):
        net, count = self.net, self.count
        for step in range(1, NC):
            j = lax.rem(net.c - step + NC, NC)
            dsts = self.dst(j)
            for i in range(count):
                net.wait(self.base + j * count + i, dsts[i])


class GatherSide:
    def __init__(self, net, views):
        self.net, self.views = net, views
        self.far, self.near = net.slots(NB), net.slots(NB)

    def give(self, j, src):
        net = self.net
        net.send(src, self.views(j), (net.b, net.side), self.far + j)

    def relay(self, j):
        net, ref = self.net, self.views(j)
        net.wait(self.far + j, ref)
        net.send(ref, ref, (net.sib, net.c), self.near + j)

    def finish(self):
        net = self.net
        for j in (net.sib, net.diag):
            net.wait(self.near + j, self.views(j))


class GatherBatch:
    def __init__(self, net, views, count=1):
        self.net, self.views, self.count = net, views, count
        self.base = net.slots(NB * count)

    def start(self, srcs):
        net = self.net
        dsts = self.views(net.b)
        for i in range(self.count):
            slot = self.base + net.b * self.count + i
            net.send(srcs[i], dsts[i], (net.across, net.c), slot)
        for i in range(self.count):
            slot = self.base + net.b * self.count + i
            net.send(srcs[i], dsts[i], (net.sib, net.c), slot)

    def relay(self):
        net = self.net
        refs = self.views(net.across)
        for i in range(self.count):
            slot = self.base + net.across * self.count + i
            net.wait(slot, refs[i])
            net.send(refs[i], refs[i], (net.sib, net.c), slot)

    def take(self, j):
        refs = self.views(j)
        for i in range(self.count):
            self.net.wait(self.base + j * self.count + i, refs[i])

    def near(self):
        self.take(self.net.sib)

    def far(self):
        self.take(self.net.diag)

    def finish(self):
        self.near()
        self.far()


class ReduceBatch:
    def __init__(self, net, mine, boxes):
        self.net, self.mine, self.boxes = net, mine, boxes
        self.base = net.slots(3)

    def give(self):
        net = self.net
        net.send(self.mine(net.diag), self.boxes.at[0], (net.sib, net.c), self.base)

    def cross(self):
        net = self.net
        net.wait(self.base, self.boxes.at[0])
        block = self.mine(net.across)
        add_into(block, [block, self.boxes.at[0]])
        net.send(block, self.boxes.at[1], (net.across, net.c), self.base + 1)

    def keep(self):
        net = self.net
        net.send(self.mine(net.sib), self.boxes.at[2], (net.sib, net.c), self.base + 2)

    def finish(self):
        net = self.net
        net.wait(self.base + 2, self.boxes.at[2])
        net.wait(self.base + 1, self.boxes.at[1])
        return [self.mine(net.b), self.boxes.at[1], self.boxes.at[2]]


def row_of(parts, index):
    return jnp.concatenate([parts[j, index : index + 1, :] for j in range(NB)], axis=1)


def put_row(target, index, row):
    for j in range(NB):
        target[j, index : index + 1, :] = row[:, j * SHARD : (j + 1) * SHARD]


def rows_of(block, size):
    return lambda j: block.at[pl.ds(pl.multiple_of(j * size, size), size)]


def normalise(inputs):
    centre = inputs - jnp.mean(inputs, -1, keepdims=True)
    spread = jnp.mean(centre * centre, -1, keepdims=True)
    scale = lax.rsqrt(spread + epsilon)
    return centre * scale, scale


def head_lanes(h, rows):
    lane = lax.broadcasted_iota(jnp.int32, (rows, PAIR), 1)
    return (lane >= h * HEAD_DIM) & (lane < (h + 1) * HEAD_DIM)


QB = 256


def scores_of(keys, query, masked):
    scores = mm(keys, query, NT) * 0.125
    if masked:
        key_pos = lax.broadcasted_iota(jnp.int32, scores.shape, 0)
        query_pos = lax.broadcasted_iota(jnp.int32, scores.shape, 1)
        scores = jnp.where(key_pos <= query_pos, scores, masked_value)
    return scores


def attend(mix, value_t, att, lse, work, low_work, ready):
    value_t[...] = mix[:, 2 * PAIR :].astype(F32).T.astype(BF)
    for qb in reversed(range(LENGTH // QB)):
        here = slice(qb * QB, (qb + 1) * QB)
        outs = []
        for h in range(2):
            query = jnp.where(head_lanes(h, QB), mix[here, :PAIR], jnp.zeros((), BF))
            top = None
            for kb in range(qb + 1):
                keys = slice(kb * QB, (kb + 1) * QB)
                scores = scores_of(mix[keys, PAIR : 2 * PAIR], query, kb == qb)
                work[keys, :] = scores
                peak = jnp.max(scores, axis=0, keepdims=True)
                top = peak if top is None else jnp.maximum(top, peak)
            total = None
            for kb in range(qb + 1):
                keys = slice(kb * QB, (kb + 1) * QB)
                grown = jnp.exp(work[keys, :] - top)
                part = jnp.sum(grown, axis=0, keepdims=True)
                total = part if total is None else total + part
                low_work[h, keys, :] = grown.astype(BF)
            count = (qb + 1) * QB
            lanes = slice(h * HEAD_DIM, (h + 1) * HEAD_DIM)
            out = mm(value_t[lanes, :count], low_work[h, :count, :])
            outs.append(out / total)
            lse[h * 4 + qb : h * 4 + qb + 1, :] = top + jnp.log(total)
        att[here, :] = jnp.concatenate(outs, axis=0).T.astype(BF)
        ready(qb)


def attend_back(mix, key_t, dout, lse, gmix, grad_k, grad_v, work, more, low_work, low_more):
    key_t[...] = mix[:, PAIR : 2 * PAIR].astype(F32).T.astype(BF)
    grad_k[...] = jnp.zeros_like(grad_k)
    grad_v[...] = jnp.zeros_like(grad_v)
    for qb in reversed(range(LENGTH // QB)):
        here = slice(qb * QB, (qb + 1) * QB)
        outs = []
        count = (qb + 1) * QB
        for h in range(2):
            lanes = head_lanes(h, QB)
            query = jnp.where(lanes, mix[here, :PAIR], jnp.zeros((), BF))
            grad = jnp.where(lanes, dout[here, :], jnp.zeros((), BF))
            level = lse[h * 4 + qb : h * 4 + qb + 1, :]
            delta = None
            for kb in range(qb + 1):
                keys = slice(kb * QB, (kb + 1) * QB)
                probs = jnp.exp(scores_of(mix[keys, PAIR : 2 * PAIR], query, kb == qb) - level)
                grad_probs = mm(mix[keys, 2 * PAIR :], grad, NT)
                part = jnp.sum(probs * grad_probs, axis=0, keepdims=True)
                delta = part if delta is None else delta + part
                work[keys, :] = probs
                more[keys, :] = grad_probs
                low_work[h, keys, :] = probs.astype(BF)
            for kb in range(qb + 1):
                keys = slice(kb * QB, (kb + 1) * QB)
                low_more[h, keys, :] = (work[keys, :] * (more[keys, :] - delta)).astype(BF)
            grad_v[:count, :] += mm(low_work[h, :count, :], grad)
            grad_k[:count, :] += mm(low_more[h, :count, :], query)
            rows = slice(h * HEAD_DIM, (h + 1) * HEAD_DIM)
            outs.append(mm(key_t[rows, :count], low_more[h, :count, :]) * 0.125)
        gmix[here, :PAIR] = jnp.concatenate(outs, axis=0).T.astype(BF)
        gmix[here, PAIR : 2 * PAIR] = (grad_k[here, :] * 0.125).astype(BF)
        gmix[here, 2 * PAIR :] = grad_v[here, :].astype(BF)


gelu_scale = 0.7978845608028654
gelu_cubic = 0.044715


def gelu_pair(x):
    square = x * x
    bent = jnp.tanh(gelu_scale * x * (1.0 + gelu_cubic * square))
    half = 0.5 * (1.0 + bent)
    slope = half + 0.5 * x * (1.0 - bent * bent) * (gelu_scale * (1.0 + 3.0 * gelu_cubic * square))
    return x * half, slope


VECTOR_ROWS = (1, 1, 2, 1, 1, 1, 4, 1)
SCRATCH = dict(
    tokens=((ROWS, WIDTH), BF),
    **{f"v{i}": ((rows * SHARD,), BF) for i, rows in enumerate(VECTOR_ROWS)},
    small=((SMALL_ROWS, SHARD), F32),
    parts=((NB, SMALL_ROWS, SHARD), F32),
    qv_rows=((16, PAIR), F32),
    wpair=((WIDTH, 3 * PAIR), BF),
    wfull=((WIDTH, 3 * WIDTH), BF),
    wproj_all=((WIDTH, WIDTH), BF),
    wfc_mine=((WIDTH, WIDTH), BF),
    wout_mine=((WIDTH, WIDTH), BF),
    g_all=((NB * ROWS, WIDTH), BF),
    hat_one=((ROWS, WIDTH), F32),
    scale_one=((ROWS, 1), F32),
    hat_all=((LENGTH, WIDTH), BF),
    n_one=((LENGTH, WIDTH), BF),
    mix=((LENGTH, 3 * PAIR), BF),
    turned=((PAIR, LENGTH), BF),
    att=((LENGTH, PAIR), BF),
    lse=((8, QB), F32),
    work=((LENGTH, QB), F32),
    more=((LENGTH, QB), F32),
    low_work=((2, LENGTH, QB), BF),
    low_more=((2, LENGTH, QB), BF),
    att_own=((ROWS, WIDTH), BF),
    middle=((ROWS, WIDTH), F32),
    hat_two=((ROWS, WIDTH), F32),
    scale_two=((ROWS, 1), F32),
    n_two=((NB * ROWS, WIDTH), BF),
    hidden=((NB * ROWS, WIDTH), BF),
    grad_pre=((NB * ROWS, WIDTH), BF),
    p_norm=((NB * ROWS, WIDTH), BF),
    p_norm_box=((3, ROWS, WIDTH), BF),
    p_layer=((NB * ROWS, WIDTH), BF),
    p_layer_box=((3, ROWS, WIDTH), BF),
    g_side=((NB * ROWS, WIDTH), BF),
    n_side=((NB * ROWS, WIDTH), BF),
    hidden_side=((NB * ROWS, WIDTH // 2), BF),
    pre_side=((NB * ROWS, WIDTH // 2), BF),
    p_out=((2, 256, WIDTH), BF),
    out_up=((2, 4, 64, WIDTH), BF),
    out_down=((2, 4, 64, WIDTH), BF),
    out_block=((ROWS, WIDTH), BF),
    p_fc=((2, NB, 4, 64, 256), BF),
    fc_up=((2, 4, NB, 64, 256), BF),
    fc_down=((2, 4, NB, 64, 256), BF),
    fc_sum=((2, NB, 64, 256), BF),
    fc_block=((2, 64, WIDTH), BF),
    p_proj=((WIDTH, WIDTH), BF),
    p_proj_box=((3, SHARD, WIDTH), BF),
    proj_sum=((SHARD, WIDTH), BF),
    proj_beside=((4, 32, WIDTH), BF),
    proj_up=((4, 32, WIDTH), BF),
    proj_down=((4, 32, WIDTH), BF),
    proj_block=((32, WIDTH), BF),
    grad_middle=((ROWS, WIDTH), F32),
    branch=((ROWS, WIDTH), BF),
    g_att=((ROWS, WIDTH), BF),
    dout=((LENGTH, PAIR), BF),
    gmix=((LENGTH, 3 * PAIR), BF),
    grad_k=((LENGTH, PAIR), F32),
    grad_v=((LENGTH, PAIR), F32),
    gmix_own=((NC, ROWS, 3 * PAIR), BF),
    gmix_all=((ROWS, 3 * WIDTH), BF),
    p_qkv=((WIDTH, 3 * PAIR), BF),
    p_qkv_box=((3, SHARD, 3 * PAIR), BF),
    qkv_block=((SHARD, 3 * PAIR), BF),
    gn_one=((ROWS, WIDTH), F32),
    gs=((NB, SMALL_ROWS, SHARD), F32),
    gqv=((16, PAIR), F32),
    gs_box=((NB, SMALL_ROWS, SHARD), F32),
    gs_sum=((SMALL_ROWS, SHARD), F32),
    gs_far=((NC, SMALL_ROWS, SHARD), F32),
)
TURN_OUT, TURN_FC = (False, False), (False, False)
SENDS, RECVS, LOCALS = 48, 240, 26


def layer_kernel(*refs):
    tokens, cotangent = refs[:2]
    vectors = refs[2:10]
    wqkv, wproj, wfc, wout = refs[10:14]
    layer_out, grad_tokens, grad_small, o_qkv, o_proj, o_fc, o_out = refs[14:21]
    scratch = refs[21:]
    s = SimpleNamespace(**dict(zip(SCRATCH, scratch)))
    send_sems, recv_sems, local_sems = scratch[len(SCRATCH) :]
    b, c = lax.axis_index("batch"), lax.axis_index("ctx")
    net = Net(b, c, send_sems, recv_sems)
    v = SimpleNamespace(keep=[])
    locals_open = []

    def local(src, dst):
        copy = pltpu.make_async_copy(src, dst, local_sems.at[len(locals_open)])
        copy.start()
        locals_open.append(copy)
        return copy

    def own(ref, size):
        return rows_of(ref, size)(b)

    def cols(ref, start, count=PAIR):
        return ref.at[:, pl.ds(pl.multiple_of(start, 128), count)]

    def halves(ref, size, j):
        block = rows_of(ref, size)(j)
        return [block.at[0 : size // 2], block.at[size // 2 : size]]

    def loop(count, size, body):
        def step(i, carry):
            body(pl.ds(pl.multiple_of(i * size, size), size))
            return carry

        lax.fori_loop(0, count, step, 0)

    batch_others = [lax.rem(b + i, NB) for i in range(1, NB)]

    small_slots, fc_slots = net.slots(NB), net.slots(2 * NB)
    hidden_slots, pre_slots, side_slot, swap_slots = net.slots(4), net.slots(4), net.slots(1), net.slots(2 * NB)
    proj_slots, proj_side_slot, proj_near_slots = net.slots(NB), net.slots(1), net.slots(2)
    gs_slots, far_slots = net.slots(NB), net.slots(NC)
    gather_pair = GatherBatch(net, lambda j: [rows_of(s.wpair, SHARD)(j)])
    gather_one = GatherCtx(net, lambda j: halves(s.hat_all, ROWS, j), 2, True)
    gather_g = GatherBatch(net, lambda j: [rows_of(s.g_all, ROWS)(j)])
    gather_gs = GatherSide(net, rows_of(s.g_side, ROWS))
    gather_ns = GatherBatch(net, lambda j: [rows_of(s.n_side, ROWS)(j)])
    gather_two = GatherBatch(net, lambda j: halves(s.n_two, ROWS, j), 2)
    gather_full = [
        GatherBatch(net, lambda j, i=i: [rows_of(s.wfull, SHARD // 2)(2 * j + i)]) for i in range(2)
    ]
    swap_att = SwapCtx(
        net, lambda j: [rows_of(s.att, ROWS)(j)], lambda j: [cols(s.att_own, j * PAIR)], 1
    )
    swap_grad = SwapCtx(
        net, lambda j: [cols(s.g_att, j * PAIR)], lambda j: [rows_of(s.dout, ROWS)(j)], 1
    )
    swap_mix = SwapCtx(
        net, lambda j: [rows_of(s.gmix, ROWS)(j)], lambda j: [s.gmix_own.at[j]], 1
    )
    reduce_norm = ReduceBatch(net, rows_of(s.p_norm, ROWS), s.p_norm_box)
    reduce_layer = ReduceBatch(net, rows_of(s.p_layer, ROWS), s.p_layer_box)
    reduce_proj = ReduceBatch(net, rows_of(s.p_proj, SHARD), s.p_proj_box)
    reduce_qkv = ReduceBatch(net, rows_of(s.p_qkv, SHARD), s.p_qkv_box)
    reduce_part = ReduceCtx(net, rows_of(s.proj_sum, 32), s.proj_beside, s.proj_up, s.proj_down)
    reduce_out = [
        ReduceLine(net, rows_of(s.p_out.at[i], 64), s.out_up.at[i], s.out_down.at[i]) for i in range(2)
    ]
    reduce_fc = [
        ReduceLine(net, lambda k, i=i: s.p_fc.at[i, :, k], s.fc_up.at[i], s.fc_down.at[i])
        for i in range(2)
    ]

    def out_view(i, j):
        return rows_of(o_out, 64)(8 * (j % 2) + 4 * i + j // 2)

    def fc_view(i, j):
        return o_fc.at[j % 2, i, pl.ds(pl.multiple_of((j // 2) * 64, 64), 64)]

    gather_out = [GatherCtx(net, lambda j, i=i: [out_view(i, j)], 1, TURN_OUT[i]) for i in range(2)]
    gather_fc = [GatherCtx(net, lambda j, i=i: [fc_view(i, j)], 1, TURN_FC[i]) for i in range(2)]
    gather_qkv = GatherCtx(net, lambda j: halves(o_qkv.at[j], SHARD, 0), 2, True)
    gather_part = GatherCtx(net, lambda j: [rows_of(o_proj, 32)(j)], 1)

    scale, hat = s.scale_one, s.hat_one
    side_rows = pl.ds(pl.multiple_of(net.x * (SHARD // 2), SHARD // 2), SHARD // 2)
    other_side_rows = pl.ds(pl.multiple_of((1 - net.x) * (SHARD // 2), SHARD // 2), SHARD // 2)
    chip_rows = [
        pl.ds(pl.multiple_of(first * 256, 256), 256) for first in (b // 2, 1 - b // 2)
    ]
    hat_mine = rows_of(s.hat_all, ROWS)(c)
    n_two_mine = own(s.n_two, ROWS)
    g_mine = own(s.g_all, ROWS)
    n_beside = own(s.n_side, ROWS)

    def enter():
        barrier = pltpu.get_barrier_semaphore()
        others = [(j, c) for j in batch_others]
        others += [(b, lax.rem(c + i, NC)) for i in range(1, NC)]
        for device in others:
            pl.semaphore_signal(barrier, inc=1, device_id=device, device_id_type=MESH)
        get_tokens = local(tokens, s.tokens)
        own_vectors = [getattr(s, f"v{i}") for i in range(len(vectors))]
        get_vectors = [local(one, two) for one, two in zip(vectors, own_vectors)]
        get_pair = [
            local(cols(wqkv, t * WIDTH + c * PAIR), own(s.wpair, SHARD).at[:, t * PAIR : (t + 1) * PAIR])
            for t in range(3)
        ]
        v.get_proj = local(wproj, own(s.wproj_all, SHARD))
        v.get_rest = [
            local(cols(wfc, b * WIDTH, WIDTH), own(s.wfc_mine, SHARD)),
            local(wout, s.wout_mine),
            local(wqkv, own(s.wfull, SHARD)),
            local(cotangent, g_mine),
        ]
        s.small[...] = jnp.zeros_like(s.small)
        for copy in get_vectors:
            copy.wait()
        row = 0
        for vector in own_vectors:
            for i in range(vector.shape[0] // SHARD):
                piece = vector[i * SHARD : (i + 1) * SHARD].astype(F32)
                s.small[row : row + 1, :] = piece.reshape(1, SHARD)
                row += 1

        def norm_rows(at):
            hat[at, :], scale[at, :] = normalise(s.tokens[at, :].astype(F32))
            hat_mine[at, :] = hat[at, :].astype(BF)

        get_tokens.wait()
        loop(ROWS // 32, 32, norm_rows)
        for copy in get_pair:
            copy.wait()
        s.parts[pl.ds(b, 1)] = s.small[...][None]
        pl.semaphore_wait(barrier, len(others))

    def send_small():
        for j in batch_others:
            net.send(s.small, s.parts.at[b], (j, c), small_slots + b)

    def pair_start():
        gather_pair.start([own(s.wpair, SHARD)])

    def g_start():
        gather_g.start([cotangent])

    def one_start():
        gather_one.start(halves(s.hat_all, ROWS, c))

    def small_wait():
        for j in batch_others:
            net.wait(small_slots + j, s.parts.at[j])
        v.gain, v.bias = row_of(s.parts, 0), row_of(s.parts, 1)

    def proj_start():
        mine = own(s.wproj_all, SHARD)
        net.send(wproj.at[side_rows], mine.at[side_rows], (net.across, c), proj_slots + b)
        net.send(wproj, mine, (net.sib, c), proj_slots + b)

    def proj_relay():
        block = rows_of(s.wproj_all, SHARD)(net.across).at[side_rows]
        net.wait(proj_slots + net.across, block)
        net.send(block, block, (b, net.side), proj_side_slot)
        net.send(block, block, (net.sib, c), proj_near_slots)

    def proj_side():
        block = rows_of(s.wproj_all, SHARD)(net.across).at[other_side_rows]
        net.wait(proj_side_slot, block)
        net.send(block, block, (net.sib, c), proj_near_slots + 1)

    def fc_start(i):
        at = slice(i * (SHARD // 2), (i + 1) * (SHARD // 2))
        for j in (net.across, net.diag, net.sib):
            cut = wfc.at[at, pl.ds(pl.multiple_of(j * WIDTH, WIDTH), WIDTH)]
            net.send(cut, own(s.wfc_mine, SHARD).at[at], (j, c), fc_slots + 2 * b + i)

    def qv_rows():
        for p in range(NC):
            at = p * PAIR
            row, lane = 2 + (at % 512) // SHARD, at % SHARD
            s.qv_rows[p : p + 1, :] = s.parts[at // 512, row : row + 1, lane : lane + PAIR]
            s.qv_rows[8 + p : 9 + p, :] = s.parts[2 + at // 512, row : row + 1, lane : lane + PAIR]

    def g_relay():
        gather_g.relay()

    def gs_give_own():
        gather_gs.give(b, cotangent)

    def gs_give_across():
        gather_gs.give(net.across, rows_of(s.g_all, ROWS)(net.across))

    def gs_relay_own():
        gather_gs.relay(b)

    def gs_relay_across():
        gather_gs.relay(net.across)

    def mix_block(j):
        rows = pl.ds(pl.multiple_of(j * ROWS, ROWS), ROWS)
        mix_bias = jnp.concatenate(
            [s.qv_rows[pl.ds(c, 1), :], jnp.zeros((1, PAIR), F32), s.qv_rows[pl.ds(8 + c, 1), :]], axis=1
        )
        s.n_one[rows, :] = (s.hat_all[rows, :].astype(F32) * v.gain + v.bias).astype(BF)
        s.mix[rows, :] = (mm(s.n_one[rows, :], s.wpair[...]) + mix_bias).astype(BF)

    def mix_at(d):
        if d == 0:
            mix_block(c)
        for zz in (net.z - d, net.z + d)[: 2 * d]:

            @pl.when(jnp.logical_and(zz >= 0, zz <= 3))
            def _():
                mix_block(2 * zz + net.x)

    def mix_side():
        def step(zz, carry):
            mix_block(2 * zz + 1 - net.x)
            return carry

        lax.fori_loop(0, 4, step, 0)

    def att():
        def ready(qb):
            swap_att.give(2 * qb)
            swap_att.give(2 * qb + 1)

        attend(s.mix, s.turned, s.att, s.lse, s.work, s.low_work, ready)

    def proj_finish():
        v.get_proj.wait()
        net.wait(proj_slots + net.sib, rows_of(s.wproj_all, SHARD)(net.sib))
        block = rows_of(s.wproj_all, SHARD)(net.diag)
        net.wait(proj_near_slots, block.at[side_rows])
        net.wait(proj_near_slots + 1, block.at[other_side_rows])

    def middle():
        def middle_cols(at):
            s.middle[:, at] = mm(s.att_own[...], s.wproj_all[:, at]) + s.tokens[:, at].astype(F32)

        loop(WIDTH // 256, 256, middle_cols)
        proj_bias, gain_two, bias_two = row_of(s.parts, 4), row_of(s.parts, 5), row_of(s.parts, 6)

        def norm_two_rows(at):
            middle = s.middle[at, :] + proj_bias
            s.middle[at, :] = middle
            norm, width = normalise(middle)
            s.hat_two[at, :], s.scale_two[at, :] = norm, width
            n_two_mine[at, :] = (norm * gain_two + bias_two).astype(BF)

        loop(ROWS // 32, 32, norm_two_rows)
        gather_two.start(halves(s.n_two, ROWS, b))

    def ns_give():
        net.send(n_two_mine, n_beside, (b, net.side), side_slot)

    def ns_start():
        net.wait(side_slot, n_beside)
        gather_ns.start([n_beside])

    def feed_wait():
        for copy in v.get_rest:
            copy.wait()
        gather_g.finish()
        for j in batch_others:
            for i, block in enumerate(halves(s.wfc_mine, SHARD, j)):
                net.wait(fc_slots + 2 * j + i, block)
        s.gs[...] = jnp.zeros_like(s.gs)

    def feed_cols(r, i):
        n = lax.rem(2 * (1 - net.x) + i, 4)
        rows, at = chip_rows[r], pl.ds(pl.multiple_of(n * 256, 256), 256)
        pre = mm(s.n_two[rows, :], s.wfc_mine[:, at]) + s.small[pl.ds(7 + n, 1), :]
        value, slope = gelu_pair(pre)
        s.hidden[rows, at] = value.astype(BF)
        grad = (mm(s.g_all[rows, :], s.wout_mine[at, :], NT) * slope).astype(BF)
        s.grad_pre[rows, at] = grad
        s.gs[pl.ds(b, 1), pl.ds(7 + n, 1), :] += jnp.sum(grad.astype(F32), 0, keepdims=True)[None]

    def tile(ref, r, i):
        return ref.at[chip_rows[r], pl.ds(pl.multiple_of((2 * (1 - net.x) + i) * 256, 256), 256)]

    def side_tile(ref, r, i):
        return ref.at[chip_rows[r], i * 256 : (i + 1) * 256]

    def feed_i(r, i):
        feed_cols(r, i)
        net.send(tile(s.hidden, r, i), side_tile(s.hidden_side, r, i), (b, net.side), hidden_slots + 2 * r + i)

    def pre_give(r, i):
        net.send(tile(s.grad_pre, r, i), side_tile(s.pre_side, r, i), (b, net.side), pre_slots + 2 * r + i)

    def feed_rest(r):
        def step(i, carry):
            feed_cols(r, i)
            return carry

        lax.fori_loop(2, 4, step, 0)

    def norm_block(j):
        at = pl.ds(pl.multiple_of(j * ROWS, ROWS), ROWS)
        s.p_norm[at, :] = mm(s.grad_pre[at, :], s.wfc_mine[...], NT).astype(BF)

    def norm_diag():
        norm_block(net.diag)
        reduce_norm.give()

    def norm_across():
        norm_block(net.across)

    def norm_sib():
        norm_block(net.sib)
        reduce_norm.keep()

    def norm_own():
        norm_block(b)

    def back_two():
        gain_two = row_of(s.parts, 5)
        terms = reduce_norm.finish()

        def back_rows(i, carry):
            at = pl.ds(pl.multiple_of(i * 32, 32), 32)
            grad_gain, grad_bias, sum_branch, sum_g = carry
            grad = terms[0][at, :].astype(F32) + terms[1][at, :].astype(F32) + terms[2][at, :].astype(F32)
            norm = s.hat_two[at, :]
            scaled = grad * gain_two
            inner = scaled - jnp.mean(scaled, -1, keepdims=True)
            inner = inner - norm * jnp.mean(scaled * norm, -1, keepdims=True)
            g = g_mine[at, :].astype(F32)
            total = g + s.scale_two[at, :] * inner
            s.grad_middle[at, :] = total
            low = total.astype(BF)
            s.branch[at, :] = low
            return (
                grad_gain + jnp.sum(grad * norm, 0, keepdims=True),
                grad_bias + jnp.sum(grad, 0, keepdims=True),
                sum_branch + jnp.sum(low.astype(F32), 0, keepdims=True),
                sum_g + jnp.sum(g, 0, keepdims=True),
            )

        sums = lax.fori_loop(0, ROWS // 32, back_rows, (jnp.zeros((1, WIDTH), F32),) * 4)
        put_row(s.gs, 5, sums[0])
        put_row(s.gs, 6, sums[1])
        put_row(s.gs, 4, sums[2])
        put_row(s.gs, 11, sums[3])

        def att_cols(at):
            s.g_att[:, at] = mm(s.branch[...], s.wproj_all[at, :], NT).astype(BF)

        loop(4, 256, att_cols)
        swap_grad.start()

    def p_out(i):
        at = slice(i * 256, (i + 1) * 256)
        for r in range(2):
            net.wait(hidden_slots + 2 * r + i, side_tile(s.hidden_side, r, i))
        mine = cols(s.hidden, net.x * 512 + i * 256, 256)
        s.p_out[i] = (
            mm(mine[...], s.g_all[...], TN) + mm(s.hidden_side[:, at], s.g_side[...], TN)
        ).astype(BF)

    def out_done(i):
        part = s.out_block.at[i * 64 : (i + 1) * 64]
        reduce_out[i].finish(part)
        gather_out[i].begin(0, part)
        v.keep.append(local(part, out_view(i, c)))

    def p_fc(i):
        at = slice(i * 256, (i + 1) * 256)
        for r in range(2):
            net.wait(pre_slots + 2 * r + i, side_tile(s.pre_side, r, i))
        mine = cols(s.grad_pre, net.x * 512 + i * 256, 256)

        def fc_rows(k, carry):
            rows = pl.ds(pl.multiple_of(k * 256, 256), 256)
            total = mm(s.n_two[:, rows], mine[...], TN) + mm(s.n_side[:, rows], s.pre_side[:, at], TN)
            s.p_fc[i, pl.ds(k, 1)] = total.astype(BF).reshape(1, 4, 64, 256)
            return carry

        lax.fori_loop(0, 4, fc_rows, 0)

    def fc_done(i):
        reduce_fc[i].finish(s.fc_sum.at[i])
        mine = pl.ds(pl.multiple_of(b * 256, 256), 256)
        for j in batch_others:
            net.send(s.fc_sum.at[i, j], s.fc_block.at[i, :, mine], (j, c), swap_slots + 2 * b + i)
        s.fc_block[i, :, mine] = s.fc_sum[i, pl.ds(b, 1)][0]

    def fc_swap(i):
        for j in batch_others:
            at = pl.ds(pl.multiple_of(j * 256, 256), 256)
            net.wait(swap_slots + 2 * j + i, s.fc_block.at[i, :, at])
        gather_fc[i].begin(0, s.fc_block.at[i])
        v.keep.append(local(s.fc_block.at[i], fc_view(i, c)))

    def p_proj():
        def proj_rows(at):
            s.p_proj[at, :] = mm(s.att_own[:, at], s.branch[...], TN).astype(BF)

        loop(4, 256, proj_rows)
        reduce_proj.give()
        reduce_proj.keep()

    def proj_done():
        add_into(s.proj_sum, reduce_proj.finish())
        reduce_part.start()

    def part_done():
        reduce_part.line.finish(s.proj_block)
        gather_part.begin(0, s.proj_block)
        v.keep.append(local(s.proj_block, rows_of(o_proj, 32)(c)))

    def p_layer():
        def layer_block(j):
            at = pl.ds(pl.multiple_of(j * ROWS, ROWS), ROWS)
            s.p_layer[at, :] = mm(s.hidden[at, :], s.wout_mine[...]).astype(BF)

        layer_block(net.diag)
        reduce_layer.give()
        layer_block(net.sib)
        reduce_layer.keep()
        layer_block(net.across)
        layer_block(b)

    def layer_end():
        layer_bias = row_of(s.parts, 11)
        terms = reduce_layer.finish()

        def layer_rows(at):
            total = terms[0][at, :].astype(F32) + terms[1][at, :].astype(F32) + terms[2][at, :].astype(F32)
            layer_out[at, :] = (s.middle[at, :] + total + layer_bias).astype(BF)

        loop(ROWS // 32, 32, layer_rows)

    def att_back():
        attend_back(
            s.mix, s.turned, s.dout, s.lse, s.gmix, s.grad_k, s.grad_v,
            s.work, s.more, s.low_work, s.low_more,
        )

    def mix_give(k):
        swap_mix.give(2 * k)
        swap_mix.give(2 * k + 1)

    def p_qkv():
        def qkv_block(j):
            at = pl.ds(pl.multiple_of(j * SHARD, SHARD), SHARD)
            s.p_qkv[at, :] = mm(s.n_one[:, at], s.gmix[...], TN).astype(BF)

        qkv_block(net.diag)
        reduce_qkv.give()
        qkv_block(net.across)
        qkv_block(net.sib)
        reduce_qkv.keep()
        qkv_block(b)

    def qkv_done():
        terms = reduce_qkv.finish()
        add_into(s.qkv_block, terms)
        gather_qkv.start(halves(s.qkv_block, SHARD, 0))
        v.keep.append(local(s.qkv_block, o_qkv.at[c]))

    def gqv():
        s.gqv[...] = jnp.zeros_like(s.gqv)
        s.gqv[pl.ds(c, 1), :] = jnp.sum(s.gmix[:, :PAIR].astype(F32), 0, keepdims=True)
        s.gqv[pl.ds(8 + c, 1), :] = jnp.sum(s.gmix[:, 2 * PAIR :].astype(F32), 0, keepdims=True)
        for p in range(NC):
            at = p * PAIR
            row, lane = 2 + (at % 512) // SHARD, at % SHARD
            s.gs[at // 512, row : row + 1, lane : lane + PAIR] = s.gqv[p : p + 1, :]
            s.gs[2 + at // 512, row : row + 1, lane : lane + PAIR] = s.gqv[8 + p : 9 + p, :]

    def full_start(i):
        gather_full[i].start([rows_of(wqkv, SHARD // 2)(i)])

    def grad_in():
        for gather in gather_full:
            gather.finish()
        swap_mix.finish()
        for j in range(NC):
            for t in range(3):
                to, at = t * WIDTH + j * PAIR, t * PAIR
                s.gmix_all[:, to : to + PAIR] = s.gmix_own[j, :, at : at + PAIR]
        gain = v.gain

        def one_cols(at):
            s.gn_one[:, at] = mm(s.gmix_all[...], s.wfull[at, :], NT)

        loop(4, 256, one_cols)

        def token_rows(i, carry):
            at = pl.ds(pl.multiple_of(i * 32, 32), 32)
            grad_gain, grad_bias = carry
            grad, norm = s.gn_one[at, :], s.hat_one[at, :]
            scaled = grad * gain
            inner = scaled - jnp.mean(scaled, -1, keepdims=True)
            inner = inner - norm * jnp.mean(scaled * norm, -1, keepdims=True)
            grad_tokens[at, :] = (s.grad_middle[at, :] + s.scale_one[at, :] * inner).astype(BF)
            return (
                grad_gain + jnp.sum(grad * norm, 0, keepdims=True),
                grad_bias + jnp.sum(grad, 0, keepdims=True),
            )

        sums = lax.fori_loop(0, ROWS // 32, token_rows, (jnp.zeros((1, WIDTH), F32),) * 2)
        put_row(s.gs, 0, sums[0])
        put_row(s.gs, 1, sums[1])
        for j in batch_others:
            net.send(s.gs.at[j], s.gs_box.at[b], (j, c), gs_slots + b)

    def gs_sum():
        total = s.gs[pl.ds(b, 1)][0]
        for j in batch_others:
            net.wait(gs_slots + j, s.gs_box.at[j])
            total = total + s.gs_box[pl.ds(j, 1)][0]
        s.gs_sum[...] = total
        for i in range(1, NC):
            j = lax.rem(c + i, NC)
            net.send(s.gs_sum, s.gs_far.at[c], (b, j), far_slots + c)

    def far_sum():
        total = s.gs_sum[...]
        for i in range(1, NC):
            j = lax.rem(c - i + NC, NC)
            net.wait(far_slots + j, s.gs_far.at[j])
            total = total + s.gs_far[pl.ds(j, 1)][0]
        grad_small[...] = total

    enter()
    one_start()
    send_small()
    pair_start()
    small_wait()
    g_start()
    proj_start()
    gather_one.stage(1,-1)
    gather_one.stage(1,1)
    gather_one.corner()
    gather_pair.relay()
    gather_one.stage(2,-1)
    gather_one.pass_on(1)
    qv_rows()
    gather_one.stage(2,1)
    gather_one.pass_on(2)
    fc_start(0)
    gather_one.stage(3,1)
    gather_one.stage(3,-1)
    proj_relay()
    gather_pair.finish()
    mix_at(0)
    gs_give_own()
    g_relay()
    mix_at(1)
    mix_at(2)
    gather_one.pass_on(3)
    mix_at(3)
    gather_one.finish()
    mix_side()
    fc_start(1)
    att()
    proj_side()
    proj_finish()
    gs_give_across()
    swap_att.finish()
    middle()
    ns_give()
    gs_relay_own()
    gs_relay_across()
    gather_gs.finish()
    feed_wait()
    gather_two.near()
    feed_i(0,0)
    gather_two.relay()
    gather_two.far()
    feed_i(1,0)
    feed_i(1,1)
    feed_i(0,1)
    pre_give(0,0)
    pre_give(0,1)
    ns_start()
    feed_rest(1)
    norm_diag()
    feed_rest(0)
    p_out(0)
    reduce_out[0].launch(0)
    pre_give(1,0)
    norm_across()
    reduce_norm.cross()
    reduce_out[0].pass_one(0)
    pre_give(1,1)
    reduce_out[0].launch(1)
    norm_sib()
    p_out(1)
    reduce_out[1].launch(0)
    reduce_out[0].pass_one(1)
    norm_own()
    gather_ns.relay()
    reduce_out[0].pass_two()
    reduce_out[1].pass_one(0)
    reduce_out[1].launch(1)
    reduce_out[0].launch(2)
    back_two()
    p_proj()
    reduce_out[1].launch(2)
    reduce_out[1].pass_one(1)
    reduce_out[1].pass_two()
    reduce_proj.cross()
    gather_ns.finish()
    p_fc(0)
    reduce_fc[0].launch(0)
    out_done(0)
    out_done(1)
    p_fc(1)
    reduce_fc[0].pass_one(0)
    p_layer()
    full_start(0)
    gather_out[0].stage(1,-1)
    gather_out[0].stage(1,1)
    reduce_fc[0].launch(1)
    gather_out[1].stage(1,1)
    proj_done()
    gather_out[1].stage(1,-1)
    reduce_fc[0].pass_one(1)
    reduce_fc[0].pass_two()
    swap_grad.finish()
    att_back()
    mix_give(3)
    mix_give(0)
    p_qkv()
    reduce_qkv.cross()
    reduce_part.fold()
    reduce_part.line.launch(1)
    reduce_fc[0].launch(2)
    gather_out[0].stage(2,1)
    reduce_part.line.launch(0)
    gather_out[0].stage(2,-1)
    reduce_fc[1].launch(0)
    reduce_part.line.pass_one(0)
    reduce_part.line.pass_one(1)
    gqv()
    gather_full[0].relay()
    reduce_fc[1].launch(1)
    fc_done(0)
    gather_out[1].stage(2,1)
    gather_out[1].stage(2,-1)
    reduce_part.line.launch(2)
    reduce_fc[1].pass_one(0)
    reduce_part.line.pass_two()
    reduce_fc[1].launch(2)
    full_start(1)
    qkv_done()
    mix_give(2)
    reduce_fc[1].pass_one(1)
    reduce_fc[1].pass_two()
    gather_out[0].stage(3,-1)
    gather_out[0].stage(3,1)
    gather_out[1].stage(3,-1)
    gather_out[1].stage(3,1)
    mix_give(1)
    fc_swap(0)
    gather_qkv.stage(1,-1)
    part_done()
    gather_qkv.stage(1,1)
    fc_done(1)
    fc_swap(1)
    gather_part.stage(1,1)
    gather_qkv.corner()
    gather_fc[0].stage(1,1)
    reduce_layer.cross()
    gather_qkv.stage(2,-1)
    gather_full[1].relay()
    gather_fc[0].stage(1,-1)
    gather_part.stage(1,-1)
    gather_fc[1].stage(1,1)
    gather_qkv.stage(3,-1)
    gather_part.stage(2,1)
    gather_fc[0].stage(2,1)
    gather_fc[1].stage(1,-1)
    gather_qkv.stage(2,1)
    gather_fc[1].stage(2,1)
    gather_part.stage(2,-1)
    layer_end()
    gather_fc[0].stage(2,-1)
    gather_fc[1].stage(2,-1)
    gather_qkv.pass_on(1)
    grad_in()
    gather_qkv.pass_on(2)
    gather_qkv.stage(3,1)
    gather_fc[0].stage(3,-1)
    gather_fc[1].stage(3,-1)
    gather_fc[0].stage(3,1)
    gs_sum()
    gather_fc[1].stage(3,1)
    gather_part.stage(3,1)
    gather_part.stage(3,-1)
    gather_qkv.pass_on(3)
    far_sum()
    for gather in gather_out + gather_fc + [gather_qkv, gather_part]:
        gather.finish()
    for copy in v.keep:
        copy.wait()
    net.drain()


PARTS = 4


def widen_kernel(layer, grad_in, small, w_qkv, w_proj, w_fc, w_out, *refs):
    o_layer, o_grad_in, o_qkv, o_proj, o_fc, o_out = refs[:6]
    vectors, (qkv, proj, fc, out, sems) = refs[6:14], refs[14:]
    leaving = []

    def leave(src, dst):
        copy = pltpu.make_async_copy(src, dst, sems.at[len(leaving)])
        copy.start()
        leaving.append(copy)

    for k in range(PARTS):
        wide, at = slice(k * 256, (k + 1) * 256), slice(k * 64, (k + 1) * 64)
        out[wide, :] = w_out[wide, :].astype(F32)
        leave(out.at[wide], o_out.at[wide])
        for j in range(NB):
            for x in range(2):
                for i in range(2):
                    to = j * WIDTH + x * 512 + i * 256
                    fc[at, to : to + 256] = w_fc[x, i, at, j * 256 : (j + 1) * 256].astype(F32)
        leave(fc.at[at], o_fc.at[at])
        for j in range(NC):
            for t in range(3):
                to = t * WIDTH + j * PAIR
                qkv[at, to : to + PAIR] = w_qkv[j, at, t * PAIR : (t + 1) * PAIR].astype(F32)
        leave(qkv.at[at], o_qkv.at[at])
        proj[at, :] = w_proj[at, :].astype(F32)
        leave(proj.at[at], o_proj.at[at])
    leave(layer, o_layer)
    leave(grad_in, o_grad_in)
    row = 0
    for vector in vectors:
        for i in range(vector.shape[0] // SHARD):
            vector[i * SHARD : (i + 1) * SHARD] = small[row, :]
            row += 1
    for copy in leaving:
        copy.wait()


def per_device_fast(
    tokens, cotangent, ln1_gain, ln1_bias, qkv_weight, qv_bias, proj_weight, proj_bias,
    ln2_gain, ln2_bias, fc_weight, fc_bias, out_weight, out_bias,
):
    vmem, anywhere = pl.BlockSpec(memory_space=pltpu.VMEM), pl.BlockSpec(memory_space=pl.ANY)
    shape = jax.ShapeDtypeStruct
    layer, grad_in, grad_small, w_qkv, w_proj, w_fc, w_out = pl.pallas_call(
        layer_kernel,
        out_shape=(
            pltpu.VMEM((ROWS, WIDTH), BF),
            pltpu.VMEM((ROWS, WIDTH), BF),
            pltpu.VMEM((SMALL_ROWS, SHARD), F32),
            pltpu.VMEM((NC, SHARD, 3 * PAIR), BF),
            pltpu.VMEM((SHARD, WIDTH), BF),
            pltpu.VMEM((2, 2, SHARD, WIDTH), BF),
            pltpu.VMEM((FF // NB, WIDTH), BF),
        ),
        in_specs=[anywhere] * 14,
        out_specs=(vmem,) * 7,
        scratch_shapes=[pltpu.VMEM(*item) for item in SCRATCH.values()]
        + [
            pltpu.SemaphoreType.DMA((SENDS,)),
            pltpu.SemaphoreType.DMA((RECVS,)),
            pltpu.SemaphoreType.DMA((LOCALS,)),
        ],
        compiler_params=pltpu.CompilerParams(
            collective_id=0, has_side_effects=True, vmem_limit_bytes=LAYER_VMEM
        ),
    )(
        tokens.reshape(ROWS, WIDTH), cotangent.reshape(ROWS, WIDTH),
        ln1_gain, ln1_bias, qv_bias, proj_bias, ln2_gain, ln2_bias, fc_bias, out_bias,
        qkv_weight, proj_weight, fc_weight, out_weight,
    )
    layer, grad_in, w_qkv, w_proj, w_fc, w_out, *vectors = pl.pallas_call(
        widen_kernel,
        out_shape=(
            shape((ROWS, WIDTH), BF),
            shape((ROWS, WIDTH), BF),
            shape((SHARD, 3 * WIDTH), F32),
            shape((SHARD, WIDTH), F32),
            shape((SHARD, FF), F32),
            shape((FF // NB, WIDTH), F32),
            *[shape((n * SHARD,), F32) for n in VECTOR_ROWS],
        ),
        in_specs=[vmem] * 7,
        out_specs=(anywhere,) * 6 + (vmem,) * len(VECTOR_ROWS),
        scratch_shapes=[
            pltpu.VMEM((SHARD, 3 * WIDTH), F32),
            pltpu.VMEM((SHARD, WIDTH), F32),
            pltpu.VMEM((SHARD, FF), F32),
            pltpu.VMEM((FF // NB, WIDTH), F32),
            pltpu.SemaphoreType.DMA((4 * PARTS + 2,)),
        ],
        compiler_params=pltpu.CompilerParams(vmem_limit_bytes=WIDEN_VMEM),
    )(layer, grad_in, grad_small, w_qkv, w_proj, w_fc, w_out)
    return (
        layer.reshape(tokens.shape),
        grad_in.reshape(tokens.shape),
        vectors[0],
        vectors[1],
        w_qkv,
        vectors[2],
        w_proj,
        vectors[3],
        vectors[4],
        vectors[5],
        w_fc,
        vectors[6],
        w_out,
        vectors[7],
    )


LAYER_VMEM, WIDEN_VMEM = 55 * 1024 * 1024, 20 * 1024 * 1024


def solution(mesh):
    placed = (
        P("batch", "ctx", None),
        P("batch", "ctx", None),
        P("batch"),
        P("batch"),
        P("batch", None),
        P("batch"),
        P("batch", None),
        P("batch"),
        P("batch"),
        P("batch"),
        P("batch", None),
        P("batch"),
        P("batch", None),
        P("batch"),
    )
    fits = dict(mesh.shape) == {"batch": NB, "ctx": NC}
    return jax.shard_map(
        per_device_fast if fits else per_device,
        mesh=mesh,
        in_specs=placed,
        out_specs=(
            P("batch", "ctx", None),
            P("batch", "ctx", None),
            P("batch"),
            P("batch"),
            P("batch", None),
            P("batch"),
            P("batch", None),
            P("batch"),
            P("batch"),
            P("batch"),
            P("batch", None),
            P("batch"),
            P("batch", None),
            P("batch"),
        ),
        check_vma=False,
    )
```

```python
from functools import partial
from types import SimpleNamespace

import jax
import jax.numpy as jnp
from jax import lax
from jax.experimental import pallas as pl
from jax.experimental.pallas import tpu as pltpu
from jax.sharding import PartitionSpec as P

HEADS = 16
HEAD_DIM = 64


epsilon = 1e-05
masked_value = -1e30


def shifted(block, axis, distance):
    devices = range(lax.axis_size(axis))
    route = [(i - distance, i) for i in devices if i - distance in devices]
    return lax.ppermute(block, axis, route)


def from_behind(block, axis, distance):
    devices = range(lax.axis_size(axis))
    route = [((i - distance) % len(devices), i) for i in devices]
    return lax.ppermute(block, axis, route)


def layer_norm(inputs, gain_vec, bias_vec):
    centre = inputs - jnp.mean(inputs, -1, keepdims=True)
    spread = jnp.mean(centre * centre, -1, keepdims=True)
    return centre * lax.rsqrt(spread + epsilon) * gain_vec + bias_vec


def keep_same(running):
    return running


def per_device(
    tokens,
    cotangent,
    ln1_gain,
    ln1_bias,
    qkv_weight,
    qv_bias,
    proj_weight,
    proj_bias,
    ln2_gain,
    ln2_bias,
    fc_weight,
    fc_bias,
    out_weight,
    out_bias,
):
    (
        gain_one,
        bias_one,
        weight_qkv,
        bias_qv,
        weight_proj,
        bias_proj,
        gain_two,
        bias_two,
        weight_fc,
        bias_fc,
        weight_out,
        bias_out,
    ) = (
        lax.all_gather(ln1_gain, "batch", axis=0, tiled=True),
        lax.all_gather(ln1_bias, "batch", axis=0, tiled=True),
        lax.all_gather(qkv_weight, "batch", axis=0, tiled=True),
        lax.all_gather(qv_bias, "batch", axis=0, tiled=True),
        lax.all_gather(proj_weight, "batch", axis=0, tiled=True),
        lax.all_gather(proj_bias, "batch", axis=0, tiled=True),
        lax.all_gather(ln2_gain, "batch", axis=0, tiled=True),
        lax.all_gather(ln2_bias, "batch", axis=0, tiled=True),
        lax.all_gather(fc_weight, "batch", axis=0, tiled=True),
        lax.all_gather(fc_bias, "batch", axis=0, tiled=True),
        lax.all_gather(out_weight, "batch", axis=0, tiled=True),
        lax.all_gather(out_bias, "batch", axis=0, tiled=True),
    )
    seq_count, ctx_rows, model_width = tokens.shape
    row_count = seq_count * ctx_rows
    inputs = tokens.astype(jnp.float32).reshape(row_count, model_width)
    norm_one, norm_one_pull = jax.vjp(
        layer_norm, inputs, gain_one.astype(jnp.float32), bias_one.astype(jnp.float32)
    )
    normed_low = norm_one.astype(jnp.bfloat16)
    bias_float = bias_qv.astype(jnp.float32)
    bias_full = jnp.concatenate(
        [bias_float[:model_width], jnp.zeros((model_width,), jnp.float32), bias_float[model_width:]]
    )
    mixed_proj = (
        jnp.dot(normed_low, weight_qkv, preferred_element_type=jnp.float32) + bias_full
    ).astype(jnp.bfloat16)
    query_flat = mixed_proj[:, :model_width].reshape(seq_count, ctx_rows, model_width)
    key_flat = mixed_proj[:, model_width : 2 * model_width].reshape(
        seq_count, ctx_rows, model_width
    )
    value_flat = mixed_proj[:, 2 * model_width :].reshape(seq_count, ctx_rows, model_width)
    query_heads = query_flat.reshape(seq_count, ctx_rows, HEADS, HEAD_DIM)
    own_index = lax.axis_index("ctx")
    position = own_index * ctx_rows
    query_pos = position + jnp.arange(ctx_rows, dtype=jnp.int32)
    last_pos = position + ctx_rows - 1
    start_state = (
        jnp.full((seq_count, ctx_rows, HEADS), masked_value, jnp.float32),
        jnp.zeros((seq_count, ctx_rows, HEADS), jnp.float32),
        jnp.zeros((seq_count, ctx_rows, HEADS, HEAD_DIM), jnp.float32),
    )
    key_piece = lax.all_gather(key_flat, "ctx", axis=1, tiled=True)
    value_piece = lax.all_gather(value_flat, "ctx", axis=1, tiled=True)
    piece_rows = key_piece.shape[1]

    def compute(running):
        run_max, run_sum, accum = running
        key_split = key_piece.reshape(seq_count, piece_rows, HEADS, HEAD_DIM)
        value_split = value_piece.reshape(seq_count, piece_rows, HEADS, HEAD_DIM)
        scores = (
            jnp.einsum(
                "bqhd,bkhd->bqhk", query_heads, key_split, preferred_element_type=jnp.float32
            )
            * 0.125
        )
        key_pos = jnp.arange(piece_rows, dtype=jnp.int32)
        allowed = (key_pos[None, :] <= query_pos[:, None])[None, :, None, :]
        scores = jnp.where(allowed, scores, masked_value)
        new_max = jnp.maximum(run_max, jnp.max(scores, -1))
        weights_exp = jnp.where(allowed, jnp.exp(scores - new_max[..., None]), 0.0)
        new_sum = jnp.sum(weights_exp, -1)
        product = jnp.einsum(
            "bqhk,bkhd->bqhd",
            weights_exp.astype(jnp.bfloat16),
            value_split,
            preferred_element_type=jnp.float32,
        )
        return (new_max, new_sum, product)

    run_max, run_sum, accum = lax.cond(jnp.int32(0) <= last_pos, compute, keep_same, start_state)
    log_total = run_max + jnp.log(run_sum)
    attended = accum / run_sum[..., None]
    attended_low = attended.reshape(row_count, model_width).astype(jnp.bfloat16)
    middle = (
        inputs
        + jnp.dot(attended_low, weight_proj, preferred_element_type=jnp.float32)
        + bias_proj.astype(jnp.float32)
    )
    norm_two, norm_two_pull = jax.vjp(
        layer_norm, middle, gain_two.astype(jnp.float32), bias_two.astype(jnp.float32)
    )
    normed_two = norm_two.astype(jnp.bfloat16)
    pre_act = jnp.dot(normed_two, weight_fc, preferred_element_type=jnp.float32) + bias_fc.astype(
        jnp.float32
    )
    activated, gelu_pull = jax.vjp(partial(jax.nn.gelu, approximate=True), pre_act)
    hidden_low = activated.astype(jnp.bfloat16)
    output = (
        middle
        + jnp.dot(hidden_low, weight_out, preferred_element_type=jnp.float32)
        + bias_out.astype(jnp.float32)
    )
    layer_out = output.astype(jnp.bfloat16).reshape(tokens.shape)
    grad_out = cotangent.reshape(row_count, model_width)
    grad_out_float = grad_out.astype(jnp.float32)
    grad_w_out = jnp.einsum("rf,rd->fd", hidden_low, grad_out, preferred_element_type=jnp.float32)
    grad_b_out = jnp.sum(grad_out_float, 0)
    grad_hidden = jnp.einsum("rd,fd->rf", grad_out, weight_out, preferred_element_type=jnp.float32)
    (grad_pre,) = gelu_pull(grad_hidden)
    grad_pre_low = grad_pre.astype(jnp.bfloat16)
    grad_w_fc = jnp.einsum(
        "rd,rf->df", normed_two, grad_pre_low, preferred_element_type=jnp.float32
    )
    grad_b_fc = jnp.sum(grad_pre_low.astype(jnp.float32), 0)
    grad_norm_two = jnp.einsum(
        "rf,df->rd", grad_pre_low, weight_fc, preferred_element_type=jnp.float32
    )
    grad_mid_norm, grad_g_two, grad_b_two = norm_two_pull(grad_norm_two)
    grad_middle = grad_out_float + grad_mid_norm
    grad_branch = grad_middle.astype(jnp.bfloat16)
    grad_w_proj = jnp.einsum(
        "rd,re->de", attended_low, grad_branch, preferred_element_type=jnp.float32
    )
    grad_b_proj = jnp.sum(grad_branch.astype(jnp.float32), 0)
    grad_attended = jnp.einsum(
        "re,de->rd", grad_branch, weight_proj, preferred_element_type=jnp.float32
    ).astype(jnp.bfloat16)
    grad_att_flat = grad_attended.reshape(seq_count, ctx_rows, model_width)
    grad_att_heads = grad_att_flat.reshape(seq_count, ctx_rows, HEADS, HEAD_DIM)
    delta_mine = jnp.sum(grad_att_heads.astype(jnp.float32) * attended, -1)
    zero_heads = jnp.zeros((seq_count, ctx_rows, HEADS, HEAD_DIM), jnp.float32)
    cycle_count = lax.axis_size("ctx")

    def cycle_turn(turn, state):
        owner = (own_index - turn) % cycle_count
        first_row = owner * ctx_rows

        def visit(inner):
            key_piece, value_piece, grad_k, grad_v, grad_q = inner
            key_split = key_piece.reshape(seq_count, ctx_rows, HEADS, HEAD_DIM)
            value_split = value_piece.reshape(seq_count, ctx_rows, HEADS, HEAD_DIM)
            piece_pos = first_row + jnp.arange(ctx_rows, dtype=jnp.int32)
            scores = (
                jnp.einsum(
                    "bqhd,bkhd->bqhk", query_heads, key_split, preferred_element_type=jnp.float32
                )
                * 0.125
            )
            allowed = (piece_pos[None, :] <= query_pos[:, None])[None, :, None, :]
            probs = jnp.where(allowed, jnp.exp(scores - log_total[..., None]), 0.0)
            grad_probs = jnp.einsum(
                "bqhd,bkhd->bqhk", grad_att_heads, value_split, preferred_element_type=jnp.float32
            )
            grad_scores = (probs * (grad_probs - delta_mine[..., None])).astype(jnp.bfloat16)
            grad_q = (
                grad_q
                + jnp.einsum(
                    "bqhk,bkhd->bqhd", grad_scores, key_split, preferred_element_type=jnp.float32
                )
                * 0.125
            )
            grad_k = (
                grad_k
                + jnp.einsum(
                    "bqhk,bqhd->bkhd", grad_scores, query_heads, preferred_element_type=jnp.float32
                )
                * 0.125
            )
            grad_v = grad_v + jnp.einsum(
                "bqhk,bqhd->bkhd",
                probs.astype(jnp.bfloat16),
                grad_att_heads,
                preferred_element_type=jnp.float32,
            )
            return (key_piece, value_piece, grad_k, grad_v, grad_q)

        key_piece, value_piece, grad_k, grad_v, grad_q = lax.cond(
            owner <= own_index, visit, keep_same, state
        )
        key_piece, value_piece = shifted((key_piece, value_piece), "ctx", 1)
        grad_k, grad_v = (
            from_behind(grad_k.astype(jnp.bfloat16), "ctx", 1).astype(grad_k.dtype),
            from_behind(grad_v.astype(jnp.bfloat16), "ctx", 1).astype(grad_v.dtype),
        )
        return (key_piece, value_piece, grad_k, grad_v, grad_q)

    cycle_state = lax.fori_loop(
        0, cycle_count, cycle_turn, (key_flat, value_flat, zero_heads, zero_heads, zero_heads)
    )
    grad_k, grad_v, grad_q = (cycle_state[2], cycle_state[3], cycle_state[4])
    grad_mixed = jnp.concatenate(
        [
            grad_q.reshape(row_count, model_width),
            grad_k.reshape(row_count, model_width),
            grad_v.reshape(row_count, model_width),
        ],
        axis=1,
    ).astype(jnp.bfloat16)
    grad_w_qkv = jnp.einsum("rd,re->de", normed_low, grad_mixed, preferred_element_type=jnp.float32)
    grad_bias_all = jnp.sum(grad_mixed.astype(jnp.float32), 0)
    grad_b_qv = jnp.concatenate([grad_bias_all[:model_width], grad_bias_all[2 * model_width :]])
    grad_norm_one = jnp.einsum(
        "re,de->rd", grad_mixed, weight_qkv, preferred_element_type=jnp.float32
    )
    grad_in_norm, grad_g_one, grad_b_one = norm_one_pull(grad_norm_one)
    grad_tokens = (grad_middle + grad_in_norm).astype(jnp.bfloat16).reshape(tokens.shape)
    local_grads = (
        grad_g_one,
        grad_b_one,
        grad_w_qkv,
        grad_b_qv,
        grad_w_proj,
        grad_b_proj,
        grad_g_two,
        grad_b_two,
        grad_w_fc,
        grad_b_fc,
        grad_w_out,
        grad_b_out,
    )
    partial_grads = (
        lax.psum_scatter(
            local_grads[0].astype(jnp.bfloat16), "batch", scatter_dimension=0, tiled=True
        ).astype(jnp.float32),
        lax.psum_scatter(
            local_grads[1].astype(jnp.bfloat16), "batch", scatter_dimension=0, tiled=True
        ).astype(jnp.float32),
        lax.psum_scatter(
            local_grads[2].astype(jnp.bfloat16), "batch", scatter_dimension=0, tiled=True
        ).astype(jnp.float32),
        lax.psum_scatter(
            local_grads[3].astype(jnp.bfloat16), "batch", scatter_dimension=0, tiled=True
        ).astype(jnp.float32),
        lax.psum_scatter(
            local_grads[4].astype(jnp.bfloat16), "batch", scatter_dimension=0, tiled=True
        ).astype(jnp.float32),
        lax.psum_scatter(
            local_grads[5].astype(jnp.bfloat16), "batch", scatter_dimension=0, tiled=True
        ).astype(jnp.float32),
        lax.psum_scatter(
            local_grads[6].astype(jnp.bfloat16), "batch", scatter_dimension=0, tiled=True
        ).astype(jnp.float32),
        lax.psum_scatter(
            local_grads[7].astype(jnp.bfloat16), "batch", scatter_dimension=0, tiled=True
        ).astype(jnp.float32),
        lax.psum_scatter(
            local_grads[8].astype(jnp.bfloat16), "batch", scatter_dimension=0, tiled=True
        ).astype(jnp.float32),
        lax.psum_scatter(
            local_grads[9].astype(jnp.bfloat16), "batch", scatter_dimension=0, tiled=True
        ).astype(jnp.float32),
        lax.psum_scatter(
            local_grads[10].astype(jnp.bfloat16), "batch", scatter_dimension=0, tiled=True
        ).astype(jnp.float32),
        lax.psum_scatter(
            local_grads[11].astype(jnp.bfloat16), "batch", scatter_dimension=0, tiled=True
        ).astype(jnp.float32),
    )
    summed_grads = lax.psum(
        (
            partial_grads[0],
            partial_grads[1],
            partial_grads[2],
            partial_grads[3],
            partial_grads[4],
            partial_grads[5],
            partial_grads[6],
            partial_grads[7],
            partial_grads[8],
            partial_grads[9],
            partial_grads[10],
            partial_grads[11],
        ),
        "ctx",
    )
    return (
        layer_out,
        grad_tokens,
        summed_grads[0],
        summed_grads[1],
        summed_grads[2],
        summed_grads[3],
        summed_grads[4],
        summed_grads[5],
        summed_grads[6],
        summed_grads[7],
        summed_grads[8],
        summed_grads[9],
        summed_grads[10],
        summed_grads[11],
    )


BF, F32 = jnp.bfloat16, jnp.float32
NN = (((1,), (0,)), ((), ()))
NT = (((1,), (1,)), ((), ()))
TN = (((0,), (0,)), ((), ()))
MESH = pl.DeviceIdType.MESH
NB, NC, WIDTH, ROWS, FF, PAIR = 4, 8, 1024, 128, 4096, 128
SHARD = WIDTH // NB
LENGTH = ROWS * NC
SMALL_ROWS = 16


def mm(left, right, dims=NN):
    return lax.dot_general(left, right, dims, preferred_element_type=F32)


def run(when, action):
    if when is None:
        action()
    else:
        pl.when(when)(action)


def both(one, two):
    return two if one is None else (one if two is None else jnp.logical_and(one, two))


class Net:
    def __init__(self, b, c, send_sems, recv_sems):
        self.b, self.c, self.z, self.x = b, c, c // 2, c % 2
        self.side = c + 1 - 2 * self.x
        self.core = b % 2
        self.sib = b + 1 - 2 * self.core
        self.across = lax.rem(b + 2, NB)
        self.diag = lax.rem(self.sib + 2, NB)
        self.send_sems, self.recv_sems = send_sems, recv_sems
        self.taken, self.pending = 0, []

    def slots(self, count):
        base = self.taken
        self.taken += count
        assert self.taken <= self.recv_sems.shape[0]
        return base

    def send(self, src, dst, device, slot, when=None):
        index = len(self.pending)
        if index == self.send_sems.shape[0]:
            done, copy, index = self.pending.pop(0)
            run(done, copy.wait_send)
        copy = pltpu.make_async_remote_copy(
            src_ref=src,
            dst_ref=dst,
            send_sem=self.send_sems.at[index],
            recv_sem=self.recv_sems.at[slot],
            device_id=device,
            device_id_type=MESH,
        )
        run(when, copy.start)
        self.pending.append((when, copy, index))

    def wait(self, slot, ref):
        pltpu.make_async_remote_copy(
            src_ref=ref,
            dst_ref=ref,
            send_sem=self.send_sems.at[0],
            recv_sem=self.recv_sems.at[slot],
            device_id=(self.sib, self.c),
            device_id_type=MESH,
        ).wait_recv()

    def drain(self):
        for when, copy, _ in self.pending:
            run(when, copy.wait_send)


class GatherCtx:
    def __init__(self, net, views, others, count, turn=False):
        self.net, self.views, self.others, self.count, self.turn = net, views, others, count, turn
        self.along, self.beside = net.slots(4 * count), net.slots(1)
        self.turned = net.slots(4) if turn else None

    def begin(self, i, src):
        net, count = self.net, self.count
        dst, at = self.views(net.c)[i], net.z * count + i
        if self.turn and i == count - 1:
            end = jnp.logical_or(net.z == 0, net.z == 3)
            net.send(src, dst, (net.b, net.side), self.turned + 2, net.z == 0)
            net.send(src, dst, (net.b, net.side), self.turned + 3, net.z == 3)
            net.send(src, dst, (net.b, net.side), self.beside, jnp.logical_not(end))
        else:
            net.send(src, dst, (net.b, net.side), self.beside)
        net.send(src, dst, (net.b, net.c + 2), self.along + at, net.z < 3)
        net.send(src, dst, (net.b, net.c - 2), self.along + at, net.z > 0)

    def start(self, srcs):
        for i, src in enumerate(srcs):
            self.begin(i, src)

    def stage(self, d, sign):
        net, count = self.net, self.count
        zz = net.z + sign * d
        here = zz >= 0 if sign < 0 else zz <= 3
        refs = self.views(2 * zz + net.x)
        onward = both(here, net.z < 3 if sign < 0 else net.z > 0)
        for i in range(count):
            slot = self.along + zz * count + i
            pl.when(here)(lambda slot=slot, ref=refs[i]: net.wait(slot, ref))
            if d < 3:
                net.send(refs[i], refs[i], (net.b, net.c - 2 * sign), slot, onward)
            goes = here
            if self.turn and i == count - 1:
                goes = both(here, jnp.logical_and(zz > 0, zz < 3))
            net.send(refs[i], refs[i], (net.b, net.side), self.beside, goes)

    def piece(self, end):
        return self.views(2 * end + 1 - self.net.x)[self.count - 1]

    def corner(self):
        net = self.net
        for end, step in ((0, 2), (3, -2)):
            ref, slot = self.piece(end), self.turned + 2 + (end > 0)
            pl.when(net.z == end)(lambda slot=slot, ref=ref: net.wait(slot, ref))
            net.send(ref, ref, (net.b, net.c + step), self.turned + (end > 0), net.z == end)

    def pass_on(self, d):
        net = self.net
        for end, step in ((0, 2), (3, -2)):
            here = net.z == (end + d if end == 0 else end - d)
            ref, slot = self.piece(end), self.turned + (end > 0)
            pl.when(here)(lambda slot=slot, ref=ref: net.wait(slot, ref))
            if d < 3:
                net.send(ref, ref, (net.b, net.c + step), slot, here)

    def finish(self):
        self.net.wait(self.beside, self.others)


def chunks(ref):
    if len(ref.shape) == 3:
        return ref.shape[0], lambda i: (i,)
    rows = min(32, ref.shape[0])
    return ref.shape[0] // rows, lambda i: (pl.ds(pl.multiple_of(i * rows, rows), rows),)


def add_into(target, terms, dtype=BF):
    count, at = chunks(target)

    def body(i, carry):
        total = terms[0][at(i)].astype(F32)
        for term in terms[1:]:
            total = total + term[at(i)].astype(F32)
        target[at(i)] = total.astype(dtype)
        return carry

    lax.fori_loop(0, count, body, 0)


class ReduceLine:
    def __init__(self, net, mine, up, down):
        self.net, self.mine, self.up, self.down = net, mine, up, down
        self.s_up, self.s_down = net.slots(4), net.slots(4)

    def give(self, k, upward, when):
        net = self.net
        if upward:
            net.send(self.mine(k), self.up.at[k], (net.b, net.c + 2), self.s_up + k, when)
        else:
            net.send(self.mine(k), self.down.at[k], (net.b, net.c - 2), self.s_down + k, when)

    def take(self, k, upward, when):
        box, slot = (self.up, self.s_up) if upward else (self.down, self.s_down)
        mine = self.mine(k)

        @pl.when(when)
        def _():
            self.net.wait(slot + k, box.at[k])
            add_into(mine, [mine, box.at[k]])

        self.give(k, upward, when)

    def launch(self, k):
        self.give(3 - k, True, self.net.z == 0)
        self.give(k, False, self.net.z == 3)

    def pass_one(self, k):
        self.take(3 - k, True, self.net.z == 1)
        self.take(k, False, self.net.z == 2)

    def pass_two(self):
        self.take(0, False, self.net.z == 1)
        self.take(3, True, self.net.z == 2)

    def finish(self, target):
        net, z = self.net, self.net.z
        mine = self.mine(z)

        @pl.when(z >= 1)
        def _():
            net.wait(self.s_up + z, self.up.at[z])

        @pl.when(z <= 2)
        def _():
            net.wait(self.s_down + z, self.down.at[z])

        pl.when(z == 0)(lambda: add_into(target, [mine, self.down.at[z]]))
        pl.when(z == 3)(lambda: add_into(target, [mine, self.up.at[z]]))
        pl.when(jnp.logical_and(z > 0, z < 3))(
            lambda: add_into(target, [mine, self.up.at[z], self.down.at[z]])
        )


class ReduceCtx:
    def __init__(self, net, mine, beside, up, down):
        self.net, self.mine, self.beside = net, mine, beside
        self.slots = net.slots(4)
        self.line = ReduceLine(net, lambda k: mine(2 * k + net.x), up, down)

    def start(self):
        net = self.net
        for k in (3, 0, 2, 1):
            net.send(self.mine(2 * k + 1 - net.x), self.beside.at[k], (net.b, net.side), self.slots + k)

    def fold(self):
        for k in (3, 0, 2, 1):
            self.net.wait(self.slots + k, self.beside.at[k])
            mine = self.line.mine(k)
            add_into(mine, [mine, self.beside.at[k]])


class SwapCtx:
    def __init__(self, net, src, dst, others):
        self.net, self.src, self.dst, self.others = net, src, dst, others
        self.slot = net.slots(1)

    def give(self, j):
        net, src, dst = self.net, self.src(j), self.dst(self.net.c)
        net.send(src, dst, (net.b, j), self.slot, net.c != j)

        @pl.when(net.c == j)
        def _():
            dst[...] = src[...]

    def start(self):
        for j in range(NC):
            self.give(j)

    def finish(self):
        self.net.wait(self.slot, self.others)


class GatherBatch:
    def __init__(self, net, views, count=1):
        self.net, self.views, self.count = net, views, count
        self.base = net.slots(NB * count)

    def start(self, srcs):
        net = self.net
        dsts = self.views(net.b)
        for i in range(self.count):
            slot = self.base + net.b * self.count + i
            net.send(srcs[i], dsts[i], (net.across, net.c), slot)
        for i in range(self.count):
            slot = self.base + net.b * self.count + i
            net.send(srcs[i], dsts[i], (net.sib, net.c), slot)

    def relay(self):
        net = self.net
        refs = self.views(net.across)
        for i in range(self.count):
            slot = self.base + net.across * self.count + i
            net.wait(slot, refs[i])
            net.send(refs[i], refs[i], (net.sib, net.c), slot)

    def take(self, j):
        refs = self.views(j)
        for i in range(self.count):
            self.net.wait(self.base + j * self.count + i, refs[i])

    def near(self):
        self.take(self.net.sib)

    def far(self):
        self.take(self.net.diag)

    def finish(self):
        self.near()
        self.far()


class ReduceBatch:
    def __init__(self, net, mine, boxes):
        self.net, self.mine, self.boxes = net, mine, boxes
        self.base = net.slots(3)

    def give(self):
        net = self.net
        net.send(self.mine(net.diag), self.boxes.at[0], (net.sib, net.c), self.base)

    def cross(self):
        net = self.net
        net.wait(self.base, self.boxes.at[0])
        block = self.mine(net.across)
        add_into(block, [block, self.boxes.at[0]])
        net.send(block, self.boxes.at[1], (net.across, net.c), self.base + 1)

    def keep(self):
        net = self.net
        net.send(self.mine(net.sib), self.boxes.at[2], (net.sib, net.c), self.base + 2)

    def finish(self):
        net = self.net
        net.wait(self.base + 2, self.boxes.at[2])
        net.wait(self.base + 1, self.boxes.at[1])
        return [self.mine(net.b), self.boxes.at[1], self.boxes.at[2]]


def row_of(parts, index):
    return jnp.concatenate([parts[j, index : index + 1, :] for j in range(NB)], axis=1)


def put_row(target, index, row):
    for j in range(NB):
        target[j, index : index + 1, :] = row[:, j * SHARD : (j + 1) * SHARD]


def rows_of(block, size):
    return lambda j: block.at[pl.ds(pl.multiple_of(j * size, size), size)]


def normalise(inputs):
    centre = inputs - jnp.mean(inputs, -1, keepdims=True)
    spread = jnp.mean(centre * centre, -1, keepdims=True)
    scale = lax.rsqrt(spread + epsilon)
    return centre * scale, scale


def head_lanes(h, rows):
    lane = lax.broadcasted_iota(jnp.int32, (rows, PAIR), 1)
    return (lane >= h * HEAD_DIM) & (lane < (h + 1) * HEAD_DIM)


QB = 256


def scores_of(keys, query, masked):
    scores = mm(keys, query, NT) * 0.125
    if masked:
        key_pos = lax.broadcasted_iota(jnp.int32, scores.shape, 0)
        query_pos = lax.broadcasted_iota(jnp.int32, scores.shape, 1)
        scores = jnp.where(key_pos <= query_pos, scores, masked_value)
    return scores


def attend(mix, value_t, att, lse, work, low_work, ready):
    value_t[...] = mix[:, 2 * PAIR :].astype(F32).T.astype(BF)
    for qb in reversed(range(LENGTH // QB)):
        here = slice(qb * QB, (qb + 1) * QB)
        outs = []
        for h in range(2):
            query = jnp.where(head_lanes(h, QB), mix[here, :PAIR], jnp.zeros((), BF))
            top = None
            for kb in range(qb + 1):
                keys = slice(kb * QB, (kb + 1) * QB)
                scores = scores_of(mix[keys, PAIR : 2 * PAIR], query, kb == qb)
                work[keys, :] = scores
                peak = jnp.max(scores, axis=0, keepdims=True)
                top = peak if top is None else jnp.maximum(top, peak)
            total = None
            for kb in range(qb + 1):
                keys = slice(kb * QB, (kb + 1) * QB)
                grown = jnp.exp(work[keys, :] - top)
                part = jnp.sum(grown, axis=0, keepdims=True)
                total = part if total is None else total + part
                low_work[h, keys, :] = grown.astype(BF)
            count = (qb + 1) * QB
            lanes = slice(h * HEAD_DIM, (h + 1) * HEAD_DIM)
            out = mm(value_t[lanes, :count], low_work[h, :count, :])
            outs.append(out / total)
            lse[h * 4 + qb : h * 4 + qb + 1, :] = top + jnp.log(total)
        att[here, :] = jnp.concatenate(outs, axis=0).T.astype(BF)
        ready(qb)


def attend_back(mix, key_t, dout, lse, gmix, grad_k, grad_v, work, more, low_work, low_more):
    key_t[...] = mix[:, PAIR : 2 * PAIR].astype(F32).T.astype(BF)
    grad_k[...] = jnp.zeros_like(grad_k)
    grad_v[...] = jnp.zeros_like(grad_v)
    for qb in reversed(range(LENGTH // QB)):
        here = slice(qb * QB, (qb + 1) * QB)
        outs = []
        count = (qb + 1) * QB
        for h in range(2):
            lanes = head_lanes(h, QB)
            query = jnp.where(lanes, mix[here, :PAIR], jnp.zeros((), BF))
            grad = jnp.where(lanes, dout[here, :], jnp.zeros((), BF))
            level = lse[h * 4 + qb : h * 4 + qb + 1, :]
            delta = None
            for kb in range(qb + 1):
                keys = slice(kb * QB, (kb + 1) * QB)
                probs = jnp.exp(scores_of(mix[keys, PAIR : 2 * PAIR], query, kb == qb) - level)
                grad_probs = mm(mix[keys, 2 * PAIR :], grad, NT)
                part = jnp.sum(probs * grad_probs, axis=0, keepdims=True)
                delta = part if delta is None else delta + part
                work[keys, :] = probs
                more[keys, :] = grad_probs
                low_work[h, keys, :] = probs.astype(BF)
            for kb in range(qb + 1):
                keys = slice(kb * QB, (kb + 1) * QB)
                low_more[h, keys, :] = (work[keys, :] * (more[keys, :] - delta)).astype(BF)
            grad_v[:count, :] += mm(low_work[h, :count, :], grad)
            grad_k[:count, :] += mm(low_more[h, :count, :], query)
            rows = slice(h * HEAD_DIM, (h + 1) * HEAD_DIM)
            outs.append(mm(key_t[rows, :count], low_more[h, :count, :]) * 0.125)
        gmix[here, :PAIR] = jnp.concatenate(outs, axis=0).T.astype(BF)
        gmix[here, PAIR : 2 * PAIR] = (grad_k[here, :] * 0.125).astype(BF)
        gmix[here, 2 * PAIR :] = grad_v[here, :].astype(BF)


gelu_scale = 0.7978845608028654
gelu_cubic = 0.044715


def gelu_pair(x):
    square = x * x
    bent = jnp.tanh(gelu_scale * x * (1.0 + gelu_cubic * square))
    half = 0.5 * (1.0 + bent)
    slope = half + 0.5 * x * (1.0 - bent * bent) * (gelu_scale * (1.0 + 3.0 * gelu_cubic * square))
    return x * half, slope


VECTOR_ROWS = (1, 1, 2, 1, 1, 1, 4, 1)
SCRATCH = dict(
    tokens=((ROWS, WIDTH), BF),
    **{f"v{i}": ((rows * SHARD,), BF) for i, rows in enumerate(VECTOR_ROWS)},
    small=((SMALL_ROWS, SHARD), F32),
    parts=((NB, SMALL_ROWS, SHARD), F32),
    qv_rows=((16, PAIR), F32),
    wpair=((WIDTH, 3 * PAIR), BF),
    wfull=((WIDTH, 3 * WIDTH), BF),
    wproj_all=((WIDTH, WIDTH), BF),
    wfc_mine=((WIDTH, WIDTH), BF),
    wout_mine=((WIDTH, WIDTH), BF),
    g_all=((NB * ROWS, WIDTH), BF),
    hat_one=((ROWS, WIDTH), F32),
    scale_one=((ROWS, 1), F32),
    hat_all=((LENGTH, WIDTH), BF),
    n_one=((LENGTH, WIDTH), BF),
    mix=((LENGTH, 3 * PAIR), BF),
    turned=((PAIR, LENGTH), BF),
    att=((LENGTH, PAIR), BF),
    lse=((8, QB), F32),
    work=((LENGTH, QB), F32),
    more=((LENGTH, QB), F32),
    low_work=((2, LENGTH, QB), BF),
    low_more=((2, LENGTH, QB), BF),
    att_own=((ROWS, WIDTH), BF),
    middle=((ROWS, WIDTH), F32),
    hat_two=((ROWS, WIDTH), F32),
    scale_two=((ROWS, 1), F32),
    n_two=((NB * ROWS, WIDTH), BF),
    hidden=((NB * ROWS, WIDTH), BF),
    grad_pre=((NB * ROWS, WIDTH), BF),
    p_norm=((NB * ROWS, WIDTH), BF),
    p_norm_box=((3, ROWS, WIDTH), BF),
    p_layer=((NB * ROWS, WIDTH), BF),
    p_layer_box=((3, ROWS, WIDTH), BF),
    g_side=((NB * ROWS, WIDTH), BF),
    n_side=((NB * ROWS, WIDTH), BF),
    hidden_side=((NB * ROWS, WIDTH // 2), BF),
    pre_side=((NB * ROWS, WIDTH // 2), BF),
    p_out=((2, 256, WIDTH), BF),
    out_up=((2, 4, 64, WIDTH), BF),
    out_down=((2, 4, 64, WIDTH), BF),
    out_block=((ROWS, WIDTH), BF),
    p_fc=((2, NB, 4, 64, 256), BF),
    fc_up=((2, 4, NB, 64, 256), BF),
    fc_down=((2, 4, NB, 64, 256), BF),
    fc_sum=((2, NB, 64, 256), BF),
    fc_block=((2, 64, WIDTH), BF),
    p_proj=((WIDTH, WIDTH), BF),
    p_proj_box=((3, SHARD, WIDTH), BF),
    proj_sum=((SHARD, WIDTH), BF),
    proj_beside=((4, 32, WIDTH), BF),
    proj_up=((4, 32, WIDTH), BF),
    proj_down=((4, 32, WIDTH), BF),
    proj_block=((32, WIDTH), BF),
    grad_middle=((ROWS, WIDTH), F32),
    branch=((ROWS, WIDTH), BF),
    g_att=((ROWS, WIDTH), BF),
    dout=((LENGTH, PAIR), BF),
    gmix=((LENGTH, 3 * PAIR), BF),
    grad_k=((LENGTH, PAIR), F32),
    grad_v=((LENGTH, PAIR), F32),
    gmix_own=((NC, ROWS, 3 * PAIR), BF),
    gmix_all=((ROWS, 3 * WIDTH), BF),
    p_qkv=((WIDTH, 3 * PAIR), BF),
    p_qkv_box=((3, SHARD, 3 * PAIR), BF),
    qkv_block=((SHARD, 3 * PAIR), BF),
    gn_one=((ROWS, WIDTH), F32),
    gs=((NB, SMALL_ROWS, SHARD), F32),
    gqv=((16, PAIR), F32),
    gs_box=((NB, SMALL_ROWS, SHARD), F32),
    gs_sum=((SMALL_ROWS, SHARD), F32),
    gs_far=((NC, SMALL_ROWS, SHARD), F32),
)
SENDS, RECVS, LOCALS = 40, 176, 26


def layer_kernel(*refs):
    tokens, cotangent = refs[:2]
    vectors = refs[2:10]
    wqkv, wproj, wfc, wout = refs[10:14]
    layer_out, grad_tokens, grad_small, o_qkv, o_proj, o_fc, o_out = refs[14:21]
    scratch = refs[21:]
    s = SimpleNamespace(**dict(zip(SCRATCH, scratch)))
    send_sems, recv_sems, local_sems = scratch[len(SCRATCH) :]
    b, c = lax.axis_index("batch"), lax.axis_index("ctx")
    net = Net(b, c, send_sems, recv_sems)
    v = SimpleNamespace(keep=[])
    locals_open = []

    def local(src, dst):
        copy = pltpu.make_async_copy(src, dst, local_sems.at[len(locals_open)])
        copy.start()
        locals_open.append(copy)
        return copy

    def own(ref, size):
        return rows_of(ref, size)(b)

    def cols(ref, start, count=PAIR):
        return ref.at[:, pl.ds(pl.multiple_of(start, 128), count)]

    def halves(ref, size, j):
        block = rows_of(ref, size)(j)
        return [block.at[0 : size // 2], block.at[size // 2 : size]]

    def loop(count, size, body):
        def step(i, carry):
            body(pl.ds(pl.multiple_of(i * size, size), size))
            return carry

        lax.fori_loop(0, count, step, 0)

    batch_others = [lax.rem(b + i, NB) for i in range(1, NB)]

    small_slot, fc_slots, fc_side_slots = net.slots(1), net.slots(2 * NB), net.slots(NB)
    hidden_slots, pre_slots, side_slot, swap_slots = net.slots(4), net.slots(4), net.slots(2), net.slots(2)
    proj_slots, proj_side_slot, proj_near_slots = net.slots(NB), net.slots(1), net.slots(2)
    gs_slot, far_slot = net.slots(1), net.slots(1)
    gather_pair = GatherBatch(net, lambda j: [rows_of(s.wpair, SHARD)(j)])
    gather_one = GatherCtx(net, lambda j: halves(s.hat_all, ROWS, j), s.hat_all.at[: 3 * ROWS], 2, True)
    gather_g = GatherBatch(net, lambda j: [rows_of(s.g_all, ROWS)(j)])
    gather_gs = GatherBatch(net, lambda j: [rows_of(s.g_side, ROWS)(j)])
    gather_ns = GatherBatch(net, lambda j: [rows_of(s.n_side, ROWS)(j)])
    gather_two = GatherBatch(net, lambda j: halves(s.n_two, ROWS, j), 2)
    gather_full = [
        GatherBatch(net, lambda j, i=i: [rows_of(s.wfull, SHARD // 2)(2 * j + i)]) for i in range(2)
    ]
    swap_att = SwapCtx(
        net, rows_of(s.att, ROWS), lambda j: cols(s.att_own, j * PAIR), s.att_own.at[:, : 7 * PAIR]
    )
    swap_grad = SwapCtx(
        net, lambda j: cols(s.g_att, j * PAIR), rows_of(s.dout, ROWS), s.dout.at[: 7 * ROWS]
    )
    swap_mix = SwapCtx(
        net, rows_of(s.gmix, ROWS), lambda j: s.gmix_own.at[j], s.gmix_own.at[:7]
    )
    reduce_norm = ReduceBatch(net, rows_of(s.p_norm, ROWS), s.p_norm_box)
    reduce_layer = ReduceBatch(net, rows_of(s.p_layer, ROWS), s.p_layer_box)
    reduce_proj = ReduceBatch(net, rows_of(s.p_proj, SHARD), s.p_proj_box)
    reduce_qkv = ReduceBatch(net, rows_of(s.p_qkv, SHARD), s.p_qkv_box)
    reduce_part = ReduceCtx(net, rows_of(s.proj_sum, 32), s.proj_beside, s.proj_up, s.proj_down)
    reduce_out = [
        ReduceLine(net, rows_of(s.p_out.at[i], 64), s.out_up.at[i], s.out_down.at[i]) for i in range(2)
    ]
    reduce_fc = [
        ReduceLine(net, lambda k, i=i: s.p_fc.at[i, :, k], s.fc_up.at[i], s.fc_down.at[i])
        for i in range(2)
    ]

    def out_view(i, j):
        return rows_of(o_out, 64)(8 * (j % 2) + 4 * i + j // 2)

    def fc_view(i, j):
        return o_fc.at[j % 2, i, pl.ds(pl.multiple_of((j // 2) * 64, 64), 64)]

    gather_out = [GatherCtx(net, lambda j, i=i: [out_view(i, j)], o_out.at[:256], 1) for i in range(2)]
    gather_fc = [GatherCtx(net, lambda j, i=i: [fc_view(i, j)], o_fc.at[0, 0], 1) for i in range(2)]
    gather_qkv = GatherCtx(net, lambda j: halves(o_qkv.at[j], SHARD, 0), o_qkv.at[:3], 2, True)
    gather_part = GatherCtx(net, lambda j: [rows_of(o_proj, 32)(j)], o_proj.at[:128], 1)

    scale, hat = s.scale_one, s.hat_one
    half, pair_z = net.z % 2, (b, c + 2 - 4 * (net.z % 2))
    fc_rows = [
        pl.ds(pl.multiple_of(SHARD // 2 + x * (SHARD // 4), SHARD // 4), SHARD // 4) for x in (half, 1 - half)
    ]
    side_rows = pl.ds(pl.multiple_of(half * (SHARD // 2), SHARD // 2), SHARD // 2)
    other_side_rows = pl.ds(pl.multiple_of((1 - half) * (SHARD // 2), SHARD // 2), SHARD // 2)
    chip_rows = [
        pl.ds(pl.multiple_of(first * 256, 256), 256) for first in (b // 2, 1 - b // 2)
    ]
    hat_mine = rows_of(s.hat_all, ROWS)(c)
    n_two_mine = own(s.n_two, ROWS)
    g_mine = own(s.g_all, ROWS)
    n_beside = own(s.n_side, ROWS)

    def enter():
        barrier = pltpu.get_barrier_semaphore()
        others = [(j, c) for j in batch_others]
        others += [(b, lax.rem(c + i, NC)) for i in range(1, NC)]
        for device in others:
            pl.semaphore_signal(barrier, inc=1, device_id=device, device_id_type=MESH)
        get_tokens = local(tokens, s.tokens)
        own_vectors = [getattr(s, f"v{i}") for i in range(len(vectors))]
        get_vectors = [local(one, two) for one, two in zip(vectors, own_vectors)]
        get_pair = [
            local(cols(wqkv, t * WIDTH + c * PAIR), own(s.wpair, SHARD).at[:, t * PAIR : (t + 1) * PAIR])
            for t in range(3)
        ]
        v.get_proj = local(wproj, own(s.wproj_all, SHARD))
        v.get_rest = [
            local(cols(wfc, b * WIDTH, WIDTH), own(s.wfc_mine, SHARD)),
            local(wout, s.wout_mine),
            local(wqkv, own(s.wfull, SHARD)),
            local(cotangent, g_mine),
        ]
        s.small[...] = jnp.zeros_like(s.small)
        for copy in get_vectors:
            copy.wait()
        row = 0
        for vector in own_vectors:
            for i in range(vector.shape[0] // SHARD):
                piece = vector[i * SHARD : (i + 1) * SHARD].astype(F32)
                s.small[row : row + 1, :] = piece.reshape(1, SHARD)
                row += 1

        def norm_rows(at):
            hat[at, :], scale[at, :] = normalise(s.tokens[at, :].astype(F32))
            hat_mine[at, :] = hat[at, :].astype(BF)

        get_tokens.wait()
        loop(ROWS // 32, 32, norm_rows)
        for copy in get_pair:
            copy.wait()
        s.parts[pl.ds(b, 1)] = s.small[...][None]
        pl.semaphore_wait(barrier, len(others))

    def send_small():
        for j in batch_others:
            net.send(s.small, s.parts.at[b], (j, c), small_slot)

    def pair_start():
        gather_pair.start([own(s.wpair, SHARD)])

    def g_start():
        gather_g.start([cotangent])

    def one_start():
        gather_one.start(halves(s.hat_all, ROWS, c))

    def small_wait():
        net.wait(small_slot, s.parts.at[: NB - 1])
        v.gain, v.bias = row_of(s.parts, 0), row_of(s.parts, 1)

    def proj_start():
        mine = own(s.wproj_all, SHARD)
        net.send(wproj.at[side_rows], mine.at[side_rows], (net.across, c), proj_slots + b)
        net.send(wproj, mine, (net.sib, c), proj_slots + b)

    def proj_relay():
        block = rows_of(s.wproj_all, SHARD)(net.across).at[side_rows]
        net.wait(proj_slots + net.across, block)
        net.send(block, block, pair_z, proj_side_slot)
        net.send(block, block, (net.sib, c), proj_near_slots)

    def proj_side():
        block = rows_of(s.wproj_all, SHARD)(net.across).at[other_side_rows]
        net.wait(proj_side_slot, block)
        net.send(block, block, (net.sib, c), proj_near_slots + 1)

    def fc_start(i):
        at = [slice(0, SHARD // 2), fc_rows[0]][i]
        for j in (net.across, net.diag):
            cut = wfc.at[at, pl.ds(pl.multiple_of(j * WIDTH, WIDTH), WIDTH)]
            net.send(cut, own(s.wfc_mine, SHARD).at[at], (j, c), fc_slots + 2 * b + i)
        if i == 0:
            net.send(cols(wfc, net.sib * WIDTH, WIDTH), own(s.wfc_mine, SHARD), (net.sib, c), fc_slots + 2 * b)

    def fc_relay():
        for j in (net.across, net.diag):
            block = rows_of(s.wfc_mine, SHARD)(j).at[fc_rows[0]]
            net.wait(fc_slots + 2 * j + 1, block)
            net.send(block, block, pair_z, fc_side_slots + j)

    def qv_rows():
        for p in range(NC):
            at = p * PAIR
            row, lane = 2 + (at % 512) // SHARD, at % SHARD
            s.qv_rows[p : p + 1, :] = s.parts[at // 512, row : row + 1, lane : lane + PAIR]
            s.qv_rows[8 + p : 9 + p, :] = s.parts[2 + at // 512, row : row + 1, lane : lane + PAIR]

    def g_relay():
        gather_g.relay()

    def gs_give():
        net.send(cotangent, own(s.g_side, ROWS), (b, net.side), side_slot + 1)

    def gs_start():
        net.wait(side_slot + 1, own(s.g_side, ROWS))
        gather_gs.start([own(s.g_side, ROWS)])

    def mix_block(j):
        rows = pl.ds(pl.multiple_of(j * ROWS, ROWS), ROWS)
        mix_bias = jnp.concatenate(
            [s.qv_rows[pl.ds(c, 1), :], jnp.zeros((1, PAIR), F32), s.qv_rows[pl.ds(8 + c, 1), :]], axis=1
        )
        s.n_one[rows, :] = (s.hat_all[rows, :].astype(F32) * v.gain + v.bias).astype(BF)
        s.mix[rows, :] = (mm(s.n_one[rows, :], s.wpair[...]) + mix_bias).astype(BF)

    def mix_at(d):
        if d == 0:
            mix_block(c)
        for zz in (net.z - d, net.z + d)[: 2 * d]:

            @pl.when(jnp.logical_and(zz >= 0, zz <= 3))
            def _():
                mix_block(2 * zz + net.x)

    def mix_side():
        def step(zz, carry):
            mix_block(2 * zz + 1 - net.x)
            return carry

        lax.fori_loop(0, 4, step, 0)

    def att():
        def ready(qb):
            swap_att.give(2 * qb)
            swap_att.give(2 * qb + 1)

        attend(s.mix, s.turned, s.att, s.lse, s.work, s.low_work, ready)

    def proj_finish():
        v.get_proj.wait()
        net.wait(proj_slots + net.sib, rows_of(s.wproj_all, SHARD)(net.sib))
        block = rows_of(s.wproj_all, SHARD)(net.diag)
        net.wait(proj_near_slots, block.at[side_rows])
        net.wait(proj_near_slots + 1, block.at[other_side_rows])

    def middle():
        def middle_cols(at):
            s.middle[:, at] = mm(s.att_own[...], s.wproj_all[:, at]) + s.tokens[:, at].astype(F32)

        loop(WIDTH // 256, 256, middle_cols)
        proj_bias, gain_two, bias_two = row_of(s.parts, 4), row_of(s.parts, 5), row_of(s.parts, 6)

        def norm_two_rows(at):
            middle = s.middle[at, :] + proj_bias
            s.middle[at, :] = middle
            norm, width = normalise(middle)
            s.hat_two[at, :], s.scale_two[at, :] = norm, width
            n_two_mine[at, :] = (norm * gain_two + bias_two).astype(BF)

        loop(ROWS // 32, 32, norm_two_rows)
        gather_two.start(halves(s.n_two, ROWS, b))

    def ns_give():
        net.send(n_two_mine, n_beside, (b, net.side), side_slot)

    def ns_start():
        net.wait(side_slot, n_beside)
        gather_ns.start([n_beside])

    def feed_wait():
        for copy in v.get_rest:
            copy.wait()
        gather_g.finish()
        net.wait(fc_slots + 2 * net.sib, rows_of(s.wfc_mine, SHARD)(net.sib))
        for j in (net.across, net.diag):
            block = rows_of(s.wfc_mine, SHARD)(j)
            net.wait(fc_slots + 2 * j, block.at[0 : SHARD // 2])
            net.wait(fc_side_slots + j, block.at[fc_rows[1]])
        s.gs[...] = jnp.zeros_like(s.gs)

    def feed_cols(r, i):
        n = lax.rem(2 * (1 - net.x) + i, 4)
        rows, at = chip_rows[r], pl.ds(pl.multiple_of(n * 256, 256), 256)
        pre = mm(s.n_two[rows, :], s.wfc_mine[:, at]) + s.small[pl.ds(7 + n, 1), :]
        value, slope = gelu_pair(pre)
        s.hidden[rows, at] = value.astype(BF)
        grad = (mm(s.g_all[rows, :], s.wout_mine[at, :], NT) * slope).astype(BF)
        s.grad_pre[rows, at] = grad
        s.gs[pl.ds(b, 1), pl.ds(7 + n, 1), :] += jnp.sum(grad.astype(F32), 0, keepdims=True)[None]

    def tile(ref, r, i):
        return ref.at[chip_rows[r], pl.ds(pl.multiple_of((2 * (1 - net.x) + i) * 256, 256), 256)]

    def side_tile(ref, r, i):
        return ref.at[chip_rows[r], i * 256 : (i + 1) * 256]

    def feed_i(r, i):
        feed_cols(r, i)
        net.send(tile(s.hidden, r, i), side_tile(s.hidden_side, r, i), (b, net.side), hidden_slots + 2 * r + i)

    def pre_give(r, i):
        net.send(tile(s.grad_pre, r, i), side_tile(s.pre_side, r, i), (b, net.side), pre_slots + 2 * r + i)

    def feed_rest(r):
        def step(i, carry):
            feed_cols(r, i)
            return carry

        lax.fori_loop(2, 4, step, 0)

    def norm_block(j):
        at = pl.ds(pl.multiple_of(j * ROWS, ROWS), ROWS)
        s.p_norm[at, :] = mm(s.grad_pre[at, :], s.wfc_mine[...], NT).astype(BF)

    def norm_diag():
        norm_block(net.diag)
        reduce_norm.give()

    def norm_across():
        norm_block(net.across)

    def norm_sib():
        norm_block(net.sib)
        reduce_norm.keep()

    def norm_own():
        norm_block(b)

    def back_two():
        gain_two = row_of(s.parts, 5)
        terms = reduce_norm.finish()

        def back_rows(i, carry):
            at = pl.ds(pl.multiple_of(i * 32, 32), 32)
            grad_gain, grad_bias, sum_branch, sum_g = carry
            grad = terms[0][at, :].astype(F32) + terms[1][at, :].astype(F32) + terms[2][at, :].astype(F32)
            norm = s.hat_two[at, :]
            scaled = grad * gain_two
            inner = scaled - jnp.mean(scaled, -1, keepdims=True)
            inner = inner - norm * jnp.mean(scaled * norm, -1, keepdims=True)
            g = g_mine[at, :].astype(F32)
            total = g + s.scale_two[at, :] * inner
            s.grad_middle[at, :] = total
            low = total.astype(BF)
            s.branch[at, :] = low
            return (
                grad_gain + jnp.sum(grad * norm, 0, keepdims=True),
                grad_bias + jnp.sum(grad, 0, keepdims=True),
                sum_branch + jnp.sum(low.astype(F32), 0, keepdims=True),
                sum_g + jnp.sum(g, 0, keepdims=True),
            )

        sums = lax.fori_loop(0, ROWS // 32, back_rows, (jnp.zeros((1, WIDTH), F32),) * 4)
        put_row(s.gs, 5, sums[0])
        put_row(s.gs, 6, sums[1])
        put_row(s.gs, 4, sums[2])
        put_row(s.gs, 11, sums[3])

        def att_cols(at):
            s.g_att[:, at] = mm(s.branch[...], s.wproj_all[at, :], NT).astype(BF)

        loop(4, 256, att_cols)
        swap_grad.start()

    def p_out(i):
        at = slice(i * 256, (i + 1) * 256)
        for r in range(2):
            net.wait(hidden_slots + 2 * r + i, side_tile(s.hidden_side, r, i))
        mine = cols(s.hidden, net.x * 512 + i * 256, 256)
        s.p_out[i] = (
            mm(mine[...], s.g_all[...], TN) + mm(s.hidden_side[:, at], s.g_side[...], TN)
        ).astype(BF)

    def out_done(i):
        part = s.out_block.at[i * 64 : (i + 1) * 64]
        reduce_out[i].finish(part)
        gather_out[i].begin(0, part)
        v.keep.append(local(part, out_view(i, c)))

    def p_fc(i):
        at = slice(i * 256, (i + 1) * 256)
        for r in range(2):
            net.wait(pre_slots + 2 * r + i, side_tile(s.pre_side, r, i))
        mine = cols(s.grad_pre, net.x * 512 + i * 256, 256)

        def fc_rows(k, carry):
            rows = pl.ds(pl.multiple_of(k * 256, 256), 256)
            total = mm(s.n_two[:, rows], mine[...], TN) + mm(s.n_side[:, rows], s.pre_side[:, at], TN)
            s.p_fc[i, pl.ds(k, 1)] = total.astype(BF).reshape(1, 4, 64, 256)
            return carry

        lax.fori_loop(0, 4, fc_rows, 0)

    def fc_done(i):
        reduce_fc[i].finish(s.fc_sum.at[i])
        mine = pl.ds(pl.multiple_of(b * 256, 256), 256)
        for j in batch_others:
            net.send(s.fc_sum.at[i, j], s.fc_block.at[i, :, mine], (j, c), swap_slots + i)
        s.fc_block[i, :, mine] = s.fc_sum[i, pl.ds(b, 1)][0]

    def fc_swap(i):
        net.wait(swap_slots + i, s.fc_block.at[i, :, : (NB - 1) * 256])
        gather_fc[i].begin(0, s.fc_block.at[i])
        v.keep.append(local(s.fc_block.at[i], fc_view(i, c)))

    def p_proj():
        def proj_rows(at):
            s.p_proj[at, :] = mm(s.att_own[:, at], s.branch[...], TN).astype(BF)

        loop(4, 256, proj_rows)
        reduce_proj.give()
        reduce_proj.keep()

    def proj_done():
        add_into(s.proj_sum, reduce_proj.finish())
        reduce_part.start()

    def part_done():
        reduce_part.line.finish(s.proj_block)
        gather_part.begin(0, s.proj_block)
        v.keep.append(local(s.proj_block, rows_of(o_proj, 32)(c)))

    def p_layer():
        def layer_block(j):
            at = pl.ds(pl.multiple_of(j * ROWS, ROWS), ROWS)
            s.p_layer[at, :] = mm(s.hidden[at, :], s.wout_mine[...]).astype(BF)

        layer_block(net.diag)
        reduce_layer.give()
        layer_block(net.sib)
        reduce_layer.keep()
        layer_block(net.across)
        layer_block(b)

    def layer_end():
        layer_bias = row_of(s.parts, 11)
        terms = reduce_layer.finish()

        def layer_rows(at):
            total = terms[0][at, :].astype(F32) + terms[1][at, :].astype(F32) + terms[2][at, :].astype(F32)
            layer_out[at, :] = (s.middle[at, :] + total + layer_bias).astype(BF)

        loop(ROWS // 32, 32, layer_rows)

    def att_back():
        attend_back(
            s.mix, s.turned, s.dout, s.lse, s.gmix, s.grad_k, s.grad_v,
            s.work, s.more, s.low_work, s.low_more,
        )

    def mix_give(k):
        swap_mix.give(2 * k)
        swap_mix.give(2 * k + 1)

    def p_qkv():
        def qkv_block(j):
            at = pl.ds(pl.multiple_of(j * SHARD, SHARD), SHARD)
            s.p_qkv[at, :] = mm(s.n_one[:, at], s.gmix[...], TN).astype(BF)

        qkv_block(net.diag)
        reduce_qkv.give()
        qkv_block(net.across)
        qkv_block(net.sib)
        reduce_qkv.keep()
        qkv_block(b)

    def qkv_done():
        terms = reduce_qkv.finish()
        add_into(s.qkv_block, terms)
        gather_qkv.start(halves(s.qkv_block, SHARD, 0))
        v.keep.append(local(s.qkv_block, o_qkv.at[c]))

    def gqv():
        s.gqv[...] = jnp.zeros_like(s.gqv)
        s.gqv[pl.ds(c, 1), :] = jnp.sum(s.gmix[:, :PAIR].astype(F32), 0, keepdims=True)
        s.gqv[pl.ds(8 + c, 1), :] = jnp.sum(s.gmix[:, 2 * PAIR :].astype(F32), 0, keepdims=True)
        for p in range(NC):
            at = p * PAIR
            row, lane = 2 + (at % 512) // SHARD, at % SHARD
            s.gs[at // 512, row : row + 1, lane : lane + PAIR] = s.gqv[p : p + 1, :]
            s.gs[2 + at // 512, row : row + 1, lane : lane + PAIR] = s.gqv[8 + p : 9 + p, :]

    def full_start(i):
        gather_full[i].start([rows_of(wqkv, SHARD // 2)(i)])

    def grad_in():
        for gather in gather_full:
            gather.finish()
        swap_mix.finish()
        for j in range(NC):
            for t in range(3):
                to, at = t * WIDTH + j * PAIR, t * PAIR
                s.gmix_all[:, to : to + PAIR] = s.gmix_own[j, :, at : at + PAIR]
        gain = v.gain

        def one_cols(at):
            s.gn_one[:, at] = mm(s.gmix_all[...], s.wfull[at, :], NT)

        loop(4, 256, one_cols)

        def token_rows(i, carry):
            at = pl.ds(pl.multiple_of(i * 32, 32), 32)
            grad_gain, grad_bias = carry
            grad, norm = s.gn_one[at, :], s.hat_one[at, :]
            scaled = grad * gain
            inner = scaled - jnp.mean(scaled, -1, keepdims=True)
            inner = inner - norm * jnp.mean(scaled * norm, -1, keepdims=True)
            grad_tokens[at, :] = (s.grad_middle[at, :] + s.scale_one[at, :] * inner).astype(BF)
            return (
                grad_gain + jnp.sum(grad * norm, 0, keepdims=True),
                grad_bias + jnp.sum(grad, 0, keepdims=True),
            )

        sums = lax.fori_loop(0, ROWS // 32, token_rows, (jnp.zeros((1, WIDTH), F32),) * 2)
        put_row(s.gs, 0, sums[0])
        put_row(s.gs, 1, sums[1])
        for j in batch_others:
            net.send(s.gs.at[j], s.gs_box.at[b], (j, c), gs_slot)

    def gs_sum():
        total = s.gs[pl.ds(b, 1)][0]
        net.wait(gs_slot, s.gs_box.at[: NB - 1])
        for j in batch_others:
            total = total + s.gs_box[pl.ds(j, 1)][0]
        s.gs_sum[...] = total
        for i in range(1, NC):
            j = lax.rem(c + i, NC)
            net.send(s.gs_sum, s.gs_far.at[c], (b, j), far_slot)

    def far_sum():
        total = s.gs_sum[...]
        net.wait(far_slot, s.gs_far.at[: NC - 1])
        for i in range(1, NC):
            j = lax.rem(c - i + NC, NC)
            total = total + s.gs_far[pl.ds(j, 1)][0]
        grad_small[...] = total

    enter()
    one_start()
    send_small()
    pair_start()
    small_wait()
    gather_one.stage(1,-1)
    gather_one.corner()
    proj_start()
    gather_one.stage(1,1)
    fc_start(1)
    gather_pair.relay()
    gather_pair.finish()
    qv_rows()
    gather_one.stage(2,-1)
    gather_one.pass_on(1)
    gather_one.stage(2,1)
    gather_one.stage(3,-1)
    mix_at(0)
    mix_at(1)
    g_start()
    mix_at(2)
    gather_one.pass_on(2)
    gather_one.stage(3,1)
    proj_relay()
    gs_give()
    mix_at(3)
    fc_start(0)
    gather_one.pass_on(3)
    gather_one.finish()
    mix_side()
    att()
    proj_side()
    proj_finish()
    swap_att.finish()
    fc_relay()
    middle()
    gs_start()
    ns_give()
    g_relay()
    feed_wait()
    gather_two.near()
    feed_i(0,0)
    gather_two.relay()
    ns_start()
    gather_two.far()
    feed_i(1,0)
    feed_i(1,1)
    feed_rest(1)
    norm_diag()
    feed_i(0,1)
    pre_give(0,1)
    gather_gs.relay()
    feed_rest(0)
    gather_gs.finish()
    p_out(0)
    reduce_out[0].launch(0)
    norm_across()
    reduce_out[0].launch(1)
    reduce_norm.cross()
    gather_ns.relay()
    norm_own()
    p_out(1)
    reduce_out[1].launch(0)
    pre_give(1,1)
    pre_give(0,0)
    reduce_out[0].pass_one(0)
    reduce_out[0].launch(2)
    pre_give(1,0)
    norm_sib()
    reduce_out[0].pass_one(1)
    reduce_out[1].launch(1)
    back_two()
    p_proj()
    reduce_out[0].pass_two()
    reduce_out[1].pass_one(0)
    reduce_proj.cross()
    out_done(0)
    reduce_out[1].pass_one(1)
    gather_ns.finish()
    p_fc(0)
    reduce_fc[0].launch(0)
    full_start(1)
    reduce_out[1].pass_two()
    reduce_out[1].launch(2)
    gather_out[0].stage(1,1)
    gather_out[0].stage(1,-1)
    p_fc(1)
    reduce_fc[0].launch(1)
    reduce_fc[0].pass_one(0)
    out_done(1)
    reduce_fc[1].launch(0)
    swap_grad.finish()
    gather_out[0].stage(2,1)
    proj_done()
    reduce_fc[0].launch(2)
    gather_out[0].stage(2,-1)
    reduce_fc[0].pass_one(1)
    reduce_fc[0].pass_two()
    att_back()
    gather_out[0].stage(3,1)
    gather_out[1].stage(1,-1)
    gather_out[0].stage(3,-1)
    reduce_fc[1].launch(1)
    gather_out[1].stage(1,1)
    mix_give(3)
    mix_give(0)
    p_qkv()
    fc_done(0)
    reduce_qkv.cross()
    reduce_part.fold()
    reduce_part.line.launch(1)
    reduce_fc[1].pass_one(0)
    reduce_part.line.launch(0)
    gqv()
    gather_out[1].stage(2,1)
    full_start(0)
    gather_out[1].stage(2,-1)
    fc_swap(0)
    gather_full[1].relay()
    reduce_fc[1].launch(2)
    reduce_part.line.pass_one(0)
    qkv_done()
    reduce_fc[1].pass_one(1)
    reduce_fc[1].pass_two()
    gather_fc[0].stage(1,1)
    gather_out[1].stage(3,-1)
    p_layer()
    gather_fc[0].stage(1,-1)
    mix_give(1)
    reduce_part.line.pass_one(1)
    reduce_part.line.pass_two()
    gather_qkv.stage(1,1)
    gather_out[1].stage(3,1)
    gather_qkv.stage(1,-1)
    fc_done(1)
    gather_qkv.corner()
    reduce_part.line.launch(2)
    mix_give(2)
    gather_fc[0].stage(2,-1)
    fc_swap(1)
    part_done()
    gather_qkv.stage(2,-1)
    gather_full[0].relay()
    gather_fc[0].stage(3,-1)
    gather_fc[0].stage(2,1)
    gather_qkv.stage(2,1)
    gather_fc[1].stage(1,1)
    gather_fc[1].stage(1,-1)
    grad_in()
    gather_fc[0].stage(3,1)
    gather_qkv.stage(3,1)
    gather_part.stage(1,1)
    gather_qkv.stage(3,-1)
    reduce_layer.cross()
    gather_part.stage(1,-1)
    gather_fc[1].stage(2,-1)
    gather_qkv.pass_on(1)
    gather_fc[1].stage(2,1)
    gather_part.stage(2,-1)
    gs_sum()
    gather_part.stage(2,1)
    gather_fc[1].stage(3,1)
    gather_fc[1].stage(3,-1)
    gather_part.stage(3,1)
    gather_part.stage(3,-1)
    gather_qkv.pass_on(2)
    far_sum()
    gather_qkv.pass_on(3)
    layer_end()
    for gather in gather_out + gather_fc + [gather_qkv, gather_part]:
        gather.finish()
    for copy in v.keep:
        copy.wait()
    net.drain()


PARTS = 4


def widen_kernel(layer, grad_in, small, w_qkv, w_proj, w_fc, w_out, *refs):
    o_layer, o_grad_in, o_qkv, o_proj, o_fc, o_out = refs[:6]
    vectors, rows, (qkv, proj, fc, out, sems) = refs[6:14], refs[14:22], refs[22:]
    leaving = []

    def leave(src, dst):
        copy = pltpu.make_async_copy(src, dst, sems.at[len(leaving)])
        copy.start()
        leaving.append(copy)

    row = 0
    for vector, here in zip(vectors, rows):
        for i in range(vector.shape[0] // SHARD):
            here[i * SHARD : (i + 1) * SHARD] = small[row, :]
            row += 1
        leave(here, vector)
    leave(layer, o_layer)
    leave(grad_in, o_grad_in)
    for k in range(PARTS):
        wide, at = slice(k * 256, (k + 1) * 256), slice(k * 64, (k + 1) * 64)
        out[wide, :] = w_out[wide, :].astype(F32)
        leave(out.at[wide], o_out.at[wide])
        for j in range(NB):
            for x in range(2):
                for i in range(2):
                    to = j * WIDTH + x * 512 + i * 256
                    fc[at, to : to + 256] = w_fc[x, i, at, j * 256 : (j + 1) * 256].astype(F32)
        leave(fc.at[at], o_fc.at[at])
        for j in range(NC):
            for t in range(3):
                to = t * WIDTH + j * PAIR
                qkv[at, to : to + PAIR] = w_qkv[j, at, t * PAIR : (t + 1) * PAIR].astype(F32)
        leave(qkv.at[at], o_qkv.at[at])
        proj[at, :] = w_proj[at, :].astype(F32)
        leave(proj.at[at], o_proj.at[at])
    for copy in leaving:
        copy.wait()


def per_device_fast(
    tokens, cotangent, ln1_gain, ln1_bias, qkv_weight, qv_bias, proj_weight, proj_bias,
    ln2_gain, ln2_bias, fc_weight, fc_bias, out_weight, out_bias,
):
    vmem, anywhere = pl.BlockSpec(memory_space=pltpu.VMEM), pl.BlockSpec(memory_space=pl.ANY)
    shape = jax.ShapeDtypeStruct
    layer, grad_in, grad_small, w_qkv, w_proj, w_fc, w_out = pl.pallas_call(
        layer_kernel,
        out_shape=(
            pltpu.VMEM((ROWS, WIDTH), BF),
            pltpu.VMEM((ROWS, WIDTH), BF),
            pltpu.VMEM((SMALL_ROWS, SHARD), F32),
            pltpu.VMEM((NC, SHARD, 3 * PAIR), BF),
            pltpu.VMEM((SHARD, WIDTH), BF),
            pltpu.VMEM((2, 2, SHARD, WIDTH), BF),
            pltpu.VMEM((FF // NB, WIDTH), BF),
        ),
        in_specs=[anywhere] * 14,
        out_specs=(vmem,) * 7,
        scratch_shapes=[pltpu.VMEM(*item) for item in SCRATCH.values()]
        + [
            pltpu.SemaphoreType.DMA((SENDS,)),
            pltpu.SemaphoreType.DMA((RECVS,)),
            pltpu.SemaphoreType.DMA((LOCALS,)),
        ],
        compiler_params=pltpu.CompilerParams(
            collective_id=0, has_side_effects=True, vmem_limit_bytes=LAYER_VMEM
        ),
    )(
        tokens.reshape(ROWS, WIDTH), cotangent.reshape(ROWS, WIDTH),
        ln1_gain, ln1_bias, qv_bias, proj_bias, ln2_gain, ln2_bias, fc_bias, out_bias,
        qkv_weight, proj_weight, fc_weight, out_weight,
    )
    layer, grad_in, w_qkv, w_proj, w_fc, w_out, *vectors = pl.pallas_call(
        widen_kernel,
        out_shape=(
            shape((ROWS, WIDTH), BF),
            shape((ROWS, WIDTH), BF),
            shape((SHARD, 3 * WIDTH), F32),
            shape((SHARD, WIDTH), F32),
            shape((SHARD, FF), F32),
            shape((FF // NB, WIDTH), F32),
            *[shape((n * SHARD,), F32) for n in VECTOR_ROWS],
        ),
        in_specs=[vmem] * 7,
        out_specs=(anywhere,) * (6 + len(VECTOR_ROWS)),
        scratch_shapes=[
            *[pltpu.VMEM((n * SHARD,), F32) for n in VECTOR_ROWS],
            pltpu.VMEM((SHARD, 3 * WIDTH), F32),
            pltpu.VMEM((SHARD, WIDTH), F32),
            pltpu.VMEM((SHARD, FF), F32),
            pltpu.VMEM((FF // NB, WIDTH), F32),
            pltpu.SemaphoreType.DMA((4 * PARTS + 2 + len(VECTOR_ROWS),)),
        ],
        compiler_params=pltpu.CompilerParams(vmem_limit_bytes=WIDEN_VMEM),
    )(layer, grad_in, grad_small, w_qkv, w_proj, w_fc, w_out)
    return (
        layer.reshape(tokens.shape),
        grad_in.reshape(tokens.shape),
        vectors[0],
        vectors[1],
        w_qkv,
        vectors[2],
        w_proj,
        vectors[3],
        vectors[4],
        vectors[5],
        w_fc,
        vectors[6],
        w_out,
        vectors[7],
    )


LAYER_VMEM, WIDEN_VMEM = 55 * 1024 * 1024, 20 * 1024 * 1024


def solution(mesh):
    placed = (
        P("batch", "ctx", None),
        P("batch", "ctx", None),
        P("batch"),
        P("batch"),
        P("batch", None),
        P("batch"),
        P("batch", None),
        P("batch"),
        P("batch"),
        P("batch"),
        P("batch", None),
        P("batch"),
        P("batch", None),
        P("batch"),
    )
    fits = dict(mesh.shape) == {"batch": NB, "ctx": NC}
    return jax.shard_map(
        per_device_fast if fits else per_device,
        mesh=mesh,
        in_specs=placed,
        out_specs=(
            P("batch", "ctx", None),
            P("batch", "ctx", None),
            P("batch"),
            P("batch"),
            P("batch", None),
            P("batch"),
            P("batch", None),
            P("batch"),
            P("batch"),
            P("batch"),
            P("batch", None),
            P("batch"),
            P("batch", None),
            P("batch"),
        ),
        check_vma=False,
    )
```

```python
from functools import partial
from types import SimpleNamespace

import jax
import jax.numpy as jnp
from jax import lax
from jax.experimental import pallas as pl
from jax.experimental.pallas import tpu as pltpu
from jax.sharding import PartitionSpec as P

HEADS = 16
HEAD_DIM = 64


epsilon = 1e-05
masked_value = -1e30


def shifted(block, axis, distance):
    devices = range(lax.axis_size(axis))
    route = [(i - distance, i) for i in devices if i - distance in devices]
    return lax.ppermute(block, axis, route)


def from_behind(block, axis, distance):
    devices = range(lax.axis_size(axis))
    route = [((i - distance) % len(devices), i) for i in devices]
    return lax.ppermute(block, axis, route)


def layer_norm(inputs, gain_vec, bias_vec):
    centre = inputs - jnp.mean(inputs, -1, keepdims=True)
    spread = jnp.mean(centre * centre, -1, keepdims=True)
    return centre * lax.rsqrt(spread + epsilon) * gain_vec + bias_vec


def keep_same(running):
    return running


def per_device(
    tokens,
    cotangent,
    ln1_gain,
    ln1_bias,
    qkv_weight,
    qv_bias,
    proj_weight,
    proj_bias,
    ln2_gain,
    ln2_bias,
    fc_weight,
    fc_bias,
    out_weight,
    out_bias,
):
    (
        gain_one,
        bias_one,
        weight_qkv,
        bias_qv,
        weight_proj,
        bias_proj,
        gain_two,
        bias_two,
        weight_fc,
        bias_fc,
        weight_out,
        bias_out,
    ) = (
        lax.all_gather(ln1_gain, "batch", axis=0, tiled=True),
        lax.all_gather(ln1_bias, "batch", axis=0, tiled=True),
        lax.all_gather(qkv_weight, "batch", axis=0, tiled=True),
        lax.all_gather(qv_bias, "batch", axis=0, tiled=True),
        lax.all_gather(proj_weight, "batch", axis=0, tiled=True),
        lax.all_gather(proj_bias, "batch", axis=0, tiled=True),
        lax.all_gather(ln2_gain, "batch", axis=0, tiled=True),
        lax.all_gather(ln2_bias, "batch", axis=0, tiled=True),
        lax.all_gather(fc_weight, "batch", axis=0, tiled=True),
        lax.all_gather(fc_bias, "batch", axis=0, tiled=True),
        lax.all_gather(out_weight, "batch", axis=0, tiled=True),
        lax.all_gather(out_bias, "batch", axis=0, tiled=True),
    )
    seq_count, ctx_rows, model_width = tokens.shape
    row_count = seq_count * ctx_rows
    inputs = tokens.astype(jnp.float32).reshape(row_count, model_width)
    norm_one, norm_one_pull = jax.vjp(
        layer_norm, inputs, gain_one.astype(jnp.float32), bias_one.astype(jnp.float32)
    )
    normed_low = norm_one.astype(jnp.bfloat16)
    bias_float = bias_qv.astype(jnp.float32)
    bias_full = jnp.concatenate(
        [bias_float[:model_width], jnp.zeros((model_width,), jnp.float32), bias_float[model_width:]]
    )
    mixed_proj = (
        jnp.dot(normed_low, weight_qkv, preferred_element_type=jnp.float32) + bias_full
    ).astype(jnp.bfloat16)
    query_flat = mixed_proj[:, :model_width].reshape(seq_count, ctx_rows, model_width)
    key_flat = mixed_proj[:, model_width : 2 * model_width].reshape(
        seq_count, ctx_rows, model_width
    )
    value_flat = mixed_proj[:, 2 * model_width :].reshape(seq_count, ctx_rows, model_width)
    query_heads = query_flat.reshape(seq_count, ctx_rows, HEADS, HEAD_DIM)
    own_index = lax.axis_index("ctx")
    position = own_index * ctx_rows
    query_pos = position + jnp.arange(ctx_rows, dtype=jnp.int32)
    last_pos = position + ctx_rows - 1
    start_state = (
        jnp.full((seq_count, ctx_rows, HEADS), masked_value, jnp.float32),
        jnp.zeros((seq_count, ctx_rows, HEADS), jnp.float32),
        jnp.zeros((seq_count, ctx_rows, HEADS, HEAD_DIM), jnp.float32),
    )
    key_piece = lax.all_gather(key_flat, "ctx", axis=1, tiled=True)
    value_piece = lax.all_gather(value_flat, "ctx", axis=1, tiled=True)
    piece_rows = key_piece.shape[1]

    def compute(running):
        run_max, run_sum, accum = running
        key_split = key_piece.reshape(seq_count, piece_rows, HEADS, HEAD_DIM)
        value_split = value_piece.reshape(seq_count, piece_rows, HEADS, HEAD_DIM)
        scores = (
            jnp.einsum(
                "bqhd,bkhd->bqhk", query_heads, key_split, preferred_element_type=jnp.float32
            )
            * 0.125
        )
        key_pos = jnp.arange(piece_rows, dtype=jnp.int32)
        allowed = (key_pos[None, :] <= query_pos[:, None])[None, :, None, :]
        scores = jnp.where(allowed, scores, masked_value)
        new_max = jnp.maximum(run_max, jnp.max(scores, -1))
        weights_exp = jnp.where(allowed, jnp.exp(scores - new_max[..., None]), 0.0)
        new_sum = jnp.sum(weights_exp, -1)
        product = jnp.einsum(
            "bqhk,bkhd->bqhd",
            weights_exp.astype(jnp.bfloat16),
            value_split,
            preferred_element_type=jnp.float32,
        )
        return (new_max, new_sum, product)

    run_max, run_sum, accum = lax.cond(jnp.int32(0) <= last_pos, compute, keep_same, start_state)
    log_total = run_max + jnp.log(run_sum)
    attended = accum / run_sum[..., None]
    attended_low = attended.reshape(row_count, model_width).astype(jnp.bfloat16)
    middle = (
        inputs
        + jnp.dot(attended_low, weight_proj, preferred_element_type=jnp.float32)
        + bias_proj.astype(jnp.float32)
    )
    norm_two, norm_two_pull = jax.vjp(
        layer_norm, middle, gain_two.astype(jnp.float32), bias_two.astype(jnp.float32)
    )
    normed_two = norm_two.astype(jnp.bfloat16)
    pre_act = jnp.dot(normed_two, weight_fc, preferred_element_type=jnp.float32) + bias_fc.astype(
        jnp.float32
    )
    activated, gelu_pull = jax.vjp(partial(jax.nn.gelu, approximate=True), pre_act)
    hidden_low = activated.astype(jnp.bfloat16)
    output = (
        middle
        + jnp.dot(hidden_low, weight_out, preferred_element_type=jnp.float32)
        + bias_out.astype(jnp.float32)
    )
    layer_out = output.astype(jnp.bfloat16).reshape(tokens.shape)
    grad_out = cotangent.reshape(row_count, model_width)
    grad_out_float = grad_out.astype(jnp.float32)
    grad_w_out = jnp.einsum("rf,rd->fd", hidden_low, grad_out, preferred_element_type=jnp.float32)
    grad_b_out = jnp.sum(grad_out_float, 0)
    grad_hidden = jnp.einsum("rd,fd->rf", grad_out, weight_out, preferred_element_type=jnp.float32)
    (grad_pre,) = gelu_pull(grad_hidden)
    grad_pre_low = grad_pre.astype(jnp.bfloat16)
    grad_w_fc = jnp.einsum(
        "rd,rf->df", normed_two, grad_pre_low, preferred_element_type=jnp.float32
    )
    grad_b_fc = jnp.sum(grad_pre_low.astype(jnp.float32), 0)
    grad_norm_two = jnp.einsum(
        "rf,df->rd", grad_pre_low, weight_fc, preferred_element_type=jnp.float32
    )
    grad_mid_norm, grad_g_two, grad_b_two = norm_two_pull(grad_norm_two)
    grad_middle = grad_out_float + grad_mid_norm
    grad_branch = grad_middle.astype(jnp.bfloat16)
    grad_w_proj = jnp.einsum(
        "rd,re->de", attended_low, grad_branch, preferred_element_type=jnp.float32
    )
    grad_b_proj = jnp.sum(grad_branch.astype(jnp.float32), 0)
    grad_attended = jnp.einsum(
        "re,de->rd", grad_branch, weight_proj, preferred_element_type=jnp.float32
    ).astype(jnp.bfloat16)
    grad_att_flat = grad_attended.reshape(seq_count, ctx_rows, model_width)
    grad_att_heads = grad_att_flat.reshape(seq_count, ctx_rows, HEADS, HEAD_DIM)
    delta_mine = jnp.sum(grad_att_heads.astype(jnp.float32) * attended, -1)
    zero_heads = jnp.zeros((seq_count, ctx_rows, HEADS, HEAD_DIM), jnp.float32)
    cycle_count = lax.axis_size("ctx")

    def cycle_turn(turn, state):
        owner = (own_index - turn) % cycle_count
        first_row = owner * ctx_rows

        def visit(inner):
            key_piece, value_piece, grad_k, grad_v, grad_q = inner
            key_split = key_piece.reshape(seq_count, ctx_rows, HEADS, HEAD_DIM)
            value_split = value_piece.reshape(seq_count, ctx_rows, HEADS, HEAD_DIM)
            piece_pos = first_row + jnp.arange(ctx_rows, dtype=jnp.int32)
            scores = (
                jnp.einsum(
                    "bqhd,bkhd->bqhk", query_heads, key_split, preferred_element_type=jnp.float32
                )
                * 0.125
            )
            allowed = (piece_pos[None, :] <= query_pos[:, None])[None, :, None, :]
            probs = jnp.where(allowed, jnp.exp(scores - log_total[..., None]), 0.0)
            grad_probs = jnp.einsum(
                "bqhd,bkhd->bqhk", grad_att_heads, value_split, preferred_element_type=jnp.float32
            )
            grad_scores = (probs * (grad_probs - delta_mine[..., None])).astype(jnp.bfloat16)
            grad_q = (
                grad_q
                + jnp.einsum(
                    "bqhk,bkhd->bqhd", grad_scores, key_split, preferred_element_type=jnp.float32
                )
                * 0.125
            )
            grad_k = (
                grad_k
                + jnp.einsum(
                    "bqhk,bqhd->bkhd", grad_scores, query_heads, preferred_element_type=jnp.float32
                )
                * 0.125
            )
            grad_v = grad_v + jnp.einsum(
                "bqhk,bqhd->bkhd",
                probs.astype(jnp.bfloat16),
                grad_att_heads,
                preferred_element_type=jnp.float32,
            )
            return (key_piece, value_piece, grad_k, grad_v, grad_q)

        key_piece, value_piece, grad_k, grad_v, grad_q = lax.cond(
            owner <= own_index, visit, keep_same, state
        )
        key_piece, value_piece = shifted((key_piece, value_piece), "ctx", 1)
        grad_k, grad_v = (
            from_behind(grad_k.astype(jnp.bfloat16), "ctx", 1).astype(grad_k.dtype),
            from_behind(grad_v.astype(jnp.bfloat16), "ctx", 1).astype(grad_v.dtype),
        )
        return (key_piece, value_piece, grad_k, grad_v, grad_q)

    cycle_state = lax.fori_loop(
        0, cycle_count, cycle_turn, (key_flat, value_flat, zero_heads, zero_heads, zero_heads)
    )
    grad_k, grad_v, grad_q = (cycle_state[2], cycle_state[3], cycle_state[4])
    grad_mixed = jnp.concatenate(
        [
            grad_q.reshape(row_count, model_width),
            grad_k.reshape(row_count, model_width),
            grad_v.reshape(row_count, model_width),
        ],
        axis=1,
    ).astype(jnp.bfloat16)
    grad_w_qkv = jnp.einsum("rd,re->de", normed_low, grad_mixed, preferred_element_type=jnp.float32)
    grad_bias_all = jnp.sum(grad_mixed.astype(jnp.float32), 0)
    grad_b_qv = jnp.concatenate([grad_bias_all[:model_width], grad_bias_all[2 * model_width :]])
    grad_norm_one = jnp.einsum(
        "re,de->rd", grad_mixed, weight_qkv, preferred_element_type=jnp.float32
    )
    grad_in_norm, grad_g_one, grad_b_one = norm_one_pull(grad_norm_one)
    grad_tokens = (grad_middle + grad_in_norm).astype(jnp.bfloat16).reshape(tokens.shape)
    local_grads = (
        grad_g_one,
        grad_b_one,
        grad_w_qkv,
        grad_b_qv,
        grad_w_proj,
        grad_b_proj,
        grad_g_two,
        grad_b_two,
        grad_w_fc,
        grad_b_fc,
        grad_w_out,
        grad_b_out,
    )
    partial_grads = (
        lax.psum_scatter(
            local_grads[0].astype(jnp.bfloat16), "batch", scatter_dimension=0, tiled=True
        ).astype(jnp.float32),
        lax.psum_scatter(
            local_grads[1].astype(jnp.bfloat16), "batch", scatter_dimension=0, tiled=True
        ).astype(jnp.float32),
        lax.psum_scatter(
            local_grads[2].astype(jnp.bfloat16), "batch", scatter_dimension=0, tiled=True
        ).astype(jnp.float32),
        lax.psum_scatter(
            local_grads[3].astype(jnp.bfloat16), "batch", scatter_dimension=0, tiled=True
        ).astype(jnp.float32),
        lax.psum_scatter(
            local_grads[4].astype(jnp.bfloat16), "batch", scatter_dimension=0, tiled=True
        ).astype(jnp.float32),
        lax.psum_scatter(
            local_grads[5].astype(jnp.bfloat16), "batch", scatter_dimension=0, tiled=True
        ).astype(jnp.float32),
        lax.psum_scatter(
            local_grads[6].astype(jnp.bfloat16), "batch", scatter_dimension=0, tiled=True
        ).astype(jnp.float32),
        lax.psum_scatter(
            local_grads[7].astype(jnp.bfloat16), "batch", scatter_dimension=0, tiled=True
        ).astype(jnp.float32),
        lax.psum_scatter(
            local_grads[8].astype(jnp.bfloat16), "batch", scatter_dimension=0, tiled=True
        ).astype(jnp.float32),
        lax.psum_scatter(
            local_grads[9].astype(jnp.bfloat16), "batch", scatter_dimension=0, tiled=True
        ).astype(jnp.float32),
        lax.psum_scatter(
            local_grads[10].astype(jnp.bfloat16), "batch", scatter_dimension=0, tiled=True
        ).astype(jnp.float32),
        lax.psum_scatter(
            local_grads[11].astype(jnp.bfloat16), "batch", scatter_dimension=0, tiled=True
        ).astype(jnp.float32),
    )
    summed_grads = lax.psum(
        (
            partial_grads[0],
            partial_grads[1],
            partial_grads[2],
            partial_grads[3],
            partial_grads[4],
            partial_grads[5],
            partial_grads[6],
            partial_grads[7],
            partial_grads[8],
            partial_grads[9],
            partial_grads[10],
            partial_grads[11],
        ),
        "ctx",
    )
    return (
        layer_out,
        grad_tokens,
        summed_grads[0],
        summed_grads[1],
        summed_grads[2],
        summed_grads[3],
        summed_grads[4],
        summed_grads[5],
        summed_grads[6],
        summed_grads[7],
        summed_grads[8],
        summed_grads[9],
        summed_grads[10],
        summed_grads[11],
    )


BF, F32 = jnp.bfloat16, jnp.float32
NN = (((1,), (0,)), ((), ()))
NT = (((1,), (1,)), ((), ()))
TN = (((0,), (0,)), ((), ()))
MESH = pl.DeviceIdType.MESH
NB, NC, WIDTH, ROWS, FF, PAIR = 4, 8, 1024, 128, 4096, 128
SHARD = WIDTH // NB
LENGTH = ROWS * NC
SMALL_ROWS = 16


def mm(left, right, dims=NN):
    return lax.dot_general(left, right, dims, preferred_element_type=F32)


def run(when, action):
    if when is None:
        action()
    else:
        pl.when(when)(action)


def both(one, two):
    return two if one is None else (one if two is None else jnp.logical_and(one, two))


class Net:
    def __init__(self, b, c, send_sems, recv_sems):
        self.b, self.c, self.z, self.x = b, c, c // 2, c % 2
        self.side = c + 1 - 2 * self.x
        self.core = b % 2
        self.sib = b + 1 - 2 * self.core
        self.across = lax.rem(b + 2, NB)
        self.diag = lax.rem(self.sib + 2, NB)
        self.send_sems, self.recv_sems = send_sems, recv_sems
        self.taken, self.pending = 0, []

    def slots(self, count):
        base = self.taken
        self.taken += count
        assert self.taken <= self.recv_sems.shape[0]
        return base

    def send(self, src, dst, device, slot, when=None):
        index = len(self.pending)
        if index == self.send_sems.shape[0]:
            done, copy, index = self.pending.pop(0)
            run(done, copy.wait_send)
        copy = pltpu.make_async_remote_copy(
            src_ref=src,
            dst_ref=dst,
            send_sem=self.send_sems.at[index],
            recv_sem=self.recv_sems.at[slot],
            device_id=device,
            device_id_type=MESH,
        )
        run(when, copy.start)
        self.pending.append((when, copy, index))

    def wait(self, slot, ref):
        pltpu.make_async_remote_copy(
            src_ref=ref,
            dst_ref=ref,
            send_sem=self.send_sems.at[0],
            recv_sem=self.recv_sems.at[slot],
            device_id=(self.sib, self.c),
            device_id_type=MESH,
        ).wait_recv()

    def drain(self):
        for when, copy, _ in self.pending:
            run(when, copy.wait_send)


class GatherCtx:
    def __init__(self, net, views, others, count, turn=False):
        self.net, self.views, self.others, self.count, self.turn = net, views, others, count, turn
        self.along, self.beside = net.slots(4 * count), net.slots(1)
        self.turned = net.slots(4) if turn else None

    def begin(self, i, src):
        net, count = self.net, self.count
        dst, at = self.views(net.c)[i], net.z * count + i
        if self.turn and i == count - 1:
            end = jnp.logical_or(net.z == 0, net.z == 3)
            net.send(src, dst, (net.b, net.side), self.turned + 2, net.z == 0)
            net.send(src, dst, (net.b, net.side), self.turned + 3, net.z == 3)
            net.send(src, dst, (net.b, net.side), self.beside, jnp.logical_not(end))
        else:
            net.send(src, dst, (net.b, net.side), self.beside)
        net.send(src, dst, (net.b, net.c + 2), self.along + at, net.z < 3)
        net.send(src, dst, (net.b, net.c - 2), self.along + at, net.z > 0)

    def start(self, srcs):
        for i, src in enumerate(srcs):
            self.begin(i, src)

    def stage(self, d, sign):
        net, count = self.net, self.count
        zz = net.z + sign * d
        here = zz >= 0 if sign < 0 else zz <= 3
        refs = self.views(2 * zz + net.x)
        onward = both(here, net.z < 3 if sign < 0 else net.z > 0)
        for i in range(count):
            slot = self.along + zz * count + i
            pl.when(here)(lambda slot=slot, ref=refs[i]: net.wait(slot, ref))
            if d < 3:
                net.send(refs[i], refs[i], (net.b, net.c - 2 * sign), slot, onward)
            goes = here
            if self.turn and i == count - 1:
                goes = both(here, jnp.logical_and(zz > 0, zz < 3))
            net.send(refs[i], refs[i], (net.b, net.side), self.beside, goes)

    def piece(self, end):
        return self.views(2 * end + 1 - self.net.x)[self.count - 1]

    def corner(self):
        net = self.net
        for end, step in ((0, 2), (3, -2)):
            ref, slot = self.piece(end), self.turned + 2 + (end > 0)
            pl.when(net.z == end)(lambda slot=slot, ref=ref: net.wait(slot, ref))
            net.send(ref, ref, (net.b, net.c + step), self.turned + (end > 0), net.z == end)

    def pass_on(self, d):
        net = self.net
        for end, step in ((0, 2), (3, -2)):
            here = net.z == (end + d if end == 0 else end - d)
            ref, slot = self.piece(end), self.turned + (end > 0)
            pl.when(here)(lambda slot=slot, ref=ref: net.wait(slot, ref))
            if d < 3:
                net.send(ref, ref, (net.b, net.c + step), slot, here)

    def finish(self):
        self.net.wait(self.beside, self.others)


def chunks(ref):
    if len(ref.shape) == 3:
        return ref.shape[0], lambda i: (i,)
    rows = min(32, ref.shape[0])
    return ref.shape[0] // rows, lambda i: (pl.ds(pl.multiple_of(i * rows, rows), rows),)


def add_into(target, terms, dtype=BF):
    count, at = chunks(target)

    def body(i, carry):
        total = terms[0][at(i)].astype(F32)
        for term in terms[1:]:
            total = total + term[at(i)].astype(F32)
        target[at(i)] = total.astype(dtype)
        return carry

    lax.fori_loop(0, count, body, 0)


class ReduceLine:
    def __init__(self, net, mine, up, down):
        self.net, self.mine, self.up, self.down = net, mine, up, down
        self.s_up, self.s_down = net.slots(4), net.slots(4)

    def give(self, k, upward, when):
        net = self.net
        if upward:
            net.send(self.mine(k), self.up.at[k], (net.b, net.c + 2), self.s_up + k, when)
        else:
            net.send(self.mine(k), self.down.at[k], (net.b, net.c - 2), self.s_down + k, when)

    def take(self, k, upward, when):
        box, slot = (self.up, self.s_up) if upward else (self.down, self.s_down)
        mine = self.mine(k)

        @pl.when(when)
        def _():
            self.net.wait(slot + k, box.at[k])
            add_into(mine, [mine, box.at[k]])

        self.give(k, upward, when)

    def launch(self, k):
        self.give(3 - k, True, self.net.z == 0)
        self.give(k, False, self.net.z == 3)

    def pass_one(self, k):
        self.take(3 - k, True, self.net.z == 1)
        self.take(k, False, self.net.z == 2)

    def pass_two(self):
        self.take(0, False, self.net.z == 1)
        self.take(3, True, self.net.z == 2)

    def finish(self, target):
        net, z = self.net, self.net.z
        mine = self.mine(z)

        @pl.when(z >= 1)
        def _():
            net.wait(self.s_up + z, self.up.at[z])

        @pl.when(z <= 2)
        def _():
            net.wait(self.s_down + z, self.down.at[z])

        pl.when(z == 0)(lambda: add_into(target, [mine, self.down.at[z]]))
        pl.when(z == 3)(lambda: add_into(target, [mine, self.up.at[z]]))
        pl.when(jnp.logical_and(z > 0, z < 3))(
            lambda: add_into(target, [mine, self.up.at[z], self.down.at[z]])
        )


class ReduceCtx:
    def __init__(self, net, mine, beside, up, down):
        self.net, self.mine, self.beside = net, mine, beside
        self.slots = net.slots(4)
        self.line = ReduceLine(net, lambda k: mine(2 * k + net.x), up, down)

    def start(self):
        net = self.net
        for k in (3, 0, 2, 1):
            net.send(self.mine(2 * k + 1 - net.x), self.beside.at[k], (net.b, net.side), self.slots + k)

    def fold(self):
        for k in (3, 0, 2, 1):
            self.net.wait(self.slots + k, self.beside.at[k])
            mine = self.line.mine(k)
            add_into(mine, [mine, self.beside.at[k]])


class SwapCtx:
    def __init__(self, net, src, dst, others):
        self.net, self.src, self.dst, self.others = net, src, dst, others
        self.slot = net.slots(1)

    def give(self, j):
        net, src, dst = self.net, self.src(j), self.dst(self.net.c)
        net.send(src, dst, (net.b, j), self.slot, net.c != j)

        @pl.when(net.c == j)
        def _():
            dst[...] = src[...]

    def start(self):
        for j in range(NC):
            self.give(j)

    def finish(self):
        self.net.wait(self.slot, self.others)


class GatherBatch:
    def __init__(self, net, views, count=1):
        self.net, self.views, self.count = net, views, count
        self.base = net.slots(NB * count)

    def start(self, srcs):
        net = self.net
        dsts = self.views(net.b)
        for i in range(self.count):
            slot = self.base + net.b * self.count + i
            net.send(srcs[i], dsts[i], (net.across, net.c), slot)
        for i in range(self.count):
            slot = self.base + net.b * self.count + i
            net.send(srcs[i], dsts[i], (net.sib, net.c), slot)

    def relay(self):
        net = self.net
        refs = self.views(net.across)
        for i in range(self.count):
            slot = self.base + net.across * self.count + i
            net.wait(slot, refs[i])
            net.send(refs[i], refs[i], (net.sib, net.c), slot)

    def take(self, j):
        refs = self.views(j)
        for i in range(self.count):
            self.net.wait(self.base + j * self.count + i, refs[i])

    def near(self):
        self.take(self.net.sib)

    def far(self):
        self.take(self.net.diag)

    def finish(self):
        self.near()
        self.far()


class ReduceBatch:
    def __init__(self, net, mine, boxes):
        self.net, self.mine, self.boxes = net, mine, boxes
        self.base = net.slots(3)

    def give(self):
        net = self.net
        net.send(self.mine(net.diag), self.boxes.at[0], (net.sib, net.c), self.base)

    def cross(self):
        net = self.net
        net.wait(self.base, self.boxes.at[0])
        block = self.mine(net.across)
        add_into(block, [block, self.boxes.at[0]])
        net.send(block, self.boxes.at[1], (net.across, net.c), self.base + 1)

    def keep(self):
        net = self.net
        net.send(self.mine(net.sib), self.boxes.at[2], (net.sib, net.c), self.base + 2)

    def finish(self):
        net = self.net
        net.wait(self.base + 2, self.boxes.at[2])
        net.wait(self.base + 1, self.boxes.at[1])
        return [self.mine(net.b), self.boxes.at[1], self.boxes.at[2]]


def row_of(parts, index):
    return jnp.concatenate([parts[j, index : index + 1, :] for j in range(NB)], axis=1)


def put_row(target, index, row):
    for j in range(NB):
        target[j, index : index + 1, :] = row[:, j * SHARD : (j + 1) * SHARD]


def rows_of(block, size):
    return lambda j: block.at[pl.ds(pl.multiple_of(j * size, size), size)]


def normalise(inputs):
    centre = inputs - jnp.mean(inputs, -1, keepdims=True)
    spread = jnp.mean(centre * centre, -1, keepdims=True)
    scale = lax.rsqrt(spread + epsilon)
    return centre * scale, scale


def head_lanes(h, rows):
    lane = lax.broadcasted_iota(jnp.int32, (rows, PAIR), 1)
    return (lane >= h * HEAD_DIM) & (lane < (h + 1) * HEAD_DIM)


QB = 256


def scores_of(keys, query, masked):
    scores = mm(keys, query, NT) * 0.125
    if masked:
        key_pos = lax.broadcasted_iota(jnp.int32, scores.shape, 0)
        query_pos = lax.broadcasted_iota(jnp.int32, scores.shape, 1)
        scores = jnp.where(key_pos <= query_pos, scores, masked_value)
    return scores


def attend(mix, value_t, att, lse, work, low_work, ready):
    value_t[...] = mix[:, 2 * PAIR :].astype(F32).T.astype(BF)
    for qb in reversed(range(LENGTH // QB)):
        here = slice(qb * QB, (qb + 1) * QB)
        outs = []
        for h in range(2):
            query = jnp.where(head_lanes(h, QB), mix[here, :PAIR], jnp.zeros((), BF))
            top = None
            for kb in range(qb + 1):
                keys = slice(kb * QB, (kb + 1) * QB)
                scores = scores_of(mix[keys, PAIR : 2 * PAIR], query, kb == qb)
                work[keys, :] = scores
                peak = jnp.max(scores, axis=0, keepdims=True)
                top = peak if top is None else jnp.maximum(top, peak)
            total = None
            for kb in range(qb + 1):
                keys = slice(kb * QB, (kb + 1) * QB)
                grown = jnp.exp(work[keys, :] - top)
                part = jnp.sum(grown, axis=0, keepdims=True)
                total = part if total is None else total + part
                low_work[h, keys, :] = grown.astype(BF)
            count = (qb + 1) * QB
            lanes = slice(h * HEAD_DIM, (h + 1) * HEAD_DIM)
            out = mm(value_t[lanes, :count], low_work[h, :count, :])
            outs.append(out / total)
            lse[h * 4 + qb : h * 4 + qb + 1, :] = top + jnp.log(total)
        att[here, :] = jnp.concatenate(outs, axis=0).T.astype(BF)
        ready(qb)


def attend_back(mix, key_t, dout, lse, gmix, grad_k, grad_v, work, more, low_work, low_more):
    key_t[...] = mix[:, PAIR : 2 * PAIR].astype(F32).T.astype(BF)
    grad_k[...] = jnp.zeros_like(grad_k)
    grad_v[...] = jnp.zeros_like(grad_v)
    for qb in reversed(range(LENGTH // QB)):
        here = slice(qb * QB, (qb + 1) * QB)
        outs = []
        count = (qb + 1) * QB
        for h in range(2):
            lanes = head_lanes(h, QB)
            query = jnp.where(lanes, mix[here, :PAIR], jnp.zeros((), BF))
            grad = jnp.where(lanes, dout[here, :], jnp.zeros((), BF))
            level = lse[h * 4 + qb : h * 4 + qb + 1, :]
            delta = None
            for kb in range(qb + 1):
                keys = slice(kb * QB, (kb + 1) * QB)
                probs = jnp.exp(scores_of(mix[keys, PAIR : 2 * PAIR], query, kb == qb) - level)
                grad_probs = mm(mix[keys, 2 * PAIR :], grad, NT)
                part = jnp.sum(probs * grad_probs, axis=0, keepdims=True)
                delta = part if delta is None else delta + part
                work[keys, :] = probs
                more[keys, :] = grad_probs
                low_work[h, keys, :] = probs.astype(BF)
            for kb in range(qb + 1):
                keys = slice(kb * QB, (kb + 1) * QB)
                low_more[h, keys, :] = (work[keys, :] * (more[keys, :] - delta)).astype(BF)
            grad_v[:count, :] += mm(low_work[h, :count, :], grad)
            grad_k[:count, :] += mm(low_more[h, :count, :], query)
            rows = slice(h * HEAD_DIM, (h + 1) * HEAD_DIM)
            outs.append(mm(key_t[rows, :count], low_more[h, :count, :]) * 0.125)
        gmix[here, :PAIR] = jnp.concatenate(outs, axis=0).T.astype(BF)
        gmix[here, PAIR : 2 * PAIR] = (grad_k[here, :] * 0.125).astype(BF)
        gmix[here, 2 * PAIR :] = grad_v[here, :].astype(BF)


gelu_scale = 0.7978845608028654
gelu_cubic = 0.044715


def gelu_pair(x):
    square = x * x
    bent = jnp.tanh(gelu_scale * x * (1.0 + gelu_cubic * square))
    half = 0.5 * (1.0 + bent)
    slope = half + 0.5 * x * (1.0 - bent * bent) * (gelu_scale * (1.0 + 3.0 * gelu_cubic * square))
    return x * half, slope


VECTOR_ROWS = (1, 1, 2, 1, 1, 1, 4, 1)
SCRATCH = dict(
    tokens=((ROWS, WIDTH), BF),
    **{f"v{i}": ((rows * SHARD,), BF) for i, rows in enumerate(VECTOR_ROWS)},
    small=((SMALL_ROWS, SHARD), F32),
    parts=((NB, SMALL_ROWS, SHARD), F32),
    qv_rows=((16, PAIR), F32),
    wpair=((WIDTH, 3 * PAIR), BF),
    wfull=((WIDTH, 3 * WIDTH), BF),
    wproj_all=((WIDTH, WIDTH), BF),
    wfc_mine=((WIDTH, WIDTH), BF),
    wout_mine=((WIDTH, WIDTH), BF),
    g_all=((NB * ROWS, WIDTH), BF),
    hat_one=((ROWS, WIDTH), F32),
    scale_one=((ROWS, 1), F32),
    hat_all=((LENGTH, WIDTH), BF),
    n_one=((LENGTH, WIDTH), BF),
    mix=((LENGTH, 3 * PAIR), BF),
    turned=((PAIR, LENGTH), BF),
    att=((LENGTH, PAIR), BF),
    lse=((8, QB), F32),
    work=((LENGTH, QB), F32),
    more=((LENGTH, QB), F32),
    low_work=((2, LENGTH, QB), BF),
    low_more=((2, LENGTH, QB), BF),
    att_own=((ROWS, WIDTH), BF),
    middle=((ROWS, WIDTH), F32),
    hat_two=((ROWS, WIDTH), F32),
    scale_two=((ROWS, 1), F32),
    n_two=((NB * ROWS, WIDTH), BF),
    hidden=((NB * ROWS, WIDTH), BF),
    grad_pre=((NB * ROWS, WIDTH), BF),
    p_norm=((NB * ROWS, WIDTH), BF),
    p_norm_box=((3, ROWS, WIDTH), BF),
    p_layer=((NB * ROWS, WIDTH), BF),
    p_layer_box=((3, ROWS, WIDTH), BF),
    g_side=((NB * ROWS, WIDTH), BF),
    n_side=((NB * ROWS, WIDTH), BF),
    hidden_side=((NB * ROWS, WIDTH // 2), BF),
    pre_side=((NB * ROWS, WIDTH // 2), BF),
    p_out=((2, 256, WIDTH), BF),
    out_up=((2, 4, 64, WIDTH), BF),
    out_down=((2, 4, 64, WIDTH), BF),
    out_block=((ROWS, WIDTH), BF),
    p_fc=((2, NB, 4, 64, 256), BF),
    fc_up=((2, 4, NB, 64, 256), BF),
    fc_down=((2, 4, NB, 64, 256), BF),
    fc_sum=((2, NB, 64, 256), BF),
    fc_block=((2, 64, WIDTH), BF),
    p_proj=((WIDTH, WIDTH), BF),
    p_proj_box=((3, SHARD, WIDTH), BF),
    proj_sum=((SHARD, WIDTH), BF),
    proj_beside=((4, 32, WIDTH), BF),
    proj_up=((4, 32, WIDTH), BF),
    proj_down=((4, 32, WIDTH), BF),
    proj_block=((32, WIDTH), BF),
    grad_middle=((ROWS, WIDTH), F32),
    branch=((ROWS, WIDTH), BF),
    g_att=((ROWS, WIDTH), BF),
    dout=((LENGTH, PAIR), BF),
    gmix=((LENGTH, 3 * PAIR), BF),
    grad_k=((LENGTH, PAIR), F32),
    grad_v=((LENGTH, PAIR), F32),
    gmix_own=((NC, ROWS, 3 * PAIR), BF),
    gmix_all=((ROWS, 3 * WIDTH), BF),
    p_qkv=((WIDTH, 3 * PAIR), BF),
    p_qkv_box=((3, SHARD, 3 * PAIR), BF),
    qkv_block=((SHARD, 3 * PAIR), BF),
    gn_one=((ROWS, WIDTH), F32),
    gs=((NB, SMALL_ROWS, SHARD), F32),
    gqv=((16, PAIR), F32),
    gs_box=((NB, SMALL_ROWS, SHARD), F32),
    gs_sum=((SMALL_ROWS, SHARD), F32),
    gs_far=((NC, SMALL_ROWS, SHARD), F32),
)
SENDS, RECVS, LOCALS = 40, 180, 26


def layer_kernel(*refs):
    tokens, cotangent = refs[:2]
    vectors = refs[2:10]
    wqkv, wproj, wfc, wout = refs[10:14]
    layer_out, grad_tokens, grad_small, o_qkv, o_proj, o_fc, o_out = refs[14:21]
    scratch = refs[21:]
    s = SimpleNamespace(**dict(zip(SCRATCH, scratch)))
    send_sems, recv_sems, local_sems = scratch[len(SCRATCH) :]
    b, c = lax.axis_index("batch"), lax.axis_index("ctx")
    net = Net(b, c, send_sems, recv_sems)
    v = SimpleNamespace(keep=[])
    locals_open = []

    def local(src, dst):
        copy = pltpu.make_async_copy(src, dst, local_sems.at[len(locals_open)])
        copy.start()
        locals_open.append(copy)
        return copy

    def own(ref, size):
        return rows_of(ref, size)(b)

    def cols(ref, start, count=PAIR):
        return ref.at[:, pl.ds(pl.multiple_of(start, 128), count)]

    def halves(ref, size, j):
        block = rows_of(ref, size)(j)
        return [block.at[0 : size // 2], block.at[size // 2 : size]]

    def loop(count, size, body):
        def step(i, carry):
            body(pl.ds(pl.multiple_of(i * size, size), size))
            return carry

        lax.fori_loop(0, count, step, 0)

    batch_others = [lax.rem(b + i, NB) for i in range(1, NB)]

    small_slot, fc_slots, fc_side_slots = net.slots(1), net.slots(2 * NB), net.slots(NB)
    hidden_slots, pre_slots, side_slot, swap_slots = net.slots(4), net.slots(4), net.slots(2), net.slots(2)
    proj_slots, proj_side_slot, proj_near_slots = net.slots(NB), net.slots(1), net.slots(2)
    gs_slot, far_slot = net.slots(1), net.slots(1)
    gather_pair = GatherBatch(net, lambda j: [rows_of(s.wpair, SHARD)(j)])
    gather_one = GatherCtx(net, lambda j: halves(s.hat_all, ROWS, j), s.hat_all.at[: 3 * ROWS], 2, True)
    gather_g = GatherBatch(net, lambda j: [rows_of(s.g_all, ROWS)(j)])
    gather_gs = GatherBatch(net, lambda j: [rows_of(s.g_side, ROWS)(j)])
    gather_ns = GatherBatch(net, lambda j: [rows_of(s.n_side, ROWS)(j)])
    gather_two = GatherBatch(net, lambda j: halves(s.n_two, ROWS, j), 2)
    gather_full = [
        GatherBatch(net, lambda j, i=i: [rows_of(s.wfull, SHARD // 2)(2 * j + i)]) for i in range(2)
    ]
    swap_att = SwapCtx(
        net, rows_of(s.att, ROWS), lambda j: cols(s.att_own, j * PAIR), s.att_own.at[:, : 7 * PAIR]
    )
    swap_grad = SwapCtx(
        net, lambda j: cols(s.g_att, j * PAIR), rows_of(s.dout, ROWS), s.dout.at[: 7 * ROWS]
    )
    swap_mix = SwapCtx(
        net, rows_of(s.gmix, ROWS), lambda j: s.gmix_own.at[j], s.gmix_own.at[:7]
    )
    reduce_norm = ReduceBatch(net, rows_of(s.p_norm, ROWS), s.p_norm_box)
    reduce_layer = ReduceBatch(net, rows_of(s.p_layer, ROWS), s.p_layer_box)
    reduce_proj = ReduceBatch(net, rows_of(s.p_proj, SHARD), s.p_proj_box)
    reduce_qkv = ReduceBatch(net, rows_of(s.p_qkv, SHARD), s.p_qkv_box)
    reduce_part = ReduceCtx(net, rows_of(s.proj_sum, 32), s.proj_beside, s.proj_up, s.proj_down)
    reduce_out = [
        ReduceLine(net, rows_of(s.p_out.at[i], 64), s.out_up.at[i], s.out_down.at[i]) for i in range(2)
    ]
    reduce_fc = [
        ReduceLine(net, lambda k, i=i: s.p_fc.at[i, :, k], s.fc_up.at[i], s.fc_down.at[i])
        for i in range(2)
    ]

    def out_view(i, j):
        return rows_of(o_out, 64)(8 * (j % 2) + 4 * i + j // 2)

    def fc_view(i, j):
        return o_fc.at[j % 2, i, pl.ds(pl.multiple_of((j // 2) * 64, 64), 64)]

    gather_out = [GatherCtx(net, lambda j, i=i: [out_view(i, j)], o_out.at[:256], 1) for i in range(2)]
    gather_fc = [GatherCtx(net, lambda j, i=i: [fc_view(i, j)], o_fc.at[0, 0, : 256 - 128 * i], 1, i == 1) for i in range(2)]
    gather_qkv = GatherCtx(net, lambda j: halves(o_qkv.at[j], SHARD, 0), o_qkv.at[:3], 2, True)
    gather_part = GatherCtx(net, lambda j: [rows_of(o_proj, 32)(j)], o_proj.at[:128], 1)

    scale, hat = s.scale_one, s.hat_one
    half, pair_z = net.z % 2, (b, c + 2 - 4 * (net.z % 2))
    fc_rows = [
        pl.ds(pl.multiple_of(SHARD // 2 + x * (SHARD // 4), SHARD // 4), SHARD // 4) for x in (half, 1 - half)
    ]
    side_rows = pl.ds(pl.multiple_of(half * (SHARD // 2), SHARD // 2), SHARD // 2)
    other_side_rows = pl.ds(pl.multiple_of((1 - half) * (SHARD // 2), SHARD // 2), SHARD // 2)
    chip_rows = [
        pl.ds(pl.multiple_of(first * 256, 256), 256) for first in (b // 2, 1 - b // 2)
    ]
    hat_mine = rows_of(s.hat_all, ROWS)(c)
    n_two_mine = own(s.n_two, ROWS)
    g_mine = own(s.g_all, ROWS)
    n_beside = own(s.n_side, ROWS)

    def enter():
        barrier = pltpu.get_barrier_semaphore()
        others = [(j, c) for j in batch_others]
        others += [(b, lax.rem(c + i, NC)) for i in range(1, NC)]
        for device in others:
            pl.semaphore_signal(barrier, inc=1, device_id=device, device_id_type=MESH)
        get_tokens = local(tokens, s.tokens)
        own_vectors = [getattr(s, f"v{i}") for i in range(len(vectors))]
        get_vectors = [local(one, two) for one, two in zip(vectors, own_vectors)]
        get_pair = [
            local(cols(wqkv, t * WIDTH + c * PAIR), own(s.wpair, SHARD).at[:, t * PAIR : (t + 1) * PAIR])
            for t in range(3)
        ]
        v.get_proj = local(wproj, own(s.wproj_all, SHARD))
        v.get_rest = [
            local(cols(wfc, b * WIDTH, WIDTH), own(s.wfc_mine, SHARD)),
            local(wout, s.wout_mine),
            local(wqkv, own(s.wfull, SHARD)),
            local(cotangent, g_mine),
        ]
        s.small[...] = jnp.zeros_like(s.small)
        for copy in get_vectors:
            copy.wait()
        row = 0
        for vector in own_vectors:
            for i in range(vector.shape[0] // SHARD):
                piece = vector[i * SHARD : (i + 1) * SHARD].astype(F32)
                s.small[row : row + 1, :] = piece.reshape(1, SHARD)
                row += 1

        def norm_rows(at):
            hat[at, :], scale[at, :] = normalise(s.tokens[at, :].astype(F32))
            hat_mine[at, :] = hat[at, :].astype(BF)

        get_tokens.wait()
        loop(ROWS // 32, 32, norm_rows)
        for copy in get_pair:
            copy.wait()
        s.parts[pl.ds(b, 1)] = s.small[...][None]
        pl.semaphore_wait(barrier, len(others))

    def send_small():
        for j in batch_others:
            net.send(s.small, s.parts.at[b], (j, c), small_slot)

    def pair_start():
        gather_pair.start([own(s.wpair, SHARD)])

    def g_start():
        gather_g.start([cotangent])

    def one_start():
        gather_one.start(halves(s.hat_all, ROWS, c))

    def small_wait():
        net.wait(small_slot, s.parts.at[: NB - 1])
        v.gain, v.bias = row_of(s.parts, 0), row_of(s.parts, 1)

    def proj_start():
        mine = own(s.wproj_all, SHARD)
        net.send(wproj.at[side_rows], mine.at[side_rows], (net.across, c), proj_slots + b)
        net.send(wproj, mine, (net.sib, c), proj_slots + b)

    def proj_relay():
        block = rows_of(s.wproj_all, SHARD)(net.across).at[side_rows]
        net.wait(proj_slots + net.across, block)
        net.send(block, block, pair_z, proj_side_slot)
        net.send(block, block, (net.sib, c), proj_near_slots)

    def proj_side():
        block = rows_of(s.wproj_all, SHARD)(net.across).at[other_side_rows]
        net.wait(proj_side_slot, block)
        net.send(block, block, (net.sib, c), proj_near_slots + 1)

    def fc_start(i):
        at = [slice(0, SHARD // 2), fc_rows[0]][i]
        for j in (net.across, net.diag):
            cut = wfc.at[at, pl.ds(pl.multiple_of(j * WIDTH, WIDTH), WIDTH)]
            net.send(cut, own(s.wfc_mine, SHARD).at[at], (j, c), fc_slots + 2 * b + i)
        if i == 0:
            net.send(cols(wfc, net.sib * WIDTH, WIDTH), own(s.wfc_mine, SHARD), (net.sib, c), fc_slots + 2 * b)

    def fc_relay():
        for j in (net.across, net.diag):
            block = rows_of(s.wfc_mine, SHARD)(j).at[fc_rows[0]]
            net.wait(fc_slots + 2 * j + 1, block)
            net.send(block, block, pair_z, fc_side_slots + j)

    def qv_rows():
        for p in range(NC):
            at = p * PAIR
            row, lane = 2 + (at % 512) // SHARD, at % SHARD
            s.qv_rows[p : p + 1, :] = s.parts[at // 512, row : row + 1, lane : lane + PAIR]
            s.qv_rows[8 + p : 9 + p, :] = s.parts[2 + at // 512, row : row + 1, lane : lane + PAIR]

    def g_relay():
        gather_g.relay()

    def gs_give():
        net.send(cotangent, own(s.g_side, ROWS), (b, net.side), side_slot + 1)

    def gs_start():
        net.wait(side_slot + 1, own(s.g_side, ROWS))
        gather_gs.start([own(s.g_side, ROWS)])

    def mix_block(j):
        rows = pl.ds(pl.multiple_of(j * ROWS, ROWS), ROWS)
        mix_bias = jnp.concatenate(
            [s.qv_rows[pl.ds(c, 1), :], jnp.zeros((1, PAIR), F32), s.qv_rows[pl.ds(8 + c, 1), :]], axis=1
        )
        s.n_one[rows, :] = (s.hat_all[rows, :].astype(F32) * v.gain + v.bias).astype(BF)
        s.mix[rows, :] = (mm(s.n_one[rows, :], s.wpair[...]) + mix_bias).astype(BF)

    def mix_at(d):
        if d == 0:
            mix_block(c)
        for zz in (net.z - d, net.z + d)[: 2 * d]:

            @pl.when(jnp.logical_and(zz >= 0, zz <= 3))
            def _():
                mix_block(2 * zz + net.x)

    def mix_side():
        def step(zz, carry):
            mix_block(2 * zz + 1 - net.x)
            return carry

        lax.fori_loop(0, 4, step, 0)

    def att():
        def ready(qb):
            swap_att.give(2 * qb)
            swap_att.give(2 * qb + 1)

        attend(s.mix, s.turned, s.att, s.lse, s.work, s.low_work, ready)

    def proj_finish():
        v.get_proj.wait()
        net.wait(proj_slots + net.sib, rows_of(s.wproj_all, SHARD)(net.sib))
        block = rows_of(s.wproj_all, SHARD)(net.diag)
        net.wait(proj_near_slots, block.at[side_rows])
        net.wait(proj_near_slots + 1, block.at[other_side_rows])

    def middle():
        def middle_cols(at):
            s.middle[:, at] = mm(s.att_own[...], s.wproj_all[:, at]) + s.tokens[:, at].astype(F32)

        loop(WIDTH // 256, 256, middle_cols)
        proj_bias, gain_two, bias_two = row_of(s.parts, 4), row_of(s.parts, 5), row_of(s.parts, 6)

        def norm_two_rows(at):
            middle = s.middle[at, :] + proj_bias
            s.middle[at, :] = middle
            norm, width = normalise(middle)
            s.hat_two[at, :], s.scale_two[at, :] = norm, width
            n_two_mine[at, :] = (norm * gain_two + bias_two).astype(BF)

        loop(ROWS // 32, 32, norm_two_rows)
        gather_two.start(halves(s.n_two, ROWS, b))

    def ns_give():
        net.send(n_two_mine, n_beside, (b, net.side), side_slot)

    def ns_start():
        net.wait(side_slot, n_beside)
        gather_ns.start([n_beside])

    def feed_wait():
        for copy in v.get_rest:
            copy.wait()
        gather_g.finish()
        net.wait(fc_slots + 2 * net.sib, rows_of(s.wfc_mine, SHARD)(net.sib))
        for j in (net.across, net.diag):
            block = rows_of(s.wfc_mine, SHARD)(j)
            net.wait(fc_slots + 2 * j, block.at[0 : SHARD // 2])
            net.wait(fc_side_slots + j, block.at[fc_rows[1]])
        s.gs[...] = jnp.zeros_like(s.gs)

    def feed_cols(r, i):
        n = lax.rem(2 * (1 - net.x) + i, 4)
        rows, at = chip_rows[r], pl.ds(pl.multiple_of(n * 256, 256), 256)
        pre = mm(s.n_two[rows, :], s.wfc_mine[:, at]) + s.small[pl.ds(7 + n, 1), :]
        value, slope = gelu_pair(pre)
        s.hidden[rows, at] = value.astype(BF)
        grad = (mm(s.g_all[rows, :], s.wout_mine[at, :], NT) * slope).astype(BF)
        s.grad_pre[rows, at] = grad
        s.gs[pl.ds(b, 1), pl.ds(7 + n, 1), :] += jnp.sum(grad.astype(F32), 0, keepdims=True)[None]

    def tile(ref, r, i):
        return ref.at[chip_rows[r], pl.ds(pl.multiple_of((2 * (1 - net.x) + i) * 256, 256), 256)]

    def side_tile(ref, r, i):
        return ref.at[chip_rows[r], i * 256 : (i + 1) * 256]

    def feed_i(r, i):
        feed_cols(r, i)
        net.send(tile(s.hidden, r, i), side_tile(s.hidden_side, r, i), (b, net.side), hidden_slots + 2 * r + i)

    def pre_give(r, i):
        net.send(tile(s.grad_pre, r, i), side_tile(s.pre_side, r, i), (b, net.side), pre_slots + 2 * r + i)

    def feed_rest(r):
        def step(i, carry):
            feed_cols(r, i)
            return carry

        lax.fori_loop(2, 4, step, 0)

    def norm_block(j):
        at = pl.ds(pl.multiple_of(j * ROWS, ROWS), ROWS)
        s.p_norm[at, :] = mm(s.grad_pre[at, :], s.wfc_mine[...], NT).astype(BF)

    def norm_diag():
        norm_block(net.diag)
        reduce_norm.give()

    def norm_across():
        norm_block(net.across)

    def norm_sib():
        norm_block(net.sib)
        reduce_norm.keep()

    def norm_own():
        norm_block(b)

    def back_two():
        gain_two = row_of(s.parts, 5)
        terms = reduce_norm.finish()

        def back_rows(i, carry):
            at = pl.ds(pl.multiple_of(i * 32, 32), 32)
            grad_gain, grad_bias, sum_branch, sum_g = carry
            grad = terms[0][at, :].astype(F32) + terms[1][at, :].astype(F32) + terms[2][at, :].astype(F32)
            norm = s.hat_two[at, :]
            scaled = grad * gain_two
            inner = scaled - jnp.mean(scaled, -1, keepdims=True)
            inner = inner - norm * jnp.mean(scaled * norm, -1, keepdims=True)
            g = g_mine[at, :].astype(F32)
            total = g + s.scale_two[at, :] * inner
            s.grad_middle[at, :] = total
            low = total.astype(BF)
            s.branch[at, :] = low
            return (
                grad_gain + jnp.sum(grad * norm, 0, keepdims=True),
                grad_bias + jnp.sum(grad, 0, keepdims=True),
                sum_branch + jnp.sum(low.astype(F32), 0, keepdims=True),
                sum_g + jnp.sum(g, 0, keepdims=True),
            )

        sums = lax.fori_loop(0, ROWS // 32, back_rows, (jnp.zeros((1, WIDTH), F32),) * 4)
        put_row(s.gs, 5, sums[0])
        put_row(s.gs, 6, sums[1])
        put_row(s.gs, 4, sums[2])
        put_row(s.gs, 11, sums[3])

        def att_cols(at):
            s.g_att[:, at] = mm(s.branch[...], s.wproj_all[at, :], NT).astype(BF)

        loop(4, 256, att_cols)
        swap_grad.start()

    def p_out(i):
        at = slice(i * 256, (i + 1) * 256)
        for r in range(2):
            net.wait(hidden_slots + 2 * r + i, side_tile(s.hidden_side, r, i))
        mine = cols(s.hidden, net.x * 512 + i * 256, 256)
        s.p_out[i] = (
            mm(mine[...], s.g_all[...], TN) + mm(s.hidden_side[:, at], s.g_side[...], TN)
        ).astype(BF)

    def out_done(i):
        part = s.out_block.at[i * 64 : (i + 1) * 64]
        reduce_out[i].finish(part)
        gather_out[i].begin(0, part)
        v.keep.append(local(part, out_view(i, c)))

    def p_fc(i):
        at = slice(i * 256, (i + 1) * 256)
        for r in range(2):
            net.wait(pre_slots + 2 * r + i, side_tile(s.pre_side, r, i))
        mine = cols(s.grad_pre, net.x * 512 + i * 256, 256)

        def fc_rows(k, carry):
            rows = pl.ds(pl.multiple_of(k * 256, 256), 256)
            total = mm(s.n_two[:, rows], mine[...], TN) + mm(s.n_side[:, rows], s.pre_side[:, at], TN)
            s.p_fc[i, pl.ds(k, 1)] = total.astype(BF).reshape(1, 4, 64, 256)
            return carry

        lax.fori_loop(0, 4, fc_rows, 0)

    def fc_done(i):
        reduce_fc[i].finish(s.fc_sum.at[i])
        mine = pl.ds(pl.multiple_of(b * 256, 256), 256)
        for j in batch_others:
            net.send(s.fc_sum.at[i, j], s.fc_block.at[i, :, mine], (j, c), swap_slots + i)
        s.fc_block[i, :, mine] = s.fc_sum[i, pl.ds(b, 1)][0]

    def fc_swap(i):
        net.wait(swap_slots + i, s.fc_block.at[i, :, : (NB - 1) * 256])
        gather_fc[i].begin(0, s.fc_block.at[i])
        v.keep.append(local(s.fc_block.at[i], fc_view(i, c)))

    def p_proj():
        def proj_rows(at):
            s.p_proj[at, :] = mm(s.att_own[:, at], s.branch[...], TN).astype(BF)

        loop(4, 256, proj_rows)
        reduce_proj.give()
        reduce_proj.keep()

    def proj_done():
        add_into(s.proj_sum, reduce_proj.finish())
        reduce_part.start()

    def part_done():
        reduce_part.line.finish(s.proj_block)
        gather_part.begin(0, s.proj_block)
        v.keep.append(local(s.proj_block, rows_of(o_proj, 32)(c)))

    def p_layer():
        def layer_block(j):
            at = pl.ds(pl.multiple_of(j * ROWS, ROWS), ROWS)
            s.p_layer[at, :] = mm(s.hidden[at, :], s.wout_mine[...]).astype(BF)

        layer_block(net.diag)
        reduce_layer.give()
        layer_block(net.sib)
        reduce_layer.keep()
        layer_block(net.across)
        layer_block(b)

    def layer_end():
        layer_bias = row_of(s.parts, 11)
        terms = reduce_layer.finish()

        def layer_rows(at):
            total = terms[0][at, :].astype(F32) + terms[1][at, :].astype(F32) + terms[2][at, :].astype(F32)
            layer_out[at, :] = (s.middle[at, :] + total + layer_bias).astype(BF)

        loop(ROWS // 32, 32, layer_rows)

    def att_back():
        attend_back(
            s.mix, s.turned, s.dout, s.lse, s.gmix, s.grad_k, s.grad_v,
            s.work, s.more, s.low_work, s.low_more,
        )

    def mix_give(k):
        swap_mix.give(2 * k)
        swap_mix.give(2 * k + 1)

    def p_qkv():
        def qkv_block(j):
            at = pl.ds(pl.multiple_of(j * SHARD, SHARD), SHARD)
            s.p_qkv[at, :] = mm(s.n_one[:, at], s.gmix[...], TN).astype(BF)

        qkv_block(net.diag)
        reduce_qkv.give()
        qkv_block(net.across)
        qkv_block(net.sib)
        reduce_qkv.keep()
        qkv_block(b)

    def qkv_done():
        terms = reduce_qkv.finish()
        add_into(s.qkv_block, terms)
        gather_qkv.start(halves(s.qkv_block, SHARD, 0))
        v.keep.append(local(s.qkv_block, o_qkv.at[c]))

    def gqv():
        s.gqv[...] = jnp.zeros_like(s.gqv)
        s.gqv[pl.ds(c, 1), :] = jnp.sum(s.gmix[:, :PAIR].astype(F32), 0, keepdims=True)
        s.gqv[pl.ds(8 + c, 1), :] = jnp.sum(s.gmix[:, 2 * PAIR :].astype(F32), 0, keepdims=True)
        for p in range(NC):
            at = p * PAIR
            row, lane = 2 + (at % 512) // SHARD, at % SHARD
            s.gs[at // 512, row : row + 1, lane : lane + PAIR] = s.gqv[p : p + 1, :]
            s.gs[2 + at // 512, row : row + 1, lane : lane + PAIR] = s.gqv[8 + p : 9 + p, :]

    def full_start(i):
        gather_full[i].start([rows_of(wqkv, SHARD // 2)(i)])

    def grad_in():
        for gather in gather_full:
            gather.finish()
        swap_mix.finish()
        for j in range(NC):
            for t in range(3):
                to, at = t * WIDTH + j * PAIR, t * PAIR
                s.gmix_all[:, to : to + PAIR] = s.gmix_own[j, :, at : at + PAIR]
        gain = v.gain

        def one_cols(at):
            s.gn_one[:, at] = mm(s.gmix_all[...], s.wfull[at, :], NT)

        loop(4, 256, one_cols)

        def token_rows(i, carry):
            at = pl.ds(pl.multiple_of(i * 32, 32), 32)
            grad_gain, grad_bias = carry
            grad, norm = s.gn_one[at, :], s.hat_one[at, :]
            scaled = grad * gain
            inner = scaled - jnp.mean(scaled, -1, keepdims=True)
            inner = inner - norm * jnp.mean(scaled * norm, -1, keepdims=True)
            grad_tokens[at, :] = (s.grad_middle[at, :] + s.scale_one[at, :] * inner).astype(BF)
            return (
                grad_gain + jnp.sum(grad * norm, 0, keepdims=True),
                grad_bias + jnp.sum(grad, 0, keepdims=True),
            )

        sums = lax.fori_loop(0, ROWS // 32, token_rows, (jnp.zeros((1, WIDTH), F32),) * 2)
        put_row(s.gs, 0, sums[0])
        put_row(s.gs, 1, sums[1])
        for j in batch_others:
            net.send(s.gs.at[j], s.gs_box.at[b], (j, c), gs_slot)

    def gs_sum():
        total = s.gs[pl.ds(b, 1)][0]
        net.wait(gs_slot, s.gs_box.at[: NB - 1])
        for j in batch_others:
            total = total + s.gs_box[pl.ds(j, 1)][0]
        s.gs_sum[...] = total
        for i in range(1, NC):
            j = lax.rem(c + i, NC)
            net.send(s.gs_sum, s.gs_far.at[c], (b, j), far_slot)

    def far_sum():
        total = s.gs_sum[...]
        net.wait(far_slot, s.gs_far.at[: NC - 1])
        for i in range(1, NC):
            j = lax.rem(c - i + NC, NC)
            total = total + s.gs_far[pl.ds(j, 1)][0]
        grad_small[...] = total

    enter()
    one_start()
    proj_start()
    pair_start()
    g_start()
    gather_one.stage(1,-1)
    gather_one.corner()
    gather_one.stage(1,1)
    gather_one.stage(2,-1)
    gather_one.pass_on(1)
    send_small()
    gather_pair.relay()
    gather_one.stage(2,1)
    gather_one.pass_on(2)
    proj_relay()
    gather_one.stage(3,-1)
    small_wait()
    gather_one.stage(3,1)
    gs_give()
    gather_pair.finish()
    qv_rows()
    fc_start(1)
    fc_start(0)
    mix_at(0)
    mix_at(1)
    mix_at(2)
    mix_at(3)
    gather_one.pass_on(3)
    gather_one.finish()
    mix_side()
    att()
    proj_side()
    g_relay()
    proj_finish()
    swap_att.finish()
    fc_relay()
    middle()
    ns_give()
    gather_two.near()
    gs_start()
    feed_wait()
    feed_i(0,0)
    gather_two.relay()
    gather_two.far()
    feed_i(1,0)
    feed_i(0,1)
    feed_i(1,1)
    ns_start()
    pre_give(1,1)
    feed_rest(1)
    gather_gs.relay()
    pre_give(1,0)
    feed_rest(0)
    gather_gs.finish()
    p_out(0)
    reduce_out[0].launch(0)
    reduce_out[0].launch(1)
    norm_diag()
    norm_sib()
    norm_across()
    reduce_norm.cross()
    reduce_out[0].pass_one(0)
    pre_give(0,0)
    reduce_out[0].pass_one(1)
    p_out(1)
    reduce_out[1].launch(0)
    reduce_out[0].launch(2)
    reduce_out[1].launch(1)
    gather_ns.relay()
    norm_own()
    reduce_out[1].pass_one(0)
    reduce_out[0].pass_two()
    pre_give(0,1)
    back_two()
    p_proj()
    out_done(0)
    gather_ns.finish()
    reduce_proj.cross()
    reduce_out[1].launch(2)
    p_fc(0)
    reduce_fc[0].launch(0)
    reduce_out[1].pass_one(1)
    reduce_out[1].pass_two()
    gather_out[0].stage(1,1)
    p_fc(1)
    reduce_fc[1].launch(0)
    reduce_fc[0].launch(1)
    full_start(1)
    gather_out[0].stage(1,-1)
    reduce_fc[1].launch(1)
    out_done(1)
    reduce_fc[1].launch(2)
    swap_grad.finish()
    gather_out[0].stage(2,1)
    reduce_fc[0].pass_one(0)
    att_back()
    mix_give(3)
    mix_give(0)
    proj_done()
    reduce_fc[1].pass_one(0)
    gather_out[1].stage(1,-1)
    reduce_fc[0].pass_one(1)
    reduce_fc[0].pass_two()
    reduce_fc[1].pass_one(1)
    p_qkv()
    reduce_fc[1].pass_two()
    gather_out[0].stage(2,-1)
    reduce_qkv.cross()
    gather_out[1].stage(1,1)
    reduce_fc[0].launch(2)
    reduce_part.fold()
    reduce_part.line.launch(0)
    reduce_part.line.launch(1)
    gather_out[1].stage(2,-1)
    gather_out[0].stage(3,1)
    reduce_part.line.pass_one(0)
    fc_done(0)
    reduce_part.line.launch(2)
    qkv_done()
    reduce_part.line.pass_one(1)
    fc_done(1)
    reduce_part.line.pass_two()
    gather_out[0].stage(3,-1)
    fc_swap(0)
    fc_swap(1)
    full_start(0)
    gather_qkv.stage(1,-1)
    gather_out[1].stage(2,1)
    gather_fc[0].stage(1,1)
    gather_full[1].relay()
    part_done()
    mix_give(1)
    gather_fc[1].stage(1,1)
    gather_fc[1].corner()
    gather_qkv.stage(1,1)
    gather_part.stage(1,1)
    mix_give(2)
    gather_fc[0].stage(1,-1)
    gather_qkv.stage(2,-1)
    gather_out[1].stage(3,1)
    gather_fc[1].stage(1,-1)
    p_layer()
    gather_full[0].relay()
    gqv()
    gather_fc[0].stage(2,1)
    gather_fc[0].stage(2,-1)
    gather_qkv.corner()
    reduce_layer.cross()
    gather_out[1].stage(3,-1)
    gather_qkv.stage(3,-1)
    gather_fc[1].stage(2,1)
    gather_part.stage(1,-1)
    gather_fc[1].stage(2,-1)
    gather_fc[1].pass_on(1)
    grad_in()
    gather_qkv.stage(2,1)
    gather_part.stage(2,1)
    gather_fc[0].stage(3,1)
    gather_part.stage(2,-1)
    gather_qkv.pass_on(1)
    gather_fc[1].pass_on(2)
    gather_fc[0].stage(3,-1)
    layer_end()
    gs_sum()
    gather_qkv.pass_on(2)
    gather_part.stage(3,-1)
    gather_qkv.stage(3,1)
    gather_part.stage(3,1)
    gather_fc[1].stage(3,-1)
    far_sum()
    gather_fc[1].pass_on(3)
    gather_fc[1].stage(3,1)
    gather_qkv.pass_on(3)
    for gather in gather_out + gather_fc + [gather_qkv, gather_part]:
        gather.finish()
    for copy in v.keep:
        copy.wait()
    net.drain()


PARTS = 4


def widen_kernel(layer, grad_in, small, w_qkv, w_proj, w_fc, w_out, *refs):
    o_layer, o_grad_in, o_qkv, o_proj, o_fc, o_out = refs[:6]
    vectors, rows, (qkv, proj, fc, out, sems) = refs[6:14], refs[14:22], refs[22:]
    leaving = []

    def leave(src, dst):
        copy = pltpu.make_async_copy(src, dst, sems.at[len(leaving)])
        copy.start()
        leaving.append(copy)

    row = 0
    for vector, here in zip(vectors, rows):
        for i in range(vector.shape[0] // SHARD):
            here[i * SHARD : (i + 1) * SHARD] = small[row, :]
            row += 1
        leave(here, vector)
    leave(layer, o_layer)
    leave(grad_in, o_grad_in)
    for k in range(PARTS):
        wide, at = slice(k * 256, (k + 1) * 256), slice(k * 64, (k + 1) * 64)
        out[wide, :] = w_out[wide, :].astype(F32)
        leave(out.at[wide], o_out.at[wide])
        for j in range(NB):
            for x in range(2):
                for i in range(2):
                    to = j * WIDTH + x * 512 + i * 256
                    fc[at, to : to + 256] = w_fc[x, i, at, j * 256 : (j + 1) * 256].astype(F32)
        leave(fc.at[at], o_fc.at[at])
        for j in range(NC):
            for t in range(3):
                to = t * WIDTH + j * PAIR
                qkv[at, to : to + PAIR] = w_qkv[j, at, t * PAIR : (t + 1) * PAIR].astype(F32)
        leave(qkv.at[at], o_qkv.at[at])
        proj[at, :] = w_proj[at, :].astype(F32)
        leave(proj.at[at], o_proj.at[at])
    for copy in leaving:
        copy.wait()


def per_device_fast(
    tokens, cotangent, ln1_gain, ln1_bias, qkv_weight, qv_bias, proj_weight, proj_bias,
    ln2_gain, ln2_bias, fc_weight, fc_bias, out_weight, out_bias,
):
    vmem, anywhere = pl.BlockSpec(memory_space=pltpu.VMEM), pl.BlockSpec(memory_space=pl.ANY)
    shape = jax.ShapeDtypeStruct
    layer, grad_in, grad_small, w_qkv, w_proj, w_fc, w_out = pl.pallas_call(
        layer_kernel,
        out_shape=(
            pltpu.VMEM((ROWS, WIDTH), BF),
            pltpu.VMEM((ROWS, WIDTH), BF),
            pltpu.VMEM((SMALL_ROWS, SHARD), F32),
            pltpu.VMEM((NC, SHARD, 3 * PAIR), BF),
            pltpu.VMEM((SHARD, WIDTH), BF),
            pltpu.VMEM((2, 2, SHARD, WIDTH), BF),
            pltpu.VMEM((FF // NB, WIDTH), BF),
        ),
        in_specs=[anywhere] * 14,
        out_specs=(vmem,) * 7,
        scratch_shapes=[pltpu.VMEM(*item) for item in SCRATCH.values()]
        + [
            pltpu.SemaphoreType.DMA((SENDS,)),
            pltpu.SemaphoreType.DMA((RECVS,)),
            pltpu.SemaphoreType.DMA((LOCALS,)),
        ],
        compiler_params=pltpu.CompilerParams(
            collective_id=0, has_side_effects=True, vmem_limit_bytes=LAYER_VMEM
        ),
    )(
        tokens.reshape(ROWS, WIDTH), cotangent.reshape(ROWS, WIDTH),
        ln1_gain, ln1_bias, qv_bias, proj_bias, ln2_gain, ln2_bias, fc_bias, out_bias,
        qkv_weight, proj_weight, fc_weight, out_weight,
    )
    layer, grad_in, w_qkv, w_proj, w_fc, w_out, *vectors = pl.pallas_call(
        widen_kernel,
        out_shape=(
            shape((ROWS, WIDTH), BF),
            shape((ROWS, WIDTH), BF),
            shape((SHARD, 3 * WIDTH), F32),
            shape((SHARD, WIDTH), F32),
            shape((SHARD, FF), F32),
            shape((FF // NB, WIDTH), F32),
            *[shape((n * SHARD,), F32) for n in VECTOR_ROWS],
        ),
        in_specs=[vmem] * 7,
        out_specs=(anywhere,) * (6 + len(VECTOR_ROWS)),
        scratch_shapes=[
            *[pltpu.VMEM((n * SHARD,), F32) for n in VECTOR_ROWS],
            pltpu.VMEM((SHARD, 3 * WIDTH), F32),
            pltpu.VMEM((SHARD, WIDTH), F32),
            pltpu.VMEM((SHARD, FF), F32),
            pltpu.VMEM((FF // NB, WIDTH), F32),
            pltpu.SemaphoreType.DMA((4 * PARTS + 2 + len(VECTOR_ROWS),)),
        ],
        compiler_params=pltpu.CompilerParams(vmem_limit_bytes=WIDEN_VMEM),
    )(layer, grad_in, grad_small, w_qkv, w_proj, w_fc, w_out)
    return (
        layer.reshape(tokens.shape),
        grad_in.reshape(tokens.shape),
        vectors[0],
        vectors[1],
        w_qkv,
        vectors[2],
        w_proj,
        vectors[3],
        vectors[4],
        vectors[5],
        w_fc,
        vectors[6],
        w_out,
        vectors[7],
    )


LAYER_VMEM, WIDEN_VMEM = 55 * 1024 * 1024, 20 * 1024 * 1024


def solution(mesh):
    placed = (
        P("batch", "ctx", None),
        P("batch", "ctx", None),
        P("batch"),
        P("batch"),
        P("batch", None),
        P("batch"),
        P("batch", None),
        P("batch"),
        P("batch"),
        P("batch"),
        P("batch", None),
        P("batch"),
        P("batch", None),
        P("batch"),
    )
    fits = dict(mesh.shape) == {"batch": NB, "ctx": NC}
    return jax.shard_map(
        per_device_fast if fits else per_device,
        mesh=mesh,
        in_specs=placed,
        out_specs=(
            P("batch", "ctx", None),
            P("batch", "ctx", None),
            P("batch"),
            P("batch"),
            P("batch", None),
            P("batch"),
            P("batch", None),
            P("batch"),
            P("batch"),
            P("batch"),
            P("batch", None),
            P("batch"),
            P("batch", None),
            P("batch"),
        ),
        check_vma=False,
    )
```

```python
from functools import partial
from types import SimpleNamespace

import jax
import jax.numpy as jnp
from jax import lax
from jax.experimental import pallas as pl
from jax.experimental.pallas import tpu as pltpu
from jax.sharding import PartitionSpec as P

HEADS = 16
HEAD_DIM = 64


epsilon = 1e-05
masked_value = -1e30


def shifted(block, axis, distance):
    devices = range(lax.axis_size(axis))
    route = [(i - distance, i) for i in devices if i - distance in devices]
    return lax.ppermute(block, axis, route)


def from_behind(block, axis, distance):
    devices = range(lax.axis_size(axis))
    route = [((i - distance) % len(devices), i) for i in devices]
    return lax.ppermute(block, axis, route)


def layer_norm(inputs, gain_vec, bias_vec):
    centre = inputs - jnp.mean(inputs, -1, keepdims=True)
    spread = jnp.mean(centre * centre, -1, keepdims=True)
    return centre * lax.rsqrt(spread + epsilon) * gain_vec + bias_vec


def keep_same(running):
    return running


def per_device(
    tokens,
    cotangent,
    ln1_gain,
    ln1_bias,
    qkv_weight,
    qv_bias,
    proj_weight,
    proj_bias,
    ln2_gain,
    ln2_bias,
    fc_weight,
    fc_bias,
    out_weight,
    out_bias,
):
    (
        gain_one,
        bias_one,
        weight_qkv,
        bias_qv,
        weight_proj,
        bias_proj,
        gain_two,
        bias_two,
        weight_fc,
        bias_fc,
        weight_out,
        bias_out,
    ) = (
        lax.all_gather(ln1_gain, "batch", axis=0, tiled=True),
        lax.all_gather(ln1_bias, "batch", axis=0, tiled=True),
        lax.all_gather(qkv_weight, "batch", axis=0, tiled=True),
        lax.all_gather(qv_bias, "batch", axis=0, tiled=True),
        lax.all_gather(proj_weight, "batch", axis=0, tiled=True),
        lax.all_gather(proj_bias, "batch", axis=0, tiled=True),
        lax.all_gather(ln2_gain, "batch", axis=0, tiled=True),
        lax.all_gather(ln2_bias, "batch", axis=0, tiled=True),
        lax.all_gather(fc_weight, "batch", axis=0, tiled=True),
        lax.all_gather(fc_bias, "batch", axis=0, tiled=True),
        lax.all_gather(out_weight, "batch", axis=0, tiled=True),
        lax.all_gather(out_bias, "batch", axis=0, tiled=True),
    )
    seq_count, ctx_rows, model_width = tokens.shape
    row_count = seq_count * ctx_rows
    inputs = tokens.astype(jnp.float32).reshape(row_count, model_width)
    norm_one, norm_one_pull = jax.vjp(
        layer_norm, inputs, gain_one.astype(jnp.float32), bias_one.astype(jnp.float32)
    )
    normed_low = norm_one.astype(jnp.bfloat16)
    bias_float = bias_qv.astype(jnp.float32)
    bias_full = jnp.concatenate(
        [bias_float[:model_width], jnp.zeros((model_width,), jnp.float32), bias_float[model_width:]]
    )
    mixed_proj = (
        jnp.dot(normed_low, weight_qkv, preferred_element_type=jnp.float32) + bias_full
    ).astype(jnp.bfloat16)
    query_flat = mixed_proj[:, :model_width].reshape(seq_count, ctx_rows, model_width)
    key_flat = mixed_proj[:, model_width : 2 * model_width].reshape(
        seq_count, ctx_rows, model_width
    )
    value_flat = mixed_proj[:, 2 * model_width :].reshape(seq_count, ctx_rows, model_width)
    query_heads = query_flat.reshape(seq_count, ctx_rows, HEADS, HEAD_DIM)
    own_index = lax.axis_index("ctx")
    position = own_index * ctx_rows
    query_pos = position + jnp.arange(ctx_rows, dtype=jnp.int32)
    last_pos = position + ctx_rows - 1
    start_state = (
        jnp.full((seq_count, ctx_rows, HEADS), masked_value, jnp.float32),
        jnp.zeros((seq_count, ctx_rows, HEADS), jnp.float32),
        jnp.zeros((seq_count, ctx_rows, HEADS, HEAD_DIM), jnp.float32),
    )
    key_piece = lax.all_gather(key_flat, "ctx", axis=1, tiled=True)
    value_piece = lax.all_gather(value_flat, "ctx", axis=1, tiled=True)
    piece_rows = key_piece.shape[1]

    def compute(running):
        run_max, run_sum, accum = running
        key_split = key_piece.reshape(seq_count, piece_rows, HEADS, HEAD_DIM)
        value_split = value_piece.reshape(seq_count, piece_rows, HEADS, HEAD_DIM)
        scores = (
            jnp.einsum(
                "bqhd,bkhd->bqhk", query_heads, key_split, preferred_element_type=jnp.float32
            )
            * 0.125
        )
        key_pos = jnp.arange(piece_rows, dtype=jnp.int32)
        allowed = (key_pos[None, :] <= query_pos[:, None])[None, :, None, :]
        scores = jnp.where(allowed, scores, masked_value)
        new_max = jnp.maximum(run_max, jnp.max(scores, -1))
        weights_exp = jnp.where(allowed, jnp.exp(scores - new_max[..., None]), 0.0)
        new_sum = jnp.sum(weights_exp, -1)
        product = jnp.einsum(
            "bqhk,bkhd->bqhd",
            weights_exp.astype(jnp.bfloat16),
            value_split,
            preferred_element_type=jnp.float32,
        )
        return (new_max, new_sum, product)

    run_max, run_sum, accum = lax.cond(jnp.int32(0) <= last_pos, compute, keep_same, start_state)
    log_total = run_max + jnp.log(run_sum)
    attended = accum / run_sum[..., None]
    attended_low = attended.reshape(row_count, model_width).astype(jnp.bfloat16)
    middle = (
        inputs
        + jnp.dot(attended_low, weight_proj, preferred_element_type=jnp.float32)
        + bias_proj.astype(jnp.float32)
    )
    norm_two, norm_two_pull = jax.vjp(
        layer_norm, middle, gain_two.astype(jnp.float32), bias_two.astype(jnp.float32)
    )
    normed_two = norm_two.astype(jnp.bfloat16)
    pre_act = jnp.dot(normed_two, weight_fc, preferred_element_type=jnp.float32) + bias_fc.astype(
        jnp.float32
    )
    activated, gelu_pull = jax.vjp(partial(jax.nn.gelu, approximate=True), pre_act)
    hidden_low = activated.astype(jnp.bfloat16)
    output = (
        middle
        + jnp.dot(hidden_low, weight_out, preferred_element_type=jnp.float32)
        + bias_out.astype(jnp.float32)
    )
    layer_out = output.astype(jnp.bfloat16).reshape(tokens.shape)
    grad_out = cotangent.reshape(row_count, model_width)
    grad_out_float = grad_out.astype(jnp.float32)
    grad_w_out = jnp.einsum("rf,rd->fd", hidden_low, grad_out, preferred_element_type=jnp.float32)
    grad_b_out = jnp.sum(grad_out_float, 0)
    grad_hidden = jnp.einsum("rd,fd->rf", grad_out, weight_out, preferred_element_type=jnp.float32)
    (grad_pre,) = gelu_pull(grad_hidden)
    grad_pre_low = grad_pre.astype(jnp.bfloat16)
    grad_w_fc = jnp.einsum(
        "rd,rf->df", normed_two, grad_pre_low, preferred_element_type=jnp.float32
    )
    grad_b_fc = jnp.sum(grad_pre_low.astype(jnp.float32), 0)
    grad_norm_two = jnp.einsum(
        "rf,df->rd", grad_pre_low, weight_fc, preferred_element_type=jnp.float32
    )
    grad_mid_norm, grad_g_two, grad_b_two = norm_two_pull(grad_norm_two)
    grad_middle = grad_out_float + grad_mid_norm
    grad_branch = grad_middle.astype(jnp.bfloat16)
    grad_w_proj = jnp.einsum(
        "rd,re->de", attended_low, grad_branch, preferred_element_type=jnp.float32
    )
    grad_b_proj = jnp.sum(grad_branch.astype(jnp.float32), 0)
    grad_attended = jnp.einsum(
        "re,de->rd", grad_branch, weight_proj, preferred_element_type=jnp.float32
    ).astype(jnp.bfloat16)
    grad_att_flat = grad_attended.reshape(seq_count, ctx_rows, model_width)
    grad_att_heads = grad_att_flat.reshape(seq_count, ctx_rows, HEADS, HEAD_DIM)
    delta_mine = jnp.sum(grad_att_heads.astype(jnp.float32) * attended, -1)
    zero_heads = jnp.zeros((seq_count, ctx_rows, HEADS, HEAD_DIM), jnp.float32)
    cycle_count = lax.axis_size("ctx")

    def cycle_turn(turn, state):
        owner = (own_index - turn) % cycle_count
        first_row = owner * ctx_rows

        def visit(inner):
            key_piece, value_piece, grad_k, grad_v, grad_q = inner
            key_split = key_piece.reshape(seq_count, ctx_rows, HEADS, HEAD_DIM)
            value_split = value_piece.reshape(seq_count, ctx_rows, HEADS, HEAD_DIM)
            piece_pos = first_row + jnp.arange(ctx_rows, dtype=jnp.int32)
            scores = (
                jnp.einsum(
                    "bqhd,bkhd->bqhk", query_heads, key_split, preferred_element_type=jnp.float32
                )
                * 0.125
            )
            allowed = (piece_pos[None, :] <= query_pos[:, None])[None, :, None, :]
            probs = jnp.where(allowed, jnp.exp(scores - log_total[..., None]), 0.0)
            grad_probs = jnp.einsum(
                "bqhd,bkhd->bqhk", grad_att_heads, value_split, preferred_element_type=jnp.float32
            )
            grad_scores = (probs * (grad_probs - delta_mine[..., None])).astype(jnp.bfloat16)
            grad_q = (
                grad_q
                + jnp.einsum(
                    "bqhk,bkhd->bqhd", grad_scores, key_split, preferred_element_type=jnp.float32
                )
                * 0.125
            )
            grad_k = (
                grad_k
                + jnp.einsum(
                    "bqhk,bqhd->bkhd", grad_scores, query_heads, preferred_element_type=jnp.float32
                )
                * 0.125
            )
            grad_v = grad_v + jnp.einsum(
                "bqhk,bqhd->bkhd",
                probs.astype(jnp.bfloat16),
                grad_att_heads,
                preferred_element_type=jnp.float32,
            )
            return (key_piece, value_piece, grad_k, grad_v, grad_q)

        key_piece, value_piece, grad_k, grad_v, grad_q = lax.cond(
            owner <= own_index, visit, keep_same, state
        )
        key_piece, value_piece = shifted((key_piece, value_piece), "ctx", 1)
        grad_k, grad_v = (
            from_behind(grad_k.astype(jnp.bfloat16), "ctx", 1).astype(grad_k.dtype),
            from_behind(grad_v.astype(jnp.bfloat16), "ctx", 1).astype(grad_v.dtype),
        )
        return (key_piece, value_piece, grad_k, grad_v, grad_q)

    cycle_state = lax.fori_loop(
        0, cycle_count, cycle_turn, (key_flat, value_flat, zero_heads, zero_heads, zero_heads)
    )
    grad_k, grad_v, grad_q = (cycle_state[2], cycle_state[3], cycle_state[4])
    grad_mixed = jnp.concatenate(
        [
            grad_q.reshape(row_count, model_width),
            grad_k.reshape(row_count, model_width),
            grad_v.reshape(row_count, model_width),
        ],
        axis=1,
    ).astype(jnp.bfloat16)
    grad_w_qkv = jnp.einsum("rd,re->de", normed_low, grad_mixed, preferred_element_type=jnp.float32)
    grad_bias_all = jnp.sum(grad_mixed.astype(jnp.float32), 0)
    grad_b_qv = jnp.concatenate([grad_bias_all[:model_width], grad_bias_all[2 * model_width :]])
    grad_norm_one = jnp.einsum(
        "re,de->rd", grad_mixed, weight_qkv, preferred_element_type=jnp.float32
    )
    grad_in_norm, grad_g_one, grad_b_one = norm_one_pull(grad_norm_one)
    grad_tokens = (grad_middle + grad_in_norm).astype(jnp.bfloat16).reshape(tokens.shape)
    local_grads = (
        grad_g_one,
        grad_b_one,
        grad_w_qkv,
        grad_b_qv,
        grad_w_proj,
        grad_b_proj,
        grad_g_two,
        grad_b_two,
        grad_w_fc,
        grad_b_fc,
        grad_w_out,
        grad_b_out,
    )
    partial_grads = (
        lax.psum_scatter(
            local_grads[0].astype(jnp.bfloat16), "batch", scatter_dimension=0, tiled=True
        ).astype(jnp.float32),
        lax.psum_scatter(
            local_grads[1].astype(jnp.bfloat16), "batch", scatter_dimension=0, tiled=True
        ).astype(jnp.float32),
        lax.psum_scatter(
            local_grads[2].astype(jnp.bfloat16), "batch", scatter_dimension=0, tiled=True
        ).astype(jnp.float32),
        lax.psum_scatter(
            local_grads[3].astype(jnp.bfloat16), "batch", scatter_dimension=0, tiled=True
        ).astype(jnp.float32),
        lax.psum_scatter(
            local_grads[4].astype(jnp.bfloat16), "batch", scatter_dimension=0, tiled=True
        ).astype(jnp.float32),
        lax.psum_scatter(
            local_grads[5].astype(jnp.bfloat16), "batch", scatter_dimension=0, tiled=True
        ).astype(jnp.float32),
        lax.psum_scatter(
            local_grads[6].astype(jnp.bfloat16), "batch", scatter_dimension=0, tiled=True
        ).astype(jnp.float32),
        lax.psum_scatter(
            local_grads[7].astype(jnp.bfloat16), "batch", scatter_dimension=0, tiled=True
        ).astype(jnp.float32),
        lax.psum_scatter(
            local_grads[8].astype(jnp.bfloat16), "batch", scatter_dimension=0, tiled=True
        ).astype(jnp.float32),
        lax.psum_scatter(
            local_grads[9].astype(jnp.bfloat16), "batch", scatter_dimension=0, tiled=True
        ).astype(jnp.float32),
        lax.psum_scatter(
            local_grads[10].astype(jnp.bfloat16), "batch", scatter_dimension=0, tiled=True
        ).astype(jnp.float32),
        lax.psum_scatter(
            local_grads[11].astype(jnp.bfloat16), "batch", scatter_dimension=0, tiled=True
        ).astype(jnp.float32),
    )
    summed_grads = lax.psum(
        (
            partial_grads[0],
            partial_grads[1],
            partial_grads[2],
            partial_grads[3],
            partial_grads[4],
            partial_grads[5],
            partial_grads[6],
            partial_grads[7],
            partial_grads[8],
            partial_grads[9],
            partial_grads[10],
            partial_grads[11],
        ),
        "ctx",
    )
    return (
        layer_out,
        grad_tokens,
        summed_grads[0],
        summed_grads[1],
        summed_grads[2],
        summed_grads[3],
        summed_grads[4],
        summed_grads[5],
        summed_grads[6],
        summed_grads[7],
        summed_grads[8],
        summed_grads[9],
        summed_grads[10],
        summed_grads[11],
    )


BF, F32 = jnp.bfloat16, jnp.float32
NN = (((1,), (0,)), ((), ()))
NT = (((1,), (1,)), ((), ()))
TN = (((0,), (0,)), ((), ()))
MESH = pl.DeviceIdType.MESH
NB, NC, WIDTH, ROWS, FF, PAIR = 4, 8, 1024, 128, 4096, 128
SHARD = WIDTH // NB
LENGTH = ROWS * NC
SMALL_ROWS = 16


def mm(left, right, dims=NN):
    return lax.dot_general(left, right, dims, preferred_element_type=F32)


def run(when, action):
    if when is None:
        action()
    else:
        pl.when(when)(action)


def both(one, two):
    return two if one is None else (one if two is None else jnp.logical_and(one, two))


class Net:
    def __init__(self, b, c, send_sems, recv_sems):
        self.b, self.c, self.z, self.x = b, c, c // 2, c % 2
        self.side = c + 1 - 2 * self.x
        self.core = b % 2
        self.sib = b + 1 - 2 * self.core
        self.across = lax.rem(b + 2, NB)
        self.diag = lax.rem(self.sib + 2, NB)
        self.send_sems, self.recv_sems = send_sems, recv_sems
        self.taken, self.pending = 0, []

    def slots(self, count):
        base = self.taken
        self.taken += count
        assert self.taken <= self.recv_sems.shape[0]
        return base

    def send(self, src, dst, device, slot, when=None):
        index = len(self.pending)
        if index == self.send_sems.shape[0]:
            done, copy, index = self.pending.pop(0)
            run(done, copy.wait_send)
        copy = pltpu.make_async_remote_copy(
            src_ref=src,
            dst_ref=dst,
            send_sem=self.send_sems.at[index],
            recv_sem=self.recv_sems.at[slot],
            device_id=device,
            device_id_type=MESH,
        )
        run(when, copy.start)
        self.pending.append((when, copy, index))

    def wait(self, slot, ref):
        pltpu.make_async_remote_copy(
            src_ref=ref,
            dst_ref=ref,
            send_sem=self.send_sems.at[0],
            recv_sem=self.recv_sems.at[slot],
            device_id=(self.sib, self.c),
            device_id_type=MESH,
        ).wait_recv()

    def drain(self):
        for when, copy, _ in self.pending:
            run(when, copy.wait_send)


class GatherCtx:
    def __init__(self, net, views, others, count, turn=False):
        self.net, self.views, self.others, self.count, self.turn = net, views, others, count, turn
        self.along, self.beside = net.slots(4 * count), net.slots(1)
        self.turned = net.slots(4) if turn else None

    def begin(self, i, src):
        net, count = self.net, self.count
        dst, at = self.views(net.c)[i], net.z * count + i
        if self.turn and i == count - 1:
            end = jnp.logical_or(net.z == 0, net.z == 3)
            net.send(src, dst, (net.b, net.side), self.turned + 2, net.z == 0)
            net.send(src, dst, (net.b, net.side), self.turned + 3, net.z == 3)
            net.send(src, dst, (net.b, net.side), self.beside, jnp.logical_not(end))
        else:
            net.send(src, dst, (net.b, net.side), self.beside)
        net.send(src, dst, (net.b, net.c + 2), self.along + at, net.z < 3)
        net.send(src, dst, (net.b, net.c - 2), self.along + at, net.z > 0)

    def start(self, srcs):
        for i, src in enumerate(srcs):
            self.begin(i, src)

    def stage(self, d, sign):
        net, count = self.net, self.count
        zz = net.z + sign * d
        here = zz >= 0 if sign < 0 else zz <= 3
        refs = self.views(2 * zz + net.x)
        onward = both(here, net.z < 3 if sign < 0 else net.z > 0)
        for i in range(count):
            slot = self.along + zz * count + i
            pl.when(here)(lambda slot=slot, ref=refs[i]: net.wait(slot, ref))
            if d < 3:
                net.send(refs[i], refs[i], (net.b, net.c - 2 * sign), slot, onward)
            goes = here
            if self.turn and i == count - 1:
                goes = both(here, jnp.logical_and(zz > 0, zz < 3))
            net.send(refs[i], refs[i], (net.b, net.side), self.beside, goes)

    def piece(self, end):
        return self.views(2 * end + 1 - self.net.x)[self.count - 1]

    def corner(self):
        net = self.net
        for end, step in ((0, 2), (3, -2)):
            ref, slot = self.piece(end), self.turned + 2 + (end > 0)
            pl.when(net.z == end)(lambda slot=slot, ref=ref: net.wait(slot, ref))
            net.send(ref, ref, (net.b, net.c + step), self.turned + (end > 0), net.z == end)

    def pass_on(self, d):
        net = self.net
        for end, step in ((0, 2), (3, -2)):
            here = net.z == (end + d if end == 0 else end - d)
            ref, slot = self.piece(end), self.turned + (end > 0)
            pl.when(here)(lambda slot=slot, ref=ref: net.wait(slot, ref))
            if d < 3:
                net.send(ref, ref, (net.b, net.c + step), slot, here)

    def finish(self):
        self.net.wait(self.beside, self.others)


def chunks(ref):
    if len(ref.shape) == 3:
        return ref.shape[0], lambda i: (i,)
    rows = min(32, ref.shape[0])
    return ref.shape[0] // rows, lambda i: (pl.ds(pl.multiple_of(i * rows, rows), rows),)


def add_into(target, terms, dtype=BF):
    count, at = chunks(target)

    def body(i, carry):
        total = terms[0][at(i)].astype(F32)
        for term in terms[1:]:
            total = total + term[at(i)].astype(F32)
        target[at(i)] = total.astype(dtype)
        return carry

    lax.fori_loop(0, count, body, 0)


class ReduceLine:
    def __init__(self, net, mine, up, down):
        self.net, self.mine, self.up, self.down = net, mine, up, down
        self.s_up, self.s_down = net.slots(4), net.slots(4)

    def give(self, k, upward, when):
        net = self.net
        if upward:
            net.send(self.mine(k), self.up.at[k], (net.b, net.c + 2), self.s_up + k, when)
        else:
            net.send(self.mine(k), self.down.at[k], (net.b, net.c - 2), self.s_down + k, when)

    def take(self, k, upward, when):
        box, slot = (self.up, self.s_up) if upward else (self.down, self.s_down)
        mine = self.mine(k)

        @pl.when(when)
        def _():
            self.net.wait(slot + k, box.at[k])
            add_into(mine, [mine, box.at[k]])

        self.give(k, upward, when)

    def launch(self, k):
        self.give(3 - k, True, self.net.z == 0)
        self.give(k, False, self.net.z == 3)

    def pass_one(self, k):
        self.take(3 - k, True, self.net.z == 1)
        self.take(k, False, self.net.z == 2)

    def pass_two(self):
        self.take(0, False, self.net.z == 1)
        self.take(3, True, self.net.z == 2)

    def finish(self, target):
        net, z = self.net, self.net.z
        mine = self.mine(z)

        @pl.when(z >= 1)
        def _():
            net.wait(self.s_up + z, self.up.at[z])

        @pl.when(z <= 2)
        def _():
            net.wait(self.s_down + z, self.down.at[z])

        pl.when(z == 0)(lambda: add_into(target, [mine, self.down.at[z]]))
        pl.when(z == 3)(lambda: add_into(target, [mine, self.up.at[z]]))
        pl.when(jnp.logical_and(z > 0, z < 3))(
            lambda: add_into(target, [mine, self.up.at[z], self.down.at[z]])
        )


class ReduceCtx:
    def __init__(self, net, mine, beside, up, down):
        self.net, self.mine, self.beside = net, mine, beside
        self.slots = net.slots(4)
        self.line = ReduceLine(net, lambda k: mine(2 * k + net.x), up, down)

    def start(self):
        net = self.net
        for k in (3, 0, 2, 1):
            net.send(self.mine(2 * k + 1 - net.x), self.beside.at[k], (net.b, net.side), self.slots + k)

    def fold(self):
        for k in (3, 0, 2, 1):
            self.net.wait(self.slots + k, self.beside.at[k])
            mine = self.line.mine(k)
            add_into(mine, [mine, self.beside.at[k]])


class SwapCtx:
    def __init__(self, net, src, dst, others):
        self.net, self.src, self.dst, self.others = net, src, dst, others
        self.slot = net.slots(1)

    def give(self, j):
        net, src, dst = self.net, self.src(j), self.dst(self.net.c)
        net.send(src, dst, (net.b, j), self.slot, net.c != j)

        @pl.when(net.c == j)
        def _():
            dst[...] = src[...]

    def start(self):
        for j in range(NC):
            self.give(j)

    def finish(self):
        self.net.wait(self.slot, self.others)


class GatherBatch:
    def __init__(self, net, views, count=1):
        self.net, self.views, self.count = net, views, count
        self.base = net.slots(NB * count)

    def start(self, srcs):
        net = self.net
        dsts = self.views(net.b)
        for i in range(self.count):
            slot = self.base + net.b * self.count + i
            net.send(srcs[i], dsts[i], (net.across, net.c), slot)
        for i in range(self.count):
            slot = self.base + net.b * self.count + i
            net.send(srcs[i], dsts[i], (net.sib, net.c), slot)

    def relay(self):
        net = self.net
        refs = self.views(net.across)
        for i in range(self.count):
            slot = self.base + net.across * self.count + i
            net.wait(slot, refs[i])
            net.send(refs[i], refs[i], (net.sib, net.c), slot)

    def take(self, j):
        refs = self.views(j)
        for i in range(self.count):
            self.net.wait(self.base + j * self.count + i, refs[i])

    def near(self):
        self.take(self.net.sib)

    def far(self):
        self.take(self.net.diag)

    def finish(self):
        self.near()
        self.far()


class ReduceBatch:
    def __init__(self, net, mine, boxes):
        self.net, self.mine, self.boxes = net, mine, boxes
        self.base = net.slots(3)

    def give(self):
        net = self.net
        net.send(self.mine(net.diag), self.boxes.at[0], (net.sib, net.c), self.base)

    def cross(self):
        net = self.net
        net.wait(self.base, self.boxes.at[0])
        block = self.mine(net.across)
        add_into(block, [block, self.boxes.at[0]])
        net.send(block, self.boxes.at[1], (net.across, net.c), self.base + 1)

    def keep(self):
        net = self.net
        net.send(self.mine(net.sib), self.boxes.at[2], (net.sib, net.c), self.base + 2)

    def finish(self):
        net = self.net
        net.wait(self.base + 2, self.boxes.at[2])
        net.wait(self.base + 1, self.boxes.at[1])
        return [self.mine(net.b), self.boxes.at[1], self.boxes.at[2]]


def row_of(parts, index):
    return jnp.concatenate([parts[j, index : index + 1, :] for j in range(NB)], axis=1)


def put_row(target, index, row):
    for j in range(NB):
        target[j, index : index + 1, :] = row[:, j * SHARD : (j + 1) * SHARD]


def rows_of(block, size):
    return lambda j: block.at[pl.ds(pl.multiple_of(j * size, size), size)]


def normalise(inputs):
    centre = inputs - jnp.mean(inputs, -1, keepdims=True)
    spread = jnp.mean(centre * centre, -1, keepdims=True)
    scale = lax.rsqrt(spread + epsilon)
    return centre * scale, scale


def head_lanes(h, rows):
    lane = lax.broadcasted_iota(jnp.int32, (rows, PAIR), 1)
    return (lane >= h * HEAD_DIM) & (lane < (h + 1) * HEAD_DIM)


QB = 256


log2_e = 1.4426950408889634


def scores_of(keys, query, masked):
    scores = mm(keys, query, NT) * (0.125 * log2_e)
    if masked:
        key_pos = lax.broadcasted_iota(jnp.int32, scores.shape, 0)
        query_pos = lax.broadcasted_iota(jnp.int32, scores.shape, 1)
        scores = jnp.where(key_pos <= query_pos, scores, masked_value)
    return scores


def attend(mix, value_t, att, lse, work, low_work, ready):
    value_t[...] = mix[:, 2 * PAIR :].astype(F32).T.astype(BF)
    for qb in reversed(range(LENGTH // QB)):
        here = slice(qb * QB, (qb + 1) * QB)
        outs = []
        for h in range(2):
            query = jnp.where(head_lanes(h, QB), mix[here, :PAIR], jnp.zeros((), BF))
            top = None
            for kb in range(qb + 1):
                keys = slice(kb * QB, (kb + 1) * QB)
                scores = scores_of(mix[keys, PAIR : 2 * PAIR], query, kb == qb)
                work[keys, :] = scores
                peak = jnp.max(scores, axis=0, keepdims=True)
                top = peak if top is None else jnp.maximum(top, peak)
            total = None
            for kb in range(qb + 1):
                keys = slice(kb * QB, (kb + 1) * QB)
                grown = jnp.exp2(work[keys, :] - top)
                part = jnp.sum(grown, axis=0, keepdims=True)
                total = part if total is None else total + part
                low_work[h, keys, :] = grown.astype(BF)
            count = (qb + 1) * QB
            lanes = slice(h * HEAD_DIM, (h + 1) * HEAD_DIM)
            out = mm(value_t[lanes, :count], low_work[h, :count, :])
            outs.append(out / total)
            lse[h * 4 + qb : h * 4 + qb + 1, :] = top + jnp.log2(total)
        att[here, :] = jnp.concatenate(outs, axis=0).T.astype(BF)
        ready(qb)


def attend_back(mix, key_t, dout, lse, gmix, grad_k, grad_v, work, more, low_work, low_more):
    key_t[...] = mix[:, PAIR : 2 * PAIR].astype(F32).T.astype(BF)
    grad_k[...] = jnp.zeros_like(grad_k)
    grad_v[...] = jnp.zeros_like(grad_v)
    for qb in reversed(range(LENGTH // QB)):
        here = slice(qb * QB, (qb + 1) * QB)
        outs = []
        count = (qb + 1) * QB
        for h in range(2):
            lanes = head_lanes(h, QB)
            query = jnp.where(lanes, mix[here, :PAIR], jnp.zeros((), BF))
            grad = jnp.where(lanes, dout[here, :], jnp.zeros((), BF))
            level = lse[h * 4 + qb : h * 4 + qb + 1, :]
            delta = None
            for kb in range(qb + 1):
                keys = slice(kb * QB, (kb + 1) * QB)
                probs = jnp.exp2(scores_of(mix[keys, PAIR : 2 * PAIR], query, kb == qb) - level)
                grad_probs = mm(mix[keys, 2 * PAIR :], grad, NT)
                part = jnp.sum(probs * grad_probs, axis=0, keepdims=True)
                delta = part if delta is None else delta + part
                work[keys, :] = probs
                more[keys, :] = grad_probs
                low_work[h, keys, :] = probs.astype(BF)
            for kb in range(qb + 1):
                keys = slice(kb * QB, (kb + 1) * QB)
                low_more[h, keys, :] = (work[keys, :] * (more[keys, :] - delta)).astype(BF)
            grad_v[:count, :] += mm(low_work[h, :count, :], grad)
            grad_k[:count, :] += mm(low_more[h, :count, :], query)
            rows = slice(h * HEAD_DIM, (h + 1) * HEAD_DIM)
            outs.append(mm(key_t[rows, :count], low_more[h, :count, :]) * 0.125)
        gmix[here, :PAIR] = jnp.concatenate(outs, axis=0).T.astype(BF)
        gmix[here, PAIR : 2 * PAIR] = (grad_k[here, :] * 0.125).astype(BF)
        gmix[here, 2 * PAIR :] = grad_v[here, :].astype(BF)


gelu_scale = 0.7978845608028654
gelu_cubic = 0.044715


def gelu_pair(x):
    square = x * x
    bent = jnp.tanh(gelu_scale * x * (1.0 + gelu_cubic * square))
    half = 0.5 * (1.0 + bent)
    slope = half + 0.5 * x * (1.0 - bent * bent) * (gelu_scale * (1.0 + 3.0 * gelu_cubic * square))
    return x * half, slope


VECTOR_ROWS = (1, 1, 2, 1, 1, 1, 4, 1)
SCRATCH = dict(
    tokens=((ROWS, WIDTH), BF),
    **{f"v{i}": ((rows * SHARD,), BF) for i, rows in enumerate(VECTOR_ROWS)},
    small=((SMALL_ROWS, SHARD), F32),
    parts=((NB, SMALL_ROWS, SHARD), F32),
    qv_rows=((16, PAIR), F32),
    wpair=((WIDTH, 3 * PAIR), BF),
    wfull=((WIDTH, 3 * WIDTH), BF),
    wproj_all=((WIDTH, WIDTH), BF),
    wfc_mine=((WIDTH, WIDTH), BF),
    wout_mine=((WIDTH, WIDTH), BF),
    g_all=((NB * ROWS, WIDTH), BF),
    hat_one=((ROWS, WIDTH), F32),
    scale_one=((ROWS, 1), F32),
    hat_all=((LENGTH, WIDTH), BF),
    n_one=((LENGTH, WIDTH), BF),
    mix=((LENGTH, 3 * PAIR), BF),
    turned=((PAIR, LENGTH), BF),
    att=((LENGTH, PAIR), BF),
    lse=((8, QB), F32),
    work=((LENGTH, QB), F32),
    more=((LENGTH, QB), F32),
    low_work=((2, LENGTH, QB), BF),
    low_more=((2, LENGTH, QB), BF),
    att_own=((ROWS, WIDTH), BF),
    middle=((ROWS, WIDTH), F32),
    hat_two=((ROWS, WIDTH), F32),
    scale_two=((ROWS, 1), F32),
    n_two=((NB * ROWS, WIDTH), BF),
    hidden=((NB * ROWS, WIDTH), BF),
    grad_pre=((NB * ROWS, WIDTH), BF),
    p_norm=((NB * ROWS, WIDTH), BF),
    p_norm_box=((3, ROWS, WIDTH), BF),
    p_layer=((NB * ROWS, WIDTH), BF),
    p_layer_box=((3, ROWS, WIDTH), BF),
    g_side=((NB * ROWS, WIDTH), BF),
    n_side=((NB * ROWS, WIDTH), BF),
    hidden_side=((NB * ROWS, WIDTH // 2), BF),
    pre_side=((NB * ROWS, WIDTH // 2), BF),
    p_out=((2, 256, WIDTH), BF),
    out_up=((2, 4, 64, WIDTH), BF),
    out_down=((2, 4, 64, WIDTH), BF),
    out_block=((ROWS, WIDTH), BF),
    p_fc=((2, NB, 4, 64, 256), BF),
    fc_up=((2, 4, NB, 64, 256), BF),
    fc_down=((2, 4, NB, 64, 256), BF),
    fc_sum=((2, NB, 64, 256), BF),
    fc_block=((2, 64, WIDTH), BF),
    p_proj=((WIDTH, WIDTH), BF),
    p_proj_box=((3, SHARD, WIDTH), BF),
    proj_sum=((SHARD, WIDTH), BF),
    proj_beside=((4, 32, WIDTH), BF),
    proj_up=((4, 32, WIDTH), BF),
    proj_down=((4, 32, WIDTH), BF),
    proj_block=((32, WIDTH), BF),
    grad_middle=((ROWS, WIDTH), F32),
    branch=((ROWS, WIDTH), BF),
    g_att=((ROWS, WIDTH), BF),
    dout=((LENGTH, PAIR), BF),
    gmix=((LENGTH, 3 * PAIR), BF),
    grad_k=((LENGTH, PAIR), F32),
    grad_v=((LENGTH, PAIR), F32),
    gmix_own=((NC, ROWS, 3 * PAIR), BF),
    gmix_all=((ROWS, 3 * WIDTH), BF),
    p_qkv=((WIDTH, 3 * PAIR), BF),
    p_qkv_box=((3, SHARD, 3 * PAIR), BF),
    qkv_block=((SHARD, 3 * PAIR), BF),
    gn_one=((ROWS, WIDTH), F32),
    gs=((NB, SMALL_ROWS, SHARD), F32),
    gqv=((16, PAIR), F32),
    gs_box=((NB, SMALL_ROWS, SHARD), F32),
    gs_sum=((SMALL_ROWS, SHARD), F32),
    gs_far=((NC, SMALL_ROWS, SHARD), F32),
)
SENDS, RECVS, LOCALS = 40, 180, 26


def layer_kernel(*refs):
    tokens, cotangent = refs[:2]
    vectors = refs[2:10]
    wqkv, wproj, wfc, wout = refs[10:14]
    layer_out, grad_tokens, grad_small, o_qkv, o_proj, o_fc, o_out = refs[14:21]
    scratch = refs[21:]
    s = SimpleNamespace(**dict(zip(SCRATCH, scratch)))
    send_sems, recv_sems, local_sems = scratch[len(SCRATCH) :]
    b, c = lax.axis_index("batch"), lax.axis_index("ctx")
    net = Net(b, c, send_sems, recv_sems)
    v = SimpleNamespace(keep=[])
    locals_open = []

    def local(src, dst):
        copy = pltpu.make_async_copy(src, dst, local_sems.at[len(locals_open)])
        copy.start()
        locals_open.append(copy)
        return copy

    def own(ref, size):
        return rows_of(ref, size)(b)

    def cols(ref, start, count=PAIR):
        return ref.at[:, pl.ds(pl.multiple_of(start, 128), count)]

    def halves(ref, size, j):
        block = rows_of(ref, size)(j)
        return [block.at[0 : size // 2], block.at[size // 2 : size]]

    def loop(count, size, body):
        def step(i, carry):
            body(pl.ds(pl.multiple_of(i * size, size), size))
            return carry

        lax.fori_loop(0, count, step, 0)

    batch_others = [lax.rem(b + i, NB) for i in range(1, NB)]

    small_slot, fc_slots, fc_side_slots = net.slots(1), net.slots(2 * NB), net.slots(NB)
    hidden_slots, pre_slots, side_slot, swap_slots = net.slots(4), net.slots(4), net.slots(2), net.slots(2)
    proj_slots, proj_side_slot, proj_near_slots = net.slots(NB), net.slots(1), net.slots(2)
    gs_slot, far_slot = net.slots(1), net.slots(1)
    gather_pair = GatherBatch(net, lambda j: [rows_of(s.wpair, SHARD)(j)])
    gather_one = GatherCtx(net, lambda j: halves(s.hat_all, ROWS, j), s.hat_all.at[: 3 * ROWS], 2, True)
    gather_g = GatherBatch(net, lambda j: [rows_of(s.g_all, ROWS)(j)])
    gather_gs = GatherBatch(net, lambda j: [rows_of(s.g_side, ROWS)(j)])
    gather_ns = GatherBatch(net, lambda j: [rows_of(s.n_side, ROWS)(j)])
    gather_two = GatherBatch(net, lambda j: halves(s.n_two, ROWS, j), 2)
    gather_full = [
        GatherBatch(net, lambda j, i=i: [rows_of(s.wfull, SHARD // 2)(2 * j + i)]) for i in range(2)
    ]
    swap_att = SwapCtx(
        net, rows_of(s.att, ROWS), lambda j: cols(s.att_own, j * PAIR), s.att_own.at[:, : 7 * PAIR]
    )
    swap_grad = SwapCtx(
        net, lambda j: cols(s.g_att, j * PAIR), rows_of(s.dout, ROWS), s.dout.at[: 7 * ROWS]
    )
    swap_mix = SwapCtx(
        net, rows_of(s.gmix, ROWS), lambda j: s.gmix_own.at[j], s.gmix_own.at[:7]
    )
    reduce_norm = ReduceBatch(net, rows_of(s.p_norm, ROWS), s.p_norm_box)
    reduce_layer = ReduceBatch(net, rows_of(s.p_layer, ROWS), s.p_layer_box)
    reduce_proj = ReduceBatch(net, rows_of(s.p_proj, SHARD), s.p_proj_box)
    reduce_qkv = ReduceBatch(net, rows_of(s.p_qkv, SHARD), s.p_qkv_box)
    reduce_part = ReduceCtx(net, rows_of(s.proj_sum, 32), s.proj_beside, s.proj_up, s.proj_down)
    reduce_out = [
        ReduceLine(net, rows_of(s.p_out.at[i], 64), s.out_up.at[i], s.out_down.at[i]) for i in range(2)
    ]
    reduce_fc = [
        ReduceLine(net, lambda k, i=i: s.p_fc.at[i, :, k], s.fc_up.at[i], s.fc_down.at[i])
        for i in range(2)
    ]

    def out_view(i, j):
        return rows_of(o_out, 64)(8 * (j % 2) + 4 * i + j // 2)

    def fc_view(i, j):
        return o_fc.at[j % 2, i, pl.ds(pl.multiple_of((j // 2) * 64, 64), 64)]

    gather_out = [GatherCtx(net, lambda j, i=i: [out_view(i, j)], o_out.at[:256], 1) for i in range(2)]
    gather_fc = [GatherCtx(net, lambda j, i=i: [fc_view(i, j)], o_fc.at[0, 0, : 256 - 128 * i], 1, i == 1) for i in range(2)]
    gather_qkv = GatherCtx(net, lambda j: halves(o_qkv.at[j], SHARD, 0), o_qkv.at[:3], 2, True)
    gather_part = GatherCtx(net, lambda j: [rows_of(o_proj, 32)(j)], o_proj.at[:128], 1)

    scale, hat = s.scale_one, s.hat_one
    half, pair_z = net.z % 2, (b, c + 2 - 4 * (net.z % 2))
    fc_rows = [
        pl.ds(pl.multiple_of(SHARD // 2 + x * (SHARD // 4), SHARD // 4), SHARD // 4) for x in (half, 1 - half)
    ]
    side_rows = pl.ds(pl.multiple_of(half * (SHARD // 2), SHARD // 2), SHARD // 2)
    other_side_rows = pl.ds(pl.multiple_of((1 - half) * (SHARD // 2), SHARD // 2), SHARD // 2)
    chip_rows = [
        pl.ds(pl.multiple_of(first * 256, 256), 256) for first in (b // 2, 1 - b // 2)
    ]
    hat_mine = rows_of(s.hat_all, ROWS)(c)
    n_two_mine = own(s.n_two, ROWS)
    g_mine = own(s.g_all, ROWS)
    n_beside = own(s.n_side, ROWS)

    def enter():
        barrier = pltpu.get_barrier_semaphore()
        others = [(j, c) for j in batch_others]
        others += [(b, lax.rem(c + i, NC)) for i in range(1, NC)]
        for device in others:
            pl.semaphore_signal(barrier, inc=1, device_id=device, device_id_type=MESH)
        get_tokens = local(tokens, s.tokens)
        own_vectors = [getattr(s, f"v{i}") for i in range(len(vectors))]
        get_vectors = [local(one, two) for one, two in zip(vectors, own_vectors)]
        get_pair = [
            local(cols(wqkv, t * WIDTH + c * PAIR), own(s.wpair, SHARD).at[:, t * PAIR : (t + 1) * PAIR])
            for t in range(3)
        ]
        v.get_proj = local(wproj, own(s.wproj_all, SHARD))
        v.get_rest = [
            local(cols(wfc, b * WIDTH, WIDTH), own(s.wfc_mine, SHARD)),
            local(wout, s.wout_mine),
            local(wqkv, own(s.wfull, SHARD)),
            local(cotangent, g_mine),
        ]
        s.small[...] = jnp.zeros_like(s.small)
        for copy in get_vectors:
            copy.wait()
        row = 0
        for vector in own_vectors:
            for i in range(vector.shape[0] // SHARD):
                piece = vector[i * SHARD : (i + 1) * SHARD].astype(F32)
                s.small[row : row + 1, :] = piece.reshape(1, SHARD)
                row += 1

        def norm_rows(at):
            hat[at, :], scale[at, :] = normalise(s.tokens[at, :].astype(F32))
            hat_mine[at, :] = hat[at, :].astype(BF)

        get_tokens.wait()
        loop(ROWS // 32, 32, norm_rows)
        for copy in get_pair:
            copy.wait()
        s.parts[pl.ds(b, 1)] = s.small[...][None]
        pl.semaphore_wait(barrier, len(others))

    def send_small():
        for j in batch_others:
            net.send(s.small, s.parts.at[b], (j, c), small_slot)

    def pair_start():
        gather_pair.start([own(s.wpair, SHARD)])

    def g_start():
        gather_g.start([cotangent])

    def one_start():
        gather_one.start(halves(s.hat_all, ROWS, c))

    def small_wait():
        net.wait(small_slot, s.parts.at[: NB - 1])
        v.gain, v.bias = row_of(s.parts, 0), row_of(s.parts, 1)

    def proj_start():
        mine = own(s.wproj_all, SHARD)
        net.send(wproj.at[side_rows], mine.at[side_rows], (net.across, c), proj_slots + b)
        net.send(wproj, mine, (net.sib, c), proj_slots + b)

    def proj_relay():
        block = rows_of(s.wproj_all, SHARD)(net.across).at[side_rows]
        net.wait(proj_slots + net.across, block)
        net.send(block, block, pair_z, proj_side_slot)
        net.send(block, block, (net.sib, c), proj_near_slots)

    def proj_side():
        block = rows_of(s.wproj_all, SHARD)(net.across).at[other_side_rows]
        net.wait(proj_side_slot, block)
        net.send(block, block, (net.sib, c), proj_near_slots + 1)

    def fc_start(i):
        at = [slice(0, SHARD // 2), fc_rows[0]][i]
        for j in (net.across, net.diag):
            cut = wfc.at[at, pl.ds(pl.multiple_of(j * WIDTH, WIDTH), WIDTH)]
            net.send(cut, own(s.wfc_mine, SHARD).at[at], (j, c), fc_slots + 2 * b + i)
        if i == 0:
            net.send(cols(wfc, net.sib * WIDTH, WIDTH), own(s.wfc_mine, SHARD), (net.sib, c), fc_slots + 2 * b)

    def fc_relay():
        for j in (net.across, net.diag):
            block = rows_of(s.wfc_mine, SHARD)(j).at[fc_rows[0]]
            net.wait(fc_slots + 2 * j + 1, block)
            net.send(block, block, pair_z, fc_side_slots + j)

    def qv_rows():
        for p in range(NC):
            at = p * PAIR
            row, lane = 2 + (at % 512) // SHARD, at % SHARD
            s.qv_rows[p : p + 1, :] = s.parts[at // 512, row : row + 1, lane : lane + PAIR]
            s.qv_rows[8 + p : 9 + p, :] = s.parts[2 + at // 512, row : row + 1, lane : lane + PAIR]

    def g_relay():
        gather_g.relay()

    def gs_give():
        net.send(cotangent, own(s.g_side, ROWS), (b, net.side), side_slot + 1)

    def gs_start():
        net.wait(side_slot + 1, own(s.g_side, ROWS))
        gather_gs.start([own(s.g_side, ROWS)])

    def mix_block(j):
        rows = pl.ds(pl.multiple_of(j * ROWS, ROWS), ROWS)
        mix_bias = jnp.concatenate(
            [s.qv_rows[pl.ds(c, 1), :], jnp.zeros((1, PAIR), F32), s.qv_rows[pl.ds(8 + c, 1), :]], axis=1
        )
        s.n_one[rows, :] = (s.hat_all[rows, :].astype(F32) * v.gain + v.bias).astype(BF)
        s.mix[rows, :] = (mm(s.n_one[rows, :], s.wpair[...]) + mix_bias).astype(BF)

    def mix_at(d):
        if d == 0:
            mix_block(c)
        for zz in (net.z - d, net.z + d)[: 2 * d]:

            @pl.when(jnp.logical_and(zz >= 0, zz <= 3))
            def _():
                mix_block(2 * zz + net.x)

    def mix_side():
        def step(zz, carry):
            mix_block(2 * zz + 1 - net.x)
            return carry

        lax.fori_loop(0, 4, step, 0)

    def att():
        def ready(qb):
            swap_att.give(2 * qb)
            swap_att.give(2 * qb + 1)

        attend(s.mix, s.turned, s.att, s.lse, s.work, s.low_work, ready)

    def proj_finish():
        v.get_proj.wait()
        net.wait(proj_slots + net.sib, rows_of(s.wproj_all, SHARD)(net.sib))
        block = rows_of(s.wproj_all, SHARD)(net.diag)
        net.wait(proj_near_slots, block.at[side_rows])
        net.wait(proj_near_slots + 1, block.at[other_side_rows])

    def middle():
        def middle_cols(at):
            s.middle[:, at] = mm(s.att_own[...], s.wproj_all[:, at]) + s.tokens[:, at].astype(F32)

        loop(WIDTH // 256, 256, middle_cols)
        proj_bias, gain_two, bias_two = row_of(s.parts, 4), row_of(s.parts, 5), row_of(s.parts, 6)

        def norm_two_rows(at):
            middle = s.middle[at, :] + proj_bias
            s.middle[at, :] = middle
            norm, width = normalise(middle)
            s.hat_two[at, :], s.scale_two[at, :] = norm, width
            n_two_mine[at, :] = (norm * gain_two + bias_two).astype(BF)

        loop(ROWS // 32, 32, norm_two_rows)
        gather_two.start(halves(s.n_two, ROWS, b))

    def ns_give():
        net.send(n_two_mine, n_beside, (b, net.side), side_slot)

    def ns_start():
        net.wait(side_slot, n_beside)
        gather_ns.start([n_beside])

    def feed_wait():
        for copy in v.get_rest:
            copy.wait()
        gather_g.finish()
        net.wait(fc_slots + 2 * net.sib, rows_of(s.wfc_mine, SHARD)(net.sib))
        for j in (net.across, net.diag):
            block = rows_of(s.wfc_mine, SHARD)(j)
            net.wait(fc_slots + 2 * j, block.at[0 : SHARD // 2])
            net.wait(fc_side_slots + j, block.at[fc_rows[1]])
        s.gs[...] = jnp.zeros_like(s.gs)

    def feed_cols(r, i):
        n = lax.rem(2 * (1 - net.x) + i, 4)
        rows, at = chip_rows[r], pl.ds(pl.multiple_of(n * 256, 256), 256)
        pre = mm(s.n_two[rows, :], s.wfc_mine[:, at]) + s.small[pl.ds(7 + n, 1), :]
        value, slope = gelu_pair(pre)
        s.hidden[rows, at] = value.astype(BF)
        grad = (mm(s.g_all[rows, :], s.wout_mine[at, :], NT) * slope).astype(BF)
        s.grad_pre[rows, at] = grad
        s.gs[pl.ds(b, 1), pl.ds(7 + n, 1), :] += jnp.sum(grad.astype(F32), 0, keepdims=True)[None]

    def tile(ref, r, i):
        return ref.at[chip_rows[r], pl.ds(pl.multiple_of((2 * (1 - net.x) + i) * 256, 256), 256)]

    def side_tile(ref, r, i):
        return ref.at[chip_rows[r], i * 256 : (i + 1) * 256]

    def feed_i(r, i):
        feed_cols(r, i)
        net.send(tile(s.hidden, r, i), side_tile(s.hidden_side, r, i), (b, net.side), hidden_slots + 2 * r + i)

    def pre_give(r, i):
        net.send(tile(s.grad_pre, r, i), side_tile(s.pre_side, r, i), (b, net.side), pre_slots + 2 * r + i)

    def feed_rest(r):
        def step(i, carry):
            feed_cols(r, i)
            return carry

        lax.fori_loop(2, 4, step, 0)

    def norm_block(j):
        at = pl.ds(pl.multiple_of(j * ROWS, ROWS), ROWS)
        s.p_norm[at, :] = mm(s.grad_pre[at, :], s.wfc_mine[...], NT).astype(BF)

    def norm_diag():
        norm_block(net.diag)
        reduce_norm.give()

    def norm_across():
        norm_block(net.across)

    def norm_sib():
        norm_block(net.sib)
        reduce_norm.keep()

    def norm_own():
        norm_block(b)

    def back_two():
        gain_two = row_of(s.parts, 5)
        terms = reduce_norm.finish()

        def back_rows(i, carry):
            at = pl.ds(pl.multiple_of(i * 32, 32), 32)
            grad_gain, grad_bias, sum_branch, sum_g = carry
            grad = terms[0][at, :].astype(F32) + terms[1][at, :].astype(F32) + terms[2][at, :].astype(F32)
            norm = s.hat_two[at, :]
            scaled = grad * gain_two
            inner = scaled - jnp.mean(scaled, -1, keepdims=True)
            inner = inner - norm * jnp.mean(scaled * norm, -1, keepdims=True)
            g = g_mine[at, :].astype(F32)
            total = g + s.scale_two[at, :] * inner
            s.grad_middle[at, :] = total
            low = total.astype(BF)
            s.branch[at, :] = low
            return (
                grad_gain + jnp.sum(grad * norm, 0, keepdims=True),
                grad_bias + jnp.sum(grad, 0, keepdims=True),
                sum_branch + jnp.sum(low.astype(F32), 0, keepdims=True),
                sum_g + jnp.sum(g, 0, keepdims=True),
            )

        sums = lax.fori_loop(0, ROWS // 32, back_rows, (jnp.zeros((1, WIDTH), F32),) * 4)
        put_row(s.gs, 5, sums[0])
        put_row(s.gs, 6, sums[1])
        put_row(s.gs, 4, sums[2])
        put_row(s.gs, 11, sums[3])

        def att_cols(at):
            s.g_att[:, at] = mm(s.branch[...], s.wproj_all[at, :], NT).astype(BF)

        loop(4, 256, att_cols)
        swap_grad.start()

    def p_out(i):
        at = slice(i * 256, (i + 1) * 256)
        for r in range(2):
            net.wait(hidden_slots + 2 * r + i, side_tile(s.hidden_side, r, i))
        mine = cols(s.hidden, net.x * 512 + i * 256, 256)
        s.p_out[i] = (
            mm(mine[...], s.g_all[...], TN) + mm(s.hidden_side[:, at], s.g_side[...], TN)
        ).astype(BF)

    def out_done(i):
        part = s.out_block.at[i * 64 : (i + 1) * 64]
        reduce_out[i].finish(part)
        gather_out[i].begin(0, part)
        v.keep.append(local(part, out_view(i, c)))

    def p_fc(i):
        at = slice(i * 256, (i + 1) * 256)
        for r in range(2):
            net.wait(pre_slots + 2 * r + i, side_tile(s.pre_side, r, i))
        mine = cols(s.grad_pre, net.x * 512 + i * 256, 256)

        def fc_rows(k, carry):
            rows = pl.ds(pl.multiple_of(k * 256, 256), 256)
            total = mm(s.n_two[:, rows], mine[...], TN) + mm(s.n_side[:, rows], s.pre_side[:, at], TN)
            s.p_fc[i, pl.ds(k, 1)] = total.astype(BF).reshape(1, 4, 64, 256)
            return carry

        lax.fori_loop(0, 4, fc_rows, 0)

    def fc_done(i):
        reduce_fc[i].finish(s.fc_sum.at[i])
        mine = pl.ds(pl.multiple_of(b * 256, 256), 256)
        for j in batch_others:
            net.send(s.fc_sum.at[i, j], s.fc_block.at[i, :, mine], (j, c), swap_slots + i)
        s.fc_block[i, :, mine] = s.fc_sum[i, pl.ds(b, 1)][0]

    def fc_swap(i):
        net.wait(swap_slots + i, s.fc_block.at[i, :, : (NB - 1) * 256])
        gather_fc[i].begin(0, s.fc_block.at[i])
        v.keep.append(local(s.fc_block.at[i], fc_view(i, c)))

    def p_proj():
        def proj_rows(at):
            s.p_proj[at, :] = mm(s.att_own[:, at], s.branch[...], TN).astype(BF)

        loop(4, 256, proj_rows)
        reduce_proj.give()
        reduce_proj.keep()

    def proj_done():
        add_into(s.proj_sum, reduce_proj.finish())
        reduce_part.start()

    def part_done():
        reduce_part.line.finish(s.proj_block)
        gather_part.begin(0, s.proj_block)
        v.keep.append(local(s.proj_block, rows_of(o_proj, 32)(c)))

    def p_layer():
        def layer_block(j):
            at = pl.ds(pl.multiple_of(j * ROWS, ROWS), ROWS)
            s.p_layer[at, :] = mm(s.hidden[at, :], s.wout_mine[...]).astype(BF)

        layer_block(net.diag)
        reduce_layer.give()
        layer_block(net.sib)
        reduce_layer.keep()
        layer_block(net.across)
        layer_block(b)

    def layer_end():
        layer_bias = row_of(s.parts, 11)
        terms = reduce_layer.finish()

        def layer_rows(at):
            total = terms[0][at, :].astype(F32) + terms[1][at, :].astype(F32) + terms[2][at, :].astype(F32)
            layer_out[at, :] = (s.middle[at, :] + total + layer_bias).astype(BF)

        loop(ROWS // 32, 32, layer_rows)

    def att_back():
        attend_back(
            s.mix, s.turned, s.dout, s.lse, s.gmix, s.grad_k, s.grad_v,
            s.work, s.more, s.low_work, s.low_more,
        )

    def mix_give(k):
        swap_mix.give(2 * k)
        swap_mix.give(2 * k + 1)

    def p_qkv():
        def qkv_block(j):
            at = pl.ds(pl.multiple_of(j * SHARD, SHARD), SHARD)
            s.p_qkv[at, :] = mm(s.n_one[:, at], s.gmix[...], TN).astype(BF)

        qkv_block(net.diag)
        reduce_qkv.give()
        qkv_block(net.across)
        qkv_block(net.sib)
        reduce_qkv.keep()
        qkv_block(b)

    def qkv_done():
        terms = reduce_qkv.finish()
        add_into(s.qkv_block, terms)
        gather_qkv.start(halves(s.qkv_block, SHARD, 0))
        v.keep.append(local(s.qkv_block, o_qkv.at[c]))

    def gqv():
        s.gqv[...] = jnp.zeros_like(s.gqv)
        s.gqv[pl.ds(c, 1), :] = jnp.sum(s.gmix[:, :PAIR].astype(F32), 0, keepdims=True)
        s.gqv[pl.ds(8 + c, 1), :] = jnp.sum(s.gmix[:, 2 * PAIR :].astype(F32), 0, keepdims=True)
        for p in range(NC):
            at = p * PAIR
            row, lane = 2 + (at % 512) // SHARD, at % SHARD
            s.gs[at // 512, row : row + 1, lane : lane + PAIR] = s.gqv[p : p + 1, :]
            s.gs[2 + at // 512, row : row + 1, lane : lane + PAIR] = s.gqv[8 + p : 9 + p, :]

    def full_start(i):
        gather_full[i].start([rows_of(wqkv, SHARD // 2)(i)])

    def grad_in():
        for gather in gather_full:
            gather.finish()
        swap_mix.finish()
        for j in range(NC):
            for t in range(3):
                to, at = t * WIDTH + j * PAIR, t * PAIR
                s.gmix_all[:, to : to + PAIR] = s.gmix_own[j, :, at : at + PAIR]
        gain = v.gain

        def one_cols(at):
            s.gn_one[:, at] = mm(s.gmix_all[...], s.wfull[at, :], NT)

        loop(4, 256, one_cols)

        def token_rows(i, carry):
            at = pl.ds(pl.multiple_of(i * 32, 32), 32)
            grad_gain, grad_bias = carry
            grad, norm = s.gn_one[at, :], s.hat_one[at, :]
            scaled = grad * gain
            inner = scaled - jnp.mean(scaled, -1, keepdims=True)
            inner = inner - norm * jnp.mean(scaled * norm, -1, keepdims=True)
            grad_tokens[at, :] = (s.grad_middle[at, :] + s.scale_one[at, :] * inner).astype(BF)
            return (
                grad_gain + jnp.sum(grad * norm, 0, keepdims=True),
                grad_bias + jnp.sum(grad, 0, keepdims=True),
            )

        sums = lax.fori_loop(0, ROWS // 32, token_rows, (jnp.zeros((1, WIDTH), F32),) * 2)
        put_row(s.gs, 0, sums[0])
        put_row(s.gs, 1, sums[1])
        for j in batch_others:
            net.send(s.gs.at[j], s.gs_box.at[b], (j, c), gs_slot)

    def gs_sum():
        total = s.gs[pl.ds(b, 1)][0]
        net.wait(gs_slot, s.gs_box.at[: NB - 1])
        for j in batch_others:
            total = total + s.gs_box[pl.ds(j, 1)][0]
        s.gs_sum[...] = total
        for i in range(1, NC):
            j = lax.rem(c + i, NC)
            net.send(s.gs_sum, s.gs_far.at[c], (b, j), far_slot)

    def far_sum():
        total = s.gs_sum[...]
        net.wait(far_slot, s.gs_far.at[: NC - 1])
        for i in range(1, NC):
            j = lax.rem(c - i + NC, NC)
            total = total + s.gs_far[pl.ds(j, 1)][0]
        grad_small[...] = total

    enter()
    one_start()
    proj_start()
    pair_start()
    g_start()
    gather_one.stage(1,-1)
    gather_one.corner()
    gather_one.stage(1,1)
    gather_one.stage(2,-1)
    gather_one.pass_on(1)
    send_small()
    gather_pair.relay()
    gather_one.stage(2,1)
    gather_one.pass_on(2)
    proj_relay()
    gather_one.stage(3,-1)
    small_wait()
    gather_one.stage(3,1)
    gs_give()
    gather_pair.finish()
    qv_rows()
    fc_start(1)
    fc_start(0)
    mix_at(0)
    mix_at(1)
    mix_at(2)
    mix_at(3)
    gather_one.pass_on(3)
    gather_one.finish()
    mix_side()
    att()
    proj_side()
    g_relay()
    proj_finish()
    swap_att.finish()
    fc_relay()
    middle()
    ns_give()
    gather_two.near()
    gs_start()
    feed_wait()
    feed_i(0,0)
    gather_two.relay()
    gather_two.far()
    feed_i(1,0)
    feed_i(0,1)
    feed_i(1,1)
    ns_start()
    pre_give(1,1)
    feed_rest(1)
    gather_gs.relay()
    pre_give(1,0)
    feed_rest(0)
    gather_gs.finish()
    p_out(0)
    reduce_out[0].launch(0)
    reduce_out[0].launch(1)
    norm_diag()
    norm_sib()
    norm_across()
    reduce_norm.cross()
    reduce_out[0].pass_one(0)
    pre_give(0,0)
    reduce_out[0].pass_one(1)
    p_out(1)
    reduce_out[1].launch(0)
    reduce_out[0].launch(2)
    reduce_out[1].launch(1)
    gather_ns.relay()
    norm_own()
    reduce_out[1].pass_one(0)
    reduce_out[0].pass_two()
    pre_give(0,1)
    back_two()
    p_proj()
    out_done(0)
    gather_ns.finish()
    reduce_proj.cross()
    reduce_out[1].launch(2)
    p_fc(0)
    reduce_fc[0].launch(0)
    reduce_out[1].pass_one(1)
    reduce_out[1].pass_two()
    gather_out[0].stage(1,1)
    p_fc(1)
    reduce_fc[1].launch(0)
    reduce_fc[0].launch(1)
    full_start(1)
    gather_out[0].stage(1,-1)
    reduce_fc[1].launch(1)
    out_done(1)
    reduce_fc[1].launch(2)
    swap_grad.finish()
    gather_out[0].stage(2,1)
    reduce_fc[0].pass_one(0)
    att_back()
    mix_give(3)
    mix_give(0)
    proj_done()
    reduce_fc[1].pass_one(0)
    gather_out[1].stage(1,-1)
    reduce_fc[0].pass_one(1)
    reduce_fc[0].pass_two()
    reduce_fc[1].pass_one(1)
    p_qkv()
    reduce_fc[1].pass_two()
    gather_out[0].stage(2,-1)
    reduce_qkv.cross()
    gather_out[1].stage(1,1)
    reduce_fc[0].launch(2)
    reduce_part.fold()
    reduce_part.line.launch(0)
    reduce_part.line.launch(1)
    gather_out[1].stage(2,-1)
    gather_out[0].stage(3,1)
    reduce_part.line.pass_one(0)
    fc_done(0)
    reduce_part.line.launch(2)
    qkv_done()
    reduce_part.line.pass_one(1)
    fc_done(1)
    reduce_part.line.pass_two()
    gather_out[0].stage(3,-1)
    fc_swap(0)
    fc_swap(1)
    full_start(0)
    gather_qkv.stage(1,-1)
    gather_out[1].stage(2,1)
    gather_fc[0].stage(1,1)
    gather_full[1].relay()
    part_done()
    mix_give(1)
    gather_fc[1].stage(1,1)
    gather_fc[1].corner()
    gather_qkv.stage(1,1)
    gather_part.stage(1,1)
    mix_give(2)
    gather_fc[0].stage(1,-1)
    gather_qkv.stage(2,-1)
    gather_out[1].stage(3,1)
    gather_fc[1].stage(1,-1)
    p_layer()
    gather_full[0].relay()
    gqv()
    gather_fc[0].stage(2,1)
    gather_fc[0].stage(2,-1)
    gather_qkv.corner()
    reduce_layer.cross()
    gather_out[1].stage(3,-1)
    gather_qkv.stage(3,-1)
    gather_fc[1].stage(2,1)
    gather_part.stage(1,-1)
    gather_fc[1].stage(2,-1)
    gather_fc[1].pass_on(1)
    grad_in()
    gather_qkv.stage(2,1)
    gather_part.stage(2,1)
    gather_fc[0].stage(3,1)
    gather_part.stage(2,-1)
    gather_qkv.pass_on(1)
    gather_fc[1].pass_on(2)
    gather_fc[0].stage(3,-1)
    layer_end()
    gs_sum()
    gather_qkv.pass_on(2)
    gather_part.stage(3,-1)
    gather_qkv.stage(3,1)
    gather_part.stage(3,1)
    gather_fc[1].stage(3,-1)
    far_sum()
    gather_fc[1].pass_on(3)
    gather_fc[1].stage(3,1)
    gather_qkv.pass_on(3)
    for gather in gather_out + gather_fc + [gather_qkv, gather_part]:
        gather.finish()
    for copy in v.keep:
        copy.wait()
    net.drain()


PARTS = 4


def widen_kernel(layer, grad_in, small, w_qkv, w_proj, w_fc, w_out, *refs):
    o_layer, o_grad_in, o_qkv, o_proj, o_fc, o_out = refs[:6]
    vectors, rows, (qkv, proj, fc, out, sems) = refs[6:14], refs[14:22], refs[22:]
    leaving = []

    def leave(src, dst):
        copy = pltpu.make_async_copy(src, dst, sems.at[len(leaving)])
        copy.start()
        leaving.append(copy)

    row = 0
    for vector, here in zip(vectors, rows):
        for i in range(vector.shape[0] // SHARD):
            here[i * SHARD : (i + 1) * SHARD] = small[row, :]
            row += 1
        leave(here, vector)
    leave(layer, o_layer)
    leave(grad_in, o_grad_in)
    for k in range(PARTS):
        wide, at = slice(k * 256, (k + 1) * 256), slice(k * 64, (k + 1) * 64)
        out[wide, :] = w_out[wide, :].astype(F32)
        leave(out.at[wide], o_out.at[wide])
        for j in range(NB):
            for x in range(2):
                for i in range(2):
                    to = j * WIDTH + x * 512 + i * 256
                    fc[at, to : to + 256] = w_fc[x, i, at, j * 256 : (j + 1) * 256].astype(F32)
        leave(fc.at[at], o_fc.at[at])
        for j in range(NC):
            for t in range(3):
                to = t * WIDTH + j * PAIR
                qkv[at, to : to + PAIR] = w_qkv[j, at, t * PAIR : (t + 1) * PAIR].astype(F32)
        leave(qkv.at[at], o_qkv.at[at])
        proj[at, :] = w_proj[at, :].astype(F32)
        leave(proj.at[at], o_proj.at[at])
    for copy in leaving:
        copy.wait()


def per_device_fast(
    tokens, cotangent, ln1_gain, ln1_bias, qkv_weight, qv_bias, proj_weight, proj_bias,
    ln2_gain, ln2_bias, fc_weight, fc_bias, out_weight, out_bias,
):
    vmem, anywhere = pl.BlockSpec(memory_space=pltpu.VMEM), pl.BlockSpec(memory_space=pl.ANY)
    shape = jax.ShapeDtypeStruct
    layer, grad_in, grad_small, w_qkv, w_proj, w_fc, w_out = pl.pallas_call(
        layer_kernel,
        out_shape=(
            pltpu.VMEM((ROWS, WIDTH), BF),
            pltpu.VMEM((ROWS, WIDTH), BF),
            pltpu.VMEM((SMALL_ROWS, SHARD), F32),
            pltpu.VMEM((NC, SHARD, 3 * PAIR), BF),
            pltpu.VMEM((SHARD, WIDTH), BF),
            pltpu.VMEM((2, 2, SHARD, WIDTH), BF),
            pltpu.VMEM((FF // NB, WIDTH), BF),
        ),
        in_specs=[anywhere] * 14,
        out_specs=(vmem,) * 7,
        scratch_shapes=[pltpu.VMEM(*item) for item in SCRATCH.values()]
        + [
            pltpu.SemaphoreType.DMA((SENDS,)),
            pltpu.SemaphoreType.DMA((RECVS,)),
            pltpu.SemaphoreType.DMA((LOCALS,)),
        ],
        compiler_params=pltpu.CompilerParams(
            collective_id=0, has_side_effects=True, vmem_limit_bytes=LAYER_VMEM
        ),
    )(
        tokens.reshape(ROWS, WIDTH), cotangent.reshape(ROWS, WIDTH),
        ln1_gain, ln1_bias, qv_bias, proj_bias, ln2_gain, ln2_bias, fc_bias, out_bias,
        qkv_weight, proj_weight, fc_weight, out_weight,
    )
    layer, grad_in, w_qkv, w_proj, w_fc, w_out, *vectors = pl.pallas_call(
        widen_kernel,
        out_shape=(
            shape((ROWS, WIDTH), BF),
            shape((ROWS, WIDTH), BF),
            shape((SHARD, 3 * WIDTH), F32),
            shape((SHARD, WIDTH), F32),
            shape((SHARD, FF), F32),
            shape((FF // NB, WIDTH), F32),
            *[shape((n * SHARD,), F32) for n in VECTOR_ROWS],
        ),
        in_specs=[vmem] * 7,
        out_specs=(anywhere,) * (6 + len(VECTOR_ROWS)),
        scratch_shapes=[
            *[pltpu.VMEM((n * SHARD,), F32) for n in VECTOR_ROWS],
            pltpu.VMEM((SHARD, 3 * WIDTH), F32),
            pltpu.VMEM((SHARD, WIDTH), F32),
            pltpu.VMEM((SHARD, FF), F32),
            pltpu.VMEM((FF // NB, WIDTH), F32),
            pltpu.SemaphoreType.DMA((4 * PARTS + 2 + len(VECTOR_ROWS),)),
        ],
        compiler_params=pltpu.CompilerParams(vmem_limit_bytes=WIDEN_VMEM),
    )(layer, grad_in, grad_small, w_qkv, w_proj, w_fc, w_out)
    return (
        layer.reshape(tokens.shape),
        grad_in.reshape(tokens.shape),
        vectors[0],
        vectors[1],
        w_qkv,
        vectors[2],
        w_proj,
        vectors[3],
        vectors[4],
        vectors[5],
        w_fc,
        vectors[6],
        w_out,
        vectors[7],
    )


LAYER_VMEM, WIDEN_VMEM = 55 * 1024 * 1024, 20 * 1024 * 1024


def solution(mesh):
    placed = (
        P("batch", "ctx", None),
        P("batch", "ctx", None),
        P("batch"),
        P("batch"),
        P("batch", None),
        P("batch"),
        P("batch", None),
        P("batch"),
        P("batch"),
        P("batch"),
        P("batch", None),
        P("batch"),
        P("batch", None),
        P("batch"),
    )
    fits = dict(mesh.shape) == {"batch": NB, "ctx": NC}
    return jax.shard_map(
        per_device_fast if fits else per_device,
        mesh=mesh,
        in_specs=placed,
        out_specs=(
            P("batch", "ctx", None),
            P("batch", "ctx", None),
            P("batch"),
            P("batch"),
            P("batch", None),
            P("batch"),
            P("batch", None),
            P("batch"),
            P("batch"),
            P("batch"),
            P("batch", None),
            P("batch"),
            P("batch", None),
            P("batch"),
        ),
        check_vma=False,
    )
```
